32 devices in a mesh: rows: 4 (over z), cols: 8 (over y, x, core).
Axes of the slice: x: 2, y: 2, z: 4, core: 2. Of those that a mesh axis runs over, the one named last changes fastest.
Arguments:
- latents: bfloat16 [2048, 1024], P(('rows', 'cols')), may hold values from -6 to 6
- pixel_colors: bfloat16 [3, 4, 288, 72], P(None, None, 'rows', 'cols'), may hold values from -4 to 4
- image_boxes: int32 [4, 4], replicated, may hold values from 0 to 288, as said below
- cotangent: bfloat16 [2048, 1024], P(('rows', 'cols')), may hold values from -6 to 6
- cross_matrices: bfloat16 [3, 1024, 1024], replicated, may hold values from -0.1875 to 0.1875
- cross_out: bfloat16 [1024, 1024], replicated, may hold values from -0.5 to 0.5
- input_matrices: bfloat16 [2, 261, 1024], replicated, may hold values from -0.375 to 0.375
- in_gain: bfloat16 [261], replicated, may hold values from 0.5 to 1.5
- in_bias: bfloat16 [261], replicated, may hold values from -1.5 to 1.5
- cross_gains: bfloat16 [2, 1024], replicated, may hold values from 0.5 to 1.5
- cross_biases: bfloat16 [7, 1024], replicated, may hold values from -1.5 to 1.5
- self_matrices: bfloat16 [5, 1024, 1024], replicated, may hold values from -0.1875 to 0.1875
- self_out: bfloat16 [1024, 1024], replicated, may hold values from -0.25 to 0.25
- self_gains: bfloat16 [2, 1024], replicated, may hold values from 0.5 to 1.5
- self_biases: bfloat16 [7, 1024], replicated, may hold values from -1.5 to 1.5
- prior_cross_matrices: float32 [3, 1024, 1024], P(None, None, ('rows', 'cols')), may hold values from -6 to 6
- prior_cross_out: float32 [1024, 1024], P(None, ('rows', 'cols')), may hold values from -6 to 6
- prior_input_matrices: float32 [2, 261, 1024], P(None, None, ('rows', 'cols')), may hold values from -96 to 96
Outputs:
- new_latents: bfloat16 [2048, 1024], P(('rows', 'cols'))
- latent_grad: float32 [2048, 1024], P(('rows', 'cols'))
- color_grad: float32 [3, 4, 288, 72], P(None, None, 'rows', 'cols')
- cross_matrices_total: float32 [3, 1024, 1024], P(None, None, ('rows', 'cols'))
- cross_out_total: float32 [1024, 1024], P(None, ('rows', 'cols'))
- input_matrices_total: float32 [2, 261, 1024], P(None, None, ('rows', 'cols'))
- in_gain_grad: float32 [261], replicated
- in_bias_grad: float32 [261], replicated
- cross_gains_grad: float32 [2, 1024], P(None, ('rows', 'cols'))
- cross_biases_grad: float32 [7, 1024], P(None, ('rows', 'cols'))
- self_matrices_grad: float32 [5, 1024, 1024], P(None, None, ('rows', 'cols'))
- self_out_grad: float32 [1024, 1024], P(None, ('rows', 'cols'))
- self_gains_grad: float32 [2, 1024], P(None, ('rows', 'cols'))
- self_biases_grad: float32 [7, 1024], P(None, ('rows', 'cols'))
The draws below stay inside these ranges and needn't reach their ends.
Inputs may be any that keep to these rules, and one draw needn't show every extreme that they name: `image_boxes`: each row is an image's top row, left column, height and width on the canvas of 288 x 72 pixels; height is (288 * j) // 9 and width (72 * j) // 9 for one j of 5, 7, 9; every box lies inside the canvas, and at least one image fills the whole canvas.
All inputs are finite; a program needn't handle non-finite values.
Results may differ from the reference program's by a relative error of at most 0.019.
Values may be sent and summed in bfloat16 or wider, within the bound.
A program may use at most 256 MiB of HBM per device.

```python
import jax
import jax.numpy as jnp
from jax import lax

D = 1024
HEADS = 8
LATENTS = 512
NBANDS = 64
IMAGES = 4
HEAD_DIM = 128
INPUT = 261
H = 288
W = 72
LATROWS = 2048


def draw_image_boxes(key, part):
    key = jax.random.fold_in(key, 7)
    class_key, full_key, top_key, left_key = jax.random.split(key, 4)
    size_class = jax.random.randint(class_key, (IMAGES,), 0, 3)
    chosen = jax.random.randint(full_key, (), 0, IMAGES)
    size_class = jnp.where(jnp.arange(IMAGES) == chosen, 2, size_class)
    factor = 5 + 2 * size_class
    heights = H * factor // 9
    widths = W * factor // 9
    box_tops = jax.random.randint(top_key, (IMAGES,), 0, H - heights + 1)
    box_lefts = jax.random.randint(left_key, (IMAGES,), 0, W - widths + 1)
    return jnp.stack([box_tops, box_lefts, heights, widths], axis=1).astype(jnp.int32)


def steps_of(own_key, extent, pieces, smallest, top_value):
    level = 1.0
    for dim, shards_of in pieces:
        draws = jax.random.uniform(jax.random.fold_in(jax.random.fold_in(own_key, 6), dim), (shards_of,), jnp.float32, smallest / len(pieces), top_value / len(pieces))
        level = level * jnp.repeat(jnp.exp(draws), extent[dim] // shards_of).reshape((-1,) + (1,) * (len(extent) - 1 - dim))
    return level


def normal_values(own_key, dims, width, reach, shards=(), held_as=jnp.bfloat16):
    result = width * jax.random.normal(own_key, dims, jnp.float32)
    if shards:
        result = result * steps_of(own_key, dims, shards, -0.22, 0.18)
    return jnp.clip(result, -reach, reach).astype(held_as)


def setup_inputs(seed: int = 0) -> dict:
    arg_keys = jax.random.split(jax.random.key(seed), 19)
    latents = normal_values(arg_keys[0], (LATROWS, D), 1.0, 6.0, ((0, 32),))
    pixel_colors = normal_values(arg_keys[1], (3, IMAGES, H, W), 1.0, 4.0, ((2, 4), (3, 8)))
    image_boxes = draw_image_boxes(jax.random.fold_in(arg_keys[18], 71), 0)
    cotangent = normal_values(arg_keys[3], (LATROWS, D), 1.0, 6.0, ((0, 32),))
    cross_matrices = normal_values(arg_keys[4], (3, D, D), D ** -0.5, 0.1875)
    cross_out = normal_values(arg_keys[5], (D, D), (D // 8) ** -0.5, 0.5)
    input_matrices = normal_values(arg_keys[6], (2, INPUT, D), INPUT ** -0.5, 0.375)
    in_gain = jnp.clip(1.0 + 0.1 * jax.random.normal(arg_keys[7], (INPUT,), jnp.float32), 0.5, 1.5).astype(jnp.bfloat16)
    in_bias = normal_values(arg_keys[8], (INPUT,), 0.3, 1.5)
    cross_gains = jnp.clip(1.0 + 0.1 * jax.random.normal(arg_keys[9], (2, D), jnp.float32), 0.5, 1.5).astype(jnp.bfloat16)
    cross_biases = normal_values(arg_keys[10], (7, D), 0.3, 1.5)
    self_matrices = normal_values(arg_keys[11], (5, D, D), D ** -0.5, 0.1875)
    self_out = normal_values(arg_keys[12], (D, D), (D // 2) ** -0.5, 0.25)
    self_gains = jnp.clip(1.0 + 0.1 * jax.random.normal(arg_keys[13], (2, D), jnp.float32), 0.5, 1.5).astype(jnp.bfloat16)
    self_biases = normal_values(arg_keys[14], (7, D), 0.3, 1.5)
    prior_cross_matrices = normal_values(arg_keys[15], (3, D, D), 1.0, 6.0, ((2, 32),), jnp.float32)
    prior_cross_out = normal_values(arg_keys[16], (D, D), 1.0, 6.0, ((1, 32),), jnp.float32)
    prior_input_matrices = normal_values(arg_keys[17], (2, INPUT, D), 16.0, 96.0, ((2, 32),), jnp.float32)
    return {"latents": latents, "pixel_colors": pixel_colors, "image_boxes": image_boxes, "cotangent": cotangent, "cross_matrices": cross_matrices, "cross_out": cross_out, "input_matrices": input_matrices, "in_gain": in_gain, "in_bias": in_bias, "cross_gains": cross_gains, "cross_biases": cross_biases, "self_matrices": self_matrices, "self_out": self_out, "self_gains": self_gains, "self_biases": self_biases, "prior_cross_matrices": prior_cross_matrices, "prior_cross_out": prior_cross_out, "prior_input_matrices": prior_input_matrices}


EPS = 1e-05
NEG = -1e+30
FREQ_TOP = 112.0

@jax.custom_vjp
def low(v):
    return lax.optimization_barrier(v.astype(jnp.bfloat16)).astype(jnp.float32)

@jax.custom_vjp
def low_back(v):
    return v

def low_keep(v):
    return (low(v), None)

def low_pass(kept, grad):
    return (grad,)

def back_keep(v):
    return (v, None)

def back_low(kept, grad):
    return (low(grad),)
low.defvjp(low_keep, low_pass)
low_back.defvjp(back_keep, back_low)

def matmul(former, latter):
    return jnp.dot(former, latter, precision=lax.Precision.HIGHEST)

def to_float(values):
    return values.astype(jnp.float32)

def layer_norm(values, gain, offset):
    middle = lax.optimization_barrier(jnp.mean(values, axis=-1, keepdims=True))
    centered = values - middle
    spread = lax.optimization_barrier(jnp.mean(centered * centered, axis=-1, keepdims=True))
    return centered * lax.rsqrt(spread + EPS) * gain + offset

def gelu_tanh(values):
    return jax.nn.gelu(values, approximate=True)

def pixel_features(colors, image_box, row_start, col_start):
    channels = colors.shape[0]
    tile_rows = colors.shape[1]
    tile_cols = colors.shape[2]
    box_top = image_box[0]
    box_left = image_box[1]
    box_height = image_box[2]
    box_width = image_box[3]
    rows_here = row_start + jnp.arange(tile_rows, dtype=jnp.int32)
    cols_here = col_start + jnp.arange(tile_cols, dtype=jnp.int32)
    grid_rows = jnp.repeat(rows_here, tile_cols)
    grid_cols = jnp.tile(cols_here, tile_rows)
    inside = (grid_rows >= box_top) & (grid_rows < box_top + box_height) & (grid_cols >= box_left) & (grid_cols < box_left + box_width)
    y_place = -1.0 + 2.0 * (grid_rows - box_top).astype(jnp.float32) / (box_height - 1).astype(jnp.float32)
    x_place = -1.0 + 2.0 * (grid_cols - box_left).astype(jnp.float32) / (box_width - 1).astype(jnp.float32)
    frequency = 1.0 + jnp.arange(NBANDS, dtype=jnp.float32) * ((FREQ_TOP - 1.0) / (NBANDS - 1))
    y_angle = jnp.pi * y_place[:, None] * frequency[None, :]
    x_angle = jnp.pi * x_place[:, None] * frequency[None, :]
    color_rows = jnp.transpose(colors.reshape(channels, tile_rows * tile_cols)).astype(jnp.float32)
    features = jnp.concatenate([color_rows, y_place[:, None], x_place[:, None], jnp.sin(y_angle), jnp.sin(x_angle), jnp.cos(y_angle), jnp.cos(x_angle)], axis=1)
    return (features, inside)

def cross_image(query_image, colors, image_box, key_weight, value_weight, value_bias, gain, offset):
    features, inside = pixel_features(colors, image_box, 0, 0)
    normed = low(layer_norm(features, gain, offset))
    keys_here = low(low_back(matmul(normed, key_weight)))
    values_here = low(low_back(matmul(normed, value_weight)) + value_bias)
    scores = low_back(matmul(query_image, jnp.transpose(keys_here))) * D ** (-0.5)
    scores = jnp.where(inside[None, :], scores, NEG)
    peak_score = lax.optimization_barrier(jnp.max(scores, axis=1, keepdims=True))
    weights = jnp.where(inside[None, :], jnp.exp(scores - peak_score), 0.0)
    probs = low(weights / lax.optimization_barrier(jnp.sum(weights, axis=1, keepdims=True)))
    return low_back(matmul(probs, values_here))

def tower_image(query_image, key_image, value_image):
    scores = low_back(jnp.einsum('qhd,khd->hqk', query_image, key_image, precision=lax.Precision.HIGHEST)) * HEAD_DIM ** (-0.5)
    weights = jnp.exp(scores - lax.optimization_barrier(jnp.max(scores, axis=2, keepdims=True)))
    probs = low(weights / lax.optimization_barrier(jnp.sum(weights, axis=2, keepdims=True)))
    return low_back(jnp.einsum('hqk,khd->qhd', probs, value_image, precision=lax.Precision.HIGHEST))

def feed_forward(row_values, gain, offset, w_in, b_in, w_out, b_out):
    normed = low(layer_norm(row_values, gain, offset))
    hidden = low(gelu_tanh(low_back(matmul(normed, w_in)) + b_in))
    return low_back(matmul(hidden, w_out)) + b_out

def forward(latent_rows, colors, weights, image_boxes):
    w_cross, w_cross_out, w_input, g_input, b_input, g_cross, b_cross, w_self, w_self_out, g_self, b_self = weights
    normed_q = low(layer_norm(latent_rows, g_cross[0], b_cross[0]))
    queries = low(low_back(matmul(normed_q, w_cross[0])) + b_cross[2])

    def cross_item(image_items):
        return cross_image(image_items[0], image_items[1], image_items[2], w_input[0], w_input[1], b_cross[3], g_input, b_input)
    attended = lax.map(jax.checkpoint(cross_item), (queries.reshape(IMAGES, LATENTS, D), jnp.transpose(colors, (1, 0, 2, 3)), image_boxes))
    attended = low(attended.reshape(IMAGES * LATENTS, D))
    first = latent_rows + low_back(matmul(attended, w_cross_out)) + b_cross[4]
    second = first + feed_forward(first, g_cross[1], b_cross[1], w_cross[1], b_cross[5], w_cross[2], b_cross[6])
    normed_t = low(layer_norm(second, g_self[0], b_self[0]))
    head_shape = (IMAGES, LATENTS, HEADS, HEAD_DIM)
    tower_queries = low(low_back(matmul(normed_t, w_self[0])) + b_self[2]).reshape(head_shape)
    tower_keys = low(low_back(matmul(normed_t, w_self[1]))).reshape(head_shape)
    tower_values = low(low_back(matmul(normed_t, w_self[2])) + b_self[3]).reshape(head_shape)

    def tower_item(image_items):
        return tower_image(image_items[0], image_items[1], image_items[2])
    mixed = lax.map(jax.checkpoint(tower_item), (tower_queries, tower_keys, tower_values))
    mixed = low(mixed.reshape(IMAGES * LATENTS, D))
    third = second + low_back(matmul(mixed, w_self_out)) + b_self[4]
    return third + feed_forward(third, g_self[1], b_self[1], w_self[3], b_self[5], w_self[4], b_self[6])

def reference(latents, pixel_colors, image_boxes, cotangent, cross_matrices, cross_out, input_matrices, in_gain, in_bias, cross_gains, cross_biases, self_matrices, self_out, self_gains, self_biases, prior_cross_matrices, prior_cross_out, prior_input_matrices):
    params = (to_float(cross_matrices), to_float(cross_out), to_float(input_matrices), to_float(in_gain), to_float(in_bias), to_float(cross_gains), to_float(cross_biases), to_float(self_matrices), to_float(self_out), to_float(self_gains), to_float(self_biases))

    def closed(latent_rows, colors, weights):
        return forward(latent_rows, colors, weights, image_boxes)
    output, pullback = jax.vjp(closed, to_float(latents), to_float(pixel_colors), params)
    latent_grad, color_grad, weight_grads = pullback(to_float(cotangent))
    return (output.astype(jnp.bfloat16), latent_grad, color_grad, prior_cross_matrices + weight_grads[0], prior_cross_out + weight_grads[1], prior_input_matrices + weight_grads[2], weight_grads[3], weight_grads[4], weight_grads[5], weight_grads[6], weight_grads[7], weight_grads[8], weight_grads[9], weight_grads[10])
```

```python
import jax
import jax.numpy as jnp
from jax import lax
from jax.sharding import PartitionSpec as P

HEADS = 8
LATENTS = 512
NBANDS = 64
HEAD_DIM = 128


EPS = 1e-05
NEG = -1e30
FREQ_TOP = 112.0


def narrow(values):
    return values.astype(jnp.bfloat16)


def to_float(values):
    return values.astype(jnp.float32)


def matmul(former, latter):
    return jnp.dot(former, latter, preferred_element_type=jnp.float32)


def inner_left(former, latter):
    return lax.dot_general(
        former, latter, (((0,), (0,)), ((), ())), preferred_element_type=jnp.float32
    )


def inner_right(former, latter):
    return lax.dot_general(
        former, latter, (((1,), (1,)), ((), ())), preferred_element_type=jnp.float32
    )


def layer_norm(values, gain, offset):
    middle = jnp.mean(values, axis=-1, keepdims=True)
    centered = values - middle
    spread = jnp.mean(centered * centered, axis=-1, keepdims=True)
    return centered * lax.rsqrt(spread + EPS) * gain + offset


def norm_back(values, gain, offset, gradient):
    result, pullback = jax.vjp(layer_norm, values, gain, offset)
    return pullback(gradient)


def gelu_tanh(values):
    return jax.nn.gelu(values, approximate=True)


def gelu_back(pre_gelu, gradient):
    result, pullback = jax.vjp(gelu_tanh, pre_gelu)
    return pullback(gradient)[0]


def axis_features(places, extent):
    frequency = 1.0 + jnp.arange(NBANDS, dtype=jnp.float32) * ((FREQ_TOP - 1.0) / (NBANDS - 1))
    angle = jnp.pi * places[:, None] * frequency[None, :]
    return (places, jnp.sin(angle), jnp.cos(angle))


def canvas_of(colors, image_box):
    channels, wide, tall = colors.shape
    top, left, height, width = image_box[0], image_box[1], image_box[2], image_box[3]
    row_at = jnp.arange(tall, dtype=jnp.int32)
    col_at = jnp.arange(wide, dtype=jnp.int32)
    y_place = -1.0 + 2.0 * to_float(row_at - top) / to_float(height - 1)
    x_place = -1.0 + 2.0 * to_float(col_at - left) / to_float(width - 1)
    y_parts = axis_features(y_place, height)
    x_parts = axis_features(x_place, width)
    y_all = jnp.concatenate([y_parts[0][:, None], y_parts[1], y_parts[2]], axis=1)
    x_all = jnp.concatenate([x_parts[0][:, None], x_parts[1], x_parts[2]], axis=1)
    count = channels + 2 + 4 * NBANDS
    color_sum = jnp.sum(colors, axis=0)
    color_square = jnp.sum(colors * colors, axis=0)
    mean = (color_sum + jnp.sum(y_all, axis=1)[None, :] + jnp.sum(x_all, axis=1)[:, None]) / count
    square = (
        color_square
        + jnp.sum(y_all * y_all, axis=1)[None, :]
        + jnp.sum(x_all * x_all, axis=1)[:, None]
    ) / count
    deviation = lax.rsqrt(square - mean * mean + EPS)
    row_in = (row_at >= top) & (row_at < top + height)
    col_in = (col_at >= left) & (col_at < left + width)
    return (y_all, x_all, mean, deviation, row_in, col_in)


def split_channels(rows, channels):
    n = NBANDS
    c = channels
    y_part = jnp.concatenate(
        [rows[:, c : c + 1], rows[:, c + 2 : c + 2 + n], rows[:, c + 2 + 2 * n : c + 2 + 3 * n]],
        axis=1,
    )
    x_part = jnp.concatenate(
        [
            rows[:, c + 1 : c + 2],
            rows[:, c + 2 + n : c + 2 + 2 * n],
            rows[:, c + 2 + 3 * n : c + 2 + 4 * n],
        ],
        axis=1,
    )
    return (rows[:, :c], y_part, x_part)


def join_channels(color_part, y_part, x_part):
    n = NBANDS
    return jnp.concatenate(
        [
            color_part,
            y_part[:, :1],
            x_part[:, :1],
            y_part[:, 1 : n + 1],
            x_part[:, 1 : n + 1],
            y_part[:, n + 1 :],
            x_part[:, n + 1 :],
        ],
        axis=1,
    )


def against_pixels(rows, colors, canvas):
    y_all, x_all, mean, deviation = canvas[:4]
    color_part, y_part, x_part = split_channels(rows, colors.shape[0])
    by_row = inner_right(narrow(y_part), narrow(y_all))
    by_col = inner_right(narrow(x_part), narrow(x_all))
    total = by_row[:, None, :] + by_col[:, :, None]
    for j in range(colors.shape[0]):
        total = total + color_part[:, j][:, None, None] * colors[j][None]
    total = total - jnp.sum(rows, axis=1)[:, None, None] * mean[None]
    return total * deviation[None]


def over_pixels(weights, colors, canvas):
    y_all, x_all, mean, deviation = canvas[:4]
    scaled = weights * deviation[None]
    y_part = matmul(narrow(jnp.sum(scaled, axis=1)), narrow(y_all))
    x_part = matmul(narrow(jnp.sum(scaled, axis=2)), narrow(x_all))
    color_part = jnp.stack(
        [jnp.sum(scaled * colors[j][None], axis=(1, 2)) for j in range(colors.shape[0])], axis=1
    )
    middle = jnp.sum(scaled * mean[None], axis=(1, 2))
    return join_channels(color_part, y_part, x_part) - middle[:, None]


def mlp_forward(row_values, gain, offset, w_in, b_in, w_out, b_out):
    normed = narrow(layer_norm(row_values, gain, offset))
    pre_gelu = matmul(normed, w_in) + b_in
    hidden = narrow(gelu_tanh(pre_gelu))
    return (matmul(hidden, w_out) + b_out, (normed, pre_gelu, hidden))


def mlp_backward(row_values, gain, offset, w_in, w_out, stored, gradient):
    normed, pre_gelu, hidden = stored
    grad_low = narrow(gradient)
    d_w_out = inner_left(hidden, grad_low)
    d_b_out = jnp.sum(gradient, axis=0)
    d_pre = gelu_back(pre_gelu, inner_right(grad_low, w_out))
    pre_low = narrow(d_pre)
    d_w_in = inner_left(normed, pre_low)
    d_b_in = jnp.sum(d_pre, axis=0)
    d_rows, d_gain, d_offset = norm_back(row_values, gain, offset, inner_right(pre_low, w_in))
    return (
        gradient + d_rows,
        (d_w_in, d_w_out),
        (d_gain, d_offset, d_b_in, d_b_out),
        (pre_low, grad_low),
    )


def local(
    latents,
    pixel_colors,
    image_boxes,
    cotangent,
    cross_matrices,
    cross_out,
    input_matrices,
    in_gain,
    in_bias,
    cross_gains,
    cross_biases,
    self_matrices,
    self_out,
    self_gains,
    self_biases,
    prior_cross_matrices,
    prior_cross_out,
    prior_input_matrices,
):
    rows_dev = latents.shape[0]
    model_width = latents.shape[1]
    image_count = image_boxes.shape[0]
    tile_rows = pixel_colors.shape[2]
    tile_cols = pixel_colors.shape[3]
    input_width = input_matrices.shape[1]
    grid_rows = lax.axis_size("rows")
    grid_cols = lax.axis_size("cols")
    all_rows = rows_dev * grid_rows * grid_cols
    row_place = lax.axis_index("rows")
    col_place = lax.axis_index("cols")
    row_start = row_place * tile_rows
    col_start = col_place * tile_cols
    score_scale = model_width ** (-0.5)
    head_scale = HEAD_DIM ** (-0.5)
    g_cross = to_float(cross_gains)
    b_cross = to_float(cross_biases)
    g_self = to_float(self_gains)
    b_self = to_float(self_biases)
    g_input = to_float(in_gain)
    b_input = to_float(in_bias)
    latent_state = to_float(latents)
    normed_q = narrow(layer_norm(latent_state, g_cross[0], b_cross[0]))
    query_rows = narrow(matmul(normed_q, cross_matrices[0]) + b_cross[2])
    colors_low = lax.all_gather(pixel_colors, ("rows", "cols"), axis=0, tiled=False)
    colors_low = lax.dynamic_index_in_dim(colors_low, row_place, axis=2, keepdims=False)
    colors_low = colors_low.reshape(grid_rows, grid_cols, 3, tile_rows, tile_cols)
    colors = to_float(
        jnp.transpose(colors_low, (2, 1, 4, 0, 3)).reshape(
            3, grid_cols * tile_cols, grid_rows * tile_rows
        )
    )
    image_box = lax.dynamic_index_in_dim(image_boxes, row_place, axis=0, keepdims=False)
    canvas = canvas_of(colors, image_box)
    mean, deviation, row_in, col_in = canvas[2:]
    inside = (col_in[:, None] & row_in[None, :])[None]
    key_weight = input_matrices[0]
    value_weight = input_matrices[1]
    query_inputs = inner_right(query_rows, key_weight)
    query_lines = against_pixels(query_inputs * g_input, colors, canvas)
    query_shift = jnp.sum(query_inputs * b_input, axis=1)
    scores = jnp.where(
        inside, (query_lines + query_shift[:, None, None]) * score_scale, NEG
    )
    peak_score = jnp.max(scores, axis=(1, 2), keepdims=True)
    weights = jnp.where(inside, jnp.exp(scores - peak_score), 0.0)
    cross_probs = weights / jnp.sum(weights, axis=(1, 2), keepdims=True)
    plain_mixed = over_pixels(cross_probs, colors, canvas)
    mixed_inputs = (
        plain_mixed * g_input + jnp.sum(cross_probs, axis=(1, 2))[:, None] * b_input
    )
    mixed_low = narrow(mixed_inputs)
    attended = matmul(mixed_low, value_weight) + b_cross[3]
    attended_low = narrow(attended)
    first = latent_state + matmul(attended_low, cross_out) + b_cross[4]
    branch, cross_stored = mlp_forward(
        first, g_cross[1], b_cross[1], cross_matrices[1], b_cross[5], cross_matrices[2], b_cross[6]
    )
    second = first + branch
    normed_t = narrow(layer_norm(second, g_self[0], b_self[0]))
    tower_queries = narrow(matmul(normed_t, self_matrices[0]) + b_self[2])
    tower_keys = narrow(matmul(normed_t, self_matrices[1]))
    tower_values = narrow(matmul(normed_t, self_matrices[2]) + b_self[3])
    keys_group, values_group = (
        lax.all_gather(tower_keys, "cols", axis=0, tiled=True),
        lax.all_gather(tower_values, "cols", axis=0, tiled=True),
    )
    group_rows = keys_group.shape[0]
    query_image = (
        (row_place * grid_cols + col_place) * rows_dev + jnp.arange(rows_dev, dtype=jnp.int32)
    ) // LATENTS
    key_image = (row_place * group_rows + jnp.arange(group_rows, dtype=jnp.int32)) // LATENTS
    same_image = (query_image[:, None] == key_image[None, :])[None]
    query_heads = tower_queries.reshape(rows_dev, HEADS, HEAD_DIM)
    key_heads = keys_group.reshape(group_rows, HEADS, HEAD_DIM)
    value_heads = values_group.reshape(group_rows, HEADS, HEAD_DIM)
    head_scores = jnp.where(
        same_image,
        jnp.einsum("qhd,khd->hqk", query_heads, key_heads, preferred_element_type=jnp.float32)
        * head_scale,
        NEG,
    )
    head_weights = jnp.where(
        same_image, jnp.exp(head_scores - jnp.max(head_scores, axis=2, keepdims=True)), 0.0
    )
    head_probs = head_weights / jnp.sum(head_weights, axis=2, keepdims=True)
    probs_low = narrow(head_probs)
    tower_mixed = narrow(
        jnp.einsum(
            "hqk,khd->qhd", probs_low, value_heads, preferred_element_type=jnp.float32
        ).reshape(rows_dev, model_width)
    )
    third = second + matmul(tower_mixed, self_out) + b_self[4]
    branch, tower_stored = mlp_forward(
        third, g_self[1], b_self[1], self_matrices[3], b_self[5], self_matrices[4], b_self[6]
    )
    new_latents = narrow(third + branch)
    gradient = to_float(cotangent)
    gradient, tower_mlp_w, tower_mlp_v, tower_lows = mlp_backward(
        third, g_self[1], b_self[1], self_matrices[3], self_matrices[4], tower_stored, gradient
    )
    tower_out_low = narrow(gradient)
    d_self_out = inner_left(tower_mixed, tower_out_low)
    d_self_out_bias = jnp.sum(gradient, axis=0)
    d_mixed = narrow(inner_right(tower_out_low, self_out)).reshape(rows_dev, HEADS, HEAD_DIM)
    d_probs = jnp.einsum("qhd,khd->hqk", d_mixed, value_heads, preferred_element_type=jnp.float32)
    d_value_heads = jnp.einsum(
        "hqk,qhd->khd", probs_low, d_mixed, preferred_element_type=jnp.float32
    )
    d_scores = head_probs * (d_probs - jnp.sum(head_probs * d_probs, axis=2, keepdims=True))
    d_scores_low = narrow(d_scores * head_scale)
    d_query_heads = jnp.einsum(
        "hqk,khd->qhd", d_scores_low, key_heads, preferred_element_type=jnp.float32
    ).reshape(rows_dev, model_width)
    d_key_heads = jnp.einsum(
        "hqk,qhd->khd", d_scores_low, query_heads, preferred_element_type=jnp.float32
    )
    d_tower_keys, d_tower_values = (
        lax.psum_scatter(
            d_key_heads.reshape(group_rows, model_width).astype(jnp.bfloat16),
            "cols",
            scatter_dimension=0,
            tiled=True,
        ).astype(jnp.float32),
        lax.psum_scatter(
            d_value_heads.reshape(group_rows, model_width).astype(jnp.bfloat16),
            "cols",
            scatter_dimension=0,
            tiled=True,
        ).astype(jnp.float32),
    )
    tq_low = narrow(d_query_heads)
    tk_low = narrow(d_tower_keys)
    tv_low = narrow(d_tower_values)
    d_normed_t = (
        inner_right(tq_low, self_matrices[0])
        + inner_right(tk_low, self_matrices[1])
        + inner_right(tv_low, self_matrices[2])
    )
    d_second, d_self_gain, d_self_bias = norm_back(second, g_self[0], b_self[0], d_normed_t)
    gradient = gradient + d_second
    self_gain_grad = jnp.stack([d_self_gain, tower_mlp_v[0]])
    self_bias_grad = jnp.stack(
        [
            d_self_bias,
            tower_mlp_v[1],
            jnp.sum(d_query_heads, axis=0),
            jnp.sum(d_tower_values, axis=0),
            d_self_out_bias,
            tower_mlp_v[2],
            tower_mlp_v[3],
        ]
    )
    gradient, cross_mlp_w, cross_mlp_v, cross_lows = mlp_backward(
        first, g_cross[1], b_cross[1], cross_matrices[1], cross_matrices[2], cross_stored, gradient
    )
    cross_out_low = narrow(gradient)
    d_cross_out = inner_left(attended_low, cross_out_low)
    d_cross_out_bias = jnp.sum(gradient, axis=0)
    d_attended = narrow(inner_right(cross_out_low, cross_out))
    value_shift = jnp.sum(to_float(d_attended) * b_cross[3], axis=1)
    row_delta = jnp.sum(to_float(d_attended) * attended, axis=1) - value_shift
    grad_inputs = inner_right(d_attended, value_weight)
    grad_shift = jnp.sum(grad_inputs * b_input, axis=1)
    grad_lines = against_pixels(grad_inputs * g_input, colors, canvas)
    d_scores = (
        cross_probs * (grad_lines + (grad_shift - row_delta)[:, None, None]) * score_scale
    )
    plain_scores = over_pixels(d_scores, colors, canvas)
    score_sum = jnp.sum(d_scores, axis=(1, 2))
    prob_sum = jnp.sum(cross_probs, axis=(1, 2))
    score_inputs = plain_scores * g_input + score_sum[:, None] * b_input
    score_low = narrow(score_inputs)
    d_query_rows = matmul(score_low, key_weight)
    in_gain_part = jnp.sum(query_inputs * plain_scores + grad_inputs * plain_mixed, axis=0)
    in_bias_part = jnp.sum(
        query_inputs * score_sum[:, None] + grad_inputs * prob_sum[:, None], axis=0
    )
    query_scaled = query_inputs * g_input
    grad_scaled = grad_inputs * g_input
    query_away = query_scaled[:, :3] - jnp.mean(query_scaled, axis=1, keepdims=True)
    grad_away = grad_scaled[:, :3] - jnp.mean(grad_scaled, axis=1, keepdims=True)
    along = jnp.sum(d_scores * query_lines + cross_probs * grad_lines, axis=0) / input_width
    color_parts = jnp.einsum(
        "rj,rcy->jcy", query_away, d_scores, precision=lax.Precision.HIGHEST
    ) + jnp.einsum("rj,rcy->jcy", grad_away, cross_probs, precision=lax.Precision.HIGHEST)
    color_parts = deviation[None] * (
        color_parts - (colors - mean[None]) * deviation[None] * along[None]
    )
    color_parts = color_parts.reshape(3, grid_cols, tile_cols, grid_rows, tile_rows)
    color_parts = jnp.transpose(color_parts, (3, 1, 0, 4, 2)).reshape(
        grid_rows * grid_cols, 3, tile_rows, tile_cols
    )
    color_grad = lax.all_to_all(
        color_parts, ("rows", "cols"), split_axis=0, concat_axis=0, tiled=True
    ).reshape(image_count, grid_cols, 3, tile_rows, tile_cols)
    color_grad = jnp.transpose(jnp.sum(color_grad, axis=1), (1, 0, 2, 3))
    query_low = narrow(d_query_rows)
    d_latent, d_cross_gain, d_cross_bias = norm_back(
        latent_state, g_cross[0], b_cross[0], inner_right(query_low, cross_matrices[0])
    )
    latent_grad = gradient + d_latent
    in_gain_grad, in_bias_grad = lax.psum((in_gain_part, in_bias_part), ("rows", "cols"))
    vectors = jnp.stack(
        [
            d_cross_gain,
            cross_mlp_v[0],
            d_cross_bias,
            cross_mlp_v[1],
            jnp.sum(d_query_rows, axis=0),
            jnp.sum(to_float(d_attended), axis=0),
            d_cross_out_bias,
            cross_mlp_v[2],
            cross_mlp_v[3],
            d_self_gain,
            tower_mlp_v[0],
            d_self_bias,
            tower_mlp_v[1],
            jnp.sum(d_query_heads, axis=0),
            jnp.sum(d_tower_values, axis=0),
            d_self_out_bias,
            tower_mlp_v[2],
            tower_mlp_v[3],
        ]
    )
    vector_sums = lax.psum_scatter(vectors, ("rows", "cols"), scatter_dimension=1, tiled=True)
    lefts = jnp.stack(
        [
            normed_q,
            cross_stored[0],
            cross_stored[2],
            attended_low,
            normed_t,
            tower_stored[0],
            tower_stored[2],
            tower_mixed,
        ]
    )
    rights = jnp.stack(
        [
            query_low,
            cross_lows[0],
            cross_lows[1],
            cross_out_low,
            d_attended,
            query_rows,
            tq_low,
            tk_low,
            tv_low,
            tower_lows[0],
            tower_lows[1],
            tower_out_low,
        ]
    )
    small_lefts = jnp.stack([mixed_low, score_low])
    lefts = lax.all_gather(lefts, "cols", axis=1, tiled=True)
    small_lefts = lax.all_gather(small_lefts, "cols", axis=1, tiled=True)
    own = model_width // (grid_rows * grid_cols)
    rights = rights.reshape(rights.shape[0], rows_dev, grid_rows, grid_cols, own)
    rights = lax.all_to_all(
        jnp.transpose(rights, (3, 0, 1, 2, 4)), "cols", split_axis=0, concat_axis=0, tiled=False
    )
    rights = jnp.transpose(rights, (1, 0, 2, 3, 4)).reshape(
        rights.shape[1], grid_cols * rows_dev, grid_rows * own
    )
    pairs = ((0, 0), (1, 1), (2, 2), (3, 3), (4, 6), (4, 7), (4, 8), (5, 9), (6, 10), (7, 11))
    big = [inner_left(rights[k], lefts[i]).reshape(grid_rows, own, model_width) for i, k in pairs]
    small = [
        inner_left(rights[k], small_lefts[i]).reshape(grid_rows, own, input_width)
        for i, k in ((1, 5), (0, 4))
    ]
    big = lax.psum_scatter(jnp.stack(big, axis=1), "rows", scatter_dimension=0, tiled=False)
    small = lax.psum_scatter(jnp.stack(small, axis=1), "rows", scatter_dimension=0, tiled=False)
    big = jnp.transpose(big, (0, 2, 1))
    small = jnp.transpose(small, (0, 2, 1))
    all_sums = (
        big[:3],
        big[3],
        small,
        vector_sums[:2],
        vector_sums[2:9],
        big[4:9],
        big[9],
        vector_sums[9:11],
        vector_sums[11:],
    )
    cross_sums = all_sums[:5]
    self_sums = all_sums[5:]
    return (
        new_latents,
        latent_grad,
        color_grad,
        prior_cross_matrices + cross_sums[0],
        prior_cross_out + cross_sums[1],
        prior_input_matrices + cross_sums[2],
        in_gain_grad,
        in_bias_grad,
        cross_sums[3],
        cross_sums[4],
        self_sums[0],
        self_sums[1],
        self_sums[2],
        self_sums[3],
    )


def solution(mesh):
    placed = (
        P(("rows", "cols"), None),
        P(None, None, "rows", "cols"),
        P(),
        P(("rows", "cols"), None),
        P(),
        P(),
        P(),
        P(),
        P(),
        P(),
        P(),
        P(),
        P(),
        P(),
        P(),
        P(None, None, ("rows", "cols")),
        P(None, ("rows", "cols")),
        P(None, None, ("rows", "cols")),
    )
    return jax.shard_map(
        local,
        mesh=mesh,
        in_specs=placed,
        out_specs=(
            P(("rows", "cols"), None),
            P(("rows", "cols"), None),
            P(None, None, "rows", "cols"),
            P(None, None, ("rows", "cols")),
            P(None, ("rows", "cols")),
            P(None, None, ("rows", "cols")),
            P(),
            P(),
            P(None, ("rows", "cols")),
            P(None, ("rows", "cols")),
            P(None, None, ("rows", "cols")),
            P(None, ("rows", "cols")),
            P(None, ("rows", "cols")),
            P(None, ("rows", "cols")),
        ),
        check_vma=False,
    )
```

```python
import functools

import jax
import jax.numpy as jnp
import ml_dtypes
import numpy as np
from jax import lax
from jax.experimental import pallas as pl
from jax.experimental.pallas import tpu as pltpu
from jax.sharding import PartitionSpec as P

HEADS = 8
LATENTS = 512
NBANDS = 64
HEAD_DIM = 128


EPS = 1e-05
NEG = -1e30
FREQ_TOP = 112.0
VMEM_BYTES = 63 * 1024 * 1024


def narrow(values):
    return values.astype(jnp.bfloat16)


def to_float(values):
    return values.astype(jnp.float32)


def matmul(former, latter):
    return jnp.dot(former, latter, preferred_element_type=jnp.float32)


def inner_left(former, latter):
    return lax.dot_general(
        former, latter, (((0,), (0,)), ((), ())), preferred_element_type=jnp.float32
    )


def inner_right(former, latter):
    return lax.dot_general(
        former, latter, (((1,), (1,)), ((), ())), preferred_element_type=jnp.float32
    )


def layer_norm(values, gain, offset):
    middle = jnp.mean(values, axis=-1, keepdims=True)
    centered = values - middle
    spread = jnp.mean(centered * centered, axis=-1, keepdims=True)
    return centered * lax.rsqrt(spread + EPS) * gain + offset


def norm_back(values, gain, offset, gradient):
    result, pullback = jax.vjp(layer_norm, values, gain, offset)
    return pullback(gradient)


def gelu_tanh(values):
    return jax.nn.gelu(values, approximate=True)


def gelu_back(pre_gelu, gradient):
    result, pullback = jax.vjp(gelu_tanh, pre_gelu)
    return pullback(gradient)[0]


def axis_features(places, extent):
    frequency = 1.0 + jnp.arange(NBANDS, dtype=jnp.float32) * ((FREQ_TOP - 1.0) / (NBANDS - 1))
    angle = jnp.pi * places[:, None] * frequency[None, :]
    return (places, jnp.sin(angle), jnp.cos(angle))


def canvas_of(colors, image_box):
    channels, wide, tall = colors.shape
    top, left, height, width = image_box[0], image_box[1], image_box[2], image_box[3]
    row_at = jnp.arange(tall, dtype=jnp.int32)
    col_at = jnp.arange(wide, dtype=jnp.int32)
    y_place = -1.0 + 2.0 * to_float(row_at - top) / to_float(height - 1)
    x_place = -1.0 + 2.0 * to_float(col_at - left) / to_float(width - 1)
    y_parts = axis_features(y_place, height)
    x_parts = axis_features(x_place, width)
    y_all = jnp.concatenate([y_parts[0][:, None], y_parts[1], y_parts[2]], axis=1)
    x_all = jnp.concatenate([x_parts[0][:, None], x_parts[1], x_parts[2]], axis=1)
    count = channels + 2 + 4 * NBANDS
    color_sum = jnp.sum(colors, axis=0)
    color_square = jnp.sum(colors * colors, axis=0)
    mean = (color_sum + jnp.sum(y_all, axis=1)[None, :] + jnp.sum(x_all, axis=1)[:, None]) / count
    square = (
        color_square
        + jnp.sum(y_all * y_all, axis=1)[None, :]
        + jnp.sum(x_all * x_all, axis=1)[:, None]
    ) / count
    deviation = lax.rsqrt(square - mean * mean + EPS)
    row_in = (row_at >= top) & (row_at < top + height)
    col_in = (col_at >= left) & (col_at < left + width)
    return (y_all, x_all, mean, deviation, row_in, col_in)


def split_channels(rows, channels):
    n = NBANDS
    c = channels
    y_part = jnp.concatenate(
        [rows[:, c : c + 1], rows[:, c + 2 : c + 2 + n], rows[:, c + 2 + 2 * n : c + 2 + 3 * n]],
        axis=1,
    )
    x_part = jnp.concatenate(
        [
            rows[:, c + 1 : c + 2],
            rows[:, c + 2 + n : c + 2 + 2 * n],
            rows[:, c + 2 + 3 * n : c + 2 + 4 * n],
        ],
        axis=1,
    )
    return (rows[:, :c], y_part, x_part)


def join_channels(color_part, y_part, x_part):
    n = NBANDS
    return jnp.concatenate(
        [
            color_part,
            y_part[:, :1],
            x_part[:, :1],
            y_part[:, 1 : n + 1],
            x_part[:, 1 : n + 1],
            y_part[:, n + 1 :],
            x_part[:, n + 1 :],
        ],
        axis=1,
    )


def against_pixels(rows, colors, canvas):
    y_all, x_all, mean, deviation = canvas[:4]
    color_part, y_part, x_part = split_channels(rows, colors.shape[0])
    by_row = inner_right(narrow(y_part), narrow(y_all))
    by_col = inner_right(narrow(x_part), narrow(x_all))
    total = by_row[:, None, :] + by_col[:, :, None]
    for j in range(colors.shape[0]):
        total = total + color_part[:, j][:, None, None] * colors[j][None]
    total = total - jnp.sum(rows, axis=1)[:, None, None] * mean[None]
    return total * deviation[None]


def over_pixels(weights, colors, canvas):
    y_all, x_all, mean, deviation = canvas[:4]
    scaled = weights * deviation[None]
    y_part = matmul(narrow(jnp.sum(scaled, axis=1)), narrow(y_all))
    x_part = matmul(narrow(jnp.sum(scaled, axis=2)), narrow(x_all))
    color_part = jnp.stack(
        [jnp.sum(scaled * colors[j][None], axis=(1, 2)) for j in range(colors.shape[0])], axis=1
    )
    middle = jnp.sum(scaled * mean[None], axis=(1, 2))
    return join_channels(color_part, y_part, x_part) - middle[:, None]


def mlp_forward(row_values, gain, offset, w_in, b_in, w_out, b_out):
    normed = narrow(layer_norm(row_values, gain, offset))
    pre_gelu = matmul(normed, w_in) + b_in
    hidden = narrow(gelu_tanh(pre_gelu))
    return (matmul(hidden, w_out) + b_out, (normed, pre_gelu, hidden))


def mlp_backward(row_values, gain, offset, w_in, w_out, stored, gradient):
    normed, pre_gelu, hidden = stored
    grad_low = narrow(gradient)
    d_w_out = inner_left(hidden, grad_low)
    d_b_out = jnp.sum(gradient, axis=0)
    d_pre = gelu_back(pre_gelu, inner_right(grad_low, w_out))
    pre_low = narrow(d_pre)
    d_w_in = inner_left(normed, pre_low)
    d_b_in = jnp.sum(d_pre, axis=0)
    d_rows, d_gain, d_offset = norm_back(row_values, gain, offset, inner_right(pre_low, w_in))
    return (
        gradient + d_rows,
        (d_w_in, d_w_out),
        (d_gain, d_offset, d_b_in, d_b_out),
        (pre_low, grad_low),
    )


def local(
    latents,
    pixel_colors,
    image_boxes,
    cotangent,
    cross_matrices,
    cross_out,
    input_matrices,
    in_gain,
    in_bias,
    cross_gains,
    cross_biases,
    self_matrices,
    self_out,
    self_gains,
    self_biases,
    prior_cross_matrices,
    prior_cross_out,
    prior_input_matrices,
):
    rows_dev = latents.shape[0]
    model_width = latents.shape[1]
    image_count = image_boxes.shape[0]
    tile_rows = pixel_colors.shape[2]
    tile_cols = pixel_colors.shape[3]
    input_width = input_matrices.shape[1]
    grid_rows = lax.axis_size("rows")
    grid_cols = lax.axis_size("cols")
    all_rows = rows_dev * grid_rows * grid_cols
    row_place = lax.axis_index("rows")
    col_place = lax.axis_index("cols")
    row_start = row_place * tile_rows
    col_start = col_place * tile_cols
    score_scale = model_width ** (-0.5)
    head_scale = HEAD_DIM ** (-0.5)
    g_cross = to_float(cross_gains)
    b_cross = to_float(cross_biases)
    g_self = to_float(self_gains)
    b_self = to_float(self_biases)
    g_input = to_float(in_gain)
    b_input = to_float(in_bias)
    latent_state = to_float(latents)
    normed_q = narrow(layer_norm(latent_state, g_cross[0], b_cross[0]))
    query_rows = narrow(matmul(normed_q, cross_matrices[0]) + b_cross[2])
    colors_low = lax.all_gather(pixel_colors, ("rows", "cols"), axis=0, tiled=False)
    colors_low = lax.dynamic_index_in_dim(colors_low, row_place, axis=2, keepdims=False)
    colors_low = colors_low.reshape(grid_rows, grid_cols, 3, tile_rows, tile_cols)
    colors = to_float(
        jnp.transpose(colors_low, (2, 1, 4, 0, 3)).reshape(
            3, grid_cols * tile_cols, grid_rows * tile_rows
        )
    )
    image_box = lax.dynamic_index_in_dim(image_boxes, row_place, axis=0, keepdims=False)
    canvas = canvas_of(colors, image_box)
    mean, deviation, row_in, col_in = canvas[2:]
    inside = (col_in[:, None] & row_in[None, :])[None]
    key_weight = input_matrices[0]
    value_weight = input_matrices[1]
    query_inputs = inner_right(query_rows, key_weight)
    query_lines = against_pixels(query_inputs * g_input, colors, canvas)
    query_shift = jnp.sum(query_inputs * b_input, axis=1)
    scores = jnp.where(
        inside, (query_lines + query_shift[:, None, None]) * score_scale, NEG
    )
    peak_score = jnp.max(scores, axis=(1, 2), keepdims=True)
    weights = jnp.where(inside, jnp.exp(scores - peak_score), 0.0)
    cross_probs = weights / jnp.sum(weights, axis=(1, 2), keepdims=True)
    plain_mixed = over_pixels(cross_probs, colors, canvas)
    mixed_inputs = (
        plain_mixed * g_input + jnp.sum(cross_probs, axis=(1, 2))[:, None] * b_input
    )
    mixed_low = narrow(mixed_inputs)
    attended = matmul(mixed_low, value_weight) + b_cross[3]
    attended_low = narrow(attended)
    first = latent_state + matmul(attended_low, cross_out) + b_cross[4]
    branch, cross_stored = mlp_forward(
        first, g_cross[1], b_cross[1], cross_matrices[1], b_cross[5], cross_matrices[2], b_cross[6]
    )
    second = first + branch
    normed_t = narrow(layer_norm(second, g_self[0], b_self[0]))
    tower_queries = narrow(matmul(normed_t, self_matrices[0]) + b_self[2])
    tower_keys = narrow(matmul(normed_t, self_matrices[1]))
    tower_values = narrow(matmul(normed_t, self_matrices[2]) + b_self[3])
    keys_group, values_group = (
        lax.all_gather(tower_keys, "cols", axis=0, tiled=True),
        lax.all_gather(tower_values, "cols", axis=0, tiled=True),
    )
    group_rows = keys_group.shape[0]
    query_image = (
        (row_place * grid_cols + col_place) * rows_dev + jnp.arange(rows_dev, dtype=jnp.int32)
    ) // LATENTS
    key_image = (row_place * group_rows + jnp.arange(group_rows, dtype=jnp.int32)) // LATENTS
    same_image = (query_image[:, None] == key_image[None, :])[None]
    query_heads = tower_queries.reshape(rows_dev, HEADS, HEAD_DIM)
    key_heads = keys_group.reshape(group_rows, HEADS, HEAD_DIM)
    value_heads = values_group.reshape(group_rows, HEADS, HEAD_DIM)
    head_scores = jnp.where(
        same_image,
        jnp.einsum("qhd,khd->hqk", query_heads, key_heads, preferred_element_type=jnp.float32)
        * head_scale,
        NEG,
    )
    head_weights = jnp.where(
        same_image, jnp.exp(head_scores - jnp.max(head_scores, axis=2, keepdims=True)), 0.0
    )
    head_probs = head_weights / jnp.sum(head_weights, axis=2, keepdims=True)
    probs_low = narrow(head_probs)
    tower_mixed = narrow(
        jnp.einsum(
            "hqk,khd->qhd", probs_low, value_heads, preferred_element_type=jnp.float32
        ).reshape(rows_dev, model_width)
    )
    third = second + matmul(tower_mixed, self_out) + b_self[4]
    branch, tower_stored = mlp_forward(
        third, g_self[1], b_self[1], self_matrices[3], b_self[5], self_matrices[4], b_self[6]
    )
    new_latents = narrow(third + branch)
    gradient = to_float(cotangent)
    gradient, tower_mlp_w, tower_mlp_v, tower_lows = mlp_backward(
        third, g_self[1], b_self[1], self_matrices[3], self_matrices[4], tower_stored, gradient
    )
    tower_out_low = narrow(gradient)
    d_self_out = inner_left(tower_mixed, tower_out_low)
    d_self_out_bias = jnp.sum(gradient, axis=0)
    d_mixed = narrow(inner_right(tower_out_low, self_out)).reshape(rows_dev, HEADS, HEAD_DIM)
    d_probs = jnp.einsum("qhd,khd->hqk", d_mixed, value_heads, preferred_element_type=jnp.float32)
    d_value_heads = jnp.einsum(
        "hqk,qhd->khd", probs_low, d_mixed, preferred_element_type=jnp.float32
    )
    d_scores = head_probs * (d_probs - jnp.sum(head_probs * d_probs, axis=2, keepdims=True))
    d_scores_low = narrow(d_scores * head_scale)
    d_query_heads = jnp.einsum(
        "hqk,khd->qhd", d_scores_low, key_heads, preferred_element_type=jnp.float32
    ).reshape(rows_dev, model_width)
    d_key_heads = jnp.einsum(
        "hqk,qhd->khd", d_scores_low, query_heads, preferred_element_type=jnp.float32
    )
    d_tower_keys, d_tower_values = (
        lax.psum_scatter(
            d_key_heads.reshape(group_rows, model_width).astype(jnp.bfloat16),
            "cols",
            scatter_dimension=0,
            tiled=True,
        ).astype(jnp.float32),
        lax.psum_scatter(
            d_value_heads.reshape(group_rows, model_width).astype(jnp.bfloat16),
            "cols",
            scatter_dimension=0,
            tiled=True,
        ).astype(jnp.float32),
    )
    tq_low = narrow(d_query_heads)
    tk_low = narrow(d_tower_keys)
    tv_low = narrow(d_tower_values)
    d_normed_t = (
        inner_right(tq_low, self_matrices[0])
        + inner_right(tk_low, self_matrices[1])
        + inner_right(tv_low, self_matrices[2])
    )
    d_second, d_self_gain, d_self_bias = norm_back(second, g_self[0], b_self[0], d_normed_t)
    gradient = gradient + d_second
    self_gain_grad = jnp.stack([d_self_gain, tower_mlp_v[0]])
    self_bias_grad = jnp.stack(
        [
            d_self_bias,
            tower_mlp_v[1],
            jnp.sum(d_query_heads, axis=0),
            jnp.sum(d_tower_values, axis=0),
            d_self_out_bias,
            tower_mlp_v[2],
            tower_mlp_v[3],
        ]
    )
    gradient, cross_mlp_w, cross_mlp_v, cross_lows = mlp_backward(
        first, g_cross[1], b_cross[1], cross_matrices[1], cross_matrices[2], cross_stored, gradient
    )
    cross_out_low = narrow(gradient)
    d_cross_out = inner_left(attended_low, cross_out_low)
    d_cross_out_bias = jnp.sum(gradient, axis=0)
    d_attended = narrow(inner_right(cross_out_low, cross_out))
    value_shift = jnp.sum(to_float(d_attended) * b_cross[3], axis=1)
    row_delta = jnp.sum(to_float(d_attended) * attended, axis=1) - value_shift
    grad_inputs = inner_right(d_attended, value_weight)
    grad_shift = jnp.sum(grad_inputs * b_input, axis=1)
    grad_lines = against_pixels(grad_inputs * g_input, colors, canvas)
    d_scores = (
        cross_probs * (grad_lines + (grad_shift - row_delta)[:, None, None]) * score_scale
    )
    plain_scores = over_pixels(d_scores, colors, canvas)
    score_sum = jnp.sum(d_scores, axis=(1, 2))
    prob_sum = jnp.sum(cross_probs, axis=(1, 2))
    score_inputs = plain_scores * g_input + score_sum[:, None] * b_input
    score_low = narrow(score_inputs)
    d_query_rows = matmul(score_low, key_weight)
    in_gain_part = jnp.sum(query_inputs * plain_scores + grad_inputs * plain_mixed, axis=0)
    in_bias_part = jnp.sum(
        query_inputs * score_sum[:, None] + grad_inputs * prob_sum[:, None], axis=0
    )
    query_scaled = query_inputs * g_input
    grad_scaled = grad_inputs * g_input
    query_away = query_scaled[:, :3] - jnp.mean(query_scaled, axis=1, keepdims=True)
    grad_away = grad_scaled[:, :3] - jnp.mean(grad_scaled, axis=1, keepdims=True)
    along = jnp.sum(d_scores * query_lines + cross_probs * grad_lines, axis=0) / input_width
    color_parts = jnp.einsum(
        "rj,rcy->jcy", query_away, d_scores, precision=lax.Precision.HIGHEST
    ) + jnp.einsum("rj,rcy->jcy", grad_away, cross_probs, precision=lax.Precision.HIGHEST)
    color_parts = deviation[None] * (
        color_parts - (colors - mean[None]) * deviation[None] * along[None]
    )
    color_parts = color_parts.reshape(3, grid_cols, tile_cols, grid_rows, tile_rows)
    color_parts = jnp.transpose(color_parts, (3, 1, 0, 4, 2)).reshape(
        grid_rows * grid_cols, 3, tile_rows, tile_cols
    )
    color_grad = lax.all_to_all(
        color_parts, ("rows", "cols"), split_axis=0, concat_axis=0, tiled=True
    ).reshape(image_count, grid_cols, 3, tile_rows, tile_cols)
    color_grad = jnp.transpose(jnp.sum(color_grad, axis=1), (1, 0, 2, 3))
    query_low = narrow(d_query_rows)
    d_latent, d_cross_gain, d_cross_bias = norm_back(
        latent_state, g_cross[0], b_cross[0], inner_right(query_low, cross_matrices[0])
    )
    latent_grad = gradient + d_latent
    in_gain_grad, in_bias_grad = lax.psum((in_gain_part, in_bias_part), ("rows", "cols"))
    vectors = jnp.stack(
        [
            d_cross_gain,
            cross_mlp_v[0],
            d_cross_bias,
            cross_mlp_v[1],
            jnp.sum(d_query_rows, axis=0),
            jnp.sum(to_float(d_attended), axis=0),
            d_cross_out_bias,
            cross_mlp_v[2],
            cross_mlp_v[3],
            d_self_gain,
            tower_mlp_v[0],
            d_self_bias,
            tower_mlp_v[1],
            jnp.sum(d_query_heads, axis=0),
            jnp.sum(d_tower_values, axis=0),
            d_self_out_bias,
            tower_mlp_v[2],
            tower_mlp_v[3],
        ]
    )
    vector_sums = lax.psum_scatter(vectors, ("rows", "cols"), scatter_dimension=1, tiled=True)
    lefts = jnp.stack(
        [
            normed_q,
            cross_stored[0],
            cross_stored[2],
            attended_low,
            normed_t,
            tower_stored[0],
            tower_stored[2],
            tower_mixed,
        ]
    )
    rights = jnp.stack(
        [
            query_low,
            cross_lows[0],
            cross_lows[1],
            cross_out_low,
            d_attended,
            query_rows,
            tq_low,
            tk_low,
            tv_low,
            tower_lows[0],
            tower_lows[1],
            tower_out_low,
        ]
    )
    small_lefts = jnp.stack([mixed_low, score_low])
    lefts = lax.all_gather(lefts, "cols", axis=1, tiled=True)
    small_lefts = lax.all_gather(small_lefts, "cols", axis=1, tiled=True)
    own = model_width // (grid_rows * grid_cols)
    rights = rights.reshape(rights.shape[0], rows_dev, grid_rows, grid_cols, own)
    rights = lax.all_to_all(
        jnp.transpose(rights, (3, 0, 1, 2, 4)), "cols", split_axis=0, concat_axis=0, tiled=False
    )
    rights = jnp.transpose(rights, (1, 0, 2, 3, 4)).reshape(
        rights.shape[1], grid_cols * rows_dev, grid_rows * own
    )
    pairs = ((0, 0), (1, 1), (2, 2), (3, 3), (4, 6), (4, 7), (4, 8), (5, 9), (6, 10), (7, 11))
    big = [inner_left(rights[k], lefts[i]).reshape(grid_rows, own, model_width) for i, k in pairs]
    small = [
        inner_left(rights[k], small_lefts[i]).reshape(grid_rows, own, input_width)
        for i, k in ((1, 5), (0, 4))
    ]
    big = lax.psum_scatter(jnp.stack(big, axis=1), "rows", scatter_dimension=0, tiled=False)
    small = lax.psum_scatter(jnp.stack(small, axis=1), "rows", scatter_dimension=0, tiled=False)
    big = jnp.transpose(big, (0, 2, 1))
    small = jnp.transpose(small, (0, 2, 1))
    all_sums = (
        big[:3],
        big[3],
        small,
        vector_sums[:2],
        vector_sums[2:9],
        big[4:9],
        big[9],
        vector_sums[9:11],
        vector_sums[11:],
    )
    cross_sums = all_sums[:5]
    self_sums = all_sums[5:]
    return (
        new_latents,
        latent_grad,
        color_grad,
        prior_cross_matrices + cross_sums[0],
        prior_cross_out + cross_sums[1],
        prior_input_matrices + cross_sums[2],
        in_gain_grad,
        in_bias_grad,
        cross_sums[3],
        cross_sums[4],
        self_sums[0],
        self_sums[1],
        self_sums[2],
        self_sums[3],
    )


STEPS_HELD = 8
LANES = 128
MESH = pl.DeviceIdType.MESH
WIDE = 3 * LANES


def own_dot(former, latter, former_dim, latter_dim):
    return lax.dot_general(
        former,
        latter,
        (((former_dim,), (latter_dim,)), ((), ())),
        preferred_element_type=jnp.float32,
    )


def selections(tile_cols, grid_cols, steps):
    held = STEPS_HELD
    blocks = -(-steps // held)
    place = np.zeros((grid_cols * 32, WIDE), np.float32)
    back = np.zeros((grid_cols * 32, blocks * LANES), np.float32)
    for tile in range(grid_cols):
        for channel in range(3):
            for offset in range(tile_cols):
                col = tile * tile_cols + offset
                line = tile * 32 + channel * tile_cols + offset
                place[line, channel * LANES + col] = 1
                half, step = divmod(col, steps)
                back[line, step * 16 + half * 8 + channel] = 1
    pick = np.zeros((7 * LANES, blocks * LANES), np.float32)
    for step in range(steps):
        for half in range(2):
            for slot, kind in enumerate((0, 1, 2, 3, 4, 3, 5, 6)):
                pick[kind * LANES + half * steps + step, step * 16 + half * 8 + slot] = 1
    spread = np.zeros((LANES, 2 * LANES), np.float32)
    for group in range(16):
        for channel in range(3):
            for slot in (3, 4):
                spread[group * 8 + slot, group * 8 + channel] = 1
            for slot in (6, 7):
                spread[group * 8 + slot, LANES + group * 8 + channel] = 1
    low = lambda values: np.asarray(values, ml_dtypes.bfloat16)
    return (low(place), low(pick), low(pick.T), low(spread), low(back))


def norm_parts(values):
    middle = jnp.mean(values, axis=1, keepdims=True)
    centered = values - middle
    spread = jnp.mean(centered * centered, axis=1, keepdims=True)
    factor = lax.rsqrt(spread + EPS)
    return (centered * factor, factor)


def norm_forward(values, gain, offset):
    return narrow(norm_parts(values)[0] * gain + offset)


def norm_gradient(values, gain, gradient):
    plain, factor = norm_parts(values)
    inner = gradient * gain
    first = jnp.mean(inner, axis=1, keepdims=True)
    second = jnp.mean(inner * plain, axis=1, keepdims=True)
    return (
        factor * (inner - first - plain * second),
        jnp.sum(gradient * plain, axis=0, keepdims=True),
        jnp.sum(gradient, axis=0, keepdims=True),
    )


GELU_RATE = 0.7978845608028654
GELU_CUBE = 0.044715


def gelu_value(u):
    return 0.5 * u * (1.0 + jnp.tanh(GELU_RATE * (u + GELU_CUBE * u * u * u)))


def gelu_slope(u):
    bent = jnp.tanh(GELU_RATE * (u + GELU_CUBE * u * u * u))
    return 0.5 * (1.0 + bent) + 0.5 * u * (1.0 - bent * bent) * GELU_RATE * (
        1.0 + 3.0 * GELU_CUBE * u * u
    )


def waves(turns):
    near = turns - 2.0 * jnp.floor(turns * 0.5 + 0.5)
    return (jnp.sin(jnp.pi * near), jnp.cos(jnp.pi * near))


def axis_lines(place, slot):
    lane = lax.broadcasted_iota(jnp.int32, (place.shape[0], LANES), 1)
    band = lax.rem(lane, NBANDS)
    frequency = 1.0 + to_float(band) * ((FREQ_TOP - 1.0) / (NBANDS - 1))
    sine, cosine = waves(place * frequency)
    return jnp.concatenate(
        [jnp.where(lane < NBANDS, sine, cosine), jnp.where(lane == slot, place, 0.0)], axis=1
    )


def layer_kernel(
    sizes,
    boxes, latents, cotangent, color_tiles, input_gains, cross_gains, cross_biases, self_gains,
    self_biases, place, pick, pick_t, spread, back, prior_cross, prior_out,
    w_cross, w_out, w_self, w_self_out, w_input,
    new_latents, latent_grad, color_out, cross_total, out_total, self_total, self_out_total,
    input_parts, vector_out, input_vector_out,
    wts, win, xbuf, xsmall, gsrc, gbuf, staged, arrived, staged_small, arrived_small,
    colbuf, img, img7, fa, ft, sl, ycoef, xcoef, yfeat, xfeat, mixrow,
    cgright, rowsum, colsum, cgacc, cgsend, cgbuf,
    act, lnvec, lnbuf, biasvec, vecsend, vecbuf, ivec, ivbuf,
    heads, probs, prob_grad, mix_s, mix_b, dmix_b, dqkv_s, dqkv_b,
    weight_sem, x_send, x_recv, y_send, y_recv, g_send, g_recv, a_send, a_recv, r_send, r_recv,
    misc_send, misc_recv,
):
    grid_rows, grid_cols, rows, steps, tile_rows, tile_cols = sizes
    n_dev = grid_rows * grid_cols
    width = latents.shape[1]
    quads = grid_cols // 2
    chunk = width // grid_cols
    own = chunk // grid_rows
    tall = grid_rows * tile_rows
    z = lax.axis_index("rows")
    j = lax.axis_index("cols")
    core = lax.rem(j, 2)
    quad = j // 2
    me = z * grid_cols + j
    f32, bf16 = jnp.float32, jnp.bfloat16
    score_scale = width ** (-0.5)
    head_scale = HEAD_DIM ** (-0.5)

    def at_device(d):
        return {"rows": d // grid_cols, "cols": lax.rem(d, grid_cols)}

    def lanes_of(index):
        return pl.ds(pl.multiple_of(index * chunk, chunk), chunk)

    def push(src, dst, send, recv, where):
        pltpu.make_async_remote_copy(
            src_ref=src, dst_ref=dst, send_sem=send, recv_sem=recv, device_id=where,
            device_id_type=MESH,
        ).start()

    def wait_for(ref, sem):
        pltpu.make_async_copy(ref, ref, sem).wait()

    barrier = pltpu.get_barrier_semaphore()

    def greet(step, carry):
        pl.semaphore_signal(
            barrier, inc=1, device_id=at_device(lax.rem(me + step, n_dev)), device_id_type=MESH
        )
        return carry

    lax.fori_loop(1, n_dev, greet, 0)

    sources = (
        [w_cross.at[0], w_out, w_cross.at[1], w_cross.at[2]]
        + [w_self.at[0], w_self.at[1], w_self.at[2], w_self_out, w_self.at[3], w_self.at[4]]
    )
    CQ, CO, C1, C2, SQ, SK, SV, SO, S1, S2 = range(10)
    loads = [pltpu.make_async_copy(s, wts.at[k], weight_sem.at[k]) for k, s in enumerate(sources)]
    loads.append(pltpu.make_async_copy(w_input, win, weight_sem.at[10]))
    loads[CQ].start()
    loads[10].start()

    gc, bc = to_float(cross_gains[...]), to_float(cross_biases[...])
    gs, bs = to_float(self_gains[...]), to_float(self_biases[...])
    gin, bin_ = input_gains[0:1], input_gains[1:2]
    lat = to_float(latents[...])
    nq = norm_forward(lat, gc[0:1], bc[0:1])
    xbuf[0, core, quad] = nq

    pl.semaphore_wait(barrier, n_dev - 1)

    def send_color(step, carry):
        d = lax.rem(me + step, n_dev)
        push(color_tiles.at[d // grid_cols], colbuf.at[me], misc_send.at[0], misc_recv.at[0], at_device(d))
        return carry

    lax.fori_loop(1, n_dev, send_color, 0)
    colbuf[me] = color_tiles[z]

    def x_spread(block, sem):
        def one(step, carry):
            peer = 2 * lax.rem(quad + step, quads) + core
            push(block, block, x_send.at[sem], x_recv.at[sem], {"cols": peer})
            return carry

        lax.fori_loop(1, quads, one, 0)

    def x_relay(half, sem):
        wait_for(half.at[pl.ds(0, quads - 1)], x_recv.at[sem])
        push(half, half, y_send.at[sem], y_recv.at[sem], {"cols": j + 1 - 2 * core})

    def x_arrived(half, sem):
        wait_for(half, y_recv.at[sem])

    def spread_x(k):
        x_spread(xbuf.at[k, core, quad], k)

    def relay_x(k):
        x_relay(xbuf.at[k, core], k)

    def have_x(k):
        x_arrived(xbuf.at[k, 1 - core], k)

    def to_plane(step):
        peer = lax.rem(j + step, grid_cols)
        return peer, {"cols": peer}

    def spread_g(k, values):
        gsrc[k] = values

        def one(step, carry):
            peer, where = to_plane(step)
            push(gsrc.at[k, :, lanes_of(peer)], gbuf.at[k, core, quad], g_send.at[k], g_recv.at[k], where)
            return carry

        lax.fori_loop(1, grid_cols, one, 0)
        gbuf[k, core, quad] = gsrc[k, :, lanes_of(j)]

    def have_g(k):
        wait_for(gsrc.at[k, :, pl.ds(0, chunk * (grid_cols - 1))], g_recv.at[k])
        return gbuf[k].reshape(grid_cols * rows, chunk)

    def send_parts(src, dst, sem):
        for part in range(grid_rows):
            d = grid_rows * j + part
            block = src.at[pl.ds(part * own, own)]

            @pl.when(d != me)
            def _():
                push(block, dst.at[z], r_send.at[sem], r_recv.at[sem], at_device(d))

            @pl.when(d == me)
            def _():
                pltpu.make_async_copy(block, dst.at[z], r_recv.at[sem]).start()

    def weight_part(m, right, left):
        def one(n, carry):
            at = pl.ds(pl.multiple_of(n * 256, 256), 256)
            block = left[:, :, :, at].reshape(grid_cols * rows, 256)
            staged[m, :, at] = narrow(own_dot(right, block, 0, 0))
            return carry

        lax.fori_loop(0, width // 256, one, 0)
        send_parts(staged.at[m], arrived.at[m], m)

    def small_part(m, right, left):
        staged_small[m] = narrow(own_dot(right, left[...].reshape(grid_cols * rows, WIDE), 0, 0))
        send_parts(staged_small.at[m], arrived_small.at[m], 10 + m)

    def times(x, k, out):
        def one(n, carry):
            at = pl.ds(pl.multiple_of(n * 256, 256), 256)
            out[:, at] = own_dot(x, wts[k, :, at], 1, 0)
            return carry

        lax.fori_loop(0, width // 256, one, 0)

    def times_t(x, k, out, add=False):
        def one(n, carry):
            at = pl.ds(pl.multiple_of(n * 256, 256), 256)
            result = own_dot(x, wts[k, at, :], 1, 1)
            out[:, at] = out[:, at] + result if add else result
            return carry

        lax.fori_loop(0, width // 256, one, 0)

    FIRST, SECOND, THIRD, PRE_C, PRE_S, TMP, ATT, GRAD = range(8)
    tmp = act.at[TMP]

    spread_x(0)
    loads[CQ].wait()
    for k in range(1, 10):
        loads[k].start()
    times(nq, CQ, tmp)
    query_low = narrow(tmp[...] + bc[2:3])
    spread_g(7, query_low)
    loads[10].wait()
    query_inputs = own_dot(query_low, win[0], 1, 1)

    box = [boxes[z, k] for k in range(4)]

    def filled(value, shape):
        return to_float(jnp.full(shape, value, jnp.int32))

    row_at = lax.broadcasted_iota(jnp.int32, (tall, 1), 0)
    y_place = -1.0 + 2.0 * to_float(row_at - box[0]) / filled(box[2] - 1, (tall, 1))
    y_lines = axis_lines(y_place, 3)
    y_sum = jnp.sum(y_lines, axis=1, keepdims=True)
    row_out = jnp.where((row_at >= box[0]) & (row_at < box[0] + box[2]), 0.0, NEG)
    yfeat[...] = narrow(y_lines)
    held_rows = xfeat.shape[1]
    col_lane = lax.broadcasted_iota(jnp.int32, (held_rows, LANES), 1)
    col_row = lax.broadcasted_iota(jnp.int32, (held_rows, LANES), 0)
    x_sum = jnp.zeros((1, LANES), f32)
    col_out = []
    for half in range(2):
        col_at = lax.broadcasted_iota(jnp.int32, (held_rows, 1), 0) + half * steps
        x_place = -1.0 + 2.0 * to_float(col_at - box[1]) / filled(box[3] - 1, (held_rows, 1))
        x_lines = axis_lines(x_place, 4)
        xfeat[half] = narrow(x_lines)
        here = (col_lane == col_row + half * steps) & (col_row < steps)
        x_sum = x_sum + jnp.sum(
            jnp.where(here, jnp.sum(x_lines, axis=1, keepdims=True), 0.0), axis=0, keepdims=True
        )
        col_out.append(jnp.where((col_at >= box[1]) & (col_at < box[1] + box[3]), 0.0, NEG))
    x_lane = lax.broadcasted_iota(jnp.int32, (1, LANES), 1)
    x_here = -1.0 + 2.0 * to_float(x_lane - box[1]) / filled(box[3] - 1, (1, LANES))
    count = 3 + 2 + 4 * NBANDS

    wait_for(colbuf.at[pl.ds(0, n_dev - 1)], misc_recv.at[0])
    for part in range(grid_rows):
        at = pl.ds(part * tile_rows, tile_rows)
        tiles = colbuf[part * grid_cols : (part + 1) * grid_cols].reshape(grid_cols * 32, LANES)
        img[at, :] = own_dot(tiles, place[...], 0, 0)[:tile_rows]
    c0, c1, c2 = img[:, :LANES], img[:, LANES : 2 * LANES], img[:, 2 * LANES :]
    mean = (c0 + c1 + c2 + y_sum + x_sum) * (1.0 / count)
    square = (c0 * c0 + c1 * c1 + c2 * c2 + y_place * y_place + x_here * x_here + 2.0 * NBANDS) * (
        1.0 / count
    )
    dev = lax.rsqrt(square - mean * mean + EPS)
    mean_low, dev_low = narrow(mean), narrow(dev)
    img7[...] = jnp.concatenate(
        [
            narrow(c0), narrow(c1), narrow(c2),
            mean_low, narrow(mean - to_float(mean_low)),
            dev_low, narrow(dev - to_float(dev_low)),
        ],
        axis=1,
    )
    blocks = fa.shape[0]
    for block in range(blocks):
        at = pl.ds(block * LANES, LANES)
        fa[block] = narrow(own_dot(img7[...], pick[:, at], 1, 0))
        turned = own_dot(pick_t[at, :], img7[...], 1, 1)
        line = lax.broadcasted_iota(jnp.int32, turned.shape, 0)
        ft[at, :] = narrow(jnp.where(lax.rem(line, 8) == 5, 1.0, turned))

    lane1 = lax.broadcasted_iota(jnp.int32, (rows, LANES), 1)
    lane_half = lax.broadcasted_iota(jnp.int32, (8, LANES), 1) // rows
    sub8 = lax.broadcasted_iota(jnp.int32, (8, LANES), 0)

    def twice(values):
        return jnp.concatenate([values, values], axis=0)

    def turn(values):
        return jnp.transpose(twice(values))[:8]

    def coefficients(scaled, extra):
        tail = scaled[:, 2 * LANES :]
        total = jnp.sum(scaled, axis=1, keepdims=True)
        turned = turn(jnp.where(lane1 == 5, total, jnp.where(lane1 == 6, extra, tail)))
        total_high = to_float(narrow(turned[5:6]))
        body = jnp.where(
            sub8 < 3, turned, jnp.where(sub8 < 5, -total_high, jnp.where(sub8 == 5, total_high - turned[5:6], 0.0))
        )
        body = narrow(jnp.concatenate(
            [jnp.where(lane_half == 0, body, 0.0), jnp.where(lane_half == 1, body, 0.0)], axis=0
        ))
        ones = jnp.where(sub8 >= 6, 1.0, 0.0)
        ones = narrow(jnp.concatenate(
            [jnp.where(lane_half == 0, ones, 0.0), jnp.where(lane_half == 1, ones, 0.0)], axis=0
        ))
        mixrow[...] = jnp.zeros(mixrow.shape, bf16)
        for held in range(STEPS_HELD):
            mixrow[held, held * 16 : held * 16 + 16, :] = jnp.concatenate([body, ones], axis=1)
        scaled_low = narrow(jnp.concatenate([scaled[:, :LANES], tail], axis=1))
        ycoef[...] = own_dot(yfeat[...], twice(scaled_low), 1, 1)
        scaled_low = narrow(jnp.concatenate([scaled[:, LANES : 2 * LANES], tail], axis=1))
        nothing = jnp.zeros_like(scaled_low)
        xcoef[...] = own_dot(xfeat[0], jnp.concatenate([scaled_low, nothing], axis=0), 1, 1) + own_dot(
            xfeat[1], jnp.concatenate([nothing, scaled_low], axis=0), 1, 1
        )
        return turned

    def step_lines(s):
        block, held = s // STEPS_HELD, lax.rem(s, STEPS_HELD)
        result = own_dot(fa[block], mixrow[held], 1, 0)
        deviation = result[:, LANES:]
        lines = (ycoef[...] + xcoef[pl.ds(s, 1), :] + result[:, :LANES]) * deviation
        return lines, deviation

    def step_sums(s, weighted):
        rowsum[...] += weighted
        at = pl.ds(pl.multiple_of(s * 16, 16), 16)
        found = own_dot(ft[at, :], narrow(weighted), 1, 0)
        found = jnp.where(lane_half == 0, found[:8], found[8:])
        colsum[pl.ds(s, 1), :] = found[5:6]
        return found

    def fold(values):
        return values[:rows] + values[rows:]

    def pixel_sums(found, factor):
        by_row = fold(own_dot(narrow(rowsum[...] * factor), yfeat[...], 0, 0))
        cols = narrow(colsum[...] * factor)
        by_col = own_dot(cols, xfeat[0], 0, 0)[:rows] + own_dot(cols, xfeat[1], 0, 0)[rows:]
        padded = jnp.concatenate([found * factor, jnp.zeros((LANES - 8, LANES), f32)], axis=0)
        sums = fold(jnp.transpose(padded))
        middle = sums[:, 3:4] + sums[:, 4:5]
        tail = jnp.where(lane1 < 3, sums, 0.0) + by_row[:, LANES:] + by_col[:, LANES:]
        return jnp.concatenate([by_row[:, :LANES], by_col[:, :LANES], tail], axis=1) - middle

    def other_half(line):
        return pltpu.roll(jnp.broadcast_to(line, (8, LANES)), rows, 1)[:1]

    query_scaled = query_inputs * gin * score_scale
    coefficients(query_scaled, 0.0)
    ycoef[...] += row_out
    half_lane = lax.broadcasted_iota(jnp.int32, (held_rows, LANES), 1) // rows
    xcoef[...] += jnp.where(half_lane == 0, col_out[0], col_out[1])

    def first_pass(s, best):
        lines, deviation = step_lines(s)
        sl[s] = lines
        return jnp.maximum(best, jnp.max(lines, axis=0, keepdims=True))

    best = lax.fori_loop(0, steps, first_pass, jnp.full((1, LANES), -3e38, f32))
    best = jnp.maximum(best, other_half(best))
    rowsum[...] = jnp.zeros(rowsum.shape, f32)
    colsum[...] = jnp.zeros(colsum.shape, f32)

    def second_pass(s, carry):
        total, found = carry
        block, held = s // STEPS_HELD, lax.rem(s, STEPS_HELD)
        deviation = own_dot(fa[block], mixrow[held][:, LANES:], 1, 0)
        weights = jnp.exp(sl[s] - best)
        total = total + jnp.sum(weights, axis=0, keepdims=True)
        return total, found + step_sums(s, weights * deviation)

    total, found = lax.fori_loop(
        0, steps, second_pass, (jnp.zeros((1, LANES), f32), jnp.zeros((8, LANES), f32))
    )
    total = total + other_half(total)
    log_total = best + jnp.log(total)
    plain_mixed = pixel_sums(found, 1.0 / total)
    mixed_low = narrow(plain_mixed * gin + bin_)
    xsmall[0, core, quad] = mixed_low
    relay_x(0)
    attended = own_dot(mixed_low, win[1], 1, 0) + bc[3:4]
    act[ATT] = attended
    attended_low = narrow(attended)
    xbuf[3, core, quad] = attended_low
    loads[CO].wait()
    times(attended_low, CO, tmp)
    first = lat + tmp[...] + bc[4:5]
    act[FIRST] = first
    normed_c = norm_forward(first, gc[1:2], bc[1:2])
    xbuf[1, core, quad] = normed_c
    loads[C1].wait()
    times(normed_c, C1, tmp)
    pre = tmp[...] + bc[5:6]
    act[PRE_C] = pre
    hidden_c = narrow(gelu_value(pre))
    xbuf[2, core, quad] = hidden_c
    loads[C2].wait()
    times(hidden_c, C2, tmp)
    second = act[FIRST] + tmp[...] + bc[6:7]
    act[SECOND] = second
    normed_t = norm_forward(second, gs[0:1], bs[0:1])
    xbuf[4, core, quad] = normed_t
    spread_x(4)
    relay_x(4)
    x_spread(xsmall.at[0, core, quad], 8)
    spread_x(3)
    spread_x(1)
    spread_x(2)
    have_x(4)

    for k in (SQ, SK, SV):
        loads[k].wait()
    head_rows = grid_cols * rows
    biasvec[...] = jnp.concatenate([bs, jnp.zeros((1, width), f32)], axis=0)

    def head_in(n, carry):
        x = xbuf[4, n].reshape(quads * rows, width)
        at = pl.ds(pl.multiple_of(n * (quads * rows), quads * rows), quads * rows)
        heads[0, at, :] = narrow(own_dot(x, wts[SQ, :, lanes_of(j)], 1, 0) + biasvec[2:3, lanes_of(j)])
        heads[1, at, :] = narrow(own_dot(x, wts[SK, :, lanes_of(j)], 1, 0))
        heads[2, at, :] = narrow(own_dot(x, wts[SV, :, lanes_of(j)], 1, 0) + biasvec[3:4, lanes_of(j)])
        return carry

    lax.fori_loop(0, 2, head_in, 0)
    per = 128

    def head_forward(n, carry):
        at = pl.ds(pl.multiple_of(n * per, per), per)
        scores = own_dot(heads[0, at, :], heads[1], 1, 1) * head_scale
        weights = jnp.exp(scores - jnp.max(scores, axis=1, keepdims=True))
        found_probs = weights / jnp.sum(weights, axis=1, keepdims=True)
        probs[at, :] = found_probs
        mixed = narrow(own_dot(narrow(found_probs), heads[2], 1, 0))
        for part in range(per // rows):
            mix_s[n * (per // rows) + part] = mixed[part * rows : (part + 1) * rows]
        return carry

    lax.fori_loop(0, head_rows // per, head_forward, 0)

    def block_of(peer):
        return lax.rem(peer, 2) * quads + peer // 2

    mine = core * quads + quad

    def send_mixed(step, carry):
        peer, where = to_plane(step)
        push(mix_s.at[block_of(peer)], mix_b.at[:, lanes_of(j)], a_send.at[0], a_recv.at[0], where)
        return carry

    lax.fori_loop(1, grid_cols, send_mixed, 0)
    mix_b[:, lanes_of(j)] = mix_s[mine]
    relay_x(3)
    relay_x(1)
    relay_x(2)
    x_relay(xsmall.at[0, core], 8)
    loads[SO].wait()
    wait_for(mix_b.at[:, pl.ds(0, chunk * (grid_cols - 1))], a_recv.at[0])
    mixed_rows = mix_b[...]
    xbuf[7, core, quad] = mixed_rows
    times(mixed_rows, SO, tmp)
    third = act[SECOND] + tmp[...] + bs[4:5]
    act[THIRD] = third
    normed_s = norm_forward(third, gs[1:2], bs[1:2])
    xbuf[5, core, quad] = normed_s
    spread_x(7)
    loads[S1].wait()
    times(normed_s, S1, tmp)
    spread_x(5)
    pre = tmp[...] + bs[5:6]
    act[PRE_S] = pre
    hidden_s = narrow(gelu_value(pre))
    xbuf[6, core, quad] = hidden_s
    spread_x(6)
    loads[S2].wait()
    times(hidden_s, S2, tmp)
    new_latents[...] = narrow(act[THIRD] + tmp[...] + bs[6:7])

    cot_low = cotangent[...]
    spread_g(5, cot_low)
    times_t(cot_low, S2, tmp)
    d_pre = tmp[...] * gelu_slope(act[PRE_S])
    pre_low = narrow(d_pre)
    spread_g(4, pre_low)
    times_t(pre_low, S1, tmp)
    d_rows, lnvec[6:7, :], lnvec[7:8, :] = norm_gradient(act[THIRD], gs[1:2], tmp[...])
    gradient = to_float(cot_low) + d_rows
    act[GRAD] = gradient
    out_low = narrow(gradient)
    times_t(out_low, SO, tmp)
    mix_b2 = narrow(tmp[...])
    gsrc[9] = mix_b2

    def send_dmixed(step, carry):
        peer, where = to_plane(step)
        push(gsrc.at[9, :, lanes_of(peer)], dmix_b.at[mine], a_send.at[1], a_recv.at[1], where)
        return carry

    lax.fori_loop(1, grid_cols, send_dmixed, 0)
    dmix_b[mine] = gsrc[9, :, lanes_of(j)]
    spread_g(6, out_low)
    relay_x(7)
    relay_x(5)
    relay_x(6)
    wait_for(dmix_b.at[pl.ds(0, grid_cols - 1)], a_recv.at[1])

    def head_backward(n, carry):
        at = pl.ds(pl.multiple_of(n * per, per), per)
        parts = [dmix_b[n * (per // rows) + part] for part in range(per // rows)]
        d_mixed = jnp.concatenate(parts, axis=0)
        d_probs = own_dot(d_mixed, heads[2], 1, 1)
        found_probs = probs[at, :]
        d_scores = found_probs * (d_probs - jnp.sum(found_probs * d_probs, axis=1, keepdims=True))
        d_low = narrow(d_scores * head_scale)
        prob_grad[0, at, :] = d_low
        prob_grad[1, at, :] = narrow(found_probs)
        d_query = own_dot(d_low, heads[1], 1, 0)
        for part in range(per // rows):
            dqkv_s[n * (per // rows) + part, 0] = narrow(d_query[part * rows : (part + 1) * rows])
        return carry + jnp.sum(d_query, axis=0, keepdims=True)

    query_bias = lax.fori_loop(0, head_rows // per, head_backward, jnp.zeros((1, chunk), f32))
    d_mixed_all = dmix_b[...].reshape(head_rows, chunk)

    def head_keys(n, carry):
        at = pl.ds(pl.multiple_of(n * per, per), per)
        d_key = own_dot(prob_grad[0, :, at], heads[0], 0, 0)
        d_value = own_dot(prob_grad[1, :, at], d_mixed_all, 0, 0)
        for part in range(per // rows):
            cut = slice(part * rows, (part + 1) * rows)
            dqkv_s[n * (per // rows) + part, 1] = narrow(d_key[cut])
            dqkv_s[n * (per // rows) + part, 2] = narrow(d_value[cut])
        return carry + jnp.sum(d_value, axis=0, keepdims=True)

    value_bias = lax.fori_loop(0, head_rows // per, head_keys, jnp.zeros((1, chunk), f32))

    def send_dqkv(step, carry):
        peer, where = to_plane(step)
        push(dqkv_s.at[block_of(peer)], dqkv_b.at[:, :, lanes_of(j)], a_send.at[2], a_recv.at[2], where)
        return carry

    lax.fori_loop(1, grid_cols, send_dqkv, 0)
    dqkv_b[:, :, lanes_of(j)] = dqkv_s[mine]

    def column_sum(values):
        return jnp.sum(to_float(values), axis=0, keepdims=True)

    have_x(6)
    right = have_g(5)
    bias_s6 = column_sum(right)
    weight_part(8, right, xbuf.at[6])
    have_x(5)
    right = have_g(4)
    bias_s5 = column_sum(right)
    weight_part(7, right, xbuf.at[5])

    wait_for(dqkv_b.at[:, :, pl.ds(0, chunk * (grid_cols - 1))], a_recv.at[2])
    times_t(dqkv_b[0], SQ, tmp)
    times_t(dqkv_b[1], SK, tmp, True)
    times_t(dqkv_b[2], SV, tmp, True)
    d_rows, lnvec[4:5, :], lnvec[5:6, :] = norm_gradient(act[SECOND], gs[0:1], tmp[...])
    gradient = act[GRAD] + d_rows
    act[GRAD] = gradient
    second_low = narrow(gradient)
    spread_g(2, second_low)
    times_t(second_low, C2, tmp)
    d_pre = tmp[...] * gelu_slope(act[PRE_C])
    pre_low = narrow(d_pre)
    spread_g(1, pre_low)
    times_t(pre_low, C1, tmp)
    d_rows, lnvec[2:3, :], lnvec[3:4, :] = norm_gradient(act[FIRST], gc[1:2], tmp[...])
    gradient = act[GRAD] + d_rows
    act[GRAD] = gradient
    out_low = narrow(gradient)
    spread_g(3, out_low)
    times_t(out_low, CO, tmp)
    d_attended = narrow(tmp[...])
    spread_g(8, d_attended)

    have_x(7)
    right = have_g(6)
    bias_s4 = column_sum(right)
    weight_part(9, right, xbuf.at[7])
    for k in range(3):
        weight_part(4 + k, dqkv_s[:, k].reshape(head_rows, chunk), xbuf.at[4])

    grad_inputs = own_dot(d_attended, win[1], 1, 1)
    d_attended = to_float(d_attended)
    shift = jnp.sum(d_attended * bc[3:4], axis=1, keepdims=True)
    row_delta = jnp.sum(d_attended * act[ATT], axis=1, keepdims=True) - shift
    grad_shift = jnp.sum(grad_inputs * bin_, axis=1, keepdims=True)
    grad_scaled = grad_inputs * gin
    turned = coefficients(grad_scaled, grad_shift - row_delta)
    constant = turned[6:7]

    def away(scaled):
        values = scaled[:, 2 * LANES :] - jnp.sum(scaled, axis=1, keepdims=True) * (1.0 / count)
        values = jnp.where(lane1 < 3, values, 0.0)
        return jnp.concatenate([values, pltpu.roll(values, 8, 1)], axis=0)

    query_away, grad_away = away(query_scaled), away(grad_scaled)
    wide_lane = lax.broadcasted_iota(jnp.int32, (LANES, LANES), 1)
    wide_half = lax.broadcasted_iota(jnp.int32, (LANES, LANES), 0) // rows
    blank = jnp.zeros((LANES, LANES), bf16)
    for held in range(STEPS_HELD):
        group = wide_lane - held * 16 - wide_half * 8
        along = narrow(jnp.where((group >= 0) & (group < 3), 1.0, 0.0))
        colors_here = [query_away, grad_away]
        if held:
            colors_here = [pltpu.roll(v, held * 16, 1) for v in colors_here]
        cgright[held] = jnp.concatenate(
            [
                jnp.concatenate([narrow(colors_here[0]), blank], axis=1),
                jnp.concatenate([narrow(colors_here[1]), blank], axis=1),
                jnp.concatenate([blank, along], axis=1),
            ],
            axis=0,
        )
    rowsum[...] = jnp.zeros(rowsum.shape, f32)
    colsum[...] = jnp.zeros(colsum.shape, f32)
    cgacc[...] = jnp.zeros(cgacc.shape, f32)

    def back_pass(s, carry):
        total, found = carry
        lines, deviation = step_lines(s)
        scores = sl[s]
        found_probs = jnp.exp(scores - log_total)
        d_scores = found_probs * (lines + constant)
        left = jnp.concatenate(
            [narrow(d_scores), narrow(found_probs), narrow(d_scores * scores + found_probs * lines)], axis=1
        )
        block, held = s // STEPS_HELD, lax.rem(s, STEPS_HELD)
        cgacc[block] += own_dot(left, cgright[held], 1, 0)
        total = total + jnp.sum(d_scores, axis=0, keepdims=True)
        return total, found + step_sums(s, d_scores * deviation)

    total, found = lax.fori_loop(
        0, steps, back_pass, (jnp.zeros((1, LANES), f32), jnp.zeros((8, LANES), f32))
    )
    plain_scores = pixel_sums(found, 1.0) * score_scale
    total = total * score_scale
    score_total = fold(jnp.transpose(jnp.concatenate([total, jnp.zeros((LANES - 1, LANES), f32)], axis=0)))[:, 0:1]
    score_low = narrow(plain_scores * gin + score_total * bin_)
    xsmall[1, core, quad] = score_low
    x_spread(xsmall.at[1, core, quad], 9)

    def d_query_part(n, carry):
        at = pl.ds(pl.multiple_of(n * 256, 256), 256)
        tmp[:, at] = own_dot(score_low, win[0, :, at], 1, 0)
        return carry

    lax.fori_loop(0, width // 256, d_query_part, 0)
    query_grad_low = narrow(tmp[...])
    spread_g(0, query_grad_low)
    gain_part = jnp.sum(query_inputs * plain_scores + grad_inputs * plain_mixed, axis=0, keepdims=True)
    bias_part = jnp.sum(query_inputs * score_total + grad_inputs, axis=0, keepdims=True)
    ivec[...] = jnp.concatenate([gain_part, bias_part, jnp.zeros((6, WIDE), f32)], axis=0)
    ivbuf[me] = ivec[...]

    def send_ivec(step, carry):
        push(ivec, ivbuf.at[me], misc_send.at[1], misc_recv.at[1], at_device(lax.rem(me + step, n_dev)))
        return carry

    lax.fori_loop(1, n_dev, send_ivec, 0)

    times_t(query_grad_low, CQ, tmp)
    d_rows, lnvec[0:1, :], lnvec[1:2, :] = norm_gradient(to_float(latents[...]), gc[0:1], tmp[...])
    latent_grad[...] = act[GRAD] + d_rows

    def send_ln(step, carry):
        peer, where = to_plane(step)
        push(lnvec.at[:, lanes_of(peer)], lnbuf.at[j], misc_send.at[2], misc_recv.at[2], where)
        return carry

    lax.fori_loop(1, grid_cols, send_ln, 0)
    lnbuf[j] = lnvec[:, lanes_of(j)]

    for block in range(blocks):
        both = own_dot(fa[block], spread[...], 1, 0)
        center, factor = both[:, :LANES], both[:, LANES:]
        here = cgacc[block]
        cgacc[block, :, :LANES] = factor * (
            here[:, :LANES] - (to_float(fa[block]) - center) * factor * here[:, LANES:] * (1.0 / count)
        )
    for part in range(grid_rows):
        at = pl.ds(part * tile_rows, tile_rows)
        lines = jnp.concatenate([narrow(cgacc[block, at, :LANES]) for block in range(blocks)], axis=1)
        tiles = narrow(own_dot(back[...], lines, 1, 1))
        for tile in range(grid_cols):
            cgsend[part * grid_cols + tile, :, :tile_rows] = tiles[tile * 32 : tile * 32 + 32]
    cgbuf[me] = cgsend[me]

    def send_cg(step, carry):
        d = lax.rem(me + step, n_dev)
        push(cgsend.at[d], cgbuf.at[me], misc_send.at[3], misc_recv.at[3], at_device(d))
        return carry

    lax.fori_loop(1, n_dev, send_cg, 0)

    x_relay(xsmall.at[1, core], 9)
    for m, (left, g) in ((2, (2, 2)), (1, (1, 1)), (3, (3, 3))):
        have_x(left)
        right = have_g(g)
        if m == 2:
            bias_c6 = column_sum(right)
        elif m == 1:
            bias_c5 = column_sum(right)
        else:
            bias_c4 = column_sum(right)
        weight_part(m, right, xbuf.at[left])
    x_arrived(xsmall.at[0, 1 - core], 8)
    right = have_g(8)
    bias_c3 = column_sum(right)
    small_part(1, right, xsmall.at[0])
    have_x(0)
    right = have_g(0)
    bias_c2 = column_sum(right)
    weight_part(0, right, xbuf.at[0])
    x_arrived(xsmall.at[1, 1 - core], 9)
    small_part(0, have_g(7), xsmall.at[1])

    wait_for(lnbuf.at[pl.ds(0, grid_cols - 1)], misc_recv.at[2])
    norms = lnbuf[0]
    for peer in range(1, grid_cols):
        norms = norms + lnbuf[peer]
    vecsend[...] = jnp.concatenate(
        [
            norms, bias_c2, bias_c3, bias_c4, bias_c5, bias_c6, query_bias, value_bias,
            bias_s4, bias_s5, bias_s6, jnp.zeros((6, chunk), f32),
        ],
        axis=0,
    )
    for part in range(grid_rows):
        d = grid_rows * j + part

        @pl.when(d != me)
        def _():
            push(vecsend, vecbuf.at[z], misc_send.at[4], misc_recv.at[4], at_device(d))

        @pl.when(d == me)
        def _():
            pltpu.make_async_copy(vecsend, vecbuf.at[z], misc_recv.at[4]).start()

    wait_for(cgbuf.at[pl.ds(0, n_dev - 1)], misc_recv.at[3])
    for part in range(grid_rows):
        tile = to_float(cgbuf[part * grid_cols])
        for peer in range(1, grid_cols):
            tile = tile + to_float(cgbuf[part * grid_cols + peer])
        color_out[part] = tile
    wait_for(ivbuf.at[pl.ds(0, n_dev - 1)], misc_recv.at[1])
    sums = ivbuf[0]
    for d in range(1, n_dev):
        sums = sums + ivbuf[d]
    input_vector_out[...] = sums

    def gathered(ref):
        result = to_float(ref[0])
        for part in range(1, grid_rows):
            result = result + to_float(ref[part])
        return result

    order = (8, 7, 9, 4, 5, 6, 2, 1, 3, 0)
    for m in order:
        wait_for(arrived.at[m], r_recv.at[m])
        result = gathered(arrived.at[m])
        if m < 3:
            cross_total[m] = prior_cross[m] + result
        elif m == 3:
            out_total[...] = prior_out[...] + result
        elif m < 9:
            self_total[m - 4] = result
        else:
            self_out_total[...] = result
    for m in (1, 0):
        wait_for(arrived_small.at[m], r_recv.at[10 + m])
        input_parts[m] = gathered(arrived_small.at[m])
    wait_for(vecbuf, misc_recv.at[4])
    vector_out[...] = gathered(vecbuf)

    for k in range(8):
        wait_for(xbuf.at[k, 0, pl.ds(0, quads - 1)], x_send.at[k])
        wait_for(xbuf.at[k, 0], y_send.at[k])
    for k in range(2):
        wait_for(xsmall.at[k, 0, pl.ds(0, quads - 1)], x_send.at[8 + k])
        wait_for(xsmall.at[k, 0], y_send.at[8 + k])
    for k in range(9):
        wait_for(gsrc.at[k, :, pl.ds(0, chunk * (grid_cols - 1))], g_send.at[k])
    wait_for(mix_s.at[pl.ds(0, grid_cols - 1)], a_send.at[0])
    wait_for(dmix_b.at[pl.ds(0, grid_cols - 1)], a_send.at[1])
    wait_for(dqkv_s.at[pl.ds(0, grid_cols - 1)], a_send.at[2])
    wait_for(colbuf.at[pl.ds(0, n_dev - 1)], misc_send.at[0])
    wait_for(ivbuf.at[pl.ds(0, n_dev - 1)], misc_send.at[1])
    wait_for(lnbuf.at[pl.ds(0, grid_cols - 1)], misc_send.at[2])
    wait_for(cgbuf.at[pl.ds(0, n_dev - 1)], misc_send.at[3])
    away_from_me = me // grid_rows != j

    @pl.when(away_from_me)
    def _():
        for m in range(10):
            wait_for(staged.at[m], r_send.at[m])
        for m in range(2):
            wait_for(staged_small.at[m], r_send.at[10 + m])
        wait_for(vecbuf, misc_send.at[4])

    @pl.when(jnp.logical_not(away_from_me))
    def _():
        for m in range(10):
            wait_for(staged.at[m, pl.ds(0, chunk - own)], r_send.at[m])
        for m in range(2):
            wait_for(staged_small.at[m, pl.ds(0, chunk - own)], r_send.at[10 + m])
        wait_for(vecbuf.at[pl.ds(0, grid_rows - 1)], misc_send.at[4])


def by_kind(rows):
    n = NBANDS
    parts = [rows[:, 5 : 5 + n], rows[:, 5 + 2 * n : 5 + 3 * n], rows[:, 5 + n : 5 + 2 * n]]
    parts += [rows[:, 5 + 3 * n :], rows[:, :5]]
    spare = WIDE - rows.shape[1]
    return jnp.pad(jnp.concatenate(parts, axis=1), ((0, 0), (0, spare)) + ((0, 0),) * (rows.ndim - 2))


def by_channel(lines):
    n = NBANDS
    parts = [lines[..., 4 * n : 4 * n + 5], lines[..., :n], lines[..., 2 * n : 3 * n]]
    parts += [lines[..., n : 2 * n], lines[..., 3 * n : 4 * n]]
    return jnp.concatenate(parts, axis=-1)


def local_kernel(
    latents,
    pixel_colors,
    image_boxes,
    cotangent,
    cross_matrices,
    cross_out,
    input_matrices,
    in_gain,
    in_bias,
    cross_gains,
    cross_biases,
    self_matrices,
    self_out,
    self_gains,
    self_biases,
    prior_cross_matrices,
    prior_cross_out,
    prior_input_matrices,
):
    rows, width = latents.shape
    channels, image_count, tile_rows, tile_cols = pixel_colors.shape
    grid_rows = lax.axis_size("rows")
    grid_cols = lax.axis_size("cols")
    n_dev = grid_rows * grid_cols
    tall, wide = grid_rows * tile_rows, grid_cols * tile_cols
    steps = wide // 2
    chunk = width // grid_cols
    own = chunk // grid_rows
    quads = grid_cols // 2
    place, pick, pick_t, spread, back = selections(tile_cols, grid_cols, steps)
    blocks = back.shape[1] // LANES
    held_rows = -(-steps // 8) * 8
    color_tiles = jnp.transpose(pixel_colors, (1, 0, 3, 2)).reshape(
        image_count, channels * tile_cols, tile_rows
    )
    color_tiles = jnp.pad(
        color_tiles, ((0, 0), (0, 32 - channels * tile_cols), (0, LANES - tile_rows))
    )
    w_input = by_kind(input_matrices)
    input_gains = by_kind(to_float(jnp.stack([in_gain, in_bias])))
    input_gains = jnp.pad(input_gains, ((0, 6), (0, 0)))
    f32, bf16 = jnp.float32, jnp.bfloat16
    vmem = pl.BlockSpec(memory_space=pltpu.VMEM)
    away = pl.BlockSpec(memory_space=pl.ANY)
    shape = jax.ShapeDtypeStruct
    sizes = (grid_rows, grid_cols, rows, steps, tile_rows, tile_cols)
    dma = pltpu.SemaphoreType.DMA
    scratch = [
        ((10, width, width), bf16),
        ((2, WIDE, width), bf16),
        ((8, 2, quads, rows, width), bf16),
        ((2, 2, quads, rows, WIDE), bf16),
        ((10, rows, width), bf16),
        ((9, 2, quads, rows, chunk), bf16),
        ((10, chunk, width), bf16),
        ((10, grid_rows, own, width), bf16),
        ((2, chunk, WIDE), bf16),
        ((2, grid_rows, own, WIDE), bf16),
        ((n_dev, 32, LANES), bf16),
        ((tall, WIDE), f32),
        ((tall, 7 * LANES), bf16),
        ((blocks, tall, LANES), bf16),
        ((blocks * LANES, tall), bf16),
        ((steps, tall, LANES), f32),
        ((tall, LANES), f32),
        ((held_rows, LANES), f32),
        ((tall, 2 * LANES), bf16),
        ((2, held_rows, 2 * LANES), bf16),
        ((STEPS_HELD, LANES, 2 * LANES), bf16),
        ((STEPS_HELD, WIDE, 2 * LANES), bf16),
        ((tall, LANES), f32),
        ((held_rows, LANES), f32),
        ((blocks, tall, 2 * LANES), f32),
        ((n_dev, 32, LANES), bf16),
        ((n_dev, 32, LANES), bf16),
        ((8, rows, width), f32),
        ((8, width), f32),
        ((grid_cols, 8, chunk), f32),
        ((8, width), f32),
        ((24, chunk), f32),
        ((grid_rows, 24, chunk), f32),
        ((8, WIDE), f32),
        ((n_dev, 8, WIDE), f32),
        ((3, grid_cols * rows, chunk), bf16),
        ((grid_cols * rows, grid_cols * rows), f32),
        ((2, grid_cols * rows, grid_cols * rows), bf16),
        ((grid_cols, rows, chunk), bf16),
        ((rows, width), bf16),
        ((grid_cols, rows, chunk), bf16),
        ((grid_cols, 3, rows, chunk), bf16),
        ((3, rows, width), bf16),
    ]
    scratch = [pltpu.VMEM(dims, kind) for dims, kind in scratch]
    scratch += [dma((count,)) for count in (11, 10, 10, 10, 10, 9, 9, 3, 3, 12, 12, 5, 5)]
    outs = [
        ((rows, width), bf16),
        ((rows, width), f32),
        ((image_count, 32, LANES), f32),
        ((3, own, width), f32),
        ((own, width), f32),
        ((5, own, width), f32),
        ((own, width), f32),
        ((2, own, WIDE), f32),
        ((24, chunk), f32),
        ((8, WIDE), f32),
    ]
    results = pl.pallas_call(
        functools.partial(layer_kernel, sizes),
        out_shape=[shape(dims, kind) for dims, kind in outs],
        in_specs=[pl.BlockSpec(memory_space=pltpu.SMEM)] + [vmem] * 15 + [away] * 5,
        out_specs=[vmem] * len(outs),
        scratch_shapes=scratch,
        compiler_params=pltpu.CompilerParams(
            collective_id=0, has_side_effects=True, vmem_limit_bytes=VMEM_BYTES
        ),
        cost_estimate=pl.CostEstimate(
            flops=20_000_000_000, bytes_accessed=40_000_000, transcendentals=4_000_000
        ),
    )(
        image_boxes,
        latents,
        cotangent,
        color_tiles,
        input_gains,
        cross_gains,
        cross_biases,
        self_gains,
        self_biases,
        place,
        pick,
        pick_t,
        spread,
        back,
        jnp.transpose(prior_cross_matrices, (0, 2, 1)),
        jnp.transpose(prior_cross_out),
        cross_matrices,
        cross_out,
        self_matrices,
        self_out,
        w_input,
    )
    new_latents, latent_grad, colors, cross_total, out_total = results[:5]
    self_total, self_out_total, input_parts, vectors, input_vectors = results[5:]
    me = lax.axis_index("rows") * grid_cols + lax.axis_index("cols")
    vectors = lax.dynamic_slice_in_dim(vectors, lax.rem(me, grid_rows) * own, own, axis=1)
    colors = colors[:, : channels * tile_cols, :tile_rows].reshape(
        image_count, channels, tile_cols, tile_rows
    )
    input_total = prior_input_matrices + jnp.transpose(by_channel(input_parts), (0, 2, 1))
    input_vectors = by_channel(input_vectors[:2])
    return (
        new_latents,
        latent_grad,
        jnp.transpose(colors, (1, 0, 3, 2)),
        jnp.transpose(cross_total, (0, 2, 1)),
        jnp.transpose(out_total),
        input_total,
        input_vectors[0],
        input_vectors[1],
        jnp.stack([vectors[0], vectors[2]]),
        jnp.concatenate([vectors[1:2], vectors[3:4], vectors[8:13]]),
        jnp.transpose(self_total, (0, 2, 1)),
        jnp.transpose(self_out_total),
        jnp.stack([vectors[4], vectors[6]]),
        jnp.concatenate([vectors[5:6], vectors[7:8], vectors[13:18]]),
    )


def solution(mesh):
    placed = (
        P(("rows", "cols"), None),
        P(None, None, "rows", "cols"),
        P(),
        P(("rows", "cols"), None),
        P(),
        P(),
        P(),
        P(),
        P(),
        P(),
        P(),
        P(),
        P(),
        P(),
        P(),
        P(None, None, ("rows", "cols")),
        P(None, ("rows", "cols")),
        P(None, None, ("rows", "cols")),
    )
    one_head_each = mesh.shape["cols"] == HEADS
    return jax.shard_map(
        local_kernel if one_head_each else local,
        mesh=mesh,
        in_specs=placed,
        out_specs=(
            P(("rows", "cols"), None),
            P(("rows", "cols"), None),
            P(None, None, "rows", "cols"),
            P(None, None, ("rows", "cols")),
            P(None, ("rows", "cols")),
            P(None, None, ("rows", "cols")),
            P(),
            P(),
            P(None, ("rows", "cols")),
            P(None, ("rows", "cols")),
            P(None, None, ("rows", "cols")),
            P(None, ("rows", "cols")),
            P(None, ("rows", "cols")),
            P(None, ("rows", "cols")),
        ),
        check_vma=False,
    )
```

```python
import functools

import jax
import jax.numpy as jnp
import ml_dtypes
import numpy as np
from jax import lax
from jax.experimental import pallas as pl
from jax.experimental.pallas import tpu as pltpu
from jax.sharding import PartitionSpec as P

HEADS = 8
LATENTS = 512
NBANDS = 64
HEAD_DIM = 128


EPS = 1e-05
NEG = -1e30
FREQ_TOP = 112.0
VMEM_BYTES = 63 * 1024 * 1024
SEND = (4, 2, 0, 4, 4, 4, 4)


def narrow(values):
    return values.astype(jnp.bfloat16)


def to_float(values):
    return values.astype(jnp.float32)


def matmul(former, latter):
    return jnp.dot(former, latter, preferred_element_type=jnp.float32)


def inner_left(former, latter):
    return lax.dot_general(
        former, latter, (((0,), (0,)), ((), ())), preferred_element_type=jnp.float32
    )


def inner_right(former, latter):
    return lax.dot_general(
        former, latter, (((1,), (1,)), ((), ())), preferred_element_type=jnp.float32
    )


def layer_norm(values, gain, offset):
    middle = jnp.mean(values, axis=-1, keepdims=True)
    centered = values - middle
    spread = jnp.mean(centered * centered, axis=-1, keepdims=True)
    return centered * lax.rsqrt(spread + EPS) * gain + offset


def norm_back(values, gain, offset, gradient):
    result, pullback = jax.vjp(layer_norm, values, gain, offset)
    return pullback(gradient)


def gelu_tanh(values):
    return jax.nn.gelu(values, approximate=True)


def gelu_back(pre_gelu, gradient):
    result, pullback = jax.vjp(gelu_tanh, pre_gelu)
    return pullback(gradient)[0]


def axis_features(places, extent):
    frequency = 1.0 + jnp.arange(NBANDS, dtype=jnp.float32) * ((FREQ_TOP - 1.0) / (NBANDS - 1))
    angle = jnp.pi * places[:, None] * frequency[None, :]
    return (places, jnp.sin(angle), jnp.cos(angle))


def canvas_of(colors, image_box):
    channels, wide, tall = colors.shape
    top, left, height, width = image_box[0], image_box[1], image_box[2], image_box[3]
    row_at = jnp.arange(tall, dtype=jnp.int32)
    col_at = jnp.arange(wide, dtype=jnp.int32)
    y_place = -1.0 + 2.0 * to_float(row_at - top) / to_float(height - 1)
    x_place = -1.0 + 2.0 * to_float(col_at - left) / to_float(width - 1)
    y_parts = axis_features(y_place, height)
    x_parts = axis_features(x_place, width)
    y_all = jnp.concatenate([y_parts[0][:, None], y_parts[1], y_parts[2]], axis=1)
    x_all = jnp.concatenate([x_parts[0][:, None], x_parts[1], x_parts[2]], axis=1)
    count = channels + 2 + 4 * NBANDS
    color_sum = jnp.sum(colors, axis=0)
    color_square = jnp.sum(colors * colors, axis=0)
    mean = (color_sum + jnp.sum(y_all, axis=1)[None, :] + jnp.sum(x_all, axis=1)[:, None]) / count
    square = (
        color_square
        + jnp.sum(y_all * y_all, axis=1)[None, :]
        + jnp.sum(x_all * x_all, axis=1)[:, None]
    ) / count
    deviation = lax.rsqrt(square - mean * mean + EPS)
    row_in = (row_at >= top) & (row_at < top + height)
    col_in = (col_at >= left) & (col_at < left + width)
    return (y_all, x_all, mean, deviation, row_in, col_in)


def split_channels(rows, channels):
    n = NBANDS
    c = channels
    y_part = jnp.concatenate(
        [rows[:, c : c + 1], rows[:, c + 2 : c + 2 + n], rows[:, c + 2 + 2 * n : c + 2 + 3 * n]],
        axis=1,
    )
    x_part = jnp.concatenate(
        [
            rows[:, c + 1 : c + 2],
            rows[:, c + 2 + n : c + 2 + 2 * n],
            rows[:, c + 2 + 3 * n : c + 2 + 4 * n],
        ],
        axis=1,
    )
    return (rows[:, :c], y_part, x_part)


def join_channels(color_part, y_part, x_part):
    n = NBANDS
    return jnp.concatenate(
        [
            color_part,
            y_part[:, :1],
            x_part[:, :1],
            y_part[:, 1 : n + 1],
            x_part[:, 1 : n + 1],
            y_part[:, n + 1 :],
            x_part[:, n + 1 :],
        ],
        axis=1,
    )


def against_pixels(rows, colors, canvas):
    y_all, x_all, mean, deviation = canvas[:4]
    color_part, y_part, x_part = split_channels(rows, colors.shape[0])
    by_row = inner_right(narrow(y_part), narrow(y_all))
    by_col = inner_right(narrow(x_part), narrow(x_all))
    total = by_row[:, None, :] + by_col[:, :, None]
    for j in range(colors.shape[0]):
        total = total + color_part[:, j][:, None, None] * colors[j][None]
    total = total - jnp.sum(rows, axis=1)[:, None, None] * mean[None]
    return total * deviation[None]


def over_pixels(weights, colors, canvas):
    y_all, x_all, mean, deviation = canvas[:4]
    scaled = weights * deviation[None]
    y_part = matmul(narrow(jnp.sum(scaled, axis=1)), narrow(y_all))
    x_part = matmul(narrow(jnp.sum(scaled, axis=2)), narrow(x_all))
    color_part = jnp.stack(
        [jnp.sum(scaled * colors[j][None], axis=(1, 2)) for j in range(colors.shape[0])], axis=1
    )
    middle = jnp.sum(scaled * mean[None], axis=(1, 2))
    return join_channels(color_part, y_part, x_part) - middle[:, None]


def mlp_forward(row_values, gain, offset, w_in, b_in, w_out, b_out):
    normed = narrow(layer_norm(row_values, gain, offset))
    pre_gelu = matmul(normed, w_in) + b_in
    hidden = narrow(gelu_tanh(pre_gelu))
    return (matmul(hidden, w_out) + b_out, (normed, pre_gelu, hidden))


def mlp_backward(row_values, gain, offset, w_in, w_out, stored, gradient):
    normed, pre_gelu, hidden = stored
    grad_low = narrow(gradient)
    d_w_out = inner_left(hidden, grad_low)
    d_b_out = jnp.sum(gradient, axis=0)
    d_pre = gelu_back(pre_gelu, inner_right(grad_low, w_out))
    pre_low = narrow(d_pre)
    d_w_in = inner_left(normed, pre_low)
    d_b_in = jnp.sum(d_pre, axis=0)
    d_rows, d_gain, d_offset = norm_back(row_values, gain, offset, inner_right(pre_low, w_in))
    return (
        gradient + d_rows,
        (d_w_in, d_w_out),
        (d_gain, d_offset, d_b_in, d_b_out),
        (pre_low, grad_low),
    )


def local(
    latents,
    pixel_colors,
    image_boxes,
    cotangent,
    cross_matrices,
    cross_out,
    input_matrices,
    in_gain,
    in_bias,
    cross_gains,
    cross_biases,
    self_matrices,
    self_out,
    self_gains,
    self_biases,
    prior_cross_matrices,
    prior_cross_out,
    prior_input_matrices,
):
    rows_dev = latents.shape[0]
    model_width = latents.shape[1]
    image_count = image_boxes.shape[0]
    tile_rows = pixel_colors.shape[2]
    tile_cols = pixel_colors.shape[3]
    input_width = input_matrices.shape[1]
    grid_rows = lax.axis_size("rows")
    grid_cols = lax.axis_size("cols")
    all_rows = rows_dev * grid_rows * grid_cols
    row_place = lax.axis_index("rows")
    col_place = lax.axis_index("cols")
    row_start = row_place * tile_rows
    col_start = col_place * tile_cols
    score_scale = model_width ** (-0.5)
    head_scale = HEAD_DIM ** (-0.5)
    g_cross = to_float(cross_gains)
    b_cross = to_float(cross_biases)
    g_self = to_float(self_gains)
    b_self = to_float(self_biases)
    g_input = to_float(in_gain)
    b_input = to_float(in_bias)
    latent_state = to_float(latents)
    normed_q = narrow(layer_norm(latent_state, g_cross[0], b_cross[0]))
    query_rows = narrow(matmul(normed_q, cross_matrices[0]) + b_cross[2])
    colors_low = lax.all_gather(pixel_colors, ("rows", "cols"), axis=0, tiled=False)
    colors_low = lax.dynamic_index_in_dim(colors_low, row_place, axis=2, keepdims=False)
    colors_low = colors_low.reshape(grid_rows, grid_cols, 3, tile_rows, tile_cols)
    colors = to_float(
        jnp.transpose(colors_low, (2, 1, 4, 0, 3)).reshape(
            3, grid_cols * tile_cols, grid_rows * tile_rows
        )
    )
    image_box = lax.dynamic_index_in_dim(image_boxes, row_place, axis=0, keepdims=False)
    canvas = canvas_of(colors, image_box)
    mean, deviation, row_in, col_in = canvas[2:]
    inside = (col_in[:, None] & row_in[None, :])[None]
    key_weight = input_matrices[0]
    value_weight = input_matrices[1]
    query_inputs = inner_right(query_rows, key_weight)
    query_lines = against_pixels(query_inputs * g_input, colors, canvas)
    query_shift = jnp.sum(query_inputs * b_input, axis=1)
    scores = jnp.where(
        inside, (query_lines + query_shift[:, None, None]) * score_scale, NEG
    )
    peak_score = jnp.max(scores, axis=(1, 2), keepdims=True)
    weights = jnp.where(inside, jnp.exp(scores - peak_score), 0.0)
    cross_probs = weights / jnp.sum(weights, axis=(1, 2), keepdims=True)
    plain_mixed = over_pixels(cross_probs, colors, canvas)
    mixed_inputs = (
        plain_mixed * g_input + jnp.sum(cross_probs, axis=(1, 2))[:, None] * b_input
    )
    mixed_low = narrow(mixed_inputs)
    attended = matmul(mixed_low, value_weight) + b_cross[3]
    attended_low = narrow(attended)
    first = latent_state + matmul(attended_low, cross_out) + b_cross[4]
    branch, cross_stored = mlp_forward(
        first, g_cross[1], b_cross[1], cross_matrices[1], b_cross[5], cross_matrices[2], b_cross[6]
    )
    second = first + branch
    normed_t = narrow(layer_norm(second, g_self[0], b_self[0]))
    tower_queries = narrow(matmul(normed_t, self_matrices[0]) + b_self[2])
    tower_keys = narrow(matmul(normed_t, self_matrices[1]))
    tower_values = narrow(matmul(normed_t, self_matrices[2]) + b_self[3])
    keys_group, values_group = (
        lax.all_gather(tower_keys, "cols", axis=0, tiled=True),
        lax.all_gather(tower_values, "cols", axis=0, tiled=True),
    )
    group_rows = keys_group.shape[0]
    query_image = (
        (row_place * grid_cols + col_place) * rows_dev + jnp.arange(rows_dev, dtype=jnp.int32)
    ) // LATENTS
    key_image = (row_place * group_rows + jnp.arange(group_rows, dtype=jnp.int32)) // LATENTS
    same_image = (query_image[:, None] == key_image[None, :])[None]
    query_heads = tower_queries.reshape(rows_dev, HEADS, HEAD_DIM)
    key_heads = keys_group.reshape(group_rows, HEADS, HEAD_DIM)
    value_heads = values_group.reshape(group_rows, HEADS, HEAD_DIM)
    head_scores = jnp.where(
        same_image,
        jnp.einsum("qhd,khd->hqk", query_heads, key_heads, preferred_element_type=jnp.float32)
        * head_scale,
        NEG,
    )
    head_weights = jnp.where(
        same_image, jnp.exp(head_scores - jnp.max(head_scores, axis=2, keepdims=True)), 0.0
    )
    head_probs = head_weights / jnp.sum(head_weights, axis=2, keepdims=True)
    probs_low = narrow(head_probs)
    tower_mixed = narrow(
        jnp.einsum(
            "hqk,khd->qhd", probs_low, value_heads, preferred_element_type=jnp.float32
        ).reshape(rows_dev, model_width)
    )
    third = second + matmul(tower_mixed, self_out) + b_self[4]
    branch, tower_stored = mlp_forward(
        third, g_self[1], b_self[1], self_matrices[3], b_self[5], self_matrices[4], b_self[6]
    )
    new_latents = narrow(third + branch)
    gradient = to_float(cotangent)
    gradient, tower_mlp_w, tower_mlp_v, tower_lows = mlp_backward(
        third, g_self[1], b_self[1], self_matrices[3], self_matrices[4], tower_stored, gradient
    )
    tower_out_low = narrow(gradient)
    d_self_out = inner_left(tower_mixed, tower_out_low)
    d_self_out_bias = jnp.sum(gradient, axis=0)
    d_mixed = narrow(inner_right(tower_out_low, self_out)).reshape(rows_dev, HEADS, HEAD_DIM)
    d_probs = jnp.einsum("qhd,khd->hqk", d_mixed, value_heads, preferred_element_type=jnp.float32)
    d_value_heads = jnp.einsum(
        "hqk,qhd->khd", probs_low, d_mixed, preferred_element_type=jnp.float32
    )
    d_scores = head_probs * (d_probs - jnp.sum(head_probs * d_probs, axis=2, keepdims=True))
    d_scores_low = narrow(d_scores * head_scale)
    d_query_heads = jnp.einsum(
        "hqk,khd->qhd", d_scores_low, key_heads, preferred_element_type=jnp.float32
    ).reshape(rows_dev, model_width)
    d_key_heads = jnp.einsum(
        "hqk,qhd->khd", d_scores_low, query_heads, preferred_element_type=jnp.float32
    )
    d_tower_keys, d_tower_values = (
        lax.psum_scatter(
            d_key_heads.reshape(group_rows, model_width).astype(jnp.bfloat16),
            "cols",
            scatter_dimension=0,
            tiled=True,
        ).astype(jnp.float32),
        lax.psum_scatter(
            d_value_heads.reshape(group_rows, model_width).astype(jnp.bfloat16),
            "cols",
            scatter_dimension=0,
            tiled=True,
        ).astype(jnp.float32),
    )
    tq_low = narrow(d_query_heads)
    tk_low = narrow(d_tower_keys)
    tv_low = narrow(d_tower_values)
    d_normed_t = (
        inner_right(tq_low, self_matrices[0])
        + inner_right(tk_low, self_matrices[1])
        + inner_right(tv_low, self_matrices[2])
    )
    d_second, d_self_gain, d_self_bias = norm_back(second, g_self[0], b_self[0], d_normed_t)
    gradient = gradient + d_second
    self_gain_grad = jnp.stack([d_self_gain, tower_mlp_v[0]])
    self_bias_grad = jnp.stack(
        [
            d_self_bias,
            tower_mlp_v[1],
            jnp.sum(d_query_heads, axis=0),
            jnp.sum(d_tower_values, axis=0),
            d_self_out_bias,
            tower_mlp_v[2],
            tower_mlp_v[3],
        ]
    )
    gradient, cross_mlp_w, cross_mlp_v, cross_lows = mlp_backward(
        first, g_cross[1], b_cross[1], cross_matrices[1], cross_matrices[2], cross_stored, gradient
    )
    cross_out_low = narrow(gradient)
    d_cross_out = inner_left(attended_low, cross_out_low)
    d_cross_out_bias = jnp.sum(gradient, axis=0)
    d_attended = narrow(inner_right(cross_out_low, cross_out))
    value_shift = jnp.sum(to_float(d_attended) * b_cross[3], axis=1)
    row_delta = jnp.sum(to_float(d_attended) * attended, axis=1) - value_shift
    grad_inputs = inner_right(d_attended, value_weight)
    grad_shift = jnp.sum(grad_inputs * b_input, axis=1)
    grad_lines = against_pixels(grad_inputs * g_input, colors, canvas)
    d_scores = (
        cross_probs * (grad_lines + (grad_shift - row_delta)[:, None, None]) * score_scale
    )
    plain_scores = over_pixels(d_scores, colors, canvas)
    score_sum = jnp.sum(d_scores, axis=(1, 2))
    prob_sum = jnp.sum(cross_probs, axis=(1, 2))
    score_inputs = plain_scores * g_input + score_sum[:, None] * b_input
    score_low = narrow(score_inputs)
    d_query_rows = matmul(score_low, key_weight)
    in_gain_part = jnp.sum(query_inputs * plain_scores + grad_inputs * plain_mixed, axis=0)
    in_bias_part = jnp.sum(
        query_inputs * score_sum[:, None] + grad_inputs * prob_sum[:, None], axis=0
    )
    query_scaled = query_inputs * g_input
    grad_scaled = grad_inputs * g_input
    query_away = query_scaled[:, :3] - jnp.mean(query_scaled, axis=1, keepdims=True)
    grad_away = grad_scaled[:, :3] - jnp.mean(grad_scaled, axis=1, keepdims=True)
    along = jnp.sum(d_scores * query_lines + cross_probs * grad_lines, axis=0) / input_width
    color_parts = jnp.einsum(
        "rj,rcy->jcy", query_away, d_scores, precision=lax.Precision.HIGHEST
    ) + jnp.einsum("rj,rcy->jcy", grad_away, cross_probs, precision=lax.Precision.HIGHEST)
    color_parts = deviation[None] * (
        color_parts - (colors - mean[None]) * deviation[None] * along[None]
    )
    color_parts = color_parts.reshape(3, grid_cols, tile_cols, grid_rows, tile_rows)
    color_parts = jnp.transpose(color_parts, (3, 1, 0, 4, 2)).reshape(
        grid_rows * grid_cols, 3, tile_rows, tile_cols
    )
    color_grad = lax.all_to_all(
        color_parts, ("rows", "cols"), split_axis=0, concat_axis=0, tiled=True
    ).reshape(image_count, grid_cols, 3, tile_rows, tile_cols)
    color_grad = jnp.transpose(jnp.sum(color_grad, axis=1), (1, 0, 2, 3))
    query_low = narrow(d_query_rows)
    d_latent, d_cross_gain, d_cross_bias = norm_back(
        latent_state, g_cross[0], b_cross[0], inner_right(query_low, cross_matrices[0])
    )
    latent_grad = gradient + d_latent
    in_gain_grad, in_bias_grad = lax.psum((in_gain_part, in_bias_part), ("rows", "cols"))
    vectors = jnp.stack(
        [
            d_cross_gain,
            cross_mlp_v[0],
            d_cross_bias,
            cross_mlp_v[1],
            jnp.sum(d_query_rows, axis=0),
            jnp.sum(to_float(d_attended), axis=0),
            d_cross_out_bias,
            cross_mlp_v[2],
            cross_mlp_v[3],
            d_self_gain,
            tower_mlp_v[0],
            d_self_bias,
            tower_mlp_v[1],
            jnp.sum(d_query_heads, axis=0),
            jnp.sum(d_tower_values, axis=0),
            d_self_out_bias,
            tower_mlp_v[2],
            tower_mlp_v[3],
        ]
    )
    vector_sums = lax.psum_scatter(vectors, ("rows", "cols"), scatter_dimension=1, tiled=True)
    lefts = jnp.stack(
        [
            normed_q,
            cross_stored[0],
            cross_stored[2],
            attended_low,
            normed_t,
            tower_stored[0],
            tower_stored[2],
            tower_mixed,
        ]
    )
    rights = jnp.stack(
        [
            query_low,
            cross_lows[0],
            cross_lows[1],
            cross_out_low,
            d_attended,
            query_rows,
            tq_low,
            tk_low,
            tv_low,
            tower_lows[0],
            tower_lows[1],
            tower_out_low,
        ]
    )
    small_lefts = jnp.stack([mixed_low, score_low])
    lefts = lax.all_gather(lefts, "cols", axis=1, tiled=True)
    small_lefts = lax.all_gather(small_lefts, "cols", axis=1, tiled=True)
    own = model_width // (grid_rows * grid_cols)
    rights = rights.reshape(rights.shape[0], rows_dev, grid_rows, grid_cols, own)
    rights = lax.all_to_all(
        jnp.transpose(rights, (3, 0, 1, 2, 4)), "cols", split_axis=0, concat_axis=0, tiled=False
    )
    rights = jnp.transpose(rights, (1, 0, 2, 3, 4)).reshape(
        rights.shape[1], grid_cols * rows_dev, grid_rows * own
    )
    pairs = ((0, 0), (1, 1), (2, 2), (3, 3), (4, 6), (4, 7), (4, 8), (5, 9), (6, 10), (7, 11))
    big = [inner_left(rights[k], lefts[i]).reshape(grid_rows, own, model_width) for i, k in pairs]
    small = [
        inner_left(rights[k], small_lefts[i]).reshape(grid_rows, own, input_width)
        for i, k in ((1, 5), (0, 4))
    ]
    big = lax.psum_scatter(jnp.stack(big, axis=1), "rows", scatter_dimension=0, tiled=False)
    small = lax.psum_scatter(jnp.stack(small, axis=1), "rows", scatter_dimension=0, tiled=False)
    big = jnp.transpose(big, (0, 2, 1))
    small = jnp.transpose(small, (0, 2, 1))
    all_sums = (
        big[:3],
        big[3],
        small,
        vector_sums[:2],
        vector_sums[2:9],
        big[4:9],
        big[9],
        vector_sums[9:11],
        vector_sums[11:],
    )
    cross_sums = all_sums[:5]
    self_sums = all_sums[5:]
    return (
        new_latents,
        latent_grad,
        color_grad,
        prior_cross_matrices + cross_sums[0],
        prior_cross_out + cross_sums[1],
        prior_input_matrices + cross_sums[2],
        in_gain_grad,
        in_bias_grad,
        cross_sums[3],
        cross_sums[4],
        self_sums[0],
        self_sums[1],
        self_sums[2],
        self_sums[3],
    )


STEPS_HELD = 8
LANES = 128
MESH = pl.DeviceIdType.MESH
WIDE = 3 * LANES


def own_dot(former, latter, former_dim, latter_dim):
    return lax.dot_general(
        former,
        latter,
        (((former_dim,), (latter_dim,)), ((), ())),
        preferred_element_type=jnp.float32,
    )


def selections(tile_cols, grid_cols, steps):
    held = STEPS_HELD
    blocks = -(-steps // held)
    place = np.zeros((grid_cols * 32, WIDE), np.float32)
    back = np.zeros((grid_cols * 32, blocks * LANES), np.float32)
    for tile in range(grid_cols):
        for channel in range(3):
            for offset in range(tile_cols):
                col = tile * tile_cols + offset
                line = tile * 32 + channel * tile_cols + offset
                place[line, channel * LANES + col] = 1
                half, step = divmod(col, steps)
                back[line, step * 16 + half * 8 + channel] = 1
    pick = np.zeros((7 * LANES, blocks * LANES), np.float32)
    for step in range(steps):
        for half in range(2):
            for slot, kind in enumerate((0, 1, 2, 3, 4, 3, 5, 6)):
                pick[kind * LANES + half * steps + step, step * 16 + half * 8 + slot] = 1
    spread = np.zeros((LANES, 2 * LANES), np.float32)
    for group in range(16):
        for channel in range(3):
            for slot in (3, 4):
                spread[group * 8 + slot, group * 8 + channel] = 1
            for slot in (6, 7):
                spread[group * 8 + slot, LANES + group * 8 + channel] = 1
    low = lambda values: np.asarray(values, ml_dtypes.bfloat16)
    return (low(place), low(pick), low(spread), low(back))


def norm_parts(values):
    middle = jnp.mean(values, axis=1, keepdims=True)
    centered = values - middle
    spread = jnp.mean(centered * centered, axis=1, keepdims=True)
    factor = lax.rsqrt(spread + EPS)
    return (centered * factor, factor)


def norm_forward(values, gain, offset):
    return narrow(norm_parts(values)[0] * gain + offset)


def norm_gradient(values, gain, gradient):
    plain, factor = norm_parts(values)
    inner = gradient * gain
    first = jnp.mean(inner, axis=1, keepdims=True)
    second = jnp.mean(inner * plain, axis=1, keepdims=True)
    return (
        factor * (inner - first - plain * second),
        jnp.sum(gradient * plain, axis=0, keepdims=True),
        jnp.sum(gradient, axis=0, keepdims=True),
    )


GELU_RATE = 0.7978845608028654
GELU_CUBE = 0.044715


def gelu_value(u):
    return 0.5 * u * (1.0 + jnp.tanh(GELU_RATE * (u + GELU_CUBE * u * u * u)))


def gelu_slope(u):
    bent = jnp.tanh(GELU_RATE * (u + GELU_CUBE * u * u * u))
    return 0.5 * (1.0 + bent) + 0.5 * u * (1.0 - bent * bent) * GELU_RATE * (
        1.0 + 3.0 * GELU_CUBE * u * u
    )


def waves(turns):
    near = turns - 2.0 * jnp.floor(turns * 0.5 + 0.5)
    return (jnp.sin(jnp.pi * near), jnp.cos(jnp.pi * near))


def axis_lines(place, slot):
    lane = lax.broadcasted_iota(jnp.int32, (place.shape[0], LANES), 1)
    band = lax.rem(lane, NBANDS)
    frequency = 1.0 + to_float(band) * ((FREQ_TOP - 1.0) / (NBANDS - 1))
    sine, cosine = waves(place * frequency)
    return jnp.concatenate(
        [jnp.where(lane < NBANDS, sine, cosine), jnp.where(lane == slot, place, 0.0)], axis=1
    )


def layer_kernel(
    sizes,
    boxes, latents, cotangent, colors, in_gain, in_bias, order, cross_gains, cross_biases, self_gains,
    self_biases, place, pick, spread, back,
    w_cross, w_out, w_self, w_self_out, w_input,
    new_latents, latent_grad, color_out, cross_total, out_total, self_total, self_out_total,
    input_parts, vector_out, input_vector_out,
    wts, win, win_raw, xbuf, xsmall, gsrc, gbuf, staged, paired, handed, crossed, staged_small, paired_small, handed_small, crossed_small, kept_small,
    color_lines, color_tiles, colstage, colbuf, img, img7, fa, ft, sl, ycoef, xcoef, yfeat, xfeat, mixrow,
    cgright, rowsum, colsum, cgacc, cgsend, cgbuf, cgsum, cgfin,
    act, lnvec, lnsend, lnbuf, biasvec, vecsend, vecbuf, ivec, ivbuf,
    heads, probs, prob_grad, mix_s, mix_b, dmix_b, dqkv_s, dqkv_b,
    weight_sem, x_send, x_recv, y_send, y_recv, g_send, g_recv, a_send, a_recv, r_send, r_recv, f_send, f_recv,
    misc_send, misc_recv,
):
    grid_rows, grid_cols, rows, steps, tile_rows, tile_cols = sizes
    n_dev = grid_rows * grid_cols
    width = latents.shape[1]
    quads = grid_cols // 2
    chunk = width // grid_cols
    own = chunk // grid_rows
    tall = grid_rows * tile_rows
    z = lax.axis_index("rows")
    j = lax.axis_index("cols")
    core = lax.rem(j, 2)
    quad = j // 2
    me = z * grid_cols + j
    f32, bf16 = jnp.float32, jnp.bfloat16
    score_scale = width ** (-0.5)
    head_scale = HEAD_DIM ** (-0.5)

    def at_device(d):
        return {"rows": d // grid_cols, "cols": lax.rem(d, grid_cols)}

    def lanes_of(index):
        return pl.ds(pl.multiple_of(index * chunk, chunk), chunk)

    def push(src, dst, send, recv, where):
        pltpu.make_async_remote_copy(
            src_ref=src, dst_ref=dst, send_sem=send, recv_sem=recv, device_id=where,
            device_id_type=MESH,
        ).start()

    def wait_for(ref, sem):
        pltpu.make_async_copy(ref, ref, sem).wait()

    barrier = pltpu.get_barrier_semaphore()

    def greet(step, carry):
        pl.semaphore_signal(
            barrier, inc=1, device_id=at_device(lax.rem(me + step, n_dev)), device_id_type=MESH
        )
        return carry

    lax.fori_loop(1, n_dev, greet, 0)

    sources = (
        [w_cross.at[0], w_out, w_cross.at[1], w_cross.at[2]]
        + [w_self.at[0], w_self.at[1], w_self.at[2], w_self_out, w_self.at[3], w_self.at[4]]
    )
    CQ, CO, C1, C2, SQ, SK, SV, SO, S1, S2 = range(10)
    loads = [pltpu.make_async_copy(s, wts.at[k], weight_sem.at[k]) for k, s in enumerate(sources)]
    loads.append(pltpu.make_async_copy(w_input, win_raw, weight_sem.at[10]))
    loads[CQ].start()
    loads[10].start()

    color_lines[...] = jnp.zeros(color_lines.shape, f32)
    for channel in range(3):
        for col in range(tile_cols):
            line = channel * tile_cols + col
            shown = to_float(colors[channel, col])
            for image in range(grid_rows):
                color_lines[image, line : line + 1, :tile_rows] = shown[image : image + 1]
    color_tiles[...] = narrow(color_lines[...])
    gc, bc = to_float(cross_gains[...]), to_float(cross_biases[...])
    gs, bs = to_float(self_gains[...]), to_float(self_biases[...])
    gains_here = [to_float(in_gain[...]), to_float(in_bias[...])]
    gains_here = jnp.concatenate(gains_here + [jnp.zeros((6, in_gain.shape[1]), f32)], axis=0)
    gains_here = own_dot(narrow(gains_here), order[...], 1, 1)
    gin, bin_ = gains_here[0:1], gains_here[1:2]
    lat = to_float(latents[...])
    nq = norm_forward(lat, gc[0:1], bc[0:1])
    xbuf[0, core, quad] = nq

    cot_low = cotangent[...]
    pl.semaphore_wait(barrier, n_dev - 1)

    def send_color(step, carry):
        image = lax.rem(z + step, grid_rows)
        push(color_tiles.at[image], colstage.at[z], misc_send.at[5], misc_recv.at[5], {"rows": image})
        return carry

    lax.fori_loop(1, grid_rows, send_color, 0)
    colstage[z] = color_tiles[z]

    def x_spread(block, sem):
        def one(step, carry):
            peer = 2 * lax.rem(quad + step, quads) + core
            push(block, block, x_send.at[sem], x_recv.at[sem], {"cols": peer})
            return carry

        lax.fori_loop(1, quads, one, 0)

    def x_relay(half, sem):
        wait_for(half.at[pl.ds(0, quads - 1)], x_recv.at[sem])
        push(half, half, y_send.at[sem], y_recv.at[sem], {"cols": j + 1 - 2 * core})

    def x_arrived(half, sem):
        wait_for(half, y_recv.at[sem])

    waiting = []
    pieces = rows // 16

    def spread_x(k):
        x_spread(xbuf.at[k, core, quad], k)

    def later_x(k):
        waiting.extend((k, piece) for piece in range(pieces))

    def background(count):
        for k, piece in waiting[:count]:
            x_spread(xbuf.at[k, core, quad, pl.ds(piece * 16, 16)], k)
        del waiting[:count]

    def relay_x(k):
        x_relay(xbuf.at[k, core], k)

    def have_x(k):
        x_arrived(xbuf.at[k, 1 - core], k)

    def to_plane(step):
        peer = lax.rem(j + step, grid_cols)
        return peer, {"cols": peer}

    def regroup(values):
        tiles = [values[:, t * LANES : (t + 1) * LANES] for t in range(width // LANES)]
        piece = lax.broadcasted_iota(jnp.int32, tiles[0].shape, 1) // own
        result = []
        for peer in range(grid_cols):
            chunk_now = None
            for part in range(grid_rows):
                tile, offset = divmod((part * grid_cols + peer) * own, LANES)
                shift = (part * own - offset) % LANES
                moved = pltpu.roll(tiles[tile], shift, 1) if shift else tiles[tile]
                chunk_now = moved if part == 0 else jnp.where(piece == part, moved, chunk_now)
            result.append(chunk_now)
        return jnp.concatenate(result, axis=1)

    def spread_g(k, values):
        gsrc[k] = narrow(regroup(to_float(values)))

        def one(step, carry):
            peer, where = to_plane(step)
            push(gsrc.at[k, :, lanes_of(peer)], gbuf.at[k, core, quad], g_send.at[k], g_recv.at[k], where)
            return carry

        lax.fori_loop(1, grid_cols, one, 0)
        gbuf[k, core, quad] = gsrc[k, :, lanes_of(j)]

    def have_g(k):
        wait_for(gsrc.at[k, :, pl.ds(0, chunk * (grid_cols - 1))], g_recv.at[k])
        return gbuf[k].reshape(grid_cols * rows, chunk)

    partner = z + 1 - 2 * lax.rem(z, 2)
    across = lax.rem(z + 2, grid_rows)

    def block_at(part):
        return pl.ds(pl.multiple_of(part * own, own), own)

    def send_parts(src, pair, sem):
        for slot, part in enumerate((partner, lax.rem(partner + 2, grid_rows))):
            push(src.at[block_at(part)], pair.at[slot], r_send.at[sem], r_recv.at[sem], {"rows": partner})

    def join_parts(src, pair, hand, far, kept, sem):
        wait_for(pair, r_recv.at[sem])
        hand[...] = narrow(to_float(src[block_at(across)]) + to_float(pair[1]))
        push(hand, far, f_send.at[sem], f_recv.at[sem], {"rows": across})
        kept[...] = to_float(src[block_at(z)]) + to_float(pair[0])

    def kept_of(m):
        if m < 3:
            return cross_total.at[m]
        if m < 9:
            return self_total.at[m - 4]
        return self_out_total

    def slot_of(m):
        return m if m < 3 else m - 1

    def join(m):
        k = slot_of(m)
        join_parts(staged.at[k], paired.at[k], handed.at[k], crossed.at[k], kept_of(m), m)

    def join_small(m):
        join_parts(
            staged_small.at[m], paired_small.at[m], handed_small.at[m], crossed_small.at[m],
            kept_small.at[m], 10 + m,
        )

    def weight_part(m, right, left):
        turned = jnp.transpose(right)

        def one(n, carry):
            at = pl.ds(pl.multiple_of(n * 256, 256), 256)
            block = left[:, :, :, at].reshape(grid_cols * rows, 256)
            staged[slot_of(m), :, at] = narrow(own_dot(turned, block, 1, 0))
            return carry

        lax.fori_loop(0, width // 256, one, 0, unroll=4)
        send_parts(staged.at[slot_of(m)], paired.at[slot_of(m)], m)

    def small_part(m, right, left):
        staged_small[m] = narrow(own_dot(right, left[...].reshape(grid_cols * rows, WIDE), 0, 0))
        send_parts(staged_small.at[m], paired_small.at[m], 10 + m)

    def times(x, k, out):
        def one(n, carry):
            at = pl.ds(pl.multiple_of(n * 256, 256), 256)
            out[:, at] = own_dot(x, wts[k, :, at], 1, 0)
            return carry

        lax.fori_loop(0, width // 256, one, 0, unroll=4)

    def times_t(x, k, out, add=False):
        def one(n, carry):
            at = pl.ds(pl.multiple_of(n * 256, 256), 256)
            result = own_dot(x, wts[k, at, :], 1, 1)
            out[:, at] = out[:, at] + result if add else result
            return carry

        lax.fori_loop(0, width // 256, one, 0, unroll=4)

    FIRST, SECOND, THIRD, PRE_C, PRE_S, TMP, ATT, GRAD, COT_BACK = range(9)
    tmp = act.at[TMP]

    loads[CQ].wait()
    for k in range(1, 10):
        loads[k].start()
    times(nq, CQ, tmp)
    query_low = narrow(tmp[...] + bc[2:3])
    wait_for(colstage.at[pl.ds(0, grid_rows - 1)], misc_recv.at[5])

    def send_strip(step, carry):
        peer, where = to_plane(step)
        push(colstage, colbuf.at[j], misc_send.at[0], misc_recv.at[0], where)
        return carry

    lax.fori_loop(1, grid_cols, send_strip, 0)
    colbuf[j] = colstage[...]
    spread_x(0)
    spread_g(7, query_low)
    spread_g(5, cot_low)
    loads[10].wait()
    for k in range(2):
        win[k] = narrow(own_dot(order[...], win_raw[k], 1, 0))
    query_inputs = own_dot(query_low, win[0], 1, 1)
    spare = pl.ds(2 * LANES, 16)
    spare_row = lax.broadcasted_iota(jnp.int32, (16, width), 0)
    win[1, spare, :] = narrow(jnp.where(spare_row == 5, bc[3:4], to_float(win[1, spare, :])))

    box = [boxes[z, k] for k in range(4)]

    def filled(value, shape):
        return to_float(jnp.full(shape, value, jnp.int32))

    row_at = lax.broadcasted_iota(jnp.int32, (tall, 1), 0)
    y_place = -1.0 + 2.0 * to_float(row_at - box[0]) / filled(box[2] - 1, (tall, 1))
    y_lines = axis_lines(y_place, 3)
    y_sum = jnp.sum(y_lines, axis=1, keepdims=True)
    row_out = jnp.where((row_at >= box[0]) & (row_at < box[0] + box[2]), 0.0, NEG)
    yfeat[...] = narrow(y_lines)
    held_rows = xfeat.shape[1]
    col_lane = lax.broadcasted_iota(jnp.int32, (held_rows, LANES), 1)
    col_row = lax.broadcasted_iota(jnp.int32, (held_rows, LANES), 0)
    x_sum = jnp.zeros((1, LANES), f32)
    col_out = []
    for half in range(2):
        col_at = lax.broadcasted_iota(jnp.int32, (held_rows, 1), 0) + half * steps
        x_place = -1.0 + 2.0 * to_float(col_at - box[1]) / filled(box[3] - 1, (held_rows, 1))
        x_lines = axis_lines(x_place, 4)
        xfeat[half] = narrow(x_lines)
        here = (col_lane == col_row + half * steps) & (col_row < steps)
        x_sum = x_sum + jnp.sum(
            jnp.where(here, jnp.sum(x_lines, axis=1, keepdims=True), 0.0), axis=0, keepdims=True
        )
        col_out.append(jnp.where((col_at >= box[1]) & (col_at < box[1] + box[3]), 0.0, NEG))
    x_lane = lax.broadcasted_iota(jnp.int32, (1, LANES), 1)
    x_here = -1.0 + 2.0 * to_float(x_lane - box[1]) / filled(box[3] - 1, (1, LANES))
    count = 3 + 2 + 4 * NBANDS

    wait_for(colbuf.at[pl.ds(0, grid_cols - 1)], misc_recv.at[0])
    for part in range(grid_rows):
        at = pl.ds(part * tile_rows, tile_rows)
        tiles = colbuf[:, part].reshape(grid_cols * 32, LANES)
        img[at, :] = own_dot(tiles, place[...], 0, 0)[:tile_rows]
    c0, c1, c2 = img[:, :LANES], img[:, LANES : 2 * LANES], img[:, 2 * LANES :]
    mean = (c0 + c1 + c2 + y_sum + x_sum) * (1.0 / count)
    square = (c0 * c0 + c1 * c1 + c2 * c2 + y_place * y_place + x_here * x_here + 2.0 * NBANDS) * (
        1.0 / count
    )
    dev = lax.rsqrt(square - mean * mean + EPS)
    mean_low, dev_low = narrow(mean), narrow(dev)
    img7[...] = jnp.concatenate(
        [
            narrow(c0), narrow(c1), narrow(c2),
            mean_low, narrow(mean - to_float(mean_low)),
            dev_low, narrow(dev - to_float(dev_low)),
        ],
        axis=1,
    )
    blocks = fa.shape[0]
    for block in range(blocks):
        at = pl.ds(block * LANES, LANES)
        fa[block] = narrow(own_dot(img7[...], pick[:, at], 1, 0))
        turned = own_dot(pick[:, at], img7[...], 0, 1)
        line = lax.broadcasted_iota(jnp.int32, turned.shape, 0)
        ft[at, :] = narrow(jnp.where(lax.rem(line, 8) == 5, 1.0, turned))

    lane1 = lax.broadcasted_iota(jnp.int32, (rows, LANES), 1)
    lane_half = lax.broadcasted_iota(jnp.int32, (8, LANES), 1) // rows
    sub8 = lax.broadcasted_iota(jnp.int32, (8, LANES), 0)

    def twice(values):
        return jnp.concatenate([values, values], axis=0)

    def turn(values):
        return jnp.transpose(twice(values))[:8]

    def coefficients(scaled, extra):
        tail = scaled[:, 2 * LANES :]
        total = jnp.sum(scaled, axis=1, keepdims=True)
        turned = turn(jnp.where(lane1 == 5, total, jnp.where(lane1 == 6, extra, tail)))
        total_high = to_float(narrow(turned[5:6]))
        body = jnp.where(
            sub8 < 3, turned, jnp.where(sub8 < 5, -total_high, jnp.where(sub8 == 5, total_high - turned[5:6], 0.0))
        )
        body = narrow(jnp.concatenate(
            [jnp.where(lane_half == 0, body, 0.0), jnp.where(lane_half == 1, body, 0.0)], axis=0
        ))
        ones = jnp.where(sub8 >= 6, 1.0, 0.0)
        ones = narrow(jnp.concatenate(
            [jnp.where(lane_half == 0, ones, 0.0), jnp.where(lane_half == 1, ones, 0.0)], axis=0
        ))
        mixrow[...] = jnp.zeros(mixrow.shape, bf16)
        for held in range(STEPS_HELD):
            mixrow[held, held * 16 : held * 16 + 16, :] = jnp.concatenate([body, ones], axis=1)
        scaled_low = narrow(jnp.concatenate([scaled[:, :LANES], tail], axis=1))
        ycoef[...] = own_dot(yfeat[...], twice(scaled_low), 1, 1)
        scaled_low = narrow(jnp.concatenate([scaled[:, LANES : 2 * LANES], tail], axis=1))
        nothing = jnp.zeros_like(scaled_low)
        xcoef[...] = own_dot(xfeat[0], jnp.concatenate([scaled_low, nothing], axis=0), 1, 1) + own_dot(
            xfeat[1], jnp.concatenate([nothing, scaled_low], axis=0), 1, 1
        )
        return turned

    def step_lines(s):
        block, held = s // STEPS_HELD, lax.rem(s, STEPS_HELD)
        result = own_dot(fa[block], mixrow[held], 1, 0)
        deviation = result[:, LANES:]
        lines = (ycoef[...] + xcoef[pl.ds(s, 1), :] + result[:, :LANES]) * deviation
        return lines, deviation

    def step_sums(s, weighted):
        rowsum[...] += weighted
        at = pl.ds(pl.multiple_of(s * 16, 16), 16)
        found = own_dot(ft[at, :], narrow(weighted), 1, 0)
        found = jnp.where(lane_half == 0, found[:8], found[8:])
        colsum[pl.ds(s, 1), :] = found[5:6]
        return found

    def fold(values):
        return values[:rows] + values[rows:]

    def pixel_sums(found, factor):
        by_row = fold(own_dot(narrow(rowsum[...] * factor), yfeat[...], 0, 0))
        cols = narrow(colsum[...] * factor)
        by_col = own_dot(cols, xfeat[0], 0, 0)[:rows] + own_dot(cols, xfeat[1], 0, 0)[rows:]
        padded = jnp.concatenate([found * factor, jnp.zeros((LANES - 8, LANES), f32)], axis=0)
        sums = fold(jnp.transpose(padded))
        middle = sums[:, 3:4] + sums[:, 4:5]
        tail = jnp.where(lane1 < 3, sums, 0.0) + by_row[:, LANES:] + by_col[:, LANES:]
        return jnp.concatenate([by_row[:, :LANES], by_col[:, :LANES], tail], axis=1) - middle

    def other_half(line):
        return pltpu.roll(jnp.broadcast_to(line, (8, LANES)), rows, 1)[:1]

    query_scaled = query_inputs * gin * score_scale
    coefficients(query_scaled, 0.0)
    ycoef[...] += row_out
    half_lane = lax.broadcasted_iota(jnp.int32, (held_rows, LANES), 1) // rows
    xcoef[...] += jnp.where(half_lane == 0, col_out[0], col_out[1])

    def first_pass(s, best):
        lines, deviation = step_lines(s)
        sl[s] = lines
        return jnp.maximum(best, jnp.max(lines, axis=0, keepdims=True))

    best = lax.fori_loop(0, steps, first_pass, jnp.full((1, LANES), -3e38, f32), unroll=4)
    best = jnp.maximum(best, other_half(best))
    rowsum[...] = jnp.zeros(rowsum.shape, f32)
    colsum[...] = jnp.zeros(colsum.shape, f32)

    def second_pass(s, carry):
        total, found = carry
        block, held = s // STEPS_HELD, lax.rem(s, STEPS_HELD)
        deviation = own_dot(fa[block], mixrow[held][:, LANES:], 1, 0)
        weights = jnp.exp(sl[s] - best)
        total = total + jnp.sum(weights, axis=0, keepdims=True)
        return total, found + step_sums(s, weights * deviation)

    total, found = lax.fori_loop(
        0, steps, second_pass, (jnp.zeros((1, LANES), f32), jnp.zeros((8, LANES), f32)), unroll=4
    )
    total = total + other_half(total)
    log_total = best + jnp.log(total)
    plain_mixed = pixel_sums(found, 1.0 / total)
    wide1 = lax.broadcasted_iota(jnp.int32, (rows, WIDE), 1)
    mixed_low = narrow(jnp.where(wide1 == 2 * LANES + 5, 1.0, plain_mixed * gin + bin_))
    xsmall[0, core, quad] = mixed_low
    x_spread(xsmall.at[0, core, quad], 8)
    relay_x(0)
    attended = own_dot(mixed_low, win[1], 1, 0)
    act[ATT] = attended
    attended_low = narrow(attended)
    loads[CO].wait()
    times(attended_low, CO, tmp)
    first = lat + tmp[...] + bc[4:5]
    act[FIRST] = first
    normed_c = norm_forward(first, gc[1:2], bc[1:2])
    xbuf[1, core, quad] = normed_c
    loads[C1].wait()
    times(normed_c, C1, tmp)
    pre = tmp[...] + bc[5:6]
    act[PRE_C] = pre
    hidden_c = narrow(gelu_value(pre))
    xbuf[2, core, quad] = hidden_c
    loads[C2].wait()
    times(hidden_c, C2, tmp)
    second = act[FIRST] + tmp[...] + bc[6:7]
    act[SECOND] = second
    normed_t = norm_forward(second, gs[0:1], bs[0:1])
    xbuf[4, core, quad] = normed_t
    spread_x(4)
    later_x(1)
    later_x(2)
    background(SEND[0])
    loads[S2].wait()
    times_t(cot_low, S2, act.at[COT_BACK])
    relay_x(4)
    x_relay(xsmall.at[0, core], 8)
    have_x(4)

    for k in (SQ, SK, SV):
        loads[k].wait()
    head_rows = grid_cols * rows
    biasvec[...] = jnp.concatenate([bs, jnp.zeros((1, width), f32)], axis=0)

    def head_in(n, carry):
        x = xbuf[4, n].reshape(quads * rows, width)
        at = pl.ds(pl.multiple_of(n * (quads * rows), quads * rows), quads * rows)
        heads[0, at, :] = narrow(own_dot(x, wts[SQ, :, lanes_of(j)], 1, 0) + biasvec[2:3, lanes_of(j)])
        heads[1, at, :] = narrow(own_dot(x, wts[SK, :, lanes_of(j)], 1, 0))
        heads[2, at, :] = narrow(own_dot(x, wts[SV, :, lanes_of(j)], 1, 0) + biasvec[3:4, lanes_of(j)])
        return carry

    lax.fori_loop(0, 2, head_in, 0)
    per = 128

    def head_forward(n, carry):
        at = pl.ds(pl.multiple_of(n * per, per), per)
        scores = own_dot(heads[0, at, :], heads[1], 1, 1) * head_scale
        weights = jnp.exp(scores - jnp.max(scores, axis=1, keepdims=True))
        found_probs = weights / jnp.sum(weights, axis=1, keepdims=True)
        probs[at, :] = found_probs
        mixed = narrow(own_dot(narrow(found_probs), heads[2], 1, 0))
        for part in range(per // rows):
            mix_s[n * (per // rows) + part] = mixed[part * rows : (part + 1) * rows]
        return carry

    lax.fori_loop(0, head_rows // per, head_forward, 0)

    def block_of(peer):
        return lax.rem(peer, 2) * quads + peer // 2

    mine = core * quads + quad

    def send_mixed(step, carry):
        peer, where = to_plane(step)
        push(mix_s.at[block_of(peer)], mix_b.at[:, lanes_of(j)], a_send.at[0], a_recv.at[0], where)
        return carry

    lax.fori_loop(1, grid_cols, send_mixed, 0)
    background(SEND[1])
    mix_b[:, lanes_of(j)] = mix_s[mine]
    loads[SO].wait()
    wait_for(mix_b.at[:, pl.ds(0, chunk * (grid_cols - 1))], a_recv.at[0])
    mixed_rows = mix_b[...]
    xbuf[3, core, quad] = mixed_rows
    times(mixed_rows, SO, tmp)
    third = act[SECOND] + tmp[...] + bs[4:5]
    act[THIRD] = third
    normed_s = norm_forward(third, gs[1:2], bs[1:2])
    xbuf[5, core, quad] = normed_s
    later_x(5)
    background(SEND[2])
    loads[S1].wait()
    times(normed_s, S1, tmp)
    pre = tmp[...] + bs[5:6]
    act[PRE_S] = pre
    hidden_s = narrow(gelu_value(pre))
    xbuf[6, core, quad] = hidden_s
    waiting[:0] = [(6, piece) for piece in range(pieces)]
    later_x(3)
    background(SEND[3])
    relay_x(1)
    times(hidden_s, S2, tmp)
    new_latents[...] = narrow(act[THIRD] + tmp[...] + bs[6:7])

    d_pre = act[COT_BACK] * gelu_slope(act[PRE_S])
    pre_low = narrow(d_pre)
    times_t(pre_low, S1, tmp)
    d_rows, lnvec[6:7, :], lnvec[7:8, :] = norm_gradient(act[THIRD], gs[1:2], tmp[...])
    gradient = to_float(cot_low) + d_rows
    act[GRAD] = gradient
    out_low = narrow(gradient)
    times_t(out_low, SO, tmp)
    mix_b2 = narrow(tmp[...])
    gsrc[12] = mix_b2

    def send_dmixed(step, carry):
        peer, where = to_plane(step)
        push(gsrc.at[12, :, lanes_of(peer)], dmix_b.at[mine], a_send.at[1], a_recv.at[1], where)
        return carry

    lax.fori_loop(1, grid_cols, send_dmixed, 0)
    dmix_b[mine] = gsrc[12, :, lanes_of(j)]
    spread_g(4, pre_low)
    spread_g(6, out_low)
    background(SEND[4])
    wait_for(dmix_b.at[pl.ds(0, grid_cols - 1)], a_recv.at[1])

    def head_backward(n, carry):
        at = pl.ds(pl.multiple_of(n * per, per), per)
        parts = [dmix_b[n * (per // rows) + part] for part in range(per // rows)]
        d_mixed = jnp.concatenate(parts, axis=0)
        d_probs = own_dot(d_mixed, heads[2], 1, 1)
        found_probs = probs[at, :]
        d_scores = found_probs * (d_probs - jnp.sum(found_probs * d_probs, axis=1, keepdims=True))
        d_low = narrow(d_scores * head_scale)
        prob_grad[0, at, :] = d_low
        prob_grad[1, at, :] = narrow(found_probs)
        d_query = own_dot(d_low, heads[1], 1, 0)
        for part in range(per // rows):
            dqkv_s[n * (per // rows) + part, 0] = narrow(d_query[part * rows : (part + 1) * rows])
        return carry

    lax.fori_loop(0, head_rows // per, head_backward, 0)
    d_mixed_all = dmix_b[...].reshape(head_rows, chunk)

    def head_keys(n, carry):
        at = pl.ds(pl.multiple_of(n * per, per), per)
        d_key = own_dot(prob_grad[0, :, at], heads[0], 0, 0)
        d_value = own_dot(prob_grad[1, :, at], d_mixed_all, 0, 0)
        for part in range(per // rows):
            cut = slice(part * rows, (part + 1) * rows)
            dqkv_s[n * (per // rows) + part, 1] = narrow(d_key[cut])
            dqkv_s[n * (per // rows) + part, 2] = narrow(d_value[cut])
        return carry

    lax.fori_loop(0, head_rows // per, head_keys, 0)

    def send_dqkv(step, carry):
        peer, where = to_plane(step)
        push(dqkv_s.at[block_of(peer)], dqkv_b.at[:, :, lanes_of(j)], a_send.at[2], a_recv.at[2], where)
        return carry

    lax.fori_loop(1, grid_cols, send_dqkv, 0)
    background(SEND[5])
    dqkv_b[:, :, lanes_of(j)] = dqkv_s[mine]

    def column_sum(values):
        return jnp.sum(to_float(values), axis=0, keepdims=True)

    relay_x(6)
    have_x(6)
    right = have_g(5)
    bias_s6 = column_sum(right)
    weight_part(8, right, xbuf.at[6])
    wait_for(dqkv_b.at[:, :, pl.ds(0, chunk * (grid_cols - 1))], a_recv.at[2])
    for k in range(3):
        spread_g(9 + k, dqkv_b[k])
    times_t(dqkv_b[0], SQ, tmp)
    times_t(dqkv_b[1], SK, tmp, True)
    times_t(dqkv_b[2], SV, tmp, True)
    background(SEND[6])
    relay_x(5)
    relay_x(2)
    have_x(5)
    right = have_g(4)
    bias_s5 = column_sum(right)
    weight_part(7, right, xbuf.at[5])
    join(8)
    d_rows, lnvec[4:5, :], lnvec[5:6, :] = norm_gradient(act[SECOND], gs[0:1], tmp[...])
    gradient = act[GRAD] + d_rows
    act[GRAD] = gradient
    second_low = narrow(gradient)
    spread_g(2, second_low)
    times_t(second_low, C2, tmp)
    d_pre = tmp[...] * gelu_slope(act[PRE_C])
    pre_low = narrow(d_pre)
    spread_g(1, pre_low)
    times_t(pre_low, C1, tmp)
    d_rows, lnvec[2:3, :], lnvec[3:4, :] = norm_gradient(act[FIRST], gc[1:2], tmp[...])
    gradient = act[GRAD] + d_rows
    act[GRAD] = gradient
    out_low = narrow(gradient)
    spread_g(3, out_low)
    times_t(out_low, CO, tmp)
    d_attended = narrow(tmp[...])
    spread_g(8, d_attended)

    background(len(waiting))
    for k in range(3):
        right = have_g(9 + k)
        if k == 0:
            bias_s2 = column_sum(right)
        elif k == 2:
            bias_s3 = column_sum(right)
        weight_part(4 + k, right, xbuf.at[4])
    join(7)

    grad_inputs = own_dot(d_attended, win[1], 1, 1)
    d_attended = to_float(d_attended)
    shift = grad_inputs[:, 2 * LANES + 5 : 2 * LANES + 6]
    row_delta = jnp.sum(d_attended * act[ATT], axis=1, keepdims=True) - shift
    grad_shift = jnp.sum(grad_inputs * bin_, axis=1, keepdims=True)
    grad_scaled = grad_inputs * gin
    turned = coefficients(grad_scaled, grad_shift - row_delta)
    constant = turned[6:7]

    def away(scaled):
        values = scaled[:, 2 * LANES :] - jnp.sum(scaled, axis=1, keepdims=True) * (1.0 / count)
        values = jnp.where(lane1 < 3, values, 0.0)
        return jnp.concatenate([values, pltpu.roll(values, 8, 1)], axis=0)

    query_away, grad_away = away(query_scaled), away(grad_scaled)
    wide_lane = lax.broadcasted_iota(jnp.int32, (LANES, LANES), 1)
    wide_half = lax.broadcasted_iota(jnp.int32, (LANES, LANES), 0) // rows
    blank = jnp.zeros((LANES, LANES), bf16)
    for held in range(STEPS_HELD):
        group = wide_lane - held * 16 - wide_half * 8
        along = narrow(jnp.where((group >= 0) & (group < 3), 1.0, 0.0))
        colors_here = [query_away, grad_away]
        if held:
            colors_here = [pltpu.roll(v, held * 16, 1) for v in colors_here]
        cgright[held] = jnp.concatenate(
            [
                jnp.concatenate([narrow(colors_here[0]), blank], axis=1),
                jnp.concatenate([narrow(colors_here[1]), blank], axis=1),
                jnp.concatenate([blank, along], axis=1),
            ],
            axis=0,
        )
    rowsum[...] = jnp.zeros(rowsum.shape, f32)
    colsum[...] = jnp.zeros(colsum.shape, f32)
    cgacc[...] = jnp.zeros(cgacc.shape, f32)

    def back_pass(s, carry):
        total, found = carry
        lines, deviation = step_lines(s)
        scores = sl[s]
        found_probs = jnp.exp(scores - log_total)
        d_scores = found_probs * (lines + constant)
        left = jnp.concatenate(
            [narrow(d_scores), narrow(found_probs), narrow(d_scores * scores + found_probs * lines)], axis=1
        )
        block, held = s // STEPS_HELD, lax.rem(s, STEPS_HELD)
        cgacc[block] += own_dot(left, cgright[held], 1, 0)
        total = total + jnp.sum(d_scores, axis=0, keepdims=True)
        return total, found + step_sums(s, d_scores * deviation)

    carry = (jnp.zeros((1, LANES), f32), jnp.zeros((8, LANES), f32))
    third_of = steps // 3
    carry = lax.fori_loop(0, third_of, back_pass, carry, unroll=4)
    relay_x(3)
    for k in range(3):
        join(4 + k)
    have_x(3)
    right = have_g(6)
    bias_s4 = column_sum(right)
    weight_part(9, right, xbuf.at[3])
    carry = lax.fori_loop(third_of, 2 * third_of, back_pass, carry, unroll=4)
    have_x(2)
    right = have_g(2)
    bias_c6 = column_sum(right)
    weight_part(2, right, xbuf.at[2])
    have_x(1)
    right = have_g(1)
    bias_c5 = column_sum(right)
    weight_part(1, right, xbuf.at[1])
    join(9)
    x_arrived(xsmall.at[0, 1 - core], 8)
    right = have_g(3)
    bias_c4 = column_sum(right)
    small_part(2, right, xsmall.at[0])
    right = have_g(8)
    bias_c3 = column_sum(right)
    small_part(1, right, xsmall.at[0])
    total, found = lax.fori_loop(2 * third_of, steps, back_pass, carry, unroll=4)
    plain_scores = pixel_sums(found, 1.0) * score_scale
    total = total * score_scale
    score_total = fold(jnp.transpose(jnp.concatenate([total, jnp.zeros((LANES - 1, LANES), f32)], axis=0)))[:, 0:1]
    score_low = narrow(plain_scores * gin + score_total * bin_)
    xsmall[1, core, quad] = score_low
    x_spread(xsmall.at[1, core, quad], 9)

    def d_query_part(n, carry):
        at = pl.ds(pl.multiple_of(n * 256, 256), 256)
        tmp[:, at] = own_dot(score_low, win[0, :, at], 1, 0)
        return carry

    lax.fori_loop(0, width // 256, d_query_part, 0)
    query_grad_low = narrow(tmp[...])
    spread_g(0, query_grad_low)
    gain_part = jnp.sum(query_inputs * plain_scores + grad_inputs * plain_mixed, axis=0, keepdims=True)
    bias_part = jnp.sum(query_inputs * score_total + grad_inputs, axis=0, keepdims=True)
    cuts = [part[:, k * LANES : (k + 1) * LANES] for part in (gain_part, bias_part) for k in range(3)]
    ivec[...] = jnp.concatenate(cuts + [jnp.zeros((2, LANES), f32)], axis=0)
    ivbuf[me] = ivec[...]

    def send_ivec(step, carry):
        push(ivec, ivbuf.at[me], misc_send.at[1], misc_recv.at[1], at_device(lax.rem(me + step, n_dev)))
        return carry

    lax.fori_loop(1, n_dev, send_ivec, 0)

    times_t(query_grad_low, CQ, tmp)
    d_rows, lnvec[0:1, :], lnvec[1:2, :] = norm_gradient(to_float(latents[...]), gc[0:1], tmp[...])
    latent_grad[...] = act[GRAD] + d_rows

    lnsend[...] = regroup(lnvec[...])

    def send_ln(step, carry):
        peer, where = to_plane(step)
        push(lnsend.at[:, lanes_of(peer)], lnbuf.at[j], misc_send.at[2], misc_recv.at[2], where)
        return carry

    lax.fori_loop(1, grid_cols, send_ln, 0)
    lnbuf[j] = lnsend[:, lanes_of(j)]

    for block in range(blocks):
        both = own_dot(fa[block], spread[...], 1, 0)
        center, factor = both[:, :LANES], both[:, LANES:]
        here = cgacc[block]
        cgacc[block, :, :LANES] = factor * (
            here[:, :LANES] - (to_float(fa[block]) - center) * factor * here[:, LANES:] * (1.0 / count)
        )
    for part in range(grid_rows):
        at = pl.ds(part * tile_rows, tile_rows)
        lines = jnp.concatenate([narrow(cgacc[block, at, :LANES]) for block in range(blocks)], axis=1)
        tiles = narrow(own_dot(back[...], lines, 1, 1))
        for tile in range(grid_cols):
            cgsend[tile, part, :, :tile_rows] = tiles[tile * 32 : tile * 32 + 32]
    cgbuf[j] = cgsend[j]

    def send_cg(step, carry):
        peer, where = to_plane(step)
        push(cgsend.at[peer], cgbuf.at[j], misc_send.at[3], misc_recv.at[3], where)
        return carry

    lax.fori_loop(1, grid_cols, send_cg, 0)

    x_relay(xsmall.at[1, core], 9)
    for m in (2, 1):
        join(m)
    for m in (2, 1):
        join_small(m)
    have_x(0)
    right = have_g(0)
    bias_c2 = column_sum(right)
    weight_part(0, right, xbuf.at[0])
    x_arrived(xsmall.at[1, 1 - core], 9)
    small_part(0, have_g(7), xsmall.at[1])

    wait_for(cgbuf.at[pl.ds(0, grid_cols - 1)], misc_recv.at[3])
    tiles = to_float(cgbuf[0])
    for peer in range(1, grid_cols):
        tiles = tiles + to_float(cgbuf[peer])
    cgsum[...] = tiles

    def send_tile(step, carry):
        part = lax.rem(z + step, grid_rows)
        push(cgsum.at[part], cgfin.at[z], misc_send.at[6], misc_recv.at[6], {"rows": part})
        return carry

    lax.fori_loop(1, grid_rows, send_tile, 0)
    cgfin[z] = cgsum[z]
    wait_for(lnbuf.at[pl.ds(0, grid_cols - 1)], misc_recv.at[2])
    norms = lnbuf[0]
    for peer in range(1, grid_cols):
        norms = norms + lnbuf[peer]
    vecsend[...] = jnp.concatenate(
        [
            norms, bias_c2, bias_c3, bias_c4, bias_c5, bias_c6, bias_s2, bias_s3,
            bias_s4, bias_s5, bias_s6, jnp.zeros((6, chunk), f32),
        ],
        axis=0,
    )

    def send_vec(step, carry):
        where = {"rows": lax.rem(z + step, grid_rows)}
        push(vecsend, vecbuf.at[z], misc_send.at[4], misc_recv.at[4], where)
        return carry

    lax.fori_loop(1, grid_rows, send_vec, 0)
    vecbuf[z] = vecsend[...]

    wait_for(cgfin.at[pl.ds(0, grid_rows - 1)], misc_recv.at[6])
    color_out[...] = cgfin[...]
    wait_for(ivbuf.at[pl.ds(0, n_dev - 1)], misc_recv.at[1])
    sums = ivbuf[0]
    for d in range(1, n_dev):
        sums = sums + ivbuf[d]
    input_vector_out[...] = sums

    join(0)
    join_small(0)
    wait_for(vecbuf.at[pl.ds(0, grid_rows - 1)], misc_recv.at[4])
    vectors = vecbuf[0]
    for part in range(1, grid_rows):
        vectors = vectors + vecbuf[part]
    vector_out[...] = vectors
    for m in (8, 7, 4, 5, 6, 9, 2, 1, 0):
        wait_for(crossed.at[slot_of(m)], f_recv.at[m])
        result = kept_of(m)[...] + to_float(crossed[slot_of(m)])
        kept_of(m)[...] = result
    sums = []
    for m in (2, 1, 0):
        wait_for(crossed_small.at[m], f_recv.at[10 + m])
        sums.append(kept_small[m] + to_float(crossed_small[m]))
    out_total[...] = own_dot(narrow(sums[0]), win[1], 1, 0)
    input_parts[1] = sums[1]
    input_parts[0] = sums[2]

    for k in range(7):
        wait_for(xbuf.at[k, 0, pl.ds(0, quads - 1)], x_send.at[k])
        wait_for(xbuf.at[k, 0], y_send.at[k])
    for k in range(2):
        wait_for(xsmall.at[k, 0, pl.ds(0, quads - 1)], x_send.at[8 + k])
        wait_for(xsmall.at[k, 0], y_send.at[8 + k])
    for k in range(12):
        wait_for(gsrc.at[k, :, pl.ds(0, chunk * (grid_cols - 1))], g_send.at[k])
    wait_for(mix_s.at[pl.ds(0, grid_cols - 1)], a_send.at[0])
    wait_for(dmix_b.at[pl.ds(0, grid_cols - 1)], a_send.at[1])
    wait_for(dqkv_s.at[pl.ds(0, grid_cols - 1)], a_send.at[2])
    wait_for(colbuf.at[pl.ds(0, grid_cols - 1)], misc_send.at[0])
    wait_for(ivbuf.at[pl.ds(0, n_dev - 1)], misc_send.at[1])
    wait_for(lnbuf.at[pl.ds(0, grid_cols - 1)], misc_send.at[2])
    wait_for(cgbuf.at[pl.ds(0, grid_cols - 1)], misc_send.at[3])
    wait_for(colstage.at[pl.ds(0, grid_rows - 1)], misc_send.at[5])
    wait_for(cgfin.at[pl.ds(0, grid_rows - 1)], misc_send.at[6])
    for m in (0, 1, 2, 4, 5, 6, 7, 8, 9):
        wait_for(paired.at[slot_of(m)], r_send.at[m])
        wait_for(handed.at[slot_of(m)], f_send.at[m])
    for m in range(3):
        wait_for(paired_small.at[m], r_send.at[10 + m])
        wait_for(handed_small.at[m], f_send.at[10 + m])
    wait_for(vecbuf.at[pl.ds(0, grid_rows - 1)], misc_send.at[4])


def channel_order(count):
    n = NBANDS
    starts = ((5, n), (5 + 2 * n, n), (5 + n, n), (5 + 3 * n, n), (0, 5))
    order = np.concatenate([np.arange(start, start + size) for start, size in starts])
    result = np.zeros((WIDE, count), np.float32)
    result[np.arange(count), order] = 1
    return np.asarray(result, ml_dtypes.bfloat16)


def by_channel(lines):
    n = NBANDS
    parts = [lines[..., 4 * n : 4 * n + 5], lines[..., :n], lines[..., 2 * n : 3 * n]]
    parts += [lines[..., n : 2 * n], lines[..., 3 * n : 4 * n]]
    return jnp.concatenate(parts, axis=-1)


def finish_kernel(
    own, tile_rows, tile_cols,
    latents, latent_grad, colors, cross, out, self_parts, self_out, inputs, vectors, input_vectors,
    prior_cross, prior_out, prior_input,
    o_latents, o_latent_grad, o_colors, o_cross, o_out, o_input, o_gain, o_bias,
    o_cross_gains, o_cross_biases, o_self, o_self_out, o_self_gains, o_self_biases,
):
    o_latents[...] = latents[...]
    o_latent_grad[...] = latent_grad[...]
    for channel in range(3):
        for col in range(tile_cols):
            line = channel * tile_cols + col
            for image in range(colors.shape[0]):
                o_colors[channel, col, image : image + 1, :] = colors[image, line : line + 1, :tile_rows]
    o_cross[...] = prior_cross[...] + cross[...]
    o_out[...] = prior_out[...] + out[...]
    o_self[...] = self_parts[...]
    o_self_out[...] = self_out[...]
    for k in range(2):
        o_input[k] = prior_input[k] + by_channel(inputs[k])
    lines = input_vectors[...]
    for k, target in enumerate((o_gain, o_bias)):
        wide = jnp.concatenate([lines[3 * k + t : 3 * k + t + 1] for t in range(3)], axis=1)
        target[...] = by_channel(wide)
    place = lax.axis_index("rows")
    width = vectors.shape[1]
    mine = pltpu.roll(vectors[...], lax.rem(width - place * own, width), 1)[:, :own]
    for target, rows in (
        (o_cross_gains, (0, 2)),
        (o_cross_biases, (1, 3, 8, 9, 10, 11, 12)),
        (o_self_gains, (4, 6)),
        (o_self_biases, (5, 7, 13, 14, 15, 16, 17)),
    ):
        for k, row in enumerate(rows):
            target[k : k + 1, :] = mine[row : row + 1]


def local_kernel(
    latents,
    pixel_colors,
    image_boxes,
    cotangent,
    cross_matrices,
    cross_out,
    input_matrices,
    in_gain,
    in_bias,
    cross_gains,
    cross_biases,
    self_matrices,
    self_out,
    self_gains,
    self_biases,
    prior_cross_matrices,
    prior_cross_out,
    prior_input_matrices,
):
    rows, width = latents.shape
    channels, image_count, tile_rows, tile_cols = pixel_colors.shape
    grid_rows = lax.axis_size("rows")
    grid_cols = lax.axis_size("cols")
    n_dev = grid_rows * grid_cols
    tall, wide = grid_rows * tile_rows, grid_cols * tile_cols
    steps = wide // 2
    chunk = width // grid_cols
    own = chunk // grid_rows
    quads = grid_cols // 2
    place, pick, spread, back = selections(tile_cols, grid_cols, steps)
    blocks = back.shape[1] // LANES
    held_rows = -(-steps // 8) * 8
    order = channel_order(input_matrices.shape[1])
    f32, bf16 = jnp.float32, jnp.bfloat16
    vmem = pl.BlockSpec(memory_space=pltpu.VMEM)
    away = pl.BlockSpec(memory_space=pl.ANY)
    shape = jax.ShapeDtypeStruct
    sizes = (grid_rows, grid_cols, rows, steps, tile_rows, tile_cols)
    dma = pltpu.SemaphoreType.DMA
    scratch = [
        ((10, width, width), bf16),
        ((2, WIDE, width), bf16),
        (input_matrices.shape, bf16),
        ((7, 2, quads, rows, width), bf16),
        ((2, 2, quads, rows, WIDE), bf16),
        ((13, rows, width), bf16),
        ((12, 2, quads, rows, chunk), bf16),
        ((9, chunk, width), bf16),
        ((9, 2, own, width), bf16),
        ((9, own, width), bf16),
        ((9, own, width), bf16),
        ((3, chunk, WIDE), bf16),
        ((3, 2, own, WIDE), bf16),
        ((3, own, WIDE), bf16),
        ((3, own, WIDE), bf16),
        ((3, own, WIDE), f32),
        ((grid_rows, 32, LANES), f32),
        ((grid_rows, 32, LANES), bf16),
        ((grid_rows, 32, LANES), bf16),
        ((grid_cols, grid_rows, 32, LANES), bf16),
        ((tall, WIDE), f32),
        ((tall, 7 * LANES), bf16),
        ((blocks, tall, LANES), bf16),
        ((blocks * LANES, tall), bf16),
        ((steps, tall, LANES), f32),
        ((tall, LANES), f32),
        ((held_rows, LANES), f32),
        ((tall, 2 * LANES), bf16),
        ((2, held_rows, 2 * LANES), bf16),
        ((STEPS_HELD, LANES, 2 * LANES), bf16),
        ((STEPS_HELD, WIDE, 2 * LANES), bf16),
        ((tall, LANES), f32),
        ((held_rows, LANES), f32),
        ((blocks, tall, 2 * LANES), f32),
        ((grid_cols, grid_rows, 32, LANES), bf16),
        ((grid_cols, grid_rows, 32, LANES), bf16),
        ((grid_rows, 32, LANES), f32),
        ((grid_rows, 32, LANES), f32),
        ((9, rows, width), f32),
        ((8, width), f32),
        ((8, width), f32),
        ((grid_cols, 8, chunk), f32),
        ((8, width), f32),
        ((24, chunk), f32),
        ((grid_rows, 24, chunk), f32),
        ((8, LANES), f32),
        ((n_dev, 8, LANES), f32),
        ((3, grid_cols * rows, chunk), bf16),
        ((grid_cols * rows, grid_cols * rows), f32),
        ((2, grid_cols * rows, grid_cols * rows), bf16),
        ((grid_cols, rows, chunk), bf16),
        ((rows, width), bf16),
        ((grid_cols, rows, chunk), bf16),
        ((grid_cols, 3, rows, chunk), bf16),
        ((3, rows, width), bf16),
    ]
    scratch = [pltpu.VMEM(dims, kind) for dims, kind in scratch]
    scratch += [dma((count,)) for count in (11, 10, 10, 10, 10, 12, 12, 3, 3, 13, 13, 13, 13, 7, 7)]
    outs = [
        ((rows, width), bf16),
        ((rows, width), f32),
        ((image_count, 32, LANES), f32),
        ((3, own, width), f32),
        ((own, width), f32),
        ((5, own, width), f32),
        ((own, width), f32),
        ((2, own, WIDE), f32),
        ((24, chunk), f32),
        ((8, LANES), f32),
    ]
    results = pl.pallas_call(
        functools.partial(layer_kernel, sizes),
        out_shape=[shape(dims, kind) for dims, kind in outs],
        in_specs=[pl.BlockSpec(memory_space=pltpu.SMEM)] + [vmem] * 14 + [away] * 5,
        out_specs=[vmem] * len(outs),
        scratch_shapes=scratch,
        compiler_params=pltpu.CompilerParams(
            collective_id=0, has_side_effects=True, vmem_limit_bytes=VMEM_BYTES
        ),
        cost_estimate=pl.CostEstimate(
            flops=20_000_000_000, bytes_accessed=40_000_000, transcendentals=4_000_000
        ),
    )(
        image_boxes,
        latents,
        cotangent,
        jnp.transpose(pixel_colors, (0, 3, 1, 2)),
        in_gain.reshape(1, -1),
        in_bias.reshape(1, -1),
        order,
        cross_gains,
        cross_biases,
        self_gains,
        self_biases,
        place,
        pick,
        spread,
        back,
        cross_matrices,
        cross_out,
        self_matrices,
        self_out,
        input_matrices,
    )
    count = input_matrices.shape[1]
    last = [
        ((rows, width), bf16),
        ((rows, width), f32),
        ((channels, tile_cols, image_count, tile_rows), f32),
        ((3, own, width), f32),
        ((own, width), f32),
        ((2, own, count), f32),
        ((1, count), f32),
        ((1, count), f32),
        ((2, own), f32),
        ((7, own), f32),
        ((5, own, width), f32),
        ((own, width), f32),
        ((2, own), f32),
        ((7, own), f32),
    ]
    done = pl.pallas_call(
        functools.partial(finish_kernel, own, tile_rows, tile_cols),
        out_shape=[shape(dims, kind) for dims, kind in last],
        in_specs=[vmem] * (len(outs) + 3),
        out_specs=[vmem] * len(last),
        compiler_params=pltpu.CompilerParams(vmem_limit_bytes=VMEM_BYTES),
    )(
        *results,
        jnp.transpose(prior_cross_matrices, (0, 2, 1)),
        jnp.transpose(prior_cross_out),
        jnp.transpose(prior_input_matrices, (0, 2, 1)),
    )
    (new_latents, latent_grad, colors, cross_total, out_total, input_total, gain, bias) = done[:8]
    cross_gain, cross_bias, self_total, self_out_total, self_gain, self_bias = done[8:]
    return (
        new_latents,
        latent_grad,
        jnp.transpose(colors, (0, 2, 3, 1)),
        jnp.transpose(cross_total, (0, 2, 1)),
        jnp.transpose(out_total),
        jnp.transpose(input_total, (0, 2, 1)),
        gain[0],
        bias[0],
        cross_gain,
        cross_bias,
        jnp.transpose(self_total, (0, 2, 1)),
        jnp.transpose(self_out_total),
        self_gain,
        self_bias,
    )


def solution(mesh):
    placed = (
        P(("rows", "cols"), None),
        P(None, None, "rows", "cols"),
        P(),
        P(("rows", "cols"), None),
        P(),
        P(),
        P(),
        P(),
        P(),
        P(),
        P(),
        P(),
        P(),
        P(),
        P(),
        P(None, None, ("rows", "cols")),
        P(None, ("rows", "cols")),
        P(None, None, ("rows", "cols")),
    )
    one_head_each = mesh.shape["cols"] == HEADS
    return jax.shard_map(
        local_kernel if one_head_each else local,
        mesh=mesh,
        in_specs=placed,
        out_specs=(
            P(("rows", "cols"), None),
            P(("rows", "cols"), None),
            P(None, None, "rows", "cols"),
            P(None, None, ("rows", "cols")),
            P(None, ("rows", "cols")),
            P(None, None, ("rows", "cols")),
            P(),
            P(),
            P(None, ("rows", "cols")),
            P(None, ("rows", "cols")),
            P(None, None, ("rows", "cols")),
            P(None, ("rows", "cols")),
            P(None, ("rows", "cols")),
            P(None, ("rows", "cols")),
        ),
        check_vma=False,
    )
```

```python
import functools

import jax
import jax.numpy as jnp
import ml_dtypes
import numpy as np
from jax import lax
from jax.experimental import pallas as pl
from jax.experimental.pallas import tpu as pltpu
from jax.sharding import PartitionSpec as P

HEADS = 8
LATENTS = 512
NBANDS = 64
HEAD_DIM = 128


EPS = 1e-05
NEG = -1e30
FREQ_TOP = 112.0
VMEM_BYTES = 63 * 1024 * 1024
PLAN = {0: ((4, 4),), 1: ((1, 2),), 3: ((5, 2),), 4: ((5, 2),), 5: ((1, 2),), 8: ((3, 4),)}


def narrow(values):
    return values.astype(jnp.bfloat16)


def to_float(values):
    return values.astype(jnp.float32)


def matmul(former, latter):
    return jnp.dot(former, latter, preferred_element_type=jnp.float32)


def inner_left(former, latter):
    return lax.dot_general(
        former, latter, (((0,), (0,)), ((), ())), preferred_element_type=jnp.float32
    )


def inner_right(former, latter):
    return lax.dot_general(
        former, latter, (((1,), (1,)), ((), ())), preferred_element_type=jnp.float32
    )


def layer_norm(values, gain, offset):
    middle = jnp.mean(values, axis=-1, keepdims=True)
    centered = values - middle
    spread = jnp.mean(centered * centered, axis=-1, keepdims=True)
    return centered * lax.rsqrt(spread + EPS) * gain + offset


def norm_back(values, gain, offset, gradient):
    result, pullback = jax.vjp(layer_norm, values, gain, offset)
    return pullback(gradient)


def gelu_tanh(values):
    return jax.nn.gelu(values, approximate=True)


def gelu_back(pre_gelu, gradient):
    result, pullback = jax.vjp(gelu_tanh, pre_gelu)
    return pullback(gradient)[0]


def axis_features(places, extent):
    frequency = 1.0 + jnp.arange(NBANDS, dtype=jnp.float32) * ((FREQ_TOP - 1.0) / (NBANDS - 1))
    angle = jnp.pi * places[:, None] * frequency[None, :]
    return (places, jnp.sin(angle), jnp.cos(angle))


def canvas_of(colors, image_box):
    channels, wide, tall = colors.shape
    top, left, height, width = image_box[0], image_box[1], image_box[2], image_box[3]
    row_at = jnp.arange(tall, dtype=jnp.int32)
    col_at = jnp.arange(wide, dtype=jnp.int32)
    y_place = -1.0 + 2.0 * to_float(row_at - top) / to_float(height - 1)
    x_place = -1.0 + 2.0 * to_float(col_at - left) / to_float(width - 1)
    y_parts = axis_features(y_place, height)
    x_parts = axis_features(x_place, width)
    y_all = jnp.concatenate([y_parts[0][:, None], y_parts[1], y_parts[2]], axis=1)
    x_all = jnp.concatenate([x_parts[0][:, None], x_parts[1], x_parts[2]], axis=1)
    count = channels + 2 + 4 * NBANDS
    color_sum = jnp.sum(colors, axis=0)
    color_square = jnp.sum(colors * colors, axis=0)
    mean = (color_sum + jnp.sum(y_all, axis=1)[None, :] + jnp.sum(x_all, axis=1)[:, None]) / count
    square = (
        color_square
        + jnp.sum(y_all * y_all, axis=1)[None, :]
        + jnp.sum(x_all * x_all, axis=1)[:, None]
    ) / count
    deviation = lax.rsqrt(square - mean * mean + EPS)
    row_in = (row_at >= top) & (row_at < top + height)
    col_in = (col_at >= left) & (col_at < left + width)
    return (y_all, x_all, mean, deviation, row_in, col_in)


def split_channels(rows, channels):
    n = NBANDS
    c = channels
    y_part = jnp.concatenate(
        [rows[:, c : c + 1], rows[:, c + 2 : c + 2 + n], rows[:, c + 2 + 2 * n : c + 2 + 3 * n]],
        axis=1,
    )
    x_part = jnp.concatenate(
        [
            rows[:, c + 1 : c + 2],
            rows[:, c + 2 + n : c + 2 + 2 * n],
            rows[:, c + 2 + 3 * n : c + 2 + 4 * n],
        ],
        axis=1,
    )
    return (rows[:, :c], y_part, x_part)


def join_channels(color_part, y_part, x_part):
    n = NBANDS
    return jnp.concatenate(
        [
            color_part,
            y_part[:, :1],
            x_part[:, :1],
            y_part[:, 1 : n + 1],
            x_part[:, 1 : n + 1],
            y_part[:, n + 1 :],
            x_part[:, n + 1 :],
        ],
        axis=1,
    )


def against_pixels(rows, colors, canvas):
    y_all, x_all, mean, deviation = canvas[:4]
    color_part, y_part, x_part = split_channels(rows, colors.shape[0])
    by_row = inner_right(narrow(y_part), narrow(y_all))
    by_col = inner_right(narrow(x_part), narrow(x_all))
    total = by_row[:, None, :] + by_col[:, :, None]
    for j in range(colors.shape[0]):
        total = total + color_part[:, j][:, None, None] * colors[j][None]
    total = total - jnp.sum(rows, axis=1)[:, None, None] * mean[None]
    return total * deviation[None]


def over_pixels(weights, colors, canvas):
    y_all, x_all, mean, deviation = canvas[:4]
    scaled = weights * deviation[None]
    y_part = matmul(narrow(jnp.sum(scaled, axis=1)), narrow(y_all))
    x_part = matmul(narrow(jnp.sum(scaled, axis=2)), narrow(x_all))
    color_part = jnp.stack(
        [jnp.sum(scaled * colors[j][None], axis=(1, 2)) for j in range(colors.shape[0])], axis=1
    )
    middle = jnp.sum(scaled * mean[None], axis=(1, 2))
    return join_channels(color_part, y_part, x_part) - middle[:, None]


def mlp_forward(row_values, gain, offset, w_in, b_in, w_out, b_out):
    normed = narrow(layer_norm(row_values, gain, offset))
    pre_gelu = matmul(normed, w_in) + b_in
    hidden = narrow(gelu_tanh(pre_gelu))
    return (matmul(hidden, w_out) + b_out, (normed, pre_gelu, hidden))


def mlp_backward(row_values, gain, offset, w_in, w_out, stored, gradient):
    normed, pre_gelu, hidden = stored
    grad_low = narrow(gradient)
    d_w_out = inner_left(hidden, grad_low)
    d_b_out = jnp.sum(gradient, axis=0)
    d_pre = gelu_back(pre_gelu, inner_right(grad_low, w_out))
    pre_low = narrow(d_pre)
    d_w_in = inner_left(normed, pre_low)
    d_b_in = jnp.sum(d_pre, axis=0)
    d_rows, d_gain, d_offset = norm_back(row_values, gain, offset, inner_right(pre_low, w_in))
    return (
        gradient + d_rows,
        (d_w_in, d_w_out),
        (d_gain, d_offset, d_b_in, d_b_out),
        (pre_low, grad_low),
    )


def local(
    latents,
    pixel_colors,
    image_boxes,
    cotangent,
    cross_matrices,
    cross_out,
    input_matrices,
    in_gain,
    in_bias,
    cross_gains,
    cross_biases,
    self_matrices,
    self_out,
    self_gains,
    self_biases,
    prior_cross_matrices,
    prior_cross_out,
    prior_input_matrices,
):
    rows_dev = latents.shape[0]
    model_width = latents.shape[1]
    image_count = image_boxes.shape[0]
    tile_rows = pixel_colors.shape[2]
    tile_cols = pixel_colors.shape[3]
    input_width = input_matrices.shape[1]
    grid_rows = lax.axis_size("rows")
    grid_cols = lax.axis_size("cols")
    all_rows = rows_dev * grid_rows * grid_cols
    row_place = lax.axis_index("rows")
    col_place = lax.axis_index("cols")
    row_start = row_place * tile_rows
    col_start = col_place * tile_cols
    score_scale = model_width ** (-0.5)
    head_scale = HEAD_DIM ** (-0.5)
    g_cross = to_float(cross_gains)
    b_cross = to_float(cross_biases)
    g_self = to_float(self_gains)
    b_self = to_float(self_biases)
    g_input = to_float(in_gain)
    b_input = to_float(in_bias)
    latent_state = to_float(latents)
    normed_q = narrow(layer_norm(latent_state, g_cross[0], b_cross[0]))
    query_rows = narrow(matmul(normed_q, cross_matrices[0]) + b_cross[2])
    colors_low = lax.all_gather(pixel_colors, ("rows", "cols"), axis=0, tiled=False)
    colors_low = lax.dynamic_index_in_dim(colors_low, row_place, axis=2, keepdims=False)
    colors_low = colors_low.reshape(grid_rows, grid_cols, 3, tile_rows, tile_cols)
    colors = to_float(
        jnp.transpose(colors_low, (2, 1, 4, 0, 3)).reshape(
            3, grid_cols * tile_cols, grid_rows * tile_rows
        )
    )
    image_box = lax.dynamic_index_in_dim(image_boxes, row_place, axis=0, keepdims=False)
    canvas = canvas_of(colors, image_box)
    mean, deviation, row_in, col_in = canvas[2:]
    inside = (col_in[:, None] & row_in[None, :])[None]
    key_weight = input_matrices[0]
    value_weight = input_matrices[1]
    query_inputs = inner_right(query_rows, key_weight)
    query_lines = against_pixels(query_inputs * g_input, colors, canvas)
    query_shift = jnp.sum(query_inputs * b_input, axis=1)
    scores = jnp.where(
        inside, (query_lines + query_shift[:, None, None]) * score_scale, NEG
    )
    peak_score = jnp.max(scores, axis=(1, 2), keepdims=True)
    weights = jnp.where(inside, jnp.exp(scores - peak_score), 0.0)
    cross_probs = weights / jnp.sum(weights, axis=(1, 2), keepdims=True)
    plain_mixed = over_pixels(cross_probs, colors, canvas)
    mixed_inputs = (
        plain_mixed * g_input + jnp.sum(cross_probs, axis=(1, 2))[:, None] * b_input
    )
    mixed_low = narrow(mixed_inputs)
    attended = matmul(mixed_low, value_weight) + b_cross[3]
    attended_low = narrow(attended)
    first = latent_state + matmul(attended_low, cross_out) + b_cross[4]
    branch, cross_stored = mlp_forward(
        first, g_cross[1], b_cross[1], cross_matrices[1], b_cross[5], cross_matrices[2], b_cross[6]
    )
    second = first + branch
    normed_t = narrow(layer_norm(second, g_self[0], b_self[0]))
    tower_queries = narrow(matmul(normed_t, self_matrices[0]) + b_self[2])
    tower_keys = narrow(matmul(normed_t, self_matrices[1]))
    tower_values = narrow(matmul(normed_t, self_matrices[2]) + b_self[3])
    keys_group, values_group = (
        lax.all_gather(tower_keys, "cols", axis=0, tiled=True),
        lax.all_gather(tower_values, "cols", axis=0, tiled=True),
    )
    group_rows = keys_group.shape[0]
    query_image = (
        (row_place * grid_cols + col_place) * rows_dev + jnp.arange(rows_dev, dtype=jnp.int32)
    ) // LATENTS
    key_image = (row_place * group_rows + jnp.arange(group_rows, dtype=jnp.int32)) // LATENTS
    same_image = (query_image[:, None] == key_image[None, :])[None]
    query_heads = tower_queries.reshape(rows_dev, HEADS, HEAD_DIM)
    key_heads = keys_group.reshape(group_rows, HEADS, HEAD_DIM)
    value_heads = values_group.reshape(group_rows, HEADS, HEAD_DIM)
    head_scores = jnp.where(
        same_image,
        jnp.einsum("qhd,khd->hqk", query_heads, key_heads, preferred_element_type=jnp.float32)
        * head_scale,
        NEG,
    )
    head_weights = jnp.where(
        same_image, jnp.exp(head_scores - jnp.max(head_scores, axis=2, keepdims=True)), 0.0
    )
    head_probs = head_weights / jnp.sum(head_weights, axis=2, keepdims=True)
    probs_low = narrow(head_probs)
    tower_mixed = narrow(
        jnp.einsum(
            "hqk,khd->qhd", probs_low, value_heads, preferred_element_type=jnp.float32
        ).reshape(rows_dev, model_width)
    )
    third = second + matmul(tower_mixed, self_out) + b_self[4]
    branch, tower_stored = mlp_forward(
        third, g_self[1], b_self[1], self_matrices[3], b_self[5], self_matrices[4], b_self[6]
    )
    new_latents = narrow(third + branch)
    gradient = to_float(cotangent)
    gradient, tower_mlp_w, tower_mlp_v, tower_lows = mlp_backward(
        third, g_self[1], b_self[1], self_matrices[3], self_matrices[4], tower_stored, gradient
    )
    tower_out_low = narrow(gradient)
    d_self_out = inner_left(tower_mixed, tower_out_low)
    d_self_out_bias = jnp.sum(gradient, axis=0)
    d_mixed = narrow(inner_right(tower_out_low, self_out)).reshape(rows_dev, HEADS, HEAD_DIM)
    d_probs = jnp.einsum("qhd,khd->hqk", d_mixed, value_heads, preferred_element_type=jnp.float32)
    d_value_heads = jnp.einsum(
        "hqk,qhd->khd", probs_low, d_mixed, preferred_element_type=jnp.float32
    )
    d_scores = head_probs * (d_probs - jnp.sum(head_probs * d_probs, axis=2, keepdims=True))
    d_scores_low = narrow(d_scores * head_scale)
    d_query_heads = jnp.einsum(
        "hqk,khd->qhd", d_scores_low, key_heads, preferred_element_type=jnp.float32
    ).reshape(rows_dev, model_width)
    d_key_heads = jnp.einsum(
        "hqk,qhd->khd", d_scores_low, query_heads, preferred_element_type=jnp.float32
    )
    d_tower_keys, d_tower_values = (
        lax.psum_scatter(
            d_key_heads.reshape(group_rows, model_width).astype(jnp.bfloat16),
            "cols",
            scatter_dimension=0,
            tiled=True,
        ).astype(jnp.float32),
        lax.psum_scatter(
            d_value_heads.reshape(group_rows, model_width).astype(jnp.bfloat16),
            "cols",
            scatter_dimension=0,
            tiled=True,
        ).astype(jnp.float32),
    )
    tq_low = narrow(d_query_heads)
    tk_low = narrow(d_tower_keys)
    tv_low = narrow(d_tower_values)
    d_normed_t = (
        inner_right(tq_low, self_matrices[0])
        + inner_right(tk_low, self_matrices[1])
        + inner_right(tv_low, self_matrices[2])
    )
    d_second, d_self_gain, d_self_bias = norm_back(second, g_self[0], b_self[0], d_normed_t)
    gradient = gradient + d_second
    self_gain_grad = jnp.stack([d_self_gain, tower_mlp_v[0]])
    self_bias_grad = jnp.stack(
        [
            d_self_bias,
            tower_mlp_v[1],
            jnp.sum(d_query_heads, axis=0),
            jnp.sum(d_tower_values, axis=0),
            d_self_out_bias,
            tower_mlp_v[2],
            tower_mlp_v[3],
        ]
    )
    gradient, cross_mlp_w, cross_mlp_v, cross_lows = mlp_backward(
        first, g_cross[1], b_cross[1], cross_matrices[1], cross_matrices[2], cross_stored, gradient
    )
    cross_out_low = narrow(gradient)
    d_cross_out = inner_left(attended_low, cross_out_low)
    d_cross_out_bias = jnp.sum(gradient, axis=0)
    d_attended = narrow(inner_right(cross_out_low, cross_out))
    value_shift = jnp.sum(to_float(d_attended) * b_cross[3], axis=1)
    row_delta = jnp.sum(to_float(d_attended) * attended, axis=1) - value_shift
    grad_inputs = inner_right(d_attended, value_weight)
    grad_shift = jnp.sum(grad_inputs * b_input, axis=1)
    grad_lines = against_pixels(grad_inputs * g_input, colors, canvas)
    d_scores = (
        cross_probs * (grad_lines + (grad_shift - row_delta)[:, None, None]) * score_scale
    )
    plain_scores = over_pixels(d_scores, colors, canvas)
    score_sum = jnp.sum(d_scores, axis=(1, 2))
    prob_sum = jnp.sum(cross_probs, axis=(1, 2))
    score_inputs = plain_scores * g_input + score_sum[:, None] * b_input
    score_low = narrow(score_inputs)
    d_query_rows = matmul(score_low, key_weight)
    in_gain_part = jnp.sum(query_inputs * plain_scores + grad_inputs * plain_mixed, axis=0)
    in_bias_part = jnp.sum(
        query_inputs * score_sum[:, None] + grad_inputs * prob_sum[:, None], axis=0
    )
    query_scaled = query_inputs * g_input
    grad_scaled = grad_inputs * g_input
    query_away = query_scaled[:, :3] - jnp.mean(query_scaled, axis=1, keepdims=True)
    grad_away = grad_scaled[:, :3] - jnp.mean(grad_scaled, axis=1, keepdims=True)
    along = jnp.sum(d_scores * query_lines + cross_probs * grad_lines, axis=0) / input_width
    color_parts = jnp.einsum(
        "rj,rcy->jcy", query_away, d_scores, precision=lax.Precision.HIGHEST
    ) + jnp.einsum("rj,rcy->jcy", grad_away, cross_probs, precision=lax.Precision.HIGHEST)
    color_parts = deviation[None] * (
        color_parts - (colors - mean[None]) * deviation[None] * along[None]
    )
    color_parts = color_parts.reshape(3, grid_cols, tile_cols, grid_rows, tile_rows)
    color_parts = jnp.transpose(color_parts, (3, 1, 0, 4, 2)).reshape(
        grid_rows * grid_cols, 3, tile_rows, tile_cols
    )
    color_grad = lax.all_to_all(
        color_parts, ("rows", "cols"), split_axis=0, concat_axis=0, tiled=True
    ).reshape(image_count, grid_cols, 3, tile_rows, tile_cols)
    color_grad = jnp.transpose(jnp.sum(color_grad, axis=1), (1, 0, 2, 3))
    query_low = narrow(d_query_rows)
    d_latent, d_cross_gain, d_cross_bias = norm_back(
        latent_state, g_cross[0], b_cross[0], inner_right(query_low, cross_matrices[0])
    )
    latent_grad = gradient + d_latent
    in_gain_grad, in_bias_grad = lax.psum((in_gain_part, in_bias_part), ("rows", "cols"))
    vectors = jnp.stack(
        [
            d_cross_gain,
            cross_mlp_v[0],
            d_cross_bias,
            cross_mlp_v[1],
            jnp.sum(d_query_rows, axis=0),
            jnp.sum(to_float(d_attended), axis=0),
            d_cross_out_bias,
            cross_mlp_v[2],
            cross_mlp_v[3],
            d_self_gain,
            tower_mlp_v[0],
            d_self_bias,
            tower_mlp_v[1],
            jnp.sum(d_query_heads, axis=0),
            jnp.sum(d_tower_values, axis=0),
            d_self_out_bias,
            tower_mlp_v[2],
            tower_mlp_v[3],
        ]
    )
    vector_sums = lax.psum_scatter(vectors, ("rows", "cols"), scatter_dimension=1, tiled=True)
    lefts = jnp.stack(
        [
            normed_q,
            cross_stored[0],
            cross_stored[2],
            attended_low,
            normed_t,
            tower_stored[0],
            tower_stored[2],
            tower_mixed,
        ]
    )
    rights = jnp.stack(
        [
            query_low,
            cross_lows[0],
            cross_lows[1],
            cross_out_low,
            d_attended,
            query_rows,
            tq_low,
            tk_low,
            tv_low,
            tower_lows[0],
            tower_lows[1],
            tower_out_low,
        ]
    )
    small_lefts = jnp.stack([mixed_low, score_low])
    lefts = lax.all_gather(lefts, "cols", axis=1, tiled=True)
    small_lefts = lax.all_gather(small_lefts, "cols", axis=1, tiled=True)
    own = model_width // (grid_rows * grid_cols)
    rights = rights.reshape(rights.shape[0], rows_dev, grid_rows, grid_cols, own)
    rights = lax.all_to_all(
        jnp.transpose(rights, (3, 0, 1, 2, 4)), "cols", split_axis=0, concat_axis=0, tiled=False
    )
    rights = jnp.transpose(rights, (1, 0, 2, 3, 4)).reshape(
        rights.shape[1], grid_cols * rows_dev, grid_rows * own
    )
    pairs = ((0, 0), (1, 1), (2, 2), (3, 3), (4, 6), (4, 7), (4, 8), (5, 9), (6, 10), (7, 11))
    big = [inner_left(rights[k], lefts[i]).reshape(grid_rows, own, model_width) for i, k in pairs]
    small = [
        inner_left(rights[k], small_lefts[i]).reshape(grid_rows, own, input_width)
        for i, k in ((1, 5), (0, 4))
    ]
    big = lax.psum_scatter(jnp.stack(big, axis=1), "rows", scatter_dimension=0, tiled=False)
    small = lax.psum_scatter(jnp.stack(small, axis=1), "rows", scatter_dimension=0, tiled=False)
    big = jnp.transpose(big, (0, 2, 1))
    small = jnp.transpose(small, (0, 2, 1))
    all_sums = (
        big[:3],
        big[3],
        small,
        vector_sums[:2],
        vector_sums[2:9],
        big[4:9],
        big[9],
        vector_sums[9:11],
        vector_sums[11:],
    )
    cross_sums = all_sums[:5]
    self_sums = all_sums[5:]
    return (
        new_latents,
        latent_grad,
        color_grad,
        prior_cross_matrices + cross_sums[0],
        prior_cross_out + cross_sums[1],
        prior_input_matrices + cross_sums[2],
        in_gain_grad,
        in_bias_grad,
        cross_sums[3],
        cross_sums[4],
        self_sums[0],
        self_sums[1],
        self_sums[2],
        self_sums[3],
    )


STEPS_HELD = 8
GROUP = 4
LANES = 128
MESH = pl.DeviceIdType.MESH
WIDE = 3 * LANES


def own_dot(former, latter, former_dim, latter_dim):
    return lax.dot_general(
        former,
        latter,
        (((former_dim,), (latter_dim,)), ((), ())),
        preferred_element_type=jnp.float32,
    )


def selections(tile_cols, grid_cols, steps):
    held = STEPS_HELD
    blocks = -(-steps // held)
    place = np.zeros((grid_cols * 32, WIDE), np.float32)
    back = np.zeros((grid_cols * 32, blocks * LANES), np.float32)
    for tile in range(grid_cols):
        for channel in range(3):
            for offset in range(tile_cols):
                col = tile * tile_cols + offset
                line = tile * 32 + channel * tile_cols + offset
                place[line, channel * LANES + col] = 1
                half, step = divmod(col, steps)
                back[line, step * 16 + half * 8 + channel] = 1
    pick = np.zeros((7 * LANES, blocks * LANES), np.float32)
    for step in range(steps):
        for half in range(2):
            for slot, kind in enumerate((0, 1, 2, 3, 4, 3, 5, 6)):
                pick[kind * LANES + half * steps + step, step * 16 + half * 8 + slot] = 1
    spread = np.zeros((LANES, 2 * LANES), np.float32)
    for group in range(16):
        for channel in range(3):
            for slot in (3, 4):
                spread[group * 8 + slot, group * 8 + channel] = 1
            for slot in (6, 7):
                spread[group * 8 + slot, LANES + group * 8 + channel] = 1
    low = lambda values: np.asarray(values, ml_dtypes.bfloat16)
    return (low(place), low(pick), low(spread), low(back))


def norm_parts(values):
    middle = jnp.mean(values, axis=1, keepdims=True)
    centered = values - middle
    spread = jnp.mean(centered * centered, axis=1, keepdims=True)
    factor = lax.rsqrt(spread + EPS)
    return (centered * factor, factor)


def norm_forward(values, gain, offset):
    return narrow(norm_parts(values)[0] * gain + offset)


def norm_gradient(values, gain, gradient):
    plain, factor = norm_parts(values)
    inner = gradient * gain
    first = jnp.mean(inner, axis=1, keepdims=True)
    second = jnp.mean(inner * plain, axis=1, keepdims=True)
    return (
        factor * (inner - first - plain * second),
        jnp.sum(gradient * plain, axis=0, keepdims=True),
        jnp.sum(gradient, axis=0, keepdims=True),
    )


GELU_RATE = 0.7978845608028654
GELU_CUBE = 0.044715


def gelu_value(u):
    return 0.5 * u * (1.0 + jnp.tanh(GELU_RATE * (u + GELU_CUBE * u * u * u)))


def gelu_slope(u):
    bent = jnp.tanh(GELU_RATE * (u + GELU_CUBE * u * u * u))
    return 0.5 * (1.0 + bent) + 0.5 * u * (1.0 - bent * bent) * GELU_RATE * (
        1.0 + 3.0 * GELU_CUBE * u * u
    )


def waves(turns):
    near = turns - 2.0 * jnp.floor(turns * 0.5 + 0.5)
    return (jnp.sin(jnp.pi * near), jnp.cos(jnp.pi * near))


def axis_lines(place, slot):
    lane = lax.broadcasted_iota(jnp.int32, (place.shape[0], LANES), 1)
    band = lax.rem(lane, NBANDS)
    frequency = 1.0 + to_float(band) * ((FREQ_TOP - 1.0) / (NBANDS - 1))
    sine, cosine = waves(place * frequency)
    return jnp.concatenate(
        [jnp.where(lane < NBANDS, sine, cosine), jnp.where(lane == slot, place, 0.0)], axis=1
    )


def layer_kernel(
    sizes,
    boxes, latents, cotangent, colors, in_gain, in_bias, order, cross_gains, cross_biases, self_gains,
    self_biases, place, pick, spread, back,
    w_cross, w_out, w_self, w_self_out, w_input,
    new_latents, latent_grad, color_out, cross_total, out_total, self_total, self_out_total,
    input_parts, vector_out, input_vector_out,
    wts, win, win_raw, xbuf, xsmall, gsrc, gbuf, staged, paired, handed, crossed, staged_small, paired_small, handed_small, crossed_small, kept_small,
    row_pair, row_hand, row_cross, row_kept, row_turned, row_done, biases,
    color_lines, color_tiles, colstage, colbuf, img, img7, fa, ft, sl, ycoef, xcoef, yfeat, xfeat, mixrow,
    cgright, rowsum, colsum, cgacc, cgsend, cgbuf, cgsum, cgfin,
    act, lnvec, lnsend, lnbuf, biasvec, vecsend, vecbuf,
    heads, probs, prob_grad, mix_s, mix_b, dmix_b, dqkv_s, dqkv_b,
    weight_sem, x_send, x_recv, y_send, y_recv, g_send, g_recv, a_send, a_recv, r_send, r_recv, f_send, f_recv,
    misc_send, misc_recv,
):
    grid_rows, grid_cols, rows, steps, tile_rows, tile_cols = sizes
    n_dev = grid_rows * grid_cols
    width = latents.shape[1]
    quads = grid_cols // 2
    chunk = width // grid_cols
    own = chunk // grid_rows
    tall = grid_rows * tile_rows
    z = lax.axis_index("rows")
    j = lax.axis_index("cols")
    core = lax.rem(j, 2)
    quad = j // 2
    me = z * grid_cols + j
    f32, bf16 = jnp.float32, jnp.bfloat16
    score_scale = width ** (-0.5)
    head_scale = HEAD_DIM ** (-0.5)

    def at_device(d):
        return {"rows": d // grid_cols, "cols": lax.rem(d, grid_cols)}

    def lanes_of(index):
        return pl.ds(pl.multiple_of(index * chunk, chunk), chunk)

    def push(src, dst, send, recv, where):
        pltpu.make_async_remote_copy(
            src_ref=src, dst_ref=dst, send_sem=send, recv_sem=recv, device_id=where,
            device_id_type=MESH,
        ).start()

    def wait_for(ref, sem):
        pltpu.make_async_copy(ref, ref, sem).wait()

    barrier = pltpu.get_barrier_semaphore()

    def greet_plane(step, carry):
        where = {"cols": lax.rem(j + step, grid_cols)}
        pl.semaphore_signal(barrier, inc=1, device_id=where, device_id_type=MESH)
        return carry

    def greet_line(step, carry):
        where = {"rows": lax.rem(z + step, grid_rows)}
        pl.semaphore_signal(barrier, inc=1, device_id=where, device_id_type=MESH)
        return carry

    lax.fori_loop(1, grid_rows, greet_line, 0)
    lax.fori_loop(1, grid_cols, greet_plane, 0)

    sources = (
        [w_cross.at[0], w_out, w_cross.at[1], w_cross.at[2]]
        + [w_self.at[0], w_self.at[1], w_self.at[2], w_self_out, w_self.at[3], w_self.at[4]]
    )
    CQ, CO, C1, C2, SQ, SK, SV, SO, S1, S2 = range(10)
    loads = [pltpu.make_async_copy(s, wts.at[k], weight_sem.at[k]) for k, s in enumerate(sources)]
    loads.append(pltpu.make_async_copy(w_input, win_raw, weight_sem.at[10]))
    loads[CQ].start()
    loads[10].start()

    color_lines[...] = jnp.zeros(color_lines.shape, f32)
    for channel in range(3):
        for col in range(tile_cols):
            line = channel * tile_cols + col
            shown = to_float(colors[channel, col])
            for image in range(grid_rows):
                color_lines[image, line : line + 1, :tile_rows] = shown[image : image + 1]
    color_tiles[...] = narrow(color_lines[...])
    gc, bc = to_float(cross_gains[...]), to_float(cross_biases[...])
    gs, bs = to_float(self_gains[...]), to_float(self_biases[...])
    gains_here = [to_float(ref[...]).reshape(1, -1) for ref in (in_gain, in_bias)]
    gains_here = jnp.concatenate(gains_here + [jnp.zeros((6, in_gain.shape[0]), f32)], axis=0)
    gains_here = own_dot(narrow(gains_here), order[...], 1, 1)
    gin, bin_ = gains_here[0:1], gains_here[1:2]
    lat = to_float(latents[...])
    nq = norm_forward(lat, gc[0:1], bc[0:1])
    xbuf[0, core, quad] = nq
    cot_low = cotangent[...]
    xbuf[6, core, quad] = cot_low
    biases[...] = jnp.concatenate([bc, jnp.zeros((1, width), f32)], axis=0)
    pl.semaphore_wait(barrier, grid_cols + grid_rows - 2)

    def send_color(step, carry):
        image = lax.rem(z + step, grid_rows)
        push(color_tiles.at[image], colstage.at[z], misc_send.at[5], misc_recv.at[5], {"rows": image})
        return carry

    lax.fori_loop(1, grid_rows, send_color, 0)
    colstage[z] = color_tiles[z]

    def x_spread(block, sem):
        def one(step, carry):
            peer = 2 * lax.rem(quad + step, quads) + core
            push(block, block, x_send.at[sem], x_recv.at[sem], {"cols": peer})
            return carry

        lax.fori_loop(1, quads, one, 0)

    def x_relay(half, sem):
        wait_for(half.at[pl.ds(0, quads - 1)], x_recv.at[sem])
        push(half, half, y_send.at[sem], y_recv.at[sem], {"cols": j + 1 - 2 * core})

    def x_arrived(half, sem):
        wait_for(half, y_recv.at[sem])

    pieces = rows // 16
    sent = {}

    def spread_x(k):
        x_spread(xbuf.at[k, core, quad], k)

    def background(point):
        for k, count in PLAN.get(point, ()):
            for piece in range(sent.get(k, 0), sent.get(k, 0) + count):
                x_spread(xbuf.at[k, core, quad, pl.ds(piece * 16, 16)], k)
            sent[k] = sent.get(k, 0) + count

    def relay_x(k):
        x_relay(xbuf.at[k, core], k)

    def have_x(k):
        x_arrived(xbuf.at[k, 1 - core], k)

    def to_plane(step):
        peer = lax.rem(j + step, grid_cols)
        return peer, {"cols": peer}

    def regroup(values):
        tiles = [values[:, t * LANES : (t + 1) * LANES] for t in range(width // LANES)]
        piece = lax.broadcasted_iota(jnp.int32, tiles[0].shape, 1) // own
        result = []
        for peer in range(grid_cols):
            chunk_now = None
            for part in range(grid_rows):
                tile, offset = divmod((part * grid_cols + peer) * own, LANES)
                shift = (part * own - offset) % LANES
                moved = pltpu.roll(tiles[tile], shift, 1) if shift else tiles[tile]
                chunk_now = moved if part == 0 else jnp.where(piece == part, moved, chunk_now)
            result.append(chunk_now)
        return jnp.concatenate(result, axis=1)

    def spread_g(k, values):
        spread_plain(k, narrow(regroup(to_float(values))))

    def spread_plain(k, values):
        gsrc[k] = values

        def one(step, carry):
            peer, where = to_plane(step)
            push(gsrc.at[k, :, lanes_of(peer)], gbuf.at[k, core, quad], g_send.at[k], g_recv.at[k], where)
            return carry

        lax.fori_loop(1, grid_cols, one, 0)
        gbuf[k, core, quad] = gsrc[k, :, lanes_of(j)]

    def have_g(k):
        wait_for(gsrc.at[k, :, pl.ds(0, chunk * (grid_cols - 1))], g_recv.at[k])
        return gbuf[k].reshape(grid_cols * rows, chunk)

    partner = z + 1 - 2 * lax.rem(z, 2)
    across = lax.rem(z + 2, grid_rows)

    def block_at(part):
        return pl.ds(pl.multiple_of(part * own, own), own)

    def send_parts(src, pair, sem):
        for slot, part in enumerate((partner, lax.rem(partner + 2, grid_rows))):
            push(src.at[block_at(part)], pair.at[slot], r_send.at[sem], r_recv.at[sem], {"rows": partner})

    def join_parts(src, pair, hand, far, kept, sem):
        wait_for(pair, r_recv.at[sem])
        hand[...] = narrow(to_float(src[block_at(across)]) + to_float(pair[1]))
        push(hand, far, f_send.at[sem], f_recv.at[sem], {"rows": across})
        kept[...] = to_float(src[block_at(z)]) + to_float(pair[0])

    def kept_of(m):
        if m < 3:
            return cross_total.at[m]
        if m < 9:
            return self_total.at[m - 4]
        return self_out_total

    def slot_of(m):
        return m if m < 3 else m - 1

    def join(m):
        k = slot_of(m)
        join_parts(staged.at[k], paired.at[k], handed.at[k], crossed.at[k], kept_of(m), m)

    def columns_of(part):
        size = width // grid_rows
        return pl.ds(pl.multiple_of(part * size, size), size)

    def send_rows(src, sem):
        for slot, part in enumerate((partner, lax.rem(partner + 2, grid_rows))):
            push(src.at[:, columns_of(part)], row_pair.at[slot], r_send.at[sem], r_recv.at[sem], {"rows": partner})

    def join_rows(src, sem):
        wait_for(row_pair, r_recv.at[sem])
        row_hand[...] = narrow(to_float(src[:, columns_of(across)]) + to_float(row_pair[1]))
        push(row_hand, row_cross, f_send.at[sem], f_recv.at[sem], {"rows": across})
        row_kept[...] = to_float(src[:, columns_of(z)]) + to_float(row_pair[0])

    def finish_rows(sem):
        wait_for(row_cross, f_recv.at[sem])
        row_turned[...] = jnp.transpose(row_kept[...] + to_float(row_cross[...]))

        def one(step, carry):
            peer, where = to_plane(step)
            push(row_turned.at[block_at(peer)], row_done.at[:, lanes_of(j)], a_send.at[3], a_recv.at[3], where)
            return carry

        lax.fori_loop(1, grid_cols, one, 0)
        row_done[:, lanes_of(j)] = row_turned[block_at(j)]

    def recompute(source, target, k, bias):
        half = grid_cols * rows // 2

        def one(n, carry):
            at = pl.ds(pl.multiple_of(lax.rem(n, 4) * 256, 256), 256)
            x = xbuf[source, n // 4].reshape(half, width)
            pre = own_dot(x, wts[k, :, at], 1, 0) + bias[:, at]
            xbuf[target, n // 4, :, :, at] = narrow(gelu_value(pre)).reshape(quads, rows, 256)
            return carry

        lax.fori_loop(0, 8, one, 0, unroll=2)

    def join_small(m):
        join_parts(
            staged_small.at[m], paired_small.at[m], handed_small.at[m], crossed_small.at[m],
            kept_small.at[m], 10 + m,
        )

    def weight_part(m, right, left):
        turned = jnp.transpose(right)

        def one(n, carry):
            at = pl.ds(pl.multiple_of(n * 256, 256), 256)
            block = left[:, :, :, at].reshape(grid_cols * rows, 256)
            staged[slot_of(m), :, at] = narrow(own_dot(turned, block, 1, 0))
            return carry

        lax.fori_loop(0, width // 256, one, 0, unroll=4)
        if m == 8:
            send_rows(staged.at[slot_of(m)], m)
        else:
            send_parts(staged.at[slot_of(m)], paired.at[slot_of(m)], m)

    def small_part(m, right, left):
        staged_small[m] = narrow(own_dot(right, left[...].reshape(grid_cols * rows, WIDE), 0, 0))
        send_parts(staged_small.at[m], paired_small.at[m], 10 + m)

    def times(x, k, out):
        def one(n, carry):
            at = pl.ds(pl.multiple_of(n * 256, 256), 256)
            out[:, at] = own_dot(x, wts[k, :, at], 1, 0)
            return carry

        lax.fori_loop(0, width // 256, one, 0, unroll=4)

    def times_t(x, k, out, add=False):
        def one(n, carry):
            at = pl.ds(pl.multiple_of(n * 256, 256), 256)
            result = own_dot(x, wts[k, at, :], 1, 1)
            out[:, at] = out[:, at] + result if add else result
            return carry

        lax.fori_loop(0, width // 256, one, 0, unroll=4)

    FIRST, SECOND, THIRD, PRE_C, PRE_S, TMP, ATT, GRAD, COT_BACK = range(9)
    tmp = act.at[TMP]

    wait_for(colstage.at[pl.ds(0, grid_rows - 1)], misc_recv.at[5])

    def send_strip(step, carry):
        peer, where = to_plane(step)
        push(colstage, colbuf.at[j], misc_send.at[0], misc_recv.at[0], where)
        return carry

    lax.fori_loop(1, grid_cols, send_strip, 0)
    colbuf[j] = colstage[...]
    loads[CQ].wait()
    for k in range(1, 10):
        loads[k].start()
    times(nq, CQ, tmp)
    query_low = narrow(tmp[...] + bc[2:3])
    spread_x(0)
    spread_g(7, query_low)
    spread_x(6)
    loads[10].wait()
    for k in range(2):
        win[k] = narrow(own_dot(order[...], win_raw[k], 1, 0))
    query_inputs = own_dot(query_low, win[0], 1, 1)
    spare = pl.ds(2 * LANES, 16)
    spare_row = lax.broadcasted_iota(jnp.int32, (16, width), 0)
    win[1, spare, :] = narrow(jnp.where(spare_row == 5, bc[3:4], to_float(win[1, spare, :])))

    box = [boxes[z, k] for k in range(4)]

    def filled(value, shape):
        return to_float(jnp.full(shape, value, jnp.int32))

    row_at = lax.broadcasted_iota(jnp.int32, (tall, 1), 0)
    y_place = -1.0 + 2.0 * to_float(row_at - box[0]) / filled(box[2] - 1, (tall, 1))
    y_lines = axis_lines(y_place, 3)
    y_sum = jnp.sum(y_lines, axis=1, keepdims=True)
    row_out = jnp.where((row_at >= box[0]) & (row_at < box[0] + box[2]), 0.0, NEG)
    yfeat[...] = narrow(y_lines)
    held_rows = xfeat.shape[1]
    col_lane = lax.broadcasted_iota(jnp.int32, (held_rows, LANES), 1)
    col_row = lax.broadcasted_iota(jnp.int32, (held_rows, LANES), 0)
    x_sum = jnp.zeros((1, LANES), f32)
    col_out = []
    for half in range(2):
        col_at = lax.broadcasted_iota(jnp.int32, (held_rows, 1), 0) + half * steps
        x_place = -1.0 + 2.0 * to_float(col_at - box[1]) / filled(box[3] - 1, (held_rows, 1))
        x_lines = axis_lines(x_place, 4)
        xfeat[half] = narrow(x_lines)
        here = (col_lane == col_row + half * steps) & (col_row < steps)
        x_sum = x_sum + jnp.sum(
            jnp.where(here, jnp.sum(x_lines, axis=1, keepdims=True), 0.0), axis=0, keepdims=True
        )
        col_out.append(jnp.where((col_at >= box[1]) & (col_at < box[1] + box[3]), 0.0, NEG))
    x_lane = lax.broadcasted_iota(jnp.int32, (1, LANES), 1)
    x_here = -1.0 + 2.0 * to_float(x_lane - box[1]) / filled(box[3] - 1, (1, LANES))
    count = 3 + 2 + 4 * NBANDS

    lane1 = lax.broadcasted_iota(jnp.int32, (rows, LANES), 1)
    lane_half = lax.broadcasted_iota(jnp.int32, (8, LANES), 1) // rows
    sub8 = lax.broadcasted_iota(jnp.int32, (8, LANES), 0)

    def twice(values):
        return jnp.concatenate([values, values], axis=0)

    def turn(values):
        return jnp.transpose(twice(values))[:8]

    def coefficients(scaled, extra):
        tail = scaled[:, 2 * LANES :]
        total = jnp.sum(scaled, axis=1, keepdims=True)
        turned = turn(jnp.where(lane1 == 5, total, jnp.where(lane1 == 6, extra, tail)))
        total_high = to_float(narrow(turned[5:6]))
        body = jnp.where(
            sub8 < 3, turned, jnp.where(sub8 < 5, -total_high, jnp.where(sub8 == 5, total_high - turned[5:6], 0.0))
        )
        body = narrow(jnp.concatenate(
            [jnp.where(lane_half == 0, body, 0.0), jnp.where(lane_half == 1, body, 0.0)], axis=0
        ))
        ones = jnp.where(sub8 >= 6, 1.0, 0.0)
        ones = narrow(jnp.concatenate(
            [jnp.where(lane_half == 0, ones, 0.0), jnp.where(lane_half == 1, ones, 0.0)], axis=0
        ))
        mixrow[...] = jnp.zeros(mixrow.shape, bf16)
        for held in range(STEPS_HELD):
            mixrow[held, held * 16 : held * 16 + 16, :] = jnp.concatenate([body, ones], axis=1)
        scaled_low = narrow(jnp.concatenate([scaled[:, :LANES], tail], axis=1))
        ycoef[...] = own_dot(yfeat[...], twice(scaled_low), 1, 1)
        scaled_low = narrow(jnp.concatenate([scaled[:, LANES : 2 * LANES], tail], axis=1))
        nothing = jnp.zeros_like(scaled_low)
        xcoef[...] = own_dot(xfeat[0], jnp.concatenate([scaled_low, nothing], axis=0), 1, 1) + own_dot(
            xfeat[1], jnp.concatenate([nothing, scaled_low], axis=0), 1, 1
        )
        return turned

    query_scaled = query_inputs * gin * score_scale
    coefficients(query_scaled, 0.0)
    ycoef[...] += row_out
    half_lane = lax.broadcasted_iota(jnp.int32, (held_rows, LANES), 1) // rows
    xcoef[...] += jnp.where(half_lane == 0, col_out[0], col_out[1])

    wait_for(colbuf.at[pl.ds(0, grid_cols - 1)], misc_recv.at[0])
    for part in range(grid_rows):
        at = pl.ds(part * tile_rows, tile_rows)
        tiles = colbuf[:, part].reshape(grid_cols * 32, LANES)
        img[at, :] = own_dot(tiles, place[...], 0, 0)[:tile_rows]
    c0, c1, c2 = img[:, :LANES], img[:, LANES : 2 * LANES], img[:, 2 * LANES :]
    mean = (c0 + c1 + c2 + y_sum + x_sum) * (1.0 / count)
    square = (c0 * c0 + c1 * c1 + c2 * c2 + y_place * y_place + x_here * x_here + 2.0 * NBANDS) * (
        1.0 / count
    )
    dev = lax.rsqrt(square - mean * mean + EPS)
    mean_low, dev_low = narrow(mean), narrow(dev)
    img7[...] = jnp.concatenate(
        [
            narrow(c0), narrow(c1), narrow(c2),
            mean_low, narrow(mean - to_float(mean_low)),
            dev_low, narrow(dev - to_float(dev_low)),
        ],
        axis=1,
    )
    blocks = fa.shape[0]
    for block in range(blocks):
        at = pl.ds(block * LANES, LANES)
        fa[block] = narrow(own_dot(img7[...], pick[:, at], 1, 0))
        turned = own_dot(pick[:, at], img7[...], 0, 1)
        line = lax.broadcasted_iota(jnp.int32, turned.shape, 0)
        ft[at, :] = narrow(jnp.where(lax.rem(line, 8) == 5, 1.0, turned))

    def step_lines(s):
        block, held = s // STEPS_HELD, lax.rem(s, STEPS_HELD)
        result = own_dot(fa[block], mixrow[held], 1, 0)
        deviation = result[:, LANES:]
        lines = (ycoef[...] + xcoef[pl.ds(s, 1), :] + result[:, :LANES]) * deviation
        return lines, deviation

    def pair_sums(s, weighted):
        at = pl.ds(pl.multiple_of(s * 16, 32), 32)
        both = own_dot(ft[at, :], jnp.concatenate([narrow(w) for w in weighted], axis=1), 1, 0)
        result = None
        for k in range(2):
            found = both[k * 16 : k * 16 + 16, k * LANES : (k + 1) * LANES]
            found = jnp.where(lane_half == 0, found[:8], found[8:])
            colsum[pl.ds(s + k, 1), :] = found[5:6]
            result = found if result is None else result + found
        return result

    def in_groups(one, first, last, start):
        def group(n, carry):
            rows_here = None
            for pair in range(GROUP // 2):
                weighted = []
                for k in range(2):
                    s = n * GROUP + pair * 2 + k
                    total, found, here = one(s, carry)
                    carry = (total, found)
                    weighted.append(here)
                    rows_here = here if rows_here is None else rows_here + here
                carry = (carry[0], carry[1] + pair_sums(n * GROUP + pair * 2, weighted))
            rowsum[...] += rows_here
            return carry

        return lax.fori_loop(first // GROUP, last // GROUP, group, start)

    def fold(values):
        return values[:rows] + values[rows:]

    def pixel_sums(found, factor):
        by_row = fold(own_dot(narrow(rowsum[...] * factor), yfeat[...], 0, 0))
        cols = narrow(colsum[...] * factor)
        by_col = own_dot(cols, xfeat[0], 0, 0)[:rows] + own_dot(cols, xfeat[1], 0, 0)[rows:]
        padded = jnp.concatenate([found * factor, jnp.zeros((LANES - 8, LANES), f32)], axis=0)
        sums = fold(jnp.transpose(padded))
        middle = sums[:, 3:4] + sums[:, 4:5]
        tail = jnp.where(lane1 < 3, sums, 0.0) + by_row[:, LANES:] + by_col[:, LANES:]
        return jnp.concatenate([by_row[:, :LANES], by_col[:, :LANES], tail], axis=1) - middle

    def other_half(line):
        return pltpu.roll(jnp.broadcast_to(line, (8, LANES)), rows, 1)[:1]

    def first_pass(s, best):
        lines, deviation = step_lines(s)
        sl[s] = lines
        return jnp.maximum(best, jnp.max(lines, axis=0, keepdims=True))

    best = lax.fori_loop(0, steps, first_pass, jnp.full((1, LANES), -3e38, f32), unroll=4)
    best = jnp.maximum(best, other_half(best))
    rowsum[...] = jnp.zeros(rowsum.shape, f32)
    colsum[...] = jnp.zeros(colsum.shape, f32)

    def second_pass(s, carry):
        total, found = carry
        block, held = s // STEPS_HELD, lax.rem(s, STEPS_HELD)
        deviation = own_dot(fa[block], mixrow[held][:, LANES:], 1, 0)
        weights = jnp.exp(sl[s] - best)
        total = total + jnp.sum(weights, axis=0, keepdims=True)
        return total, found, weights * deviation

    total, found = in_groups(
        second_pass, 0, steps, (jnp.zeros((1, LANES), f32), jnp.zeros((8, LANES), f32))
    )
    total = total + other_half(total)
    log_total = best + jnp.log(total)
    plain_mixed = pixel_sums(found, 1.0 / total)
    wide1 = lax.broadcasted_iota(jnp.int32, (rows, WIDE), 1)
    mixed_low = narrow(jnp.where(wide1 == 2 * LANES + 5, 1.0, plain_mixed * gin + bin_))
    xsmall[0, core, quad] = mixed_low
    x_spread(xsmall.at[0, core, quad], 8)
    relay_x(0)
    relay_x(6)
    attended = own_dot(mixed_low, win[1], 1, 0)
    act[ATT] = attended
    attended_low = narrow(attended)
    loads[CO].wait()
    times(attended_low, CO, tmp)
    first = lat + tmp[...] + bc[4:5]
    act[FIRST] = first
    normed_c = norm_forward(first, gc[1:2], bc[1:2])
    xbuf[1, core, quad] = normed_c
    loads[C1].wait()
    times(normed_c, C1, tmp)
    pre = tmp[...] + bc[5:6]
    act[PRE_C] = pre
    hidden_c = narrow(gelu_value(pre))
    loads[C2].wait()
    times(hidden_c, C2, tmp)
    second = act[FIRST] + tmp[...] + bc[6:7]
    act[SECOND] = second
    normed_t = norm_forward(second, gs[0:1], bs[0:1])
    xbuf[4, core, quad] = normed_t
    mine = core * quads + quad

    def block_of(peer):
        return lax.rem(peer, 2) * quads + peer // 2

    def to_heads(kind, values):
        gsrc[9 + kind] = values

        def one(step, carry):
            peer, where = to_plane(step)
            push(
                gsrc.at[9 + kind, :, lanes_of(peer)], heads.at[kind, mine],
                a_send.at[4 + kind], a_recv.at[4 + kind], where,
            )
            return carry

        lax.fori_loop(1, grid_cols, one, 0)
        heads[kind, mine] = gsrc[9 + kind, :, lanes_of(j)]

    loads[SQ].wait()
    times(normed_t, SQ, tmp)
    to_heads(0, narrow(tmp[...] + bs[2:3]))
    loads[SK].wait()
    times(normed_t, SK, tmp)
    to_heads(1, narrow(tmp[...]))
    loads[SV].wait()
    times(normed_t, SV, tmp)
    to_heads(2, narrow(tmp[...] + bs[3:4]))
    background(0)
    loads[S2].wait()
    times_t(cot_low, S2, act.at[COT_BACK])
    x_relay(xsmall.at[0, core], 8)
    head_rows = grid_cols * rows
    per = 128
    each = per // rows

    for kind in range(3):
        wait_for(heads.at[kind, pl.ds(0, grid_cols - 1)], a_recv.at[4 + kind])

    def head_of(kind):
        return heads[kind].reshape(head_rows, chunk)

    def head_part(kind, n):
        return heads[kind, pl.ds(n * each, each)].reshape(per, chunk)

    def head_forward(n, carry):
        at = pl.ds(pl.multiple_of(n * per, per), per)
        scores = own_dot(head_part(0, n), head_of(1), 1, 1) * head_scale
        weights = jnp.exp(scores - jnp.max(scores, axis=1, keepdims=True))
        found_probs = weights / jnp.sum(weights, axis=1, keepdims=True)
        probs[at, :] = found_probs
        probs_low = narrow(found_probs)
        prob_grad[1, at, :] = probs_low
        mix_s[pl.ds(n * each, each)] = narrow(own_dot(probs_low, head_of(2), 1, 0)).reshape(each, rows, chunk)
        return carry

    lax.fori_loop(0, head_rows // per, head_forward, 0, unroll=2)

    def send_mixed(step, carry):
        peer, where = to_plane(step)
        push(mix_s.at[block_of(peer)], mix_b.at[:, lanes_of(j)], a_send.at[0], a_recv.at[0], where)
        return carry

    lax.fori_loop(1, grid_cols, send_mixed, 0)
    background(1)
    mix_b[:, lanes_of(j)] = mix_s[mine]
    loads[SO].wait()
    wait_for(mix_b.at[:, pl.ds(0, chunk * (grid_cols - 1))], a_recv.at[0])
    mixed_rows = mix_b[...]
    xbuf[3, core, quad] = mixed_rows
    times(mixed_rows, SO, tmp)
    relay_x(4)
    third = act[SECOND] + tmp[...] + bs[4:5]
    act[THIRD] = third
    normed_s = norm_forward(third, gs[1:2], bs[1:2])
    xbuf[5, core, quad] = normed_s
    background(2)
    loads[S1].wait()
    times(normed_s, S1, tmp)
    pre = tmp[...] + bs[5:6]
    act[PRE_S] = pre
    hidden_s = narrow(gelu_value(pre))
    spread_plain(5, hidden_s)
    background(3)
    times(hidden_s, S2, tmp)
    new_latents[...] = narrow(act[THIRD] + tmp[...] + bs[6:7])

    d_pre = act[COT_BACK] * gelu_slope(act[PRE_S])
    pre_low = narrow(d_pre)
    times_t(pre_low, S1, tmp)
    d_rows, lnvec[6:7, :], lnvec[7:8, :] = norm_gradient(act[THIRD], gs[1:2], tmp[...])
    gradient = to_float(cot_low) + d_rows
    act[GRAD] = gradient
    out_low = narrow(gradient)
    times_t(out_low, SO, tmp)
    mix_b2 = narrow(tmp[...])
    gsrc[12] = mix_b2

    def send_dmixed(step, carry):
        peer, where = to_plane(step)
        push(gsrc.at[12, :, lanes_of(peer)], dmix_b.at[mine], a_send.at[1], a_recv.at[1], where)
        return carry

    lax.fori_loop(1, grid_cols, send_dmixed, 0)
    dmix_b[mine] = gsrc[12, :, lanes_of(j)]
    background(4)
    spread_g(4, pre_low)
    have_x(6)
    weight_part(8, have_g(5), xbuf.at[6])
    spread_g(6, out_low)
    background(5)
    wait_for(dmix_b.at[pl.ds(0, grid_cols - 1)], a_recv.at[1])

    def from_heads(kind):
        def one(step, carry):
            peer, where = to_plane(step)
            push(
                dqkv_s.at[kind, block_of(peer)], dqkv_b.at[kind, :, lanes_of(j)],
                a_send.at[7 + kind], a_recv.at[7 + kind], where,
            )
            return carry

        lax.fori_loop(1, grid_cols, one, 0)
        dqkv_b[kind, :, lanes_of(j)] = dqkv_s[kind, mine]

    def rows_back(kind):
        wait_for(dqkv_b.at[kind, :, pl.ds(0, chunk * (grid_cols - 1))], a_recv.at[7 + kind])
        wait_for(heads.at[kind, pl.ds(0, grid_cols - 1)], a_send.at[4 + kind])
        spread_g(9 + kind, dqkv_b[kind])

    def put_head(kind, n, values):
        dqkv_s[kind, pl.ds(n * each, each)] = narrow(values).reshape(each, rows, chunk)

    d_mixed_all = dmix_b[...].reshape(head_rows, chunk)

    def head_values(n, carry):
        at = pl.ds(pl.multiple_of(n * per, per), per)
        put_head(2, n, own_dot(prob_grad[1, :, at], d_mixed_all, 0, 0))
        return carry

    def head_queries(n, carry):
        at = pl.ds(pl.multiple_of(n * per, per), per)
        d_mixed = dmix_b[pl.ds(n * each, each)].reshape(per, chunk)
        d_probs = own_dot(d_mixed, head_of(2), 1, 1)
        found_probs = probs[at, :]
        d_scores = found_probs * (d_probs - jnp.sum(found_probs * d_probs, axis=1, keepdims=True))
        d_low = narrow(d_scores * head_scale)
        prob_grad[0, at, :] = d_low
        put_head(0, n, own_dot(d_low, head_of(1), 1, 0))
        return carry

    def head_keys(n, carry):
        at = pl.ds(pl.multiple_of(n * per, per), per)
        put_head(1, n, own_dot(prob_grad[0, :, at], head_of(0), 0, 0))
        return carry

    lax.fori_loop(0, head_rows // per, head_values, 0, unroll=2)
    from_heads(2)
    background(6)
    join_rows(staged.at[slot_of(8)], 8)
    lax.fori_loop(0, head_rows // per, head_queries, 0, unroll=2)
    from_heads(0)
    background(7)
    relay_x(5)
    lax.fori_loop(0, head_rows // per, head_keys, 0, unroll=2)
    from_heads(1)
    background(8)
    relay_x(1)

    def column_sum(values):
        return jnp.sum(to_float(values), axis=0, keepdims=True)

    have_x(5)
    right = have_g(4)
    bias_s5 = column_sum(right)
    weight_part(7, right, xbuf.at[5])
    rows_back(2)
    times_t(dqkv_b[2], SV, tmp)
    rows_back(0)
    times_t(dqkv_b[0], SQ, tmp, True)
    have_x(1)
    recompute(1, 2, C1, biases.at[5:6])
    rows_back(1)
    times_t(dqkv_b[1], SK, tmp, True)
    background(9)
    d_rows, lnvec[4:5, :], lnvec[5:6, :] = norm_gradient(act[SECOND], gs[0:1], tmp[...])
    gradient = act[GRAD] + d_rows
    act[GRAD] = gradient
    second_low = narrow(gradient)
    spread_g(2, second_low)
    background(10)
    times_t(second_low, C2, tmp)
    d_pre = tmp[...] * gelu_slope(act[PRE_C])
    pre_low = narrow(d_pre)
    spread_g(1, pre_low)
    background(11)
    join(7)
    relay_x(3)
    times_t(pre_low, C1, tmp)
    d_rows, lnvec[2:3, :], lnvec[3:4, :] = norm_gradient(act[FIRST], gc[1:2], tmp[...])
    gradient = act[GRAD] + d_rows
    act[GRAD] = gradient
    out_low = narrow(gradient)
    spread_g(3, out_low)
    times_t(out_low, CO, tmp)
    d_attended = narrow(tmp[...])
    spread_g(8, d_attended)

    have_x(3)
    right = have_g(6)
    bias_s4 = column_sum(right)
    weight_part(9, right, xbuf.at[3])
    have_x(4)
    for k in (2, 0, 1):
        right = have_g(9 + k)
        if k == 0:
            bias_s2 = column_sum(right)
        elif k == 2:
            bias_s3 = column_sum(right)
        weight_part(4 + k, right, xbuf.at[4])

    grad_inputs = own_dot(d_attended, win[1], 1, 1)
    d_attended = to_float(d_attended)
    shift = grad_inputs[:, 2 * LANES + 5 : 2 * LANES + 6]
    row_delta = jnp.sum(d_attended * act[ATT], axis=1, keepdims=True) - shift
    grad_shift = jnp.sum(grad_inputs * bin_, axis=1, keepdims=True)
    grad_scaled = grad_inputs * gin
    turned = coefficients(grad_scaled, grad_shift - row_delta)
    constant = turned[6:7]

    def away(scaled):
        values = scaled[:, 2 * LANES :] - jnp.sum(scaled, axis=1, keepdims=True) * (1.0 / count)
        values = jnp.where(lane1 < 3, values, 0.0)
        return jnp.concatenate([values, pltpu.roll(values, 8, 1)], axis=0)

    query_away, grad_away = away(query_scaled), away(grad_scaled)
    wide_lane = lax.broadcasted_iota(jnp.int32, (LANES, LANES), 1)
    wide_half = lax.broadcasted_iota(jnp.int32, (LANES, LANES), 0) // rows
    blank = jnp.zeros((LANES, LANES), bf16)
    for held in range(STEPS_HELD):
        group = wide_lane - held * 16 - wide_half * 8
        along = narrow(jnp.where((group >= 0) & (group < 3), 1.0, 0.0))
        colors_here = [query_away, grad_away]
        if held:
            colors_here = [pltpu.roll(v, held * 16, 1) for v in colors_here]
        cgright[held // 2, (held % 2) * WIDE : (held % 2 + 1) * WIDE, :] = jnp.concatenate(
            [
                jnp.concatenate([narrow(colors_here[0]), blank], axis=1),
                jnp.concatenate([narrow(colors_here[1]), blank], axis=1),
                jnp.concatenate([blank, along], axis=1),
            ],
            axis=0,
        )
    rowsum[...] = jnp.zeros(rowsum.shape, f32)
    colsum[...] = jnp.zeros(colsum.shape, f32)

    def kept_at(s):
        place_now = lax.rem(s, 6)
        line = pl.ds(pl.multiple_of((place_now // 2) * tall, 32), tall)
        lane = pl.ds(pl.multiple_of(lax.rem(place_now, 2) * WIDE, LANES), WIDE)
        return wts.at[1 + s // 6, line, lane]

    def back_pass(s, carry):
        total, found = carry
        lines, deviation = step_lines(s)
        scores = sl[s]
        found_probs = jnp.exp(scores - log_total)
        d_scores = found_probs * (lines + constant)
        kept_at(s)[...] = jnp.concatenate(
            [narrow(d_scores), narrow(found_probs), narrow(d_scores * scores + found_probs * lines)], axis=1
        )
        total = total + jnp.sum(d_scores, axis=0, keepdims=True)
        return total, found, d_scores * deviation

    def color_block(block):
        result = None
        for pair in range(block * STEPS_HELD // 2, min((block + 1) * STEPS_HELD, steps) // 2):
            line = pl.ds((pair % 3) * tall, tall)
            left = wts[1 + pair // 3, line, pl.ds(0, 2 * WIDE)]
            part = own_dot(left, cgright[pair % (STEPS_HELD // 2)], 1, 0)
            result = part if result is None else result + part
        cgacc[block] = result

    carry = (jnp.zeros((1, LANES), f32), jnp.zeros((8, LANES), f32))
    third_of = steps // 3
    carry = in_groups(back_pass, 0, third_of, carry)
    finish_rows(8)
    join(9)
    right = have_g(2)
    bias_c6 = column_sum(right)
    weight_part(2, right, xbuf.at[2])
    right = have_g(1)
    bias_c5 = column_sum(right)
    weight_part(1, right, xbuf.at[1])
    carry = in_groups(back_pass, third_of, 2 * third_of, carry)
    join(6)
    join(4)
    x_arrived(xsmall.at[0, 1 - core], 8)
    right = have_g(3)
    bias_c4 = column_sum(right)
    small_part(2, right, xsmall.at[0])
    right = have_g(8)
    bias_c3 = column_sum(right)
    small_part(1, right, xsmall.at[0])
    total, found = in_groups(back_pass, 2 * third_of, steps, carry)
    plain_scores = pixel_sums(found, 1.0) * score_scale
    total = total * score_scale
    score_total = fold(jnp.transpose(jnp.concatenate([total, jnp.zeros((LANES - 1, LANES), f32)], axis=0)))[:, 0:1]
    score_low = narrow(plain_scores * gin + score_total * bin_)
    xsmall[1, core, quad] = score_low
    x_spread(xsmall.at[1, core, quad], 9)

    def d_query_part(n, carry):
        at = pl.ds(pl.multiple_of(n * 256, 256), 256)
        tmp[:, at] = own_dot(score_low, win[0, :, at], 1, 0)
        return carry

    lax.fori_loop(0, width // 256, d_query_part, 0)
    query_grad_low = narrow(tmp[...])
    spread_g(0, query_grad_low)
    gain_part = jnp.sum(query_inputs * plain_scores + grad_inputs * plain_mixed, axis=0, keepdims=True)
    bias_part = jnp.sum(query_inputs * score_total + grad_inputs, axis=0, keepdims=True)
    cuts = [part[:, k * LANES : (k + 1) * LANES] for part in (gain_part, bias_part) for k in range(3)]
    shared = jnp.concatenate(cuts + [jnp.zeros((1, LANES), f32)], axis=0)
    times_t(query_grad_low, CQ, tmp)
    d_rows, lnvec[0:1, :], lnvec[1:2, :] = norm_gradient(to_float(latents[...]), gc[0:1], tmp[...])
    latent_grad[...] = act[GRAD] + d_rows
    lnvec[8:9, :] = jnp.sum(to_float(cotangent[...]), axis=0, keepdims=True)
    lines = regroup(lnvec[...])
    for peer in range(grid_cols):
        lnsend[peer] = jnp.concatenate([lines[:9, peer * chunk : (peer + 1) * chunk], shared], axis=0)

    def send_ln(step, carry):
        peer, where = to_plane(step)
        push(lnsend.at[peer], lnbuf.at[j], misc_send.at[2], misc_recv.at[2], where)
        return carry

    lax.fori_loop(1, grid_cols, send_ln, 0)
    lnbuf[j] = lnsend[j]
    join(5)
    for block in range(0, blocks // 2):
        color_block(block)
    x_relay(xsmall.at[1, core], 9)
    have_x(0)
    right = have_g(0)
    bias_c2 = column_sum(right)
    weight_part(0, right, xbuf.at[0])
    for block in range(blocks // 2, blocks - 1):
        color_block(block)
    x_arrived(xsmall.at[1, 1 - core], 9)
    small_part(0, have_g(7), xsmall.at[1])
    join(2)
    color_block(blocks - 1)
    join(1)
    for m in (2, 1):
        join_small(m)

    for block in range(blocks):
        both = own_dot(fa[block], spread[...], 1, 0)
        center, factor = both[:, :LANES], both[:, LANES:]
        here = cgacc[block]
        cgacc[block, :, :LANES] = factor * (
            here[:, :LANES] - (to_float(fa[block]) - center) * factor * here[:, LANES:] * (1.0 / count)
        )
    for part in range(grid_rows):
        at = pl.ds(part * tile_rows, tile_rows)
        lines = jnp.concatenate([narrow(cgacc[block, at, :LANES]) for block in range(blocks)], axis=1)
        tiles = narrow(own_dot(back[...], lines, 1, 1))
        for tile in range(grid_cols):
            cgsend[tile, part, :, :tile_rows] = tiles[tile * 32 : tile * 32 + 32]
    cgbuf[j] = cgsend[j]

    def send_cg(step, carry):
        peer, where = to_plane(step)
        push(cgsend.at[peer], cgbuf.at[j], misc_send.at[3], misc_recv.at[3], where)
        return carry

    lax.fori_loop(1, grid_cols, send_cg, 0)

    wait_for(lnbuf.at[pl.ds(0, grid_cols - 1)], misc_recv.at[2])
    norms = lnbuf[0]
    for peer in range(1, grid_cols):
        norms = norms + lnbuf[peer]
    vecsend[...] = jnp.concatenate(
        [
            norms[:8], bias_c2, bias_c3, bias_c4, bias_c5, bias_c6, bias_s2, bias_s3,
            bias_s4, bias_s5, norms[8:9], jnp.zeros((6, chunk), f32), norms[9:], jnp.zeros((1, chunk), f32),
        ],
        axis=0,
    )

    def send_vec(step, carry):
        where = {"rows": lax.rem(z + step, grid_rows)}
        push(vecsend, vecbuf.at[z], misc_send.at[4], misc_recv.at[4], where)
        return carry

    lax.fori_loop(1, grid_rows, send_vec, 0)
    vecbuf[z] = vecsend[...]
    join(0)
    join_small(0)
    wait_for(cgbuf.at[pl.ds(0, grid_cols - 1)], misc_recv.at[3])
    tiles = to_float(cgbuf[0])
    for peer in range(1, grid_cols):
        tiles = tiles + to_float(cgbuf[peer])
    cgsum[...] = tiles

    def send_tile(step, carry):
        part = lax.rem(z + step, grid_rows)
        push(cgsum.at[part], cgfin.at[z], misc_send.at[6], misc_recv.at[6], {"rows": part})
        return carry

    lax.fori_loop(1, grid_rows, send_tile, 0)
    cgfin[z] = cgsum[z]

    wait_for(vecbuf.at[pl.ds(0, grid_rows - 1)], misc_recv.at[4])
    vectors = vecbuf[0]
    for part in range(1, grid_rows):
        vectors = vectors + vecbuf[part]
    vector_out[...] = vectors[:24]
    input_vector_out[...] = vectors[24:]
    for m in (7, 4, 5, 6, 9, 2, 1, 0):
        wait_for(crossed.at[slot_of(m)], f_recv.at[m])
        result = kept_of(m)[...] + to_float(crossed[slot_of(m)])
        kept_of(m)[...] = result
    wait_for(row_done.at[:, pl.ds(0, chunk * (grid_cols - 1))], a_recv.at[3])
    self_total[4] = row_done[...]
    sums = []
    for m in (2, 1, 0):
        wait_for(crossed_small.at[m], f_recv.at[10 + m])
        sums.append(kept_small[m] + to_float(crossed_small[m]))
    out_total[...] = own_dot(narrow(sums[0]), win[1], 1, 0)
    input_parts[1] = sums[1]
    input_parts[0] = sums[2]
    wait_for(cgfin.at[pl.ds(0, grid_rows - 1)], misc_recv.at[6])
    color_out[...] = cgfin[...]

    for k in (0, 1, 3, 4, 5, 6):
        wait_for(xbuf.at[k, 0, pl.ds(0, quads - 1)], x_send.at[k])
        wait_for(xbuf.at[k, 0], y_send.at[k])
    for k in range(2):
        wait_for(xsmall.at[k, 0, pl.ds(0, quads - 1)], x_send.at[8 + k])
        wait_for(xsmall.at[k, 0], y_send.at[8 + k])
    for k in range(12):
        wait_for(gsrc.at[k, :, pl.ds(0, chunk * (grid_cols - 1))], g_send.at[k])
    wait_for(mix_s.at[pl.ds(0, grid_cols - 1)], a_send.at[0])
    wait_for(dmix_b.at[pl.ds(0, grid_cols - 1)], a_send.at[1])
    for kind in range(3):
        wait_for(dqkv_s.at[kind, pl.ds(0, grid_cols - 1)], a_send.at[7 + kind])
    wait_for(colbuf.at[pl.ds(0, grid_cols - 1)], misc_send.at[0])
    wait_for(row_turned.at[pl.ds(0, own * (grid_cols - 1))], a_send.at[3])
    wait_for(lnbuf.at[pl.ds(0, grid_cols - 1)], misc_send.at[2])
    wait_for(cgbuf.at[pl.ds(0, grid_cols - 1)], misc_send.at[3])
    wait_for(colstage.at[pl.ds(0, grid_rows - 1)], misc_send.at[5])
    wait_for(cgfin.at[pl.ds(0, grid_rows - 1)], misc_send.at[6])
    wait_for(row_pair, r_send.at[8])
    wait_for(row_hand, f_send.at[8])
    for m in (0, 1, 2, 4, 5, 6, 7, 9):
        wait_for(paired.at[slot_of(m)], r_send.at[m])
        wait_for(handed.at[slot_of(m)], f_send.at[m])
    for m in range(3):
        wait_for(paired_small.at[m], r_send.at[10 + m])
        wait_for(handed_small.at[m], f_send.at[10 + m])
    wait_for(vecbuf.at[pl.ds(0, grid_rows - 1)], misc_send.at[4])


def channel_order(count):
    n = NBANDS
    starts = ((5, n), (5 + 2 * n, n), (5 + n, n), (5 + 3 * n, n), (0, 5))
    order = np.concatenate([np.arange(start, start + size) for start, size in starts])
    result = np.zeros((WIDE, count), np.float32)
    result[np.arange(count), order] = 1
    return np.asarray(result, ml_dtypes.bfloat16)


def by_channel(lines):
    n = NBANDS
    parts = [lines[..., 4 * n : 4 * n + 5], lines[..., :n], lines[..., 2 * n : 3 * n]]
    parts += [lines[..., n : 2 * n], lines[..., 3 * n : 4 * n]]
    return jnp.concatenate(parts, axis=-1)


def finish_kernel(
    own, tile_rows, tile_cols,
    latents, latent_grad, colors, cross, out, self_parts, self_out, inputs, vectors, input_vectors,
    prior_cross, prior_out, prior_input,
    o_latents, o_latent_grad, o_colors, o_cross, o_out, o_input, o_gain, o_bias,
    o_cross_gains, o_cross_biases, o_self, o_self_out, o_self_gains, o_self_biases,
):
    o_latents[...] = latents[...]
    o_latent_grad[...] = latent_grad[...]
    for channel in range(3):
        for col in range(tile_cols):
            line = channel * tile_cols + col
            for image in range(colors.shape[0]):
                o_colors[channel, col, image : image + 1, :] = colors[image, line : line + 1, :tile_rows]
    o_cross[...] = prior_cross[...] + cross[...]
    o_out[...] = prior_out[...] + out[...]
    o_self[...] = self_parts[...]
    o_self_out[...] = self_out[...]
    for k in range(2):
        o_input[k] = prior_input[k] + by_channel(inputs[k])
    lines = input_vectors[...]
    for k, target in enumerate((o_gain, o_bias)):
        wide = jnp.concatenate([lines[3 * k + t : 3 * k + t + 1] for t in range(3)], axis=1)
        target[...] = by_channel(wide).reshape(-1)
    place = lax.axis_index("rows")
    width = vectors.shape[1]
    mine = pltpu.roll(vectors[...], lax.rem(width - place * own, width), 1)[:, :own]
    for target, rows in (
        (o_cross_gains, (0, 2)),
        (o_cross_biases, (1, 3, 8, 9, 10, 11, 12)),
        (o_self_gains, (4, 6)),
        (o_self_biases, (5, 7, 13, 14, 15, 16, 17)),
    ):
        for k, row in enumerate(rows):
            target[k : k + 1, :] = mine[row : row + 1]


def local_kernel(
    latents,
    pixel_colors,
    image_boxes,
    cotangent,
    cross_matrices,
    cross_out,
    input_matrices,
    in_gain,
    in_bias,
    cross_gains,
    cross_biases,
    self_matrices,
    self_out,
    self_gains,
    self_biases,
    prior_cross_matrices,
    prior_cross_out,
    prior_input_matrices,
):
    rows, width = latents.shape
    channels, image_count, tile_rows, tile_cols = pixel_colors.shape
    grid_rows = lax.axis_size("rows")
    grid_cols = lax.axis_size("cols")
    n_dev = grid_rows * grid_cols
    tall, wide = grid_rows * tile_rows, grid_cols * tile_cols
    steps = wide // 2
    chunk = width // grid_cols
    own = chunk // grid_rows
    quads = grid_cols // 2
    place, pick, spread, back = selections(tile_cols, grid_cols, steps)
    blocks = back.shape[1] // LANES
    held_rows = -(-steps // 8) * 8
    order = channel_order(input_matrices.shape[1])
    f32, bf16 = jnp.float32, jnp.bfloat16
    vmem = pl.BlockSpec(memory_space=pltpu.VMEM)
    away = pl.BlockSpec(memory_space=pl.ANY)
    shape = jax.ShapeDtypeStruct
    sizes = (grid_rows, grid_cols, rows, steps, tile_rows, tile_cols)
    dma = pltpu.SemaphoreType.DMA
    scratch = [
        ((10, width, width), bf16),
        ((2, WIDE, width), bf16),
        (input_matrices.shape, bf16),
        ((7, 2, quads, rows, width), bf16),
        ((2, 2, quads, rows, WIDE), bf16),
        ((13, rows, width), bf16),
        ((12, 2, quads, rows, chunk), bf16),
        ((9, chunk, width), bf16),
        ((9, 2, own, width), bf16),
        ((9, own, width), bf16),
        ((9, own, width), bf16),
        ((3, chunk, WIDE), bf16),
        ((3, 2, own, WIDE), bf16),
        ((3, own, WIDE), bf16),
        ((3, own, WIDE), bf16),
        ((3, own, WIDE), f32),
        ((2, chunk, width // grid_rows), bf16),
        ((chunk, width // grid_rows), bf16),
        ((chunk, width // grid_rows), bf16),
        ((chunk, width // grid_rows), f32),
        ((width // grid_rows, chunk), f32),
        ((own, width), f32),
        ((8, width), f32),
        ((grid_rows, 32, LANES), f32),
        ((grid_rows, 32, LANES), bf16),
        ((grid_rows, 32, LANES), bf16),
        ((grid_cols, grid_rows, 32, LANES), bf16),
        ((tall, WIDE), f32),
        ((tall, 7 * LANES), bf16),
        ((blocks, tall, LANES), bf16),
        ((blocks * LANES, tall), bf16),
        ((steps, tall, LANES), f32),
        ((tall, LANES), f32),
        ((held_rows, LANES), f32),
        ((tall, 2 * LANES), bf16),
        ((2, held_rows, 2 * LANES), bf16),
        ((STEPS_HELD, LANES, 2 * LANES), bf16),
        ((STEPS_HELD // 2, 2 * WIDE, 2 * LANES), bf16),
        ((tall, LANES), f32),
        ((held_rows, LANES), f32),
        ((blocks, tall, 2 * LANES), f32),
        ((grid_cols, grid_rows, 32, LANES), bf16),
        ((grid_cols, grid_rows, 32, LANES), bf16),
        ((grid_rows, 32, LANES), f32),
        ((grid_rows, 32, LANES), f32),
        ((9, rows, width), f32),
        ((16, width), f32),
        ((grid_cols, 16, chunk), f32),
        ((grid_cols, 16, chunk), f32),
        ((8, width), f32),
        ((32, chunk), f32),
        ((grid_rows, 32, chunk), f32),
        ((3, grid_cols, rows, chunk), bf16),
        ((grid_cols * rows, grid_cols * rows), f32),
        ((2, grid_cols * rows, grid_cols * rows), bf16),
        ((grid_cols, rows, chunk), bf16),
        ((rows, width), bf16),
        ((grid_cols, rows, chunk), bf16),
        ((3, grid_cols, rows, chunk), bf16),
        ((3, rows, width), bf16),
    ]
    scratch = [pltpu.VMEM(dims, kind) for dims, kind in scratch]
    scratch += [dma((count,)) for count in (11, 10, 10, 10, 10, 12, 12, 10, 10, 13, 13, 13, 13, 7, 7)]
    outs = [
        ((rows, width), bf16),
        ((rows, width), f32),
        ((image_count, 32, LANES), f32),
        ((3, own, width), f32),
        ((own, width), f32),
        ((5, own, width), f32),
        ((own, width), f32),
        ((2, own, WIDE), f32),
        ((24, chunk), f32),
        ((8, LANES), f32),
    ]
    results = pl.pallas_call(
        functools.partial(layer_kernel, sizes),
        out_shape=[shape(dims, kind) for dims, kind in outs],
        in_specs=[pl.BlockSpec(memory_space=pltpu.SMEM)] + [vmem] * 14 + [away] * 5,
        out_specs=[vmem] * len(outs),
        scratch_shapes=scratch,
        compiler_params=pltpu.CompilerParams(
            collective_id=0, has_side_effects=True, vmem_limit_bytes=VMEM_BYTES
        ),
        cost_estimate=pl.CostEstimate(
            flops=20_000_000_000, bytes_accessed=40_000_000, transcendentals=4_000_000
        ),
    )(
        image_boxes,
        latents,
        cotangent,
        jnp.transpose(pixel_colors, (0, 3, 1, 2)),
        in_gain,
        in_bias,
        order,
        cross_gains,
        cross_biases,
        self_gains,
        self_biases,
        place,
        pick,
        spread,
        back,
        cross_matrices,
        cross_out,
        self_matrices,
        self_out,
        input_matrices,
    )
    count = input_matrices.shape[1]
    last = [
        ((rows, width), bf16),
        ((rows, width), f32),
        ((channels, tile_cols, image_count, tile_rows), f32),
        ((3, own, width), f32),
        ((own, width), f32),
        ((2, own, count), f32),
        ((count,), f32),
        ((count,), f32),
        ((2, own), f32),
        ((7, own), f32),
        ((5, own, width), f32),
        ((own, width), f32),
        ((2, own), f32),
        ((7, own), f32),
    ]
    done = pl.pallas_call(
        functools.partial(finish_kernel, own, tile_rows, tile_cols),
        out_shape=[shape(dims, kind) for dims, kind in last],
        in_specs=[vmem] * (len(outs) + 3),
        out_specs=[vmem] * len(last),
        compiler_params=pltpu.CompilerParams(vmem_limit_bytes=VMEM_BYTES),
    )(
        *results,
        jnp.transpose(prior_cross_matrices, (0, 2, 1)),
        jnp.transpose(prior_cross_out),
        jnp.transpose(prior_input_matrices, (0, 2, 1)),
    )
    (new_latents, latent_grad, colors, cross_total, out_total, input_total, gain, bias) = done[:8]
    cross_gain, cross_bias, self_total, self_out_total, self_gain, self_bias = done[8:]
    return (
        new_latents,
        latent_grad,
        jnp.transpose(colors, (0, 2, 3, 1)),
        jnp.transpose(cross_total, (0, 2, 1)),
        jnp.transpose(out_total),
        jnp.transpose(input_total, (0, 2, 1)),
        gain,
        bias,
        cross_gain,
        cross_bias,
        jnp.transpose(self_total, (0, 2, 1)),
        jnp.transpose(self_out_total),
        self_gain,
        self_bias,
    )


def solution(mesh):
    placed = (
        P(("rows", "cols"), None),
        P(None, None, "rows", "cols"),
        P(),
        P(("rows", "cols"), None),
        P(),
        P(),
        P(),
        P(),
        P(),
        P(),
        P(),
        P(),
        P(),
        P(),
        P(),
        P(None, None, ("rows", "cols")),
        P(None, ("rows", "cols")),
        P(None, None, ("rows", "cols")),
    )
    one_head_each = mesh.shape["cols"] == HEADS
    return jax.shard_map(
        local_kernel if one_head_each else local,
        mesh=mesh,
        in_specs=placed,
        out_specs=(
            P(("rows", "cols"), None),
            P(("rows", "cols"), None),
            P(None, None, "rows", "cols"),
            P(None, None, ("rows", "cols")),
            P(None, ("rows", "cols")),
            P(None, None, ("rows", "cols")),
            P(),
            P(),
            P(None, ("rows", "cols")),
            P(None, ("rows", "cols")),
            P(None, None, ("rows", "cols")),
            P(None, ("rows", "cols")),
            P(None, ("rows", "cols")),
            P(None, ("rows", "cols")),
        ),
        check_vma=False,
    )
```

```python
import functools

import jax
import jax.numpy as jnp
import ml_dtypes
import numpy as np
from jax import lax
from jax.experimental import pallas as pl
from jax.experimental.pallas import tpu as pltpu
from jax.sharding import PartitionSpec as P

HEADS = 8
LATENTS = 512
NBANDS = 64
HEAD_DIM = 128


EPS = 1e-05
NEG = -1e30
FREQ_TOP = 112.0
VMEM_BYTES = 63 * 1024 * 1024
PLAN = {0: ((4, 4),), 2: ((3, 4),), 5: ((5, 1),), 6: ((5, 1),), 9: ((5, 2),)}


def narrow(values):
    return values.astype(jnp.bfloat16)


def to_float(values):
    return values.astype(jnp.float32)


def matmul(former, latter):
    return jnp.dot(former, latter, preferred_element_type=jnp.float32)


def inner_left(former, latter):
    return lax.dot_general(
        former, latter, (((0,), (0,)), ((), ())), preferred_element_type=jnp.float32
    )


def inner_right(former, latter):
    return lax.dot_general(
        former, latter, (((1,), (1,)), ((), ())), preferred_element_type=jnp.float32
    )


def layer_norm(values, gain, offset):
    middle = jnp.mean(values, axis=-1, keepdims=True)
    centered = values - middle
    spread = jnp.mean(centered * centered, axis=-1, keepdims=True)
    return centered * lax.rsqrt(spread + EPS) * gain + offset


def norm_back(values, gain, offset, gradient):
    result, pullback = jax.vjp(layer_norm, values, gain, offset)
    return pullback(gradient)


def gelu_tanh(values):
    return jax.nn.gelu(values, approximate=True)


def gelu_back(pre_gelu, gradient):
    result, pullback = jax.vjp(gelu_tanh, pre_gelu)
    return pullback(gradient)[0]


def axis_features(places, extent):
    frequency = 1.0 + jnp.arange(NBANDS, dtype=jnp.float32) * ((FREQ_TOP - 1.0) / (NBANDS - 1))
    angle = jnp.pi * places[:, None] * frequency[None, :]
    return (places, jnp.sin(angle), jnp.cos(angle))


def canvas_of(colors, image_box):
    channels, wide, tall = colors.shape
    top, left, height, width = image_box[0], image_box[1], image_box[2], image_box[3]
    row_at = jnp.arange(tall, dtype=jnp.int32)
    col_at = jnp.arange(wide, dtype=jnp.int32)
    y_place = -1.0 + 2.0 * to_float(row_at - top) / to_float(height - 1)
    x_place = -1.0 + 2.0 * to_float(col_at - left) / to_float(width - 1)
    y_parts = axis_features(y_place, height)
    x_parts = axis_features(x_place, width)
    y_all = jnp.concatenate([y_parts[0][:, None], y_parts[1], y_parts[2]], axis=1)
    x_all = jnp.concatenate([x_parts[0][:, None], x_parts[1], x_parts[2]], axis=1)
    count = channels + 2 + 4 * NBANDS
    color_sum = jnp.sum(colors, axis=0)
    color_square = jnp.sum(colors * colors, axis=0)
    mean = (color_sum + jnp.sum(y_all, axis=1)[None, :] + jnp.sum(x_all, axis=1)[:, None]) / count
    square = (
        color_square
        + jnp.sum(y_all * y_all, axis=1)[None, :]
        + jnp.sum(x_all * x_all, axis=1)[:, None]
    ) / count
    deviation = lax.rsqrt(square - mean * mean + EPS)
    row_in = (row_at >= top) & (row_at < top + height)
    col_in = (col_at >= left) & (col_at < left + width)
    return (y_all, x_all, mean, deviation, row_in, col_in)


def split_channels(rows, channels):
    n = NBANDS
    c = channels
    y_part = jnp.concatenate(
        [rows[:, c : c + 1], rows[:, c + 2 : c + 2 + n], rows[:, c + 2 + 2 * n : c + 2 + 3 * n]],
        axis=1,
    )
    x_part = jnp.concatenate(
        [
            rows[:, c + 1 : c + 2],
            rows[:, c + 2 + n : c + 2 + 2 * n],
            rows[:, c + 2 + 3 * n : c + 2 + 4 * n],
        ],
        axis=1,
    )
    return (rows[:, :c], y_part, x_part)


def join_channels(color_part, y_part, x_part):
    n = NBANDS
    return jnp.concatenate(
        [
            color_part,
            y_part[:, :1],
            x_part[:, :1],
            y_part[:, 1 : n + 1],
            x_part[:, 1 : n + 1],
            y_part[:, n + 1 :],
            x_part[:, n + 1 :],
        ],
        axis=1,
    )


def against_pixels(rows, colors, canvas):
    y_all, x_all, mean, deviation = canvas[:4]
    color_part, y_part, x_part = split_channels(rows, colors.shape[0])
    by_row = inner_right(narrow(y_part), narrow(y_all))
    by_col = inner_right(narrow(x_part), narrow(x_all))
    total = by_row[:, None, :] + by_col[:, :, None]
    for j in range(colors.shape[0]):
        total = total + color_part[:, j][:, None, None] * colors[j][None]
    total = total - jnp.sum(rows, axis=1)[:, None, None] * mean[None]
    return total * deviation[None]


def over_pixels(weights, colors, canvas):
    y_all, x_all, mean, deviation = canvas[:4]
    scaled = weights * deviation[None]
    y_part = matmul(narrow(jnp.sum(scaled, axis=1)), narrow(y_all))
    x_part = matmul(narrow(jnp.sum(scaled, axis=2)), narrow(x_all))
    color_part = jnp.stack(
        [jnp.sum(scaled * colors[j][None], axis=(1, 2)) for j in range(colors.shape[0])], axis=1
    )
    middle = jnp.sum(scaled * mean[None], axis=(1, 2))
    return join_channels(color_part, y_part, x_part) - middle[:, None]


def mlp_forward(row_values, gain, offset, w_in, b_in, w_out, b_out):
    normed = narrow(layer_norm(row_values, gain, offset))
    pre_gelu = matmul(normed, w_in) + b_in
    hidden = narrow(gelu_tanh(pre_gelu))
    return (matmul(hidden, w_out) + b_out, (normed, pre_gelu, hidden))


def mlp_backward(row_values, gain, offset, w_in, w_out, stored, gradient):
    normed, pre_gelu, hidden = stored
    grad_low = narrow(gradient)
    d_w_out = inner_left(hidden, grad_low)
    d_b_out = jnp.sum(gradient, axis=0)
    d_pre = gelu_back(pre_gelu, inner_right(grad_low, w_out))
    pre_low = narrow(d_pre)
    d_w_in = inner_left(normed, pre_low)
    d_b_in = jnp.sum(d_pre, axis=0)
    d_rows, d_gain, d_offset = norm_back(row_values, gain, offset, inner_right(pre_low, w_in))
    return (
        gradient + d_rows,
        (d_w_in, d_w_out),
        (d_gain, d_offset, d_b_in, d_b_out),
        (pre_low, grad_low),
    )


def local(
    latents,
    pixel_colors,
    image_boxes,
    cotangent,
    cross_matrices,
    cross_out,
    input_matrices,
    in_gain,
    in_bias,
    cross_gains,
    cross_biases,
    self_matrices,
    self_out,
    self_gains,
    self_biases,
    prior_cross_matrices,
    prior_cross_out,
    prior_input_matrices,
):
    rows_dev = latents.shape[0]
    model_width = latents.shape[1]
    image_count = image_boxes.shape[0]
    tile_rows = pixel_colors.shape[2]
    tile_cols = pixel_colors.shape[3]
    input_width = input_matrices.shape[1]
    grid_rows = lax.axis_size("rows")
    grid_cols = lax.axis_size("cols")
    all_rows = rows_dev * grid_rows * grid_cols
    row_place = lax.axis_index("rows")
    col_place = lax.axis_index("cols")
    row_start = row_place * tile_rows
    col_start = col_place * tile_cols
    score_scale = model_width ** (-0.5)
    head_scale = HEAD_DIM ** (-0.5)
    g_cross = to_float(cross_gains)
    b_cross = to_float(cross_biases)
    g_self = to_float(self_gains)
    b_self = to_float(self_biases)
    g_input = to_float(in_gain)
    b_input = to_float(in_bias)
    latent_state = to_float(latents)
    normed_q = narrow(layer_norm(latent_state, g_cross[0], b_cross[0]))
    query_rows = narrow(matmul(normed_q, cross_matrices[0]) + b_cross[2])
    colors_low = lax.all_gather(pixel_colors, ("rows", "cols"), axis=0, tiled=False)
    colors_low = lax.dynamic_index_in_dim(colors_low, row_place, axis=2, keepdims=False)
    colors_low = colors_low.reshape(grid_rows, grid_cols, 3, tile_rows, tile_cols)
    colors = to_float(
        jnp.transpose(colors_low, (2, 1, 4, 0, 3)).reshape(
            3, grid_cols * tile_cols, grid_rows * tile_rows
        )
    )
    image_box = lax.dynamic_index_in_dim(image_boxes, row_place, axis=0, keepdims=False)
    canvas = canvas_of(colors, image_box)
    mean, deviation, row_in, col_in = canvas[2:]
    inside = (col_in[:, None] & row_in[None, :])[None]
    key_weight = input_matrices[0]
    value_weight = input_matrices[1]
    query_inputs = inner_right(query_rows, key_weight)
    query_lines = against_pixels(query_inputs * g_input, colors, canvas)
    query_shift = jnp.sum(query_inputs * b_input, axis=1)
    scores = jnp.where(
        inside, (query_lines + query_shift[:, None, None]) * score_scale, NEG
    )
    peak_score = jnp.max(scores, axis=(1, 2), keepdims=True)
    weights = jnp.where(inside, jnp.exp(scores - peak_score), 0.0)
    cross_probs = weights / jnp.sum(weights, axis=(1, 2), keepdims=True)
    plain_mixed = over_pixels(cross_probs, colors, canvas)
    mixed_inputs = (
        plain_mixed * g_input + jnp.sum(cross_probs, axis=(1, 2))[:, None] * b_input
    )
    mixed_low = narrow(mixed_inputs)
    attended = matmul(mixed_low, value_weight) + b_cross[3]
    attended_low = narrow(attended)
    first = latent_state + matmul(attended_low, cross_out) + b_cross[4]
    branch, cross_stored = mlp_forward(
        first, g_cross[1], b_cross[1], cross_matrices[1], b_cross[5], cross_matrices[2], b_cross[6]
    )
    second = first + branch
    normed_t = narrow(layer_norm(second, g_self[0], b_self[0]))
    tower_queries = narrow(matmul(normed_t, self_matrices[0]) + b_self[2])
    tower_keys = narrow(matmul(normed_t, self_matrices[1]))
    tower_values = narrow(matmul(normed_t, self_matrices[2]) + b_self[3])
    keys_group, values_group = (
        lax.all_gather(tower_keys, "cols", axis=0, tiled=True),
        lax.all_gather(tower_values, "cols", axis=0, tiled=True),
    )
    group_rows = keys_group.shape[0]
    query_image = (
        (row_place * grid_cols + col_place) * rows_dev + jnp.arange(rows_dev, dtype=jnp.int32)
    ) // LATENTS
    key_image = (row_place * group_rows + jnp.arange(group_rows, dtype=jnp.int32)) // LATENTS
    same_image = (query_image[:, None] == key_image[None, :])[None]
    query_heads = tower_queries.reshape(rows_dev, HEADS, HEAD_DIM)
    key_heads = keys_group.reshape(group_rows, HEADS, HEAD_DIM)
    value_heads = values_group.reshape(group_rows, HEADS, HEAD_DIM)
    head_scores = jnp.where(
        same_image,
        jnp.einsum("qhd,khd->hqk", query_heads, key_heads, preferred_element_type=jnp.float32)
        * head_scale,
        NEG,
    )
    head_weights = jnp.where(
        same_image, jnp.exp(head_scores - jnp.max(head_scores, axis=2, keepdims=True)), 0.0
    )
    head_probs = head_weights / jnp.sum(head_weights, axis=2, keepdims=True)
    probs_low = narrow(head_probs)
    tower_mixed = narrow(
        jnp.einsum(
            "hqk,khd->qhd", probs_low, value_heads, preferred_element_type=jnp.float32
        ).reshape(rows_dev, model_width)
    )
    third = second + matmul(tower_mixed, self_out) + b_self[4]
    branch, tower_stored = mlp_forward(
        third, g_self[1], b_self[1], self_matrices[3], b_self[5], self_matrices[4], b_self[6]
    )
    new_latents = narrow(third + branch)
    gradient = to_float(cotangent)
    gradient, tower_mlp_w, tower_mlp_v, tower_lows = mlp_backward(
        third, g_self[1], b_self[1], self_matrices[3], self_matrices[4], tower_stored, gradient
    )
    tower_out_low = narrow(gradient)
    d_self_out = inner_left(tower_mixed, tower_out_low)
    d_self_out_bias = jnp.sum(gradient, axis=0)
    d_mixed = narrow(inner_right(tower_out_low, self_out)).reshape(rows_dev, HEADS, HEAD_DIM)
    d_probs = jnp.einsum("qhd,khd->hqk", d_mixed, value_heads, preferred_element_type=jnp.float32)
    d_value_heads = jnp.einsum(
        "hqk,qhd->khd", probs_low, d_mixed, preferred_element_type=jnp.float32
    )
    d_scores = head_probs * (d_probs - jnp.sum(head_probs * d_probs, axis=2, keepdims=True))
    d_scores_low = narrow(d_scores * head_scale)
    d_query_heads = jnp.einsum(
        "hqk,khd->qhd", d_scores_low, key_heads, preferred_element_type=jnp.float32
    ).reshape(rows_dev, model_width)
    d_key_heads = jnp.einsum(
        "hqk,qhd->khd", d_scores_low, query_heads, preferred_element_type=jnp.float32
    )
    d_tower_keys, d_tower_values = (
        lax.psum_scatter(
            d_key_heads.reshape(group_rows, model_width).astype(jnp.bfloat16),
            "cols",
            scatter_dimension=0,
            tiled=True,
        ).astype(jnp.float32),
        lax.psum_scatter(
            d_value_heads.reshape(group_rows, model_width).astype(jnp.bfloat16),
            "cols",
            scatter_dimension=0,
            tiled=True,
        ).astype(jnp.float32),
    )
    tq_low = narrow(d_query_heads)
    tk_low = narrow(d_tower_keys)
    tv_low = narrow(d_tower_values)
    d_normed_t = (
        inner_right(tq_low, self_matrices[0])
        + inner_right(tk_low, self_matrices[1])
        + inner_right(tv_low, self_matrices[2])
    )
    d_second, d_self_gain, d_self_bias = norm_back(second, g_self[0], b_self[0], d_normed_t)
    gradient = gradient + d_second
    self_gain_grad = jnp.stack([d_self_gain, tower_mlp_v[0]])
    self_bias_grad = jnp.stack(
        [
            d_self_bias,
            tower_mlp_v[1],
            jnp.sum(d_query_heads, axis=0),
            jnp.sum(d_tower_values, axis=0),
            d_self_out_bias,
            tower_mlp_v[2],
            tower_mlp_v[3],
        ]
    )
    gradient, cross_mlp_w, cross_mlp_v, cross_lows = mlp_backward(
        first, g_cross[1], b_cross[1], cross_matrices[1], cross_matrices[2], cross_stored, gradient
    )
    cross_out_low = narrow(gradient)
    d_cross_out = inner_left(attended_low, cross_out_low)
    d_cross_out_bias = jnp.sum(gradient, axis=0)
    d_attended = narrow(inner_right(cross_out_low, cross_out))
    value_shift = jnp.sum(to_float(d_attended) * b_cross[3], axis=1)
    row_delta = jnp.sum(to_float(d_attended) * attended, axis=1) - value_shift
    grad_inputs = inner_right(d_attended, value_weight)
    grad_shift = jnp.sum(grad_inputs * b_input, axis=1)
    grad_lines = against_pixels(grad_inputs * g_input, colors, canvas)
    d_scores = (
        cross_probs * (grad_lines + (grad_shift - row_delta)[:, None, None]) * score_scale
    )
    plain_scores = over_pixels(d_scores, colors, canvas)
    score_sum = jnp.sum(d_scores, axis=(1, 2))
    prob_sum = jnp.sum(cross_probs, axis=(1, 2))
    score_inputs = plain_scores * g_input + score_sum[:, None] * b_input
    score_low = narrow(score_inputs)
    d_query_rows = matmul(score_low, key_weight)
    in_gain_part = jnp.sum(query_inputs * plain_scores + grad_inputs * plain_mixed, axis=0)
    in_bias_part = jnp.sum(
        query_inputs * score_sum[:, None] + grad_inputs * prob_sum[:, None], axis=0
    )
    query_scaled = query_inputs * g_input
    grad_scaled = grad_inputs * g_input
    query_away = query_scaled[:, :3] - jnp.mean(query_scaled, axis=1, keepdims=True)
    grad_away = grad_scaled[:, :3] - jnp.mean(grad_scaled, axis=1, keepdims=True)
    along = jnp.sum(d_scores * query_lines + cross_probs * grad_lines, axis=0) / input_width
    color_parts = jnp.einsum(
        "rj,rcy->jcy", query_away, d_scores, precision=lax.Precision.HIGHEST
    ) + jnp.einsum("rj,rcy->jcy", grad_away, cross_probs, precision=lax.Precision.HIGHEST)
    color_parts = deviation[None] * (
        color_parts - (colors - mean[None]) * deviation[None] * along[None]
    )
    color_parts = color_parts.reshape(3, grid_cols, tile_cols, grid_rows, tile_rows)
    color_parts = jnp.transpose(color_parts, (3, 1, 0, 4, 2)).reshape(
        grid_rows * grid_cols, 3, tile_rows, tile_cols
    )
    color_grad = lax.all_to_all(
        color_parts, ("rows", "cols"), split_axis=0, concat_axis=0, tiled=True
    ).reshape(image_count, grid_cols, 3, tile_rows, tile_cols)
    color_grad = jnp.transpose(jnp.sum(color_grad, axis=1), (1, 0, 2, 3))
    query_low = narrow(d_query_rows)
    d_latent, d_cross_gain, d_cross_bias = norm_back(
        latent_state, g_cross[0], b_cross[0], inner_right(query_low, cross_matrices[0])
    )
    latent_grad = gradient + d_latent
    in_gain_grad, in_bias_grad = lax.psum((in_gain_part, in_bias_part), ("rows", "cols"))
    vectors = jnp.stack(
        [
            d_cross_gain,
            cross_mlp_v[0],
            d_cross_bias,
            cross_mlp_v[1],
            jnp.sum(d_query_rows, axis=0),
            jnp.sum(to_float(d_attended), axis=0),
            d_cross_out_bias,
            cross_mlp_v[2],
            cross_mlp_v[3],
            d_self_gain,
            tower_mlp_v[0],
            d_self_bias,
            tower_mlp_v[1],
            jnp.sum(d_query_heads, axis=0),
            jnp.sum(d_tower_values, axis=0),
            d_self_out_bias,
            tower_mlp_v[2],
            tower_mlp_v[3],
        ]
    )
    vector_sums = lax.psum_scatter(vectors, ("rows", "cols"), scatter_dimension=1, tiled=True)
    lefts = jnp.stack(
        [
            normed_q,
            cross_stored[0],
            cross_stored[2],
            attended_low,
            normed_t,
            tower_stored[0],
            tower_stored[2],
            tower_mixed,
        ]
    )
    rights = jnp.stack(
        [
            query_low,
            cross_lows[0],
            cross_lows[1],
            cross_out_low,
            d_attended,
            query_rows,
            tq_low,
            tk_low,
            tv_low,
            tower_lows[0],
            tower_lows[1],
            tower_out_low,
        ]
    )
    small_lefts = jnp.stack([mixed_low, score_low])
    lefts = lax.all_gather(lefts, "cols", axis=1, tiled=True)
    small_lefts = lax.all_gather(small_lefts, "cols", axis=1, tiled=True)
    own = model_width // (grid_rows * grid_cols)
    rights = rights.reshape(rights.shape[0], rows_dev, grid_rows, grid_cols, own)
    rights = lax.all_to_all(
        jnp.transpose(rights, (3, 0, 1, 2, 4)), "cols", split_axis=0, concat_axis=0, tiled=False
    )
    rights = jnp.transpose(rights, (1, 0, 2, 3, 4)).reshape(
        rights.shape[1], grid_cols * rows_dev, grid_rows * own
    )
    pairs = ((0, 0), (1, 1), (2, 2), (3, 3), (4, 6), (4, 7), (4, 8), (5, 9), (6, 10), (7, 11))
    big = [inner_left(rights[k], lefts[i]).reshape(grid_rows, own, model_width) for i, k in pairs]
    small = [
        inner_left(rights[k], small_lefts[i]).reshape(grid_rows, own, input_width)
        for i, k in ((1, 5), (0, 4))
    ]
    big = lax.psum_scatter(jnp.stack(big, axis=1), "rows", scatter_dimension=0, tiled=False)
    small = lax.psum_scatter(jnp.stack(small, axis=1), "rows", scatter_dimension=0, tiled=False)
    big = jnp.transpose(big, (0, 2, 1))
    small = jnp.transpose(small, (0, 2, 1))
    all_sums = (
        big[:3],
        big[3],
        small,
        vector_sums[:2],
        vector_sums[2:9],
        big[4:9],
        big[9],
        vector_sums[9:11],
        vector_sums[11:],
    )
    cross_sums = all_sums[:5]
    self_sums = all_sums[5:]
    return (
        new_latents,
        latent_grad,
        color_grad,
        prior_cross_matrices + cross_sums[0],
        prior_cross_out + cross_sums[1],
        prior_input_matrices + cross_sums[2],
        in_gain_grad,
        in_bias_grad,
        cross_sums[3],
        cross_sums[4],
        self_sums[0],
        self_sums[1],
        self_sums[2],
        self_sums[3],
    )


STEPS_HELD = 8
GROUP = 4
XS = {0: 0, 3: 1, 4: 2, 5: 3, 6: 4}
LANES = 128
MESH = pl.DeviceIdType.MESH
WIDE = 3 * LANES


def own_dot(former, latter, former_dim, latter_dim):
    return lax.dot_general(
        former,
        latter,
        (((former_dim,), (latter_dim,)), ((), ())),
        preferred_element_type=jnp.float32,
    )


def selections(tile_cols, grid_cols, steps):
    held = STEPS_HELD
    blocks = -(-steps // held)
    place = np.zeros((grid_cols * 32, WIDE), np.float32)
    back = np.zeros((grid_cols * 32, blocks * LANES), np.float32)
    for tile in range(grid_cols):
        for channel in range(3):
            for offset in range(tile_cols):
                col = tile * tile_cols + offset
                line = tile * 32 + channel * tile_cols + offset
                place[line, channel * LANES + col] = 1
                half, step = divmod(col, steps)
                back[line, step * 16 + half * 8 + channel] = 1
    pick = np.zeros((7 * LANES, blocks * LANES), np.float32)
    for step in range(steps):
        for half in range(2):
            for slot, kind in enumerate((0, 1, 2, 3, 4, 3, 5, 6)):
                pick[kind * LANES + half * steps + step, step * 16 + half * 8 + slot] = 1
    spread = np.zeros((LANES, 2 * LANES), np.float32)
    for group in range(16):
        for channel in range(3):
            for slot in (3, 4):
                spread[group * 8 + slot, group * 8 + channel] = 1
            for slot in (6, 7):
                spread[group * 8 + slot, LANES + group * 8 + channel] = 1
    low = lambda values: np.asarray(values, ml_dtypes.bfloat16)
    return (low(place), low(pick), low(spread), low(back))


def norm_parts(values):
    middle = jnp.mean(values, axis=1, keepdims=True)
    centered = values - middle
    spread = jnp.mean(centered * centered, axis=1, keepdims=True)
    factor = lax.rsqrt(spread + EPS)
    return (centered * factor, factor)


def norm_forward(values, gain, offset):
    return narrow(norm_parts(values)[0] * gain + offset)


def norm_gradient(values, gain, gradient):
    plain, factor = norm_parts(values)
    inner = gradient * gain
    first = jnp.mean(inner, axis=1, keepdims=True)
    second = jnp.mean(inner * plain, axis=1, keepdims=True)
    return (
        factor * (inner - first - plain * second),
        jnp.sum(gradient * plain, axis=0, keepdims=True),
        jnp.sum(gradient, axis=0, keepdims=True),
    )


GELU_RATE = 0.7978845608028654
GELU_CUBE = 0.044715


def gelu_value(u):
    return 0.5 * u * (1.0 + jnp.tanh(GELU_RATE * (u + GELU_CUBE * u * u * u)))


def gelu_slope(u):
    bent = jnp.tanh(GELU_RATE * (u + GELU_CUBE * u * u * u))
    return 0.5 * (1.0 + bent) + 0.5 * u * (1.0 - bent * bent) * GELU_RATE * (
        1.0 + 3.0 * GELU_CUBE * u * u
    )


def waves(turns):
    near = turns - 2.0 * jnp.floor(turns * 0.5 + 0.5)
    return (jnp.sin(jnp.pi * near), jnp.cos(jnp.pi * near))


def axis_lines(place, slot):
    lane = lax.broadcasted_iota(jnp.int32, (place.shape[0], LANES), 1)
    band = lax.rem(lane, NBANDS)
    frequency = 1.0 + to_float(band) * ((FREQ_TOP - 1.0) / (NBANDS - 1))
    sine, cosine = waves(place * frequency)
    return jnp.concatenate(
        [jnp.where(lane < NBANDS, sine, cosine), jnp.where(lane == slot, place, 0.0)], axis=1
    )


def layer_kernel(
    sizes,
    boxes, latents, cotangent, colors, in_gain, in_bias, cross_gains, cross_biases, self_gains,
    self_biases, far_order, far_place, far_pick, far_spread, far_back,
    w_cross, w_out, w_self, w_self_out, w_input,
    new_latents, latent_grad, color_out, cross_total, out_total, self_total, self_out_total,
    input_parts, vector_out, input_vector_out,
    order, place, pick, spread, back, wts, win, win_raw, xbuf, xsmall, gsrc, gbuf, staged, paired, handed, crossed, staged_small, paired_small, handed_small, crossed_small, kept_small,
    line_rows, line_hid, line_right, line_staged, line_near, line_hand, line_sums,
    row_pair, row_hand, row_cross, row_kept, row_turned, row_done, biases,
    color_lines, color_tiles, colstage, colbuf, img, img7, fa, ft, sl, ycoef, xcoef, yfeat, xfeat, mixrow,
    cgright, rowsum, colsum, cgacc, cgsend, cgbuf, cgsum, cgfin,
    act, lnvec, lnsend, lnbuf, biasvec, vecsend, vecbuf,
    heads, probs, prob_grad, mix_s, mix_b, dmix_b, dqkv_s, dqkv_b,
    fixed_sem, weight_sem, x_send, x_recv, y_send, y_recv, g_send, g_recv, a_send, a_recv, r_send, r_recv, f_send, f_recv, l_send, l_recv,
    misc_send, misc_recv,
):
    grid_rows, grid_cols, rows, steps, tile_rows, tile_cols = sizes
    n_dev = grid_rows * grid_cols
    width = latents.shape[1]
    quads = grid_cols // 2
    chunk = width // grid_cols
    own = chunk // grid_rows
    tall = grid_rows * tile_rows
    z = lax.axis_index("rows")
    j = lax.axis_index("cols")
    core = lax.rem(j, 2)
    quad = j // 2
    me = z * grid_cols + j
    f32, bf16 = jnp.float32, jnp.bfloat16
    score_scale = width ** (-0.5)
    head_scale = HEAD_DIM ** (-0.5)

    def at_device(d):
        return {"rows": d // grid_cols, "cols": lax.rem(d, grid_cols)}

    def lanes_of(index):
        return pl.ds(pl.multiple_of(index * chunk, chunk), chunk)

    def push(src, dst, send, recv, where):
        pltpu.make_async_remote_copy(
            src_ref=src, dst_ref=dst, send_sem=send, recv_sem=recv, device_id=where,
            device_id_type=MESH,
        ).start()

    def wait_for(ref, sem):
        pltpu.make_async_copy(ref, ref, sem).wait()

    barrier = pltpu.get_barrier_semaphore()

    def greet_plane(step, carry):
        where = {"cols": lax.rem(j + step, grid_cols)}
        pl.semaphore_signal(barrier, inc=1, device_id=where, device_id_type=MESH)
        return carry

    def greet_line(step, carry):
        where = {"rows": lax.rem(z + step, grid_rows)}
        pl.semaphore_signal(barrier, inc=1, device_id=where, device_id_type=MESH)
        return carry

    lax.fori_loop(1, grid_rows, greet_line, 0)
    lax.fori_loop(1, grid_cols, greet_plane, 0)

    sources = (
        [w_cross.at[0], w_out, w_cross.at[1], w_cross.at[2]]
        + [w_self.at[0], w_self.at[1], w_self.at[2], w_self_out, w_self.at[3], w_self.at[4]]
    )
    CQ, CO, C1, C2, SQ, SK, SV, SO, S1, S2 = range(10)
    loads = [pltpu.make_async_copy(s, wts.at[k], weight_sem.at[k]) for k, s in enumerate(sources)]
    loads.append(pltpu.make_async_copy(w_input, win_raw, weight_sem.at[10]))
    loads[CQ].start()
    loads[10].start()
    fixed = ((far_order, order), (far_place, place), (far_pick, pick), (far_spread, spread), (far_back, back))
    fixed = [pltpu.make_async_copy(src, dst, fixed_sem.at[k]) for k, (src, dst) in enumerate(fixed)]
    for copy in fixed:
        copy.start()

    color_lines[...] = jnp.zeros(color_lines.shape, f32)
    for channel in range(3):
        for col in range(tile_cols):
            line = channel * tile_cols + col
            shown = to_float(colors[channel, col])
            for image in range(grid_rows):
                color_lines[image, line : line + 1, :tile_rows] = shown[image : image + 1]
    color_tiles[...] = narrow(color_lines[...])
    gc, bc = to_float(cross_gains[...]), to_float(cross_biases[...])
    gs, bs = to_float(self_gains[...]), to_float(self_biases[...])
    fixed[0].wait()
    gains_here = [to_float(ref[...]).reshape(1, -1) for ref in (in_gain, in_bias)]
    gains_here = jnp.concatenate(gains_here + [jnp.zeros((6, in_gain.shape[0]), f32)], axis=0)
    gains_here = own_dot(narrow(gains_here), order[...], 1, 1)
    gin, bin_ = gains_here[0:1], gains_here[1:2]
    lat = to_float(latents[...])
    nq = norm_forward(lat, gc[0:1], bc[0:1])
    xbuf[0, core, quad] = nq
    cot_low = cotangent[...]
    xbuf[XS[6], core, quad] = cot_low
    biases[...] = jnp.concatenate([bc, jnp.zeros((1, width), f32)], axis=0)
    pl.semaphore_wait(barrier, grid_cols + grid_rows - 2)

    def send_color(step, carry):
        image = lax.rem(z + step, grid_rows)
        push(color_tiles.at[image], colstage.at[z], misc_send.at[5], misc_recv.at[5], {"rows": image})
        return carry

    lax.fori_loop(1, grid_rows, send_color, 0)
    colstage[z] = color_tiles[z]

    def x_spread(block, sem):
        def one(step, carry):
            peer = 2 * lax.rem(quad + step, quads) + core
            push(block, block, x_send.at[sem], x_recv.at[sem], {"cols": peer})
            return carry

        lax.fori_loop(1, quads, one, 0)

    def x_relay(half, sem):
        wait_for(half.at[pl.ds(0, quads - 1)], x_recv.at[sem])
        push(half, half, y_send.at[sem], y_recv.at[sem], {"cols": j + 1 - 2 * core})

    def x_arrived(half, sem):
        wait_for(half, y_recv.at[sem])

    pieces = rows // 16
    sent = {}

    def spread_x(k):
        x_spread(xbuf.at[XS[k], core, quad], k)

    def background(point):
        for k, count in PLAN.get(point, ()):
            for piece in range(sent.get(k, 0), sent.get(k, 0) + count):
                x_spread(xbuf.at[XS[k], core, quad, pl.ds(piece * 16, 16)], k)
            sent[k] = sent.get(k, 0) + count

    def relay_x(k):
        x_relay(xbuf.at[XS[k], core], k)

    def have_x(k):
        x_arrived(xbuf.at[XS[k], 1 - core], k)

    def to_plane(step):
        peer = lax.rem(j + step, grid_cols)
        return peer, {"cols": peer}

    def regroup(values):
        tiles = [values[:, t * LANES : (t + 1) * LANES] for t in range(width // LANES)]
        piece = lax.broadcasted_iota(jnp.int32, tiles[0].shape, 1) // own
        result = []
        for peer in range(grid_cols):
            chunk_now = None
            for part in range(grid_rows):
                tile, offset = divmod((part * grid_cols + peer) * own, LANES)
                shift = (part * own - offset) % LANES
                moved = pltpu.roll(tiles[tile], shift, 1) if shift else tiles[tile]
                chunk_now = moved if part == 0 else jnp.where(piece == part, moved, chunk_now)
            result.append(chunk_now)
        return jnp.concatenate(result, axis=1)

    def spread_g(k, values):
        spread_plain(k, narrow(regroup(to_float(values))))

    def spread_plain(k, values):
        gsrc[k] = values

        def one(step, carry):
            peer, where = to_plane(step)
            push(gsrc.at[k, :, lanes_of(peer)], gbuf.at[k, core, quad], g_send.at[k], g_recv.at[k], where)
            return carry

        lax.fori_loop(1, grid_cols, one, 0)
        gbuf[k, core, quad] = gsrc[k, :, lanes_of(j)]

    def have_g(k):
        wait_for(gsrc.at[k, :, pl.ds(0, chunk * (grid_cols - 1))], g_recv.at[k])
        return gbuf[k].reshape(grid_cols * rows, chunk)

    partner = z + 1 - 2 * lax.rem(z, 2)
    across = lax.rem(z + 2, grid_rows)

    def block_at(part):
        return pl.ds(pl.multiple_of(part * own, own), own)

    def send_parts(src, pair, sem):
        for slot, part in enumerate((partner, lax.rem(partner + 2, grid_rows))):
            push(src.at[block_at(part)], pair.at[slot], r_send.at[sem], r_recv.at[sem], {"rows": partner})

    def join_parts(src, pair, hand, far, kept, sem):
        wait_for(pair, r_recv.at[sem])
        hand[...] = narrow(to_float(src[block_at(across)]) + to_float(pair[1]))
        push(hand, far, f_send.at[sem], f_recv.at[sem], {"rows": across})
        kept[...] = to_float(src[block_at(z)]) + to_float(pair[0])

    def kept_of(m):
        if m < 3:
            return cross_total.at[m]
        if m < 9:
            return self_total.at[m - 4]
        return self_out_total

    def slot_of(m):
        return 0 if m == 0 else m - 3

    def join(m):
        k = slot_of(m)
        join_parts(staged.at[k], paired.at[k], handed.at[k], crossed.at[k], kept_of(m), m)

    def columns_of(part):
        size = width // grid_rows
        return pl.ds(pl.multiple_of(part * size, size), size)

    def send_rows(src, sem):
        for slot, part in enumerate((partner, lax.rem(partner + 2, grid_rows))):
            push(src.at[:, columns_of(part)], row_pair.at[slot], r_send.at[sem], r_recv.at[sem], {"rows": partner})

    def join_rows(src, sem):
        wait_for(row_pair, r_recv.at[sem])
        row_hand[...] = narrow(to_float(src[:, columns_of(across)]) + to_float(row_pair[1]))
        push(row_hand, row_cross, f_send.at[sem], f_recv.at[sem], {"rows": across})
        row_kept[...] = to_float(src[:, columns_of(z)]) + to_float(row_pair[0])

    def finish_rows(sem):
        wait_for(row_cross, f_recv.at[sem])
        row_turned[...] = jnp.transpose(row_kept[...] + to_float(row_cross[...]))

        def one(step, carry):
            peer, where = to_plane(step)
            push(row_turned.at[block_at(peer)], row_done.at[:, lanes_of(j)], a_send.at[3], a_recv.at[3], where)
            return carry

        lax.fori_loop(1, grid_cols, one, 0)
        row_done[:, lanes_of(j)] = row_turned[block_at(j)]

    def to_line(step):
        part = lax.rem(z + step, grid_rows)
        return part, {"rows": part}

    def spread_line():
        def one(step, carry):
            part, where = to_line(step)
            push(line_rows.at[z], line_rows.at[z], x_send.at[1], x_recv.at[1], where)
            return carry

        lax.fori_loop(1, grid_rows, one, 0)

    def line_hidden(k, bias):
        wait_for(line_rows.at[pl.ds(0, grid_rows - 1)], x_recv.at[1])

        def one(n, carry):
            at = pl.ds(pl.multiple_of(n * 256, 256), 256)
            x = line_rows[...].reshape(grid_rows * rows, width)
            pre = own_dot(x, wts[k, :, at], 1, 0) + bias[:, at]
            line_hid[:, :, at] = narrow(gelu_value(pre)).reshape(grid_rows, rows, 256)
            return carry

        lax.fori_loop(0, width // 256, one, 0, unroll=2)

    def spread_columns(m, values):
        gsrc[m] = values

        def one(step, carry):
            part, where = to_line(step)
            push(
                gsrc.at[m, :, columns_of(part)], line_right.at[m - 1, z], g_send.at[m], g_recv.at[m], where
            )
            return carry

        lax.fori_loop(1, grid_rows, one, 0)
        line_right[m - 1, z] = gsrc[m, :, columns_of(z)]

    def line_part(m, left):
        wait_for(line_right.at[m - 1, pl.ds(0, grid_rows - 1)], g_recv.at[m])
        size = width // grid_rows
        turned = jnp.transpose(line_right[m - 1].reshape(grid_rows * rows, size))

        def one(n, carry):
            at = pl.ds(pl.multiple_of(n * 256, 256), 256)
            block = left[:, :, at].reshape(grid_rows * rows, 256)
            line_staged[m - 1, :, at] = narrow(own_dot(turned, block, 1, 0))
            return carry

        lax.fori_loop(0, width // 256, one, 0, unroll=4)

        for q in range(quads):
            push(
                line_staged.at[m - 1, block_at(2 * q + 1 - core)], line_near.at[m - 1, q],
                y_send.at[m], y_recv.at[m], {"cols": j + 1 - 2 * core},
            )

    def line_join(m):
        wait_for(line_near.at[m - 1], y_recv.at[m])
        for q in range(quads):
            both = to_float(line_staged[m - 1, block_at(2 * q + core)]) + to_float(line_near[m - 1, q])
            line_hand[m - 1, q] = narrow(both)

        def give(step, carry):
            q = lax.rem(quad + step, quads)
            push(
                line_hand.at[m - 1, q], line_sums.at[m - 1, quad], l_send.at[m - 1], l_recv.at[m - 1],
                {"cols": 2 * q + core},
            )
            return carry

        lax.fori_loop(1, quads, give, 0)
        line_sums[m - 1, quad] = line_hand[m - 1, quad]

    def line_total(m):
        wait_for(line_sums.at[m - 1, pl.ds(0, quads - 1)], l_recv.at[m - 1])
        result = to_float(line_sums[m - 1, 0])
        for q in range(1, quads):
            result = result + to_float(line_sums[m - 1, q])
        cross_total[m] = result

    def join_small(m):
        join_parts(
            staged_small.at[m], paired_small.at[m], handed_small.at[m], crossed_small.at[m],
            kept_small.at[m], 10 + m,
        )

    def weight_part(m, right, left):
        turned = jnp.transpose(right)

        def one(n, carry):
            at = pl.ds(pl.multiple_of(n * 256, 256), 256)
            block = left[:, :, :, at].reshape(grid_cols * rows, 256)
            staged[slot_of(m), :, at] = narrow(own_dot(turned, block, 1, 0))
            return carry

        lax.fori_loop(0, width // 256, one, 0, unroll=4)
        if m == 8:
            send_rows(staged.at[slot_of(m)], m)
        else:
            send_parts(staged.at[slot_of(m)], paired.at[slot_of(m)], m)

    def small_part(m, right, left):
        staged_small[m] = narrow(own_dot(right, left[...].reshape(grid_cols * rows, WIDE), 0, 0))
        send_parts(staged_small.at[m], paired_small.at[m], 10 + m)

    def times(x, k, out):
        def one(n, carry):
            at = pl.ds(pl.multiple_of(n * 256, 256), 256)
            out[:, at] = own_dot(x, wts[k, :, at], 1, 0)
            return carry

        lax.fori_loop(0, width // 256, one, 0, unroll=4)

    def times_t(x, k, out, add=False):
        def one(n, carry):
            at = pl.ds(pl.multiple_of(n * 256, 256), 256)
            result = own_dot(x, wts[k, at, :], 1, 1)
            out[:, at] = out[:, at] + result if add else result
            return carry

        lax.fori_loop(0, width // 256, one, 0, unroll=4)

    FIRST, SECOND, THIRD, PRE_C, PRE_S, TMP, ATT, GRAD, COT_BACK = range(9)
    tmp = act.at[TMP]

    wait_for(colstage.at[pl.ds(0, grid_rows - 1)], misc_recv.at[5])

    def send_strip(step, carry):
        peer, where = to_plane(step)
        push(colstage, colbuf.at[j], misc_send.at[0], misc_recv.at[0], where)
        return carry

    lax.fori_loop(1, grid_cols, send_strip, 0)
    colbuf[j] = colstage[...]
    loads[CQ].wait()
    for k in range(1, 10):
        loads[k].start()
    times(nq, CQ, tmp)
    query_low = narrow(tmp[...] + bc[2:3])
    spread_x(0)
    spread_g(7, query_low)
    spread_x(6)
    loads[10].wait()
    for k in range(2):
        win[k] = narrow(own_dot(order[...], win_raw[:, k, :], 1, 0))
    query_inputs = own_dot(query_low, win[0], 1, 1)
    spare = pl.ds(2 * LANES, 16)
    spare_row = lax.broadcasted_iota(jnp.int32, (16, width), 0)
    win[1, spare, :] = narrow(jnp.where(spare_row == 5, bc[3:4], to_float(win[1, spare, :])))

    box = [boxes[z, k] for k in range(4)]

    def filled(value, shape):
        return to_float(jnp.full(shape, value, jnp.int32))

    row_at = lax.broadcasted_iota(jnp.int32, (tall, 1), 0)
    y_place = -1.0 + 2.0 * to_float(row_at - box[0]) / filled(box[2] - 1, (tall, 1))
    y_lines = axis_lines(y_place, 3)
    y_sum = jnp.sum(y_lines, axis=1, keepdims=True)
    row_out = jnp.where((row_at >= box[0]) & (row_at < box[0] + box[2]), 0.0, NEG)
    yfeat[...] = narrow(y_lines)
    held_rows = xfeat.shape[1]
    col_lane = lax.broadcasted_iota(jnp.int32, (held_rows, LANES), 1)
    col_row = lax.broadcasted_iota(jnp.int32, (held_rows, LANES), 0)
    x_sum = jnp.zeros((1, LANES), f32)
    col_out = []
    for half in range(2):
        col_at = lax.broadcasted_iota(jnp.int32, (held_rows, 1), 0) + half * steps
        x_place = -1.0 + 2.0 * to_float(col_at - box[1]) / filled(box[3] - 1, (held_rows, 1))
        x_lines = axis_lines(x_place, 4)
        xfeat[half] = narrow(x_lines)
        here = (col_lane == col_row + half * steps) & (col_row < steps)
        x_sum = x_sum + jnp.sum(
            jnp.where(here, jnp.sum(x_lines, axis=1, keepdims=True), 0.0), axis=0, keepdims=True
        )
        col_out.append(jnp.where((col_at >= box[1]) & (col_at < box[1] + box[3]), 0.0, NEG))
    x_lane = lax.broadcasted_iota(jnp.int32, (1, LANES), 1)
    x_here = -1.0 + 2.0 * to_float(x_lane - box[1]) / filled(box[3] - 1, (1, LANES))
    count = 3 + 2 + 4 * NBANDS

    lane1 = lax.broadcasted_iota(jnp.int32, (rows, LANES), 1)
    lane_half = lax.broadcasted_iota(jnp.int32, (8, LANES), 1) // rows
    sub8 = lax.broadcasted_iota(jnp.int32, (8, LANES), 0)

    def twice(values):
        return jnp.concatenate([values, values], axis=0)

    def turn(values):
        return jnp.transpose(twice(values))[:8]

    def coefficients(scaled, extra):
        tail = scaled[:, 2 * LANES :]
        total = jnp.sum(scaled, axis=1, keepdims=True)
        turned = turn(jnp.where(lane1 == 5, total, jnp.where(lane1 == 6, extra, tail)))
        total_high = to_float(narrow(turned[5:6]))
        body = jnp.where(
            sub8 < 3, turned, jnp.where(sub8 < 5, -total_high, jnp.where(sub8 == 5, total_high - turned[5:6], 0.0))
        )
        body = narrow(jnp.concatenate(
            [jnp.where(lane_half == 0, body, 0.0), jnp.where(lane_half == 1, body, 0.0)], axis=0
        ))
        ones = jnp.where(sub8 >= 6, 1.0, 0.0)
        ones = narrow(jnp.concatenate(
            [jnp.where(lane_half == 0, ones, 0.0), jnp.where(lane_half == 1, ones, 0.0)], axis=0
        ))
        mixrow[...] = jnp.zeros(mixrow.shape, bf16)
        for held in range(STEPS_HELD):
            mixrow[held, held * 16 : held * 16 + 16, :] = jnp.concatenate([body, ones], axis=1)
        scaled_low = narrow(jnp.concatenate([scaled[:, :LANES], tail], axis=1))
        ycoef[...] = own_dot(yfeat[...], twice(scaled_low), 1, 1)
        scaled_low = narrow(jnp.concatenate([scaled[:, LANES : 2 * LANES], tail], axis=1))
        nothing = jnp.zeros_like(scaled_low)
        xcoef[...] = own_dot(xfeat[0], jnp.concatenate([scaled_low, nothing], axis=0), 1, 1) + own_dot(
            xfeat[1], jnp.concatenate([nothing, scaled_low], axis=0), 1, 1
        )
        return turned

    query_scaled = query_inputs * gin * score_scale
    coefficients(query_scaled, 0.0)
    ycoef[...] += row_out
    half_lane = lax.broadcasted_iota(jnp.int32, (held_rows, LANES), 1) // rows
    xcoef[...] += jnp.where(half_lane == 0, col_out[0], col_out[1])

    for copy in fixed[1:]:
        copy.wait()
    wait_for(colbuf.at[pl.ds(0, grid_cols - 1)], misc_recv.at[0])
    for part in range(grid_rows):
        at = pl.ds(part * tile_rows, tile_rows)
        tiles = colbuf[:, part].reshape(grid_cols * 32, LANES)
        img[at, :] = own_dot(tiles, place[...], 0, 0)[:tile_rows]
    c0, c1, c2 = img[:, :LANES], img[:, LANES : 2 * LANES], img[:, 2 * LANES :]
    mean = (c0 + c1 + c2 + y_sum + x_sum) * (1.0 / count)
    square = (c0 * c0 + c1 * c1 + c2 * c2 + y_place * y_place + x_here * x_here + 2.0 * NBANDS) * (
        1.0 / count
    )
    dev = lax.rsqrt(square - mean * mean + EPS)
    mean_low, dev_low = narrow(mean), narrow(dev)
    img7[...] = jnp.concatenate(
        [
            narrow(c0), narrow(c1), narrow(c2),
            mean_low, narrow(mean - to_float(mean_low)),
            dev_low, narrow(dev - to_float(dev_low)),
        ],
        axis=1,
    )
    blocks = fa.shape[0]
    for block in range(blocks):
        at = pl.ds(block * LANES, LANES)
        fa[block] = narrow(own_dot(img7[...], pick[:, at], 1, 0))
        turned = own_dot(pick[:, at], img7[...], 0, 1)
        line = lax.broadcasted_iota(jnp.int32, turned.shape, 0)
        ft[at, :] = narrow(jnp.where(lax.rem(line, 8) == 5, 1.0, turned))

    def step_lines(s):
        block, held = s // STEPS_HELD, lax.rem(s, STEPS_HELD)
        result = own_dot(fa[block], mixrow[held], 1, 0)
        deviation = result[:, LANES:]
        lines = (ycoef[...] + xcoef[pl.ds(s, 1), :] + result[:, :LANES]) * deviation
        return lines, deviation

    def pair_sums(s, weighted):
        at = pl.ds(pl.multiple_of(s * 16, 32), 32)
        both = own_dot(ft[at, :], jnp.concatenate([narrow(w) for w in weighted], axis=1), 1, 0)
        result = None
        for k in range(2):
            found = both[k * 16 : k * 16 + 16, k * LANES : (k + 1) * LANES]
            found = jnp.where(lane_half == 0, found[:8], found[8:])
            colsum[pl.ds(s + k, 1), :] = found[5:6]
            result = found if result is None else result + found
        return result

    def in_groups(one, first, last, start):
        def group(n, carry):
            rows_here = None
            for pair in range(GROUP // 2):
                weighted = []
                for k in range(2):
                    s = n * GROUP + pair * 2 + k
                    total, found, here = one(s, carry)
                    carry = (total, found)
                    weighted.append(here)
                    rows_here = here if rows_here is None else rows_here + here
                carry = (carry[0], carry[1] + pair_sums(n * GROUP + pair * 2, weighted))
            rowsum[...] += rows_here
            return carry

        return lax.fori_loop(first // GROUP, last // GROUP, group, start)

    def fold(values):
        return values[:rows] + values[rows:]

    def pixel_sums(found, factor):
        by_row = fold(own_dot(narrow(rowsum[...] * factor), yfeat[...], 0, 0))
        cols = narrow(colsum[...] * factor)
        by_col = own_dot(cols, xfeat[0], 0, 0)[:rows] + own_dot(cols, xfeat[1], 0, 0)[rows:]
        padded = jnp.concatenate([found * factor, jnp.zeros((LANES - 8, LANES), f32)], axis=0)
        sums = fold(jnp.transpose(padded))
        middle = sums[:, 3:4] + sums[:, 4:5]
        tail = jnp.where(lane1 < 3, sums, 0.0) + by_row[:, LANES:] + by_col[:, LANES:]
        return jnp.concatenate([by_row[:, :LANES], by_col[:, :LANES], tail], axis=1) - middle

    def other_half(line):
        return pltpu.roll(jnp.broadcast_to(line, (8, LANES)), rows, 1)[:1]

    def first_pass(s, best):
        lines, deviation = step_lines(s)
        sl[s] = lines
        return jnp.maximum(best, jnp.max(lines, axis=0, keepdims=True))

    best = lax.fori_loop(0, steps, first_pass, jnp.full((1, LANES), -3e38, f32), unroll=4)
    best = jnp.maximum(best, other_half(best))
    rowsum[...] = jnp.zeros(rowsum.shape, f32)
    colsum[...] = jnp.zeros(colsum.shape, f32)

    def second_pass(s, carry):
        total, found = carry
        block, held = s // STEPS_HELD, lax.rem(s, STEPS_HELD)
        deviation = own_dot(fa[block], mixrow[held][:, LANES:], 1, 0)
        weights = jnp.exp(sl[s] - best)
        total = total + jnp.sum(weights, axis=0, keepdims=True)
        return total, found, weights * deviation

    total, found = in_groups(
        second_pass, 0, steps, (jnp.zeros((1, LANES), f32), jnp.zeros((8, LANES), f32))
    )
    total = total + other_half(total)
    log_total = best + jnp.log(total)
    plain_mixed = pixel_sums(found, 1.0 / total)
    wide1 = lax.broadcasted_iota(jnp.int32, (rows, WIDE), 1)
    mixed_low = narrow(jnp.where(wide1 == 2 * LANES + 5, 1.0, plain_mixed * gin + bin_))
    xsmall[0, core, quad] = mixed_low
    x_spread(xsmall.at[0, core, quad], 8)
    relay_x(0)
    relay_x(6)
    attended = own_dot(mixed_low, win[1], 1, 0)
    act[ATT] = attended
    attended_low = narrow(attended)
    loads[CO].wait()
    times(attended_low, CO, tmp)
    first = lat + tmp[...] + bc[4:5]
    act[FIRST] = first
    normed_c = norm_forward(first, gc[1:2], bc[1:2])
    line_rows[z] = normed_c
    spread_line()
    loads[C1].wait()
    times(normed_c, C1, tmp)
    pre = tmp[...] + bc[5:6]
    act[PRE_C] = pre
    hidden_c = narrow(gelu_value(pre))
    loads[C2].wait()
    times(hidden_c, C2, tmp)
    second = act[FIRST] + tmp[...] + bc[6:7]
    act[SECOND] = second
    normed_t = norm_forward(second, gs[0:1], bs[0:1])
    xbuf[XS[4], core, quad] = normed_t
    mine = core * quads + quad

    def block_of(peer):
        return lax.rem(peer, 2) * quads + peer // 2

    def to_heads(kind, values):
        gsrc[9 + kind] = values

        def one(step, carry):
            peer, where = to_plane(step)
            push(
                gsrc.at[9 + kind, :, lanes_of(peer)], heads.at[kind, mine],
                a_send.at[4 + kind], a_recv.at[4 + kind], where,
            )
            return carry

        lax.fori_loop(1, grid_cols, one, 0)
        heads[kind, mine] = gsrc[9 + kind, :, lanes_of(j)]

    loads[SQ].wait()
    times(normed_t, SQ, tmp)
    to_heads(0, narrow(tmp[...] + bs[2:3]))
    loads[SK].wait()
    times(normed_t, SK, tmp)
    to_heads(1, narrow(tmp[...]))
    loads[SV].wait()
    times(normed_t, SV, tmp)
    to_heads(2, narrow(tmp[...] + bs[3:4]))
    background(0)
    loads[S2].wait()
    times_t(cot_low, S2, act.at[COT_BACK])
    x_relay(xsmall.at[0, core], 8)
    head_rows = grid_cols * rows
    per = 128
    each = per // rows

    for kind in range(3):
        wait_for(heads.at[kind, pl.ds(0, grid_cols - 1)], a_recv.at[4 + kind])

    def head_of(kind):
        return heads[kind].reshape(head_rows, chunk)

    def head_part(kind, n):
        return heads[kind, pl.ds(n * each, each)].reshape(per, chunk)

    def head_forward(n, carry):
        at = pl.ds(pl.multiple_of(n * per, per), per)
        scores = own_dot(head_part(0, n), head_of(1), 1, 1) * head_scale
        weights = jnp.exp(scores - jnp.max(scores, axis=1, keepdims=True))
        found_probs = weights / jnp.sum(weights, axis=1, keepdims=True)
        probs[at, :] = found_probs
        probs_low = narrow(found_probs)
        prob_grad[1, at, :] = probs_low
        mix_s[pl.ds(n * each, each)] = narrow(own_dot(probs_low, head_of(2), 1, 0)).reshape(each, rows, chunk)
        return carry

    lax.fori_loop(0, head_rows // per, head_forward, 0, unroll=2)

    def send_mixed(step, carry):
        peer, where = to_plane(step)
        push(mix_s.at[block_of(peer)], mix_b.at[:, lanes_of(j)], a_send.at[0], a_recv.at[0], where)
        return carry

    lax.fori_loop(1, grid_cols, send_mixed, 0)
    background(1)
    mix_b[:, lanes_of(j)] = mix_s[mine]
    loads[SO].wait()
    wait_for(mix_b.at[:, pl.ds(0, chunk * (grid_cols - 1))], a_recv.at[0])
    mixed_rows = mix_b[...]
    xbuf[XS[3], core, quad] = mixed_rows
    times(mixed_rows, SO, tmp)
    relay_x(4)
    third = act[SECOND] + tmp[...] + bs[4:5]
    act[THIRD] = third
    normed_s = norm_forward(third, gs[1:2], bs[1:2])
    xbuf[XS[5], core, quad] = normed_s
    background(2)
    loads[S1].wait()
    times(normed_s, S1, tmp)
    pre = tmp[...] + bs[5:6]
    act[PRE_S] = pre
    hidden_s = narrow(gelu_value(pre))
    spread_plain(5, hidden_s)
    background(3)
    times(hidden_s, S2, tmp)
    new_latents[...] = narrow(act[THIRD] + tmp[...] + bs[6:7])

    d_pre = act[COT_BACK] * gelu_slope(act[PRE_S])
    pre_low = narrow(d_pre)
    times_t(pre_low, S1, tmp)
    d_rows, lnvec[6:7, :], lnvec[7:8, :] = norm_gradient(act[THIRD], gs[1:2], tmp[...])
    gradient = to_float(cot_low) + d_rows
    act[GRAD] = gradient
    out_low = narrow(gradient)
    times_t(out_low, SO, tmp)
    mix_b2 = narrow(tmp[...])
    gsrc[12] = mix_b2

    def send_dmixed(step, carry):
        peer, where = to_plane(step)
        push(gsrc.at[12, :, lanes_of(peer)], dmix_b.at[mine], a_send.at[1], a_recv.at[1], where)
        return carry

    lax.fori_loop(1, grid_cols, send_dmixed, 0)
    dmix_b[mine] = gsrc[12, :, lanes_of(j)]
    background(4)
    spread_g(4, pre_low)
    line_hidden(C1, biases.at[5:6])
    have_x(6)
    weight_part(8, have_g(5), xbuf.at[XS[6]])
    spread_g(6, out_low)
    background(5)
    wait_for(dmix_b.at[pl.ds(0, grid_cols - 1)], a_recv.at[1])

    def from_heads(kind):
        def one(step, carry):
            peer, where = to_plane(step)
            push(
                dqkv_s.at[kind, block_of(peer)], dqkv_b.at[kind, :, lanes_of(j)],
                a_send.at[7 + kind], a_recv.at[7 + kind], where,
            )
            return carry

        lax.fori_loop(1, grid_cols, one, 0)
        dqkv_b[kind, :, lanes_of(j)] = dqkv_s[kind, mine]

    def rows_back(kind):
        wait_for(dqkv_b.at[kind, :, pl.ds(0, chunk * (grid_cols - 1))], a_recv.at[7 + kind])
        wait_for(heads.at[kind, pl.ds(0, grid_cols - 1)], a_send.at[4 + kind])
        spread_g(9 + kind, dqkv_b[kind])

    def put_head(kind, n, values):
        dqkv_s[kind, pl.ds(n * each, each)] = narrow(values).reshape(each, rows, chunk)

    d_mixed_all = dmix_b[...].reshape(head_rows, chunk)

    def head_values(n, carry):
        at = pl.ds(pl.multiple_of(n * per, per), per)
        put_head(2, n, own_dot(prob_grad[1, :, at], d_mixed_all, 0, 0))
        return carry

    def head_queries(n, carry):
        at = pl.ds(pl.multiple_of(n * per, per), per)
        d_mixed = dmix_b[pl.ds(n * each, each)].reshape(per, chunk)
        d_probs = own_dot(d_mixed, head_of(2), 1, 1)
        found_probs = probs[at, :]
        d_scores = found_probs * (d_probs - jnp.sum(found_probs * d_probs, axis=1, keepdims=True))
        d_low = narrow(d_scores * head_scale)
        prob_grad[0, at, :] = d_low
        put_head(0, n, own_dot(d_low, head_of(1), 1, 0))
        return carry

    def head_keys(n, carry):
        at = pl.ds(pl.multiple_of(n * per, per), per)
        put_head(1, n, own_dot(prob_grad[0, :, at], head_of(0), 0, 0))
        return carry

    lax.fori_loop(0, head_rows // per, head_values, 0, unroll=2)
    from_heads(2)
    background(6)
    lax.fori_loop(0, head_rows // per, head_queries, 0, unroll=2)
    from_heads(0)
    background(7)
    relay_x(3)
    lax.fori_loop(0, head_rows // per, head_keys, 0, unroll=2)
    from_heads(1)
    background(8)
    join_rows(staged.at[slot_of(8)], 8)

    def column_sum(values):
        return jnp.sum(to_float(values), axis=0, keepdims=True)

    have_x(3)
    right = have_g(6)
    bias_s4 = column_sum(right)
    weight_part(9, right, xbuf.at[XS[3]])
    rows_back(2)
    times_t(dqkv_b[2], SV, tmp)
    rows_back(0)
    times_t(dqkv_b[0], SQ, tmp, True)
    rows_back(1)
    times_t(dqkv_b[1], SK, tmp, True)
    background(9)
    d_rows, lnvec[4:5, :], lnvec[5:6, :] = norm_gradient(act[SECOND], gs[0:1], tmp[...])
    gradient = act[GRAD] + d_rows
    act[GRAD] = gradient
    second_low = narrow(gradient)
    spread_columns(2, second_low)
    lnvec[9:10, :] = jnp.sum(gradient, axis=0, keepdims=True)
    background(10)
    times_t(second_low, C2, tmp)
    d_pre = tmp[...] * gelu_slope(act[PRE_C])
    pre_low = narrow(d_pre)
    spread_columns(1, pre_low)
    lnvec[10:11, :] = jnp.sum(d_pre, axis=0, keepdims=True)
    background(11)
    join(9)
    have_x(4)
    for k in (2, 0, 1):
        right = have_g(9 + k)
        if k == 0:
            bias_s2 = column_sum(right)
        elif k == 2:
            bias_s3 = column_sum(right)
        weight_part(4 + k, right, xbuf.at[XS[4]])
    times_t(pre_low, C1, tmp)
    d_rows, lnvec[2:3, :], lnvec[3:4, :] = norm_gradient(act[FIRST], gc[1:2], tmp[...])
    gradient = act[GRAD] + d_rows
    act[GRAD] = gradient
    out_low = narrow(gradient)
    spread_g(3, out_low)
    relay_x(5)
    times_t(out_low, CO, tmp)
    d_attended = narrow(tmp[...])
    spread_g(8, d_attended)
    background(12)
    line_part(2, line_hid)
    line_part(1, line_rows)
    line_join(2)
    have_x(5)
    right = have_g(4)
    bias_s5 = column_sum(right)
    weight_part(7, right, xbuf.at[XS[5]])

    grad_inputs = own_dot(d_attended, win[1], 1, 1)
    d_attended = to_float(d_attended)
    shift = grad_inputs[:, 2 * LANES + 5 : 2 * LANES + 6]
    row_delta = jnp.sum(d_attended * act[ATT], axis=1, keepdims=True) - shift
    grad_shift = jnp.sum(grad_inputs * bin_, axis=1, keepdims=True)
    grad_scaled = grad_inputs * gin
    turned = coefficients(grad_scaled, grad_shift - row_delta)
    constant = turned[6:7]

    def away(scaled):
        values = scaled[:, 2 * LANES :] - jnp.sum(scaled, axis=1, keepdims=True) * (1.0 / count)
        values = jnp.where(lane1 < 3, values, 0.0)
        return jnp.concatenate([values, pltpu.roll(values, 8, 1)], axis=0)

    query_away, grad_away = away(query_scaled), away(grad_scaled)
    wide_lane = lax.broadcasted_iota(jnp.int32, (LANES, LANES), 1)
    wide_half = lax.broadcasted_iota(jnp.int32, (LANES, LANES), 0) // rows
    blank = jnp.zeros((LANES, LANES), bf16)
    for held in range(STEPS_HELD):
        group = wide_lane - held * 16 - wide_half * 8
        along = narrow(jnp.where((group >= 0) & (group < 3), 1.0, 0.0))
        colors_here = [query_away, grad_away]
        if held:
            colors_here = [pltpu.roll(v, held * 16, 1) for v in colors_here]
        cgright[held // 2, (held % 2) * WIDE : (held % 2 + 1) * WIDE, :] = jnp.concatenate(
            [
                jnp.concatenate([narrow(colors_here[0]), blank], axis=1),
                jnp.concatenate([narrow(colors_here[1]), blank], axis=1),
                jnp.concatenate([blank, along], axis=1),
            ],
            axis=0,
        )
    rowsum[...] = jnp.zeros(rowsum.shape, f32)
    colsum[...] = jnp.zeros(colsum.shape, f32)

    def kept_at(s):
        place_now = lax.rem(s, 6)
        line = pl.ds(pl.multiple_of((place_now // 2) * tall, 32), tall)
        lane = pl.ds(pl.multiple_of(lax.rem(place_now, 2) * WIDE, LANES), WIDE)
        return wts.at[4 + s // 6, line, lane]

    def back_pass(s, carry):
        total, found = carry
        lines, deviation = step_lines(s)
        scores = sl[s]
        found_probs = jnp.exp(scores - log_total)
        d_scores = found_probs * (lines + constant)
        kept_at(s)[...] = jnp.concatenate(
            [narrow(d_scores), narrow(found_probs), narrow(d_scores * scores + found_probs * lines)], axis=1
        )
        total = total + jnp.sum(d_scores, axis=0, keepdims=True)
        return total, found, d_scores * deviation

    def color_block(block):
        result = None
        for pair in range(block * STEPS_HELD // 2, min((block + 1) * STEPS_HELD, steps) // 2):
            line = pl.ds((pair % 3) * tall, tall)
            left = wts[4 + pair // 3, line, pl.ds(0, 2 * WIDE)]
            part = own_dot(left, cgright[pair % (STEPS_HELD // 2)], 1, 0)
            result = part if result is None else result + part
        cgacc[block] = result

    carry = (jnp.zeros((1, LANES), f32), jnp.zeros((8, LANES), f32))
    third_of = steps // 3
    line_join(1)
    carry = in_groups(back_pass, 0, third_of, carry)
    finish_rows(8)
    join(6)
    carry = in_groups(back_pass, third_of, 2 * third_of, carry)
    join(4)
    x_arrived(xsmall.at[0, 1 - core], 8)
    right = have_g(3)
    bias_c4 = column_sum(right)
    small_part(2, right, xsmall.at[0])
    right = have_g(8)
    bias_c3 = column_sum(right)
    small_part(1, right, xsmall.at[0])
    total, found = in_groups(back_pass, 2 * third_of, steps, carry)
    join(5)
    plain_scores = pixel_sums(found, 1.0) * score_scale
    total = total * score_scale
    score_total = fold(jnp.transpose(jnp.concatenate([total, jnp.zeros((LANES - 1, LANES), f32)], axis=0)))[:, 0:1]
    score_low = narrow(plain_scores * gin + score_total * bin_)
    xsmall[1, core, quad] = score_low
    x_spread(xsmall.at[1, core, quad], 9)

    def d_query_part(n, carry):
        at = pl.ds(pl.multiple_of(n * 256, 256), 256)
        tmp[:, at] = own_dot(score_low, win[0, :, at], 1, 0)
        return carry

    lax.fori_loop(0, width // 256, d_query_part, 0)
    query_grad_low = narrow(tmp[...])
    spread_g(0, query_grad_low)
    gain_part = jnp.sum(query_inputs * plain_scores + grad_inputs * plain_mixed, axis=0, keepdims=True)
    bias_part = jnp.sum(query_inputs * score_total + grad_inputs, axis=0, keepdims=True)
    cuts = [part[:, k * LANES : (k + 1) * LANES] for part in (gain_part, bias_part) for k in range(3)]
    shared = jnp.concatenate(cuts + [jnp.zeros((1, LANES), f32)], axis=0)
    times_t(query_grad_low, CQ, tmp)
    d_rows, lnvec[0:1, :], lnvec[1:2, :] = norm_gradient(to_float(latents[...]), gc[0:1], tmp[...])
    latent_grad[...] = act[GRAD] + d_rows
    lnvec[8:9, :] = jnp.sum(to_float(cotangent[...]), axis=0, keepdims=True)
    lines = regroup(lnvec[...])
    for peer in range(grid_cols):
        lnsend[peer] = jnp.concatenate(
            [lines[:11, peer * chunk : (peer + 1) * chunk], shared, jnp.zeros((6, LANES), f32)], axis=0
        )

    def send_ln(step, carry):
        peer, where = to_plane(step)
        push(lnsend.at[peer], lnbuf.at[j], misc_send.at[2], misc_recv.at[2], where)
        return carry

    lax.fori_loop(1, grid_cols, send_ln, 0)
    lnbuf[j] = lnsend[j]
    join(7)
    for block in range(0, blocks // 2):
        color_block(block)
    x_relay(xsmall.at[1, core], 9)
    have_x(0)
    right = have_g(0)
    bias_c2 = column_sum(right)
    weight_part(0, right, xbuf.at[0])
    for block in range(blocks // 2, blocks - 1):
        color_block(block)
    x_arrived(xsmall.at[1, 1 - core], 9)
    small_part(0, have_g(7), xsmall.at[1])
    color_block(blocks - 1)
    for m in (2, 1):
        join_small(m)

    for block in range(blocks):
        both = own_dot(fa[block], spread[...], 1, 0)
        center, factor = both[:, :LANES], both[:, LANES:]
        here = cgacc[block]
        cgacc[block, :, :LANES] = factor * (
            here[:, :LANES] - (to_float(fa[block]) - center) * factor * here[:, LANES:] * (1.0 / count)
        )
    for part in range(grid_rows):
        at = pl.ds(part * tile_rows, tile_rows)
        lines = jnp.concatenate([narrow(cgacc[block, at, :LANES]) for block in range(blocks)], axis=1)
        tiles = narrow(own_dot(back[...], lines, 1, 1))
        for tile in range(grid_cols):
            cgsend[tile, part, :, :tile_rows] = tiles[tile * 32 : tile * 32 + 32]
    cgbuf[j] = cgsend[j]

    def send_cg(step, carry):
        peer, where = to_plane(step)
        push(cgsend.at[peer], cgbuf.at[j], misc_send.at[3], misc_recv.at[3], where)
        return carry

    lax.fori_loop(1, grid_cols, send_cg, 0)

    wait_for(lnbuf.at[pl.ds(0, grid_cols - 1)], misc_recv.at[2])
    norms = lnbuf[0]
    for peer in range(1, grid_cols):
        norms = norms + lnbuf[peer]
    vecsend[...] = jnp.concatenate(
        [
            norms[:8], bias_c2, bias_c3, bias_c4, norms[10:11], norms[9:10], bias_s2, bias_s3,
            bias_s4, bias_s5, norms[8:9], jnp.zeros((6, chunk), f32), norms[11:18], jnp.zeros((1, chunk), f32),
        ],
        axis=0,
    )

    def send_vec(step, carry):
        where = {"rows": lax.rem(z + step, grid_rows)}
        push(vecsend, vecbuf.at[z], misc_send.at[4], misc_recv.at[4], where)
        return carry

    lax.fori_loop(1, grid_rows, send_vec, 0)
    vecbuf[z] = vecsend[...]
    join(0)
    join_small(0)
    wait_for(cgbuf.at[pl.ds(0, grid_cols - 1)], misc_recv.at[3])
    tiles = to_float(cgbuf[0])
    for peer in range(1, grid_cols):
        tiles = tiles + to_float(cgbuf[peer])
    cgsum[...] = tiles

    def send_tile(step, carry):
        part = lax.rem(z + step, grid_rows)
        push(cgsum.at[part], cgfin.at[z], misc_send.at[6], misc_recv.at[6], {"rows": part})
        return carry

    lax.fori_loop(1, grid_rows, send_tile, 0)
    cgfin[z] = cgsum[z]

    wait_for(vecbuf.at[pl.ds(0, grid_rows - 1)], misc_recv.at[4])
    vectors = vecbuf[0]
    for part in range(1, grid_rows):
        vectors = vectors + vecbuf[part]
    vector_out[...] = vectors[:24]
    input_vector_out[...] = vectors[24:]
    for m in (2, 1):
        line_total(m)
    for m in (7, 4, 5, 6, 9, 0):
        wait_for(crossed.at[slot_of(m)], f_recv.at[m])
        result = kept_of(m)[...] + to_float(crossed[slot_of(m)])
        kept_of(m)[...] = result
    wait_for(row_done.at[:, pl.ds(0, chunk * (grid_cols - 1))], a_recv.at[3])
    self_total[4] = row_done[...]
    sums = []
    for m in (2, 1, 0):
        wait_for(crossed_small.at[m], f_recv.at[10 + m])
        sums.append(kept_small[m] + to_float(crossed_small[m]))
    out_total[...] = own_dot(narrow(sums[0]), win[1], 1, 0)
    input_parts[1] = sums[1]
    input_parts[0] = sums[2]
    wait_for(cgfin.at[pl.ds(0, grid_rows - 1)], misc_recv.at[6])
    color_out[...] = cgfin[...]

    for k in (0, 3, 4, 5, 6):
        wait_for(xbuf.at[XS[k], 0, pl.ds(0, quads - 1)], x_send.at[k])
        wait_for(xbuf.at[XS[k], 0], y_send.at[k])
    wait_for(line_rows.at[pl.ds(0, grid_rows - 1)], x_send.at[1])
    for m in (1, 2):
        wait_for(line_right.at[m - 1, pl.ds(0, grid_rows - 1)], g_send.at[m])
        wait_for(line_near.at[m - 1], y_send.at[m])
        wait_for(line_sums.at[m - 1, pl.ds(0, quads - 1)], l_send.at[m - 1])
    for k in range(2):
        wait_for(xsmall.at[k, 0, pl.ds(0, quads - 1)], x_send.at[8 + k])
        wait_for(xsmall.at[k, 0], y_send.at[8 + k])
    for k in (0, 3, 4, 5, 6, 7, 8, 9, 10, 11):
        wait_for(gsrc.at[k, :, pl.ds(0, chunk * (grid_cols - 1))], g_send.at[k])
    wait_for(mix_s.at[pl.ds(0, grid_cols - 1)], a_send.at[0])
    wait_for(dmix_b.at[pl.ds(0, grid_cols - 1)], a_send.at[1])
    for kind in range(3):
        wait_for(dqkv_s.at[kind, pl.ds(0, grid_cols - 1)], a_send.at[7 + kind])
    wait_for(colbuf.at[pl.ds(0, grid_cols - 1)], misc_send.at[0])
    wait_for(row_turned.at[pl.ds(0, own * (grid_cols - 1))], a_send.at[3])
    wait_for(lnbuf.at[pl.ds(0, grid_cols - 1)], misc_send.at[2])
    wait_for(cgbuf.at[pl.ds(0, grid_cols - 1)], misc_send.at[3])
    wait_for(colstage.at[pl.ds(0, grid_rows - 1)], misc_send.at[5])
    wait_for(cgfin.at[pl.ds(0, grid_rows - 1)], misc_send.at[6])
    wait_for(row_pair, r_send.at[8])
    wait_for(row_hand, f_send.at[8])
    for m in (0, 4, 5, 6, 7, 9):
        wait_for(paired.at[slot_of(m)], r_send.at[m])
        wait_for(handed.at[slot_of(m)], f_send.at[m])
    for m in range(3):
        wait_for(paired_small.at[m], r_send.at[10 + m])
        wait_for(handed_small.at[m], f_send.at[10 + m])
    wait_for(vecbuf.at[pl.ds(0, grid_rows - 1)], misc_send.at[4])


def channel_order(count):
    n = NBANDS
    starts = ((5, n), (5 + 2 * n, n), (5 + n, n), (5 + 3 * n, n), (0, 5))
    order = np.concatenate([np.arange(start, start + size) for start, size in starts])
    result = np.zeros((WIDE, count), np.float32)
    result[np.arange(count), order] = 1
    return np.asarray(result, ml_dtypes.bfloat16)


def by_channel(lines):
    n = NBANDS
    parts = [lines[..., 4 * n : 4 * n + 5], lines[..., :n], lines[..., 2 * n : 3 * n]]
    parts += [lines[..., n : 2 * n], lines[..., 3 * n : 4 * n]]
    return jnp.concatenate(parts, axis=-1)


def finish_kernel(
    own, tile_rows, tile_cols,
    latents, latent_grad, colors, cross, out, self_parts, self_out, inputs, vectors, input_vectors,
    prior_cross, prior_out, prior_input,
    o_latents, o_latent_grad, o_colors, o_cross, o_out, o_input, o_gain, o_bias,
    o_cross_gains, o_cross_biases, o_self, o_self_out, o_self_gains, o_self_biases,
):
    o_latents[...] = latents[...]
    o_latent_grad[...] = latent_grad[...]
    for channel in range(3):
        for col in range(tile_cols):
            line = channel * tile_cols + col
            for image in range(colors.shape[0]):
                o_colors[channel, col, image : image + 1, :] = colors[image, line : line + 1, :tile_rows]
    o_cross[...] = prior_cross[...] + cross[...]
    o_out[...] = prior_out[...] + out[...]
    o_self[...] = self_parts[...]
    o_self_out[...] = self_out[...]
    for k in range(2):
        o_input[k] = prior_input[k] + by_channel(inputs[k])
    lines = input_vectors[...]
    for k, target in enumerate((o_gain, o_bias)):
        wide = jnp.concatenate([lines[3 * k + t : 3 * k + t + 1] for t in range(3)], axis=1)
        target[...] = by_channel(wide).reshape(-1)
    place = lax.axis_index("rows")
    width = vectors.shape[1]
    mine = pltpu.roll(vectors[...], lax.rem(width - place * own, width), 1)[:, :own]
    for target, rows in (
        (o_cross_gains, (0, 2)),
        (o_cross_biases, (1, 3, 8, 9, 10, 11, 12)),
        (o_self_gains, (4, 6)),
        (o_self_biases, (5, 7, 13, 14, 15, 16, 17)),
    ):
        for k, row in enumerate(rows):
            target[k : k + 1, :] = mine[row : row + 1]


def local_kernel(
    latents,
    pixel_colors,
    image_boxes,
    cotangent,
    cross_matrices,
    cross_out,
    input_matrices,
    in_gain,
    in_bias,
    cross_gains,
    cross_biases,
    self_matrices,
    self_out,
    self_gains,
    self_biases,
    prior_cross_matrices,
    prior_cross_out,
    prior_input_matrices,
):
    rows, width = latents.shape
    channels, image_count, tile_rows, tile_cols = pixel_colors.shape
    grid_rows = lax.axis_size("rows")
    grid_cols = lax.axis_size("cols")
    n_dev = grid_rows * grid_cols
    tall, wide = grid_rows * tile_rows, grid_cols * tile_cols
    steps = wide // 2
    chunk = width // grid_cols
    own = chunk // grid_rows
    quads = grid_cols // 2
    place, pick, spread, back = selections(tile_cols, grid_cols, steps)
    blocks = back.shape[1] // LANES
    held_rows = -(-steps // 8) * 8
    order = channel_order(input_matrices.shape[1])
    f32, bf16 = jnp.float32, jnp.bfloat16
    vmem = pl.BlockSpec(memory_space=pltpu.VMEM)
    away = pl.BlockSpec(memory_space=pl.ANY)
    shape = jax.ShapeDtypeStruct
    sizes = (grid_rows, grid_cols, rows, steps, tile_rows, tile_cols)
    dma = pltpu.SemaphoreType.DMA
    scratch = [
        ((10, width, width), bf16),
        ((2, WIDE, width), bf16),
        ((input_matrices.shape[1], 2, width), bf16),
        ((5, 2, quads, rows, width), bf16),
        ((2, 2, quads, rows, WIDE), bf16),
        ((13, rows, width), bf16),
        ((12, 2, quads, rows, chunk), bf16),
        ((7, chunk, width), bf16),
        ((7, 2, own, width), bf16),
        ((7, own, width), bf16),
        ((7, own, width), bf16),
        ((3, chunk, WIDE), bf16),
        ((3, 2, own, WIDE), bf16),
        ((3, own, WIDE), bf16),
        ((3, own, WIDE), bf16),
        ((3, own, WIDE), f32),
        ((grid_rows, rows, width), bf16),
        ((grid_rows, rows, width), bf16),
        ((2, grid_rows, rows, width // grid_rows), bf16),
        ((2, width // grid_rows, width), bf16),
        ((2, quads, own, width), bf16),
        ((2, quads, own, width), bf16),
        ((2, quads, own, width), bf16),
        ((2, chunk, width // grid_rows), bf16),
        ((chunk, width // grid_rows), bf16),
        ((chunk, width // grid_rows), bf16),
        ((chunk, width // grid_rows), f32),
        ((width // grid_rows, chunk), f32),
        ((own, width), f32),
        ((8, width), f32),
        ((grid_rows, 32, LANES), f32),
        ((grid_rows, 32, LANES), bf16),
        ((grid_rows, 32, LANES), bf16),
        ((grid_cols, grid_rows, 32, LANES), bf16),
        ((tall, WIDE), f32),
        ((tall, 7 * LANES), bf16),
        ((blocks, tall, LANES), bf16),
        ((blocks * LANES, tall), bf16),
        ((steps, tall, LANES), f32),
        ((tall, LANES), f32),
        ((held_rows, LANES), f32),
        ((tall, 2 * LANES), bf16),
        ((2, held_rows, 2 * LANES), bf16),
        ((STEPS_HELD, LANES, 2 * LANES), bf16),
        ((STEPS_HELD // 2, 2 * WIDE, 2 * LANES), bf16),
        ((tall, LANES), f32),
        ((held_rows, LANES), f32),
        ((blocks, tall, 2 * LANES), f32),
        ((grid_cols, grid_rows, 32, LANES), bf16),
        ((grid_cols, grid_rows, 32, LANES), bf16),
        ((grid_rows, 32, LANES), f32),
        ((grid_rows, 32, LANES), f32),
        ((9, rows, width), f32),
        ((16, width), f32),
        ((grid_cols, 24, chunk), f32),
        ((grid_cols, 24, chunk), f32),
        ((8, width), f32),
        ((32, chunk), f32),
        ((grid_rows, 32, chunk), f32),
        ((3, grid_cols, rows, chunk), bf16),
        ((grid_cols * rows, grid_cols * rows), f32),
        ((2, grid_cols * rows, grid_cols * rows), bf16),
        ((grid_cols, rows, chunk), bf16),
        ((rows, width), bf16),
        ((grid_cols, rows, chunk), bf16),
        ((3, grid_cols, rows, chunk), bf16),
        ((3, rows, width), bf16),
    ]
    fixed = (order, place, pick, spread, back)
    scratch = [(values.shape, bf16) for values in fixed] + scratch
    scratch = [pltpu.VMEM(dims, kind) for dims, kind in scratch]
    scratch += [dma((count,)) for count in (5, 11, 10, 10, 10, 10, 12, 12, 10, 10, 13, 13, 13, 13, 2, 2, 7, 7)]
    outs = [
        ((rows, width), bf16),
        ((rows, width), f32),
        ((image_count, 32, LANES), f32),
        ((3, own, width), f32),
        ((own, width), f32),
        ((5, own, width), f32),
        ((own, width), f32),
        ((2, own, WIDE), f32),
        ((24, chunk), f32),
        ((8, LANES), f32),
    ]
    results = pl.pallas_call(
        functools.partial(layer_kernel, sizes),
        out_shape=[shape(dims, kind) for dims, kind in outs],
        in_specs=[pl.BlockSpec(memory_space=pltpu.SMEM)] + [vmem] * 9 + [away] * 10,
        out_specs=[vmem] * len(outs),
        scratch_shapes=scratch,
        compiler_params=pltpu.CompilerParams(
            collective_id=0, has_side_effects=True, vmem_limit_bytes=VMEM_BYTES
        ),
        cost_estimate=pl.CostEstimate(
            flops=20_000_000_000, bytes_accessed=40_000_000, transcendentals=4_000_000
        ),
    )(
        image_boxes,
        latents,
        cotangent,
        jnp.transpose(pixel_colors, (0, 3, 1, 2)),
        in_gain,
        in_bias,
        cross_gains,
        cross_biases,
        self_gains,
        self_biases,
        *fixed,
        cross_matrices,
        cross_out,
        self_matrices,
        self_out,
        jnp.transpose(input_matrices, (1, 0, 2)),
    )
    count = input_matrices.shape[1]
    last = [
        ((rows, width), bf16),
        ((rows, width), f32),
        ((channels, tile_cols, image_count, tile_rows), f32),
        ((3, own, width), f32),
        ((own, width), f32),
        ((2, own, count), f32),
        ((count,), f32),
        ((count,), f32),
        ((2, own), f32),
        ((7, own), f32),
        ((5, own, width), f32),
        ((own, width), f32),
        ((2, own), f32),
        ((7, own), f32),
    ]
    done = pl.pallas_call(
        functools.partial(finish_kernel, own, tile_rows, tile_cols),
        out_shape=[shape(dims, kind) for dims, kind in last],
        in_specs=[vmem] * (len(outs) + 3),
        out_specs=[vmem] * len(last),
        compiler_params=pltpu.CompilerParams(vmem_limit_bytes=VMEM_BYTES),
    )(
        *results,
        jnp.transpose(prior_cross_matrices, (0, 2, 1)),
        jnp.transpose(prior_cross_out),
        jnp.transpose(prior_input_matrices, (0, 2, 1)),
    )
    (new_latents, latent_grad, colors, cross_total, out_total, input_total, gain, bias) = done[:8]
    cross_gain, cross_bias, self_total, self_out_total, self_gain, self_bias = done[8:]
    return (
        new_latents,
        latent_grad,
        jnp.transpose(colors, (0, 2, 3, 1)),
        jnp.transpose(cross_total, (0, 2, 1)),
        jnp.transpose(out_total),
        jnp.transpose(input_total, (0, 2, 1)),
        gain,
        bias,
        cross_gain,
        cross_bias,
        jnp.transpose(self_total, (0, 2, 1)),
        jnp.transpose(self_out_total),
        self_gain,
        self_bias,
    )


def solution(mesh):
    placed = (
        P(("rows", "cols"), None),
        P(None, None, "rows", "cols"),
        P(),
        P(("rows", "cols"), None),
        P(),
        P(),
        P(),
        P(),
        P(),
        P(),
        P(),
        P(),
        P(),
        P(),
        P(),
        P(None, None, ("rows", "cols")),
        P(None, ("rows", "cols")),
        P(None, None, ("rows", "cols")),
    )
    one_head_each = mesh.shape["cols"] == HEADS
    return jax.shard_map(
        local_kernel if one_head_each else local,
        mesh=mesh,
        in_specs=placed,
        out_specs=(
            P(("rows", "cols"), None),
            P(("rows", "cols"), None),
            P(None, None, "rows", "cols"),
            P(None, None, ("rows", "cols")),
            P(None, ("rows", "cols")),
            P(None, None, ("rows", "cols")),
            P(),
            P(),
            P(None, ("rows", "cols")),
            P(None, ("rows", "cols")),
            P(None, None, ("rows", "cols")),
            P(None, ("rows", "cols")),
            P(None, ("rows", "cols")),
            P(None, ("rows", "cols")),
        ),
        check_vma=False,
    )
```

```python
import functools

import jax
import jax.numpy as jnp
import ml_dtypes
import numpy as np
from jax import lax
from jax.experimental import pallas as pl
from jax.experimental.pallas import tpu as pltpu
from jax.sharding import PartitionSpec as P

HEADS = 8
LATENTS = 512
NBANDS = 64
HEAD_DIM = 128


EPS = 1e-05
NEG = -1e30
FREQ_TOP = 112.0
VMEM_BYTES = 63 * 1024 * 1024
PLAN = {0: ((4, 4),), 2: ((3, 2),), 4: ((3, 2),), 9: ((5, 4),)}


def narrow(values):
    return values.astype(jnp.bfloat16)


def to_float(values):
    return values.astype(jnp.float32)


def matmul(former, latter):
    return jnp.dot(former, latter, preferred_element_type=jnp.float32)


def inner_left(former, latter):
    return lax.dot_general(
        former, latter, (((0,), (0,)), ((), ())), preferred_element_type=jnp.float32
    )


def inner_right(former, latter):
    return lax.dot_general(
        former, latter, (((1,), (1,)), ((), ())), preferred_element_type=jnp.float32
    )


def layer_norm(values, gain, offset):
    middle = jnp.mean(values, axis=-1, keepdims=True)
    centered = values - middle
    spread = jnp.mean(centered * centered, axis=-1, keepdims=True)
    return centered * lax.rsqrt(spread + EPS) * gain + offset


def norm_back(values, gain, offset, gradient):
    result, pullback = jax.vjp(layer_norm, values, gain, offset)
    return pullback(gradient)


def gelu_tanh(values):
    return jax.nn.gelu(values, approximate=True)


def gelu_back(pre_gelu, gradient):
    result, pullback = jax.vjp(gelu_tanh, pre_gelu)
    return pullback(gradient)[0]


def axis_features(places, extent):
    frequency = 1.0 + jnp.arange(NBANDS, dtype=jnp.float32) * ((FREQ_TOP - 1.0) / (NBANDS - 1))
    angle = jnp.pi * places[:, None] * frequency[None, :]
    return (places, jnp.sin(angle), jnp.cos(angle))


def canvas_of(colors, image_box):
    channels, wide, tall = colors.shape
    top, left, height, width = image_box[0], image_box[1], image_box[2], image_box[3]
    row_at = jnp.arange(tall, dtype=jnp.int32)
    col_at = jnp.arange(wide, dtype=jnp.int32)
    y_place = -1.0 + 2.0 * to_float(row_at - top) / to_float(height - 1)
    x_place = -1.0 + 2.0 * to_float(col_at - left) / to_float(width - 1)
    y_parts = axis_features(y_place, height)
    x_parts = axis_features(x_place, width)
    y_all = jnp.concatenate([y_parts[0][:, None], y_parts[1], y_parts[2]], axis=1)
    x_all = jnp.concatenate([x_parts[0][:, None], x_parts[1], x_parts[2]], axis=1)
    count = channels + 2 + 4 * NBANDS
    color_sum = jnp.sum(colors, axis=0)
    color_square = jnp.sum(colors * colors, axis=0)
    mean = (color_sum + jnp.sum(y_all, axis=1)[None, :] + jnp.sum(x_all, axis=1)[:, None]) / count
    square = (
        color_square
        + jnp.sum(y_all * y_all, axis=1)[None, :]
        + jnp.sum(x_all * x_all, axis=1)[:, None]
    ) / count
    deviation = lax.rsqrt(square - mean * mean + EPS)
    row_in = (row_at >= top) & (row_at < top + height)
    col_in = (col_at >= left) & (col_at < left + width)
    return (y_all, x_all, mean, deviation, row_in, col_in)


def split_channels(rows, channels):
    n = NBANDS
    c = channels
    y_part = jnp.concatenate(
        [rows[:, c : c + 1], rows[:, c + 2 : c + 2 + n], rows[:, c + 2 + 2 * n : c + 2 + 3 * n]],
        axis=1,
    )
    x_part = jnp.concatenate(
        [
            rows[:, c + 1 : c + 2],
            rows[:, c + 2 + n : c + 2 + 2 * n],
            rows[:, c + 2 + 3 * n : c + 2 + 4 * n],
        ],
        axis=1,
    )
    return (rows[:, :c], y_part, x_part)


def join_channels(color_part, y_part, x_part):
    n = NBANDS
    return jnp.concatenate(
        [
            color_part,
            y_part[:, :1],
            x_part[:, :1],
            y_part[:, 1 : n + 1],
            x_part[:, 1 : n + 1],
            y_part[:, n + 1 :],
            x_part[:, n + 1 :],
        ],
        axis=1,
    )


def against_pixels(rows, colors, canvas):
    y_all, x_all, mean, deviation = canvas[:4]
    color_part, y_part, x_part = split_channels(rows, colors.shape[0])
    by_row = inner_right(narrow(y_part), narrow(y_all))
    by_col = inner_right(narrow(x_part), narrow(x_all))
    total = by_row[:, None, :] + by_col[:, :, None]
    for j in range(colors.shape[0]):
        total = total + color_part[:, j][:, None, None] * colors[j][None]
    total = total - jnp.sum(rows, axis=1)[:, None, None] * mean[None]
    return total * deviation[None]


def over_pixels(weights, colors, canvas):
    y_all, x_all, mean, deviation = canvas[:4]
    scaled = weights * deviation[None]
    y_part = matmul(narrow(jnp.sum(scaled, axis=1)), narrow(y_all))
    x_part = matmul(narrow(jnp.sum(scaled, axis=2)), narrow(x_all))
    color_part = jnp.stack(
        [jnp.sum(scaled * colors[j][None], axis=(1, 2)) for j in range(colors.shape[0])], axis=1
    )
    middle = jnp.sum(scaled * mean[None], axis=(1, 2))
    return join_channels(color_part, y_part, x_part) - middle[:, None]


def mlp_forward(row_values, gain, offset, w_in, b_in, w_out, b_out):
    normed = narrow(layer_norm(row_values, gain, offset))
    pre_gelu = matmul(normed, w_in) + b_in
    hidden = narrow(gelu_tanh(pre_gelu))
    return (matmul(hidden, w_out) + b_out, (normed, pre_gelu, hidden))


def mlp_backward(row_values, gain, offset, w_in, w_out, stored, gradient):
    normed, pre_gelu, hidden = stored
    grad_low = narrow(gradient)
    d_w_out = inner_left(hidden, grad_low)
    d_b_out = jnp.sum(gradient, axis=0)
    d_pre = gelu_back(pre_gelu, inner_right(grad_low, w_out))
    pre_low = narrow(d_pre)
    d_w_in = inner_left(normed, pre_low)
    d_b_in = jnp.sum(d_pre, axis=0)
    d_rows, d_gain, d_offset = norm_back(row_values, gain, offset, inner_right(pre_low, w_in))
    return (
        gradient + d_rows,
        (d_w_in, d_w_out),
        (d_gain, d_offset, d_b_in, d_b_out),
        (pre_low, grad_low),
    )


def local(
    latents,
    pixel_colors,
    image_boxes,
    cotangent,
    cross_matrices,
    cross_out,
    input_matrices,
    in_gain,
    in_bias,
    cross_gains,
    cross_biases,
    self_matrices,
    self_out,
    self_gains,
    self_biases,
    prior_cross_matrices,
    prior_cross_out,
    prior_input_matrices,
):
    rows_dev = latents.shape[0]
    model_width = latents.shape[1]
    image_count = image_boxes.shape[0]
    tile_rows = pixel_colors.shape[2]
    tile_cols = pixel_colors.shape[3]
    input_width = input_matrices.shape[1]
    grid_rows = lax.axis_size("rows")
    grid_cols = lax.axis_size("cols")
    all_rows = rows_dev * grid_rows * grid_cols
    row_place = lax.axis_index("rows")
    col_place = lax.axis_index("cols")
    row_start = row_place * tile_rows
    col_start = col_place * tile_cols
    score_scale = model_width ** (-0.5)
    head_scale = HEAD_DIM ** (-0.5)
    g_cross = to_float(cross_gains)
    b_cross = to_float(cross_biases)
    g_self = to_float(self_gains)
    b_self = to_float(self_biases)
    g_input = to_float(in_gain)
    b_input = to_float(in_bias)
    latent_state = to_float(latents)
    normed_q = narrow(layer_norm(latent_state, g_cross[0], b_cross[0]))
    query_rows = narrow(matmul(normed_q, cross_matrices[0]) + b_cross[2])
    colors_low = lax.all_gather(pixel_colors, ("rows", "cols"), axis=0, tiled=False)
    colors_low = lax.dynamic_index_in_dim(colors_low, row_place, axis=2, keepdims=False)
    colors_low = colors_low.reshape(grid_rows, grid_cols, 3, tile_rows, tile_cols)
    colors = to_float(
        jnp.transpose(colors_low, (2, 1, 4, 0, 3)).reshape(
            3, grid_cols * tile_cols, grid_rows * tile_rows
        )
    )
    image_box = lax.dynamic_index_in_dim(image_boxes, row_place, axis=0, keepdims=False)
    canvas = canvas_of(colors, image_box)
    mean, deviation, row_in, col_in = canvas[2:]
    inside = (col_in[:, None] & row_in[None, :])[None]
    key_weight = input_matrices[0]
    value_weight = input_matrices[1]
    query_inputs = inner_right(query_rows, key_weight)
    query_lines = against_pixels(query_inputs * g_input, colors, canvas)
    query_shift = jnp.sum(query_inputs * b_input, axis=1)
    scores = jnp.where(
        inside, (query_lines + query_shift[:, None, None]) * score_scale, NEG
    )
    peak_score = jnp.max(scores, axis=(1, 2), keepdims=True)
    weights = jnp.where(inside, jnp.exp(scores - peak_score), 0.0)
    cross_probs = weights / jnp.sum(weights, axis=(1, 2), keepdims=True)
    plain_mixed = over_pixels(cross_probs, colors, canvas)
    mixed_inputs = (
        plain_mixed * g_input + jnp.sum(cross_probs, axis=(1, 2))[:, None] * b_input
    )
    mixed_low = narrow(mixed_inputs)
    attended = matmul(mixed_low, value_weight) + b_cross[3]
    attended_low = narrow(attended)
    first = latent_state + matmul(attended_low, cross_out) + b_cross[4]
    branch, cross_stored = mlp_forward(
        first, g_cross[1], b_cross[1], cross_matrices[1], b_cross[5], cross_matrices[2], b_cross[6]
    )
    second = first + branch
    normed_t = narrow(layer_norm(second, g_self[0], b_self[0]))
    tower_queries = narrow(matmul(normed_t, self_matrices[0]) + b_self[2])
    tower_keys = narrow(matmul(normed_t, self_matrices[1]))
    tower_values = narrow(matmul(normed_t, self_matrices[2]) + b_self[3])
    keys_group, values_group = (
        lax.all_gather(tower_keys, "cols", axis=0, tiled=True),
        lax.all_gather(tower_values, "cols", axis=0, tiled=True),
    )
    group_rows = keys_group.shape[0]
    query_image = (
        (row_place * grid_cols + col_place) * rows_dev + jnp.arange(rows_dev, dtype=jnp.int32)
    ) // LATENTS
    key_image = (row_place * group_rows + jnp.arange(group_rows, dtype=jnp.int32)) // LATENTS
    same_image = (query_image[:, None] == key_image[None, :])[None]
    query_heads = tower_queries.reshape(rows_dev, HEADS, HEAD_DIM)
    key_heads = keys_group.reshape(group_rows, HEADS, HEAD_DIM)
    value_heads = values_group.reshape(group_rows, HEADS, HEAD_DIM)
    head_scores = jnp.where(
        same_image,
        jnp.einsum("qhd,khd->hqk", query_heads, key_heads, preferred_element_type=jnp.float32)
        * head_scale,
        NEG,
    )
    head_weights = jnp.where(
        same_image, jnp.exp(head_scores - jnp.max(head_scores, axis=2, keepdims=True)), 0.0
    )
    head_probs = head_weights / jnp.sum(head_weights, axis=2, keepdims=True)
    probs_low = narrow(head_probs)
    tower_mixed = narrow(
        jnp.einsum(
            "hqk,khd->qhd", probs_low, value_heads, preferred_element_type=jnp.float32
        ).reshape(rows_dev, model_width)
    )
    third = second + matmul(tower_mixed, self_out) + b_self[4]
    branch, tower_stored = mlp_forward(
        third, g_self[1], b_self[1], self_matrices[3], b_self[5], self_matrices[4], b_self[6]
    )
    new_latents = narrow(third + branch)
    gradient = to_float(cotangent)
    gradient, tower_mlp_w, tower_mlp_v, tower_lows = mlp_backward(
        third, g_self[1], b_self[1], self_matrices[3], self_matrices[4], tower_stored, gradient
    )
    tower_out_low = narrow(gradient)
    d_self_out = inner_left(tower_mixed, tower_out_low)
    d_self_out_bias = jnp.sum(gradient, axis=0)
    d_mixed = narrow(inner_right(tower_out_low, self_out)).reshape(rows_dev, HEADS, HEAD_DIM)
    d_probs = jnp.einsum("qhd,khd->hqk", d_mixed, value_heads, preferred_element_type=jnp.float32)
    d_value_heads = jnp.einsum(
        "hqk,qhd->khd", probs_low, d_mixed, preferred_element_type=jnp.float32
    )
    d_scores = head_probs * (d_probs - jnp.sum(head_probs * d_probs, axis=2, keepdims=True))
    d_scores_low = narrow(d_scores * head_scale)
    d_query_heads = jnp.einsum(
        "hqk,khd->qhd", d_scores_low, key_heads, preferred_element_type=jnp.float32
    ).reshape(rows_dev, model_width)
    d_key_heads = jnp.einsum(
        "hqk,qhd->khd", d_scores_low, query_heads, preferred_element_type=jnp.float32
    )
    d_tower_keys, d_tower_values = (
        lax.psum_scatter(
            d_key_heads.reshape(group_rows, model_width).astype(jnp.bfloat16),
            "cols",
            scatter_dimension=0,
            tiled=True,
        ).astype(jnp.float32),
        lax.psum_scatter(
            d_value_heads.reshape(group_rows, model_width).astype(jnp.bfloat16),
            "cols",
            scatter_dimension=0,
            tiled=True,
        ).astype(jnp.float32),
    )
    tq_low = narrow(d_query_heads)
    tk_low = narrow(d_tower_keys)
    tv_low = narrow(d_tower_values)
    d_normed_t = (
        inner_right(tq_low, self_matrices[0])
        + inner_right(tk_low, self_matrices[1])
        + inner_right(tv_low, self_matrices[2])
    )
    d_second, d_self_gain, d_self_bias = norm_back(second, g_self[0], b_self[0], d_normed_t)
    gradient = gradient + d_second
    self_gain_grad = jnp.stack([d_self_gain, tower_mlp_v[0]])
    self_bias_grad = jnp.stack(
        [
            d_self_bias,
            tower_mlp_v[1],
            jnp.sum(d_query_heads, axis=0),
            jnp.sum(d_tower_values, axis=0),
            d_self_out_bias,
            tower_mlp_v[2],
            tower_mlp_v[3],
        ]
    )
    gradient, cross_mlp_w, cross_mlp_v, cross_lows = mlp_backward(
        first, g_cross[1], b_cross[1], cross_matrices[1], cross_matrices[2], cross_stored, gradient
    )
    cross_out_low = narrow(gradient)
    d_cross_out = inner_left(attended_low, cross_out_low)
    d_cross_out_bias = jnp.sum(gradient, axis=0)
    d_attended = narrow(inner_right(cross_out_low, cross_out))
    value_shift = jnp.sum(to_float(d_attended) * b_cross[3], axis=1)
    row_delta = jnp.sum(to_float(d_attended) * attended, axis=1) - value_shift
    grad_inputs = inner_right(d_attended, value_weight)
    grad_shift = jnp.sum(grad_inputs * b_input, axis=1)
    grad_lines = against_pixels(grad_inputs * g_input, colors, canvas)
    d_scores = (
        cross_probs * (grad_lines + (grad_shift - row_delta)[:, None, None]) * score_scale
    )
    plain_scores = over_pixels(d_scores, colors, canvas)
    score_sum = jnp.sum(d_scores, axis=(1, 2))
    prob_sum = jnp.sum(cross_probs, axis=(1, 2))
    score_inputs = plain_scores * g_input + score_sum[:, None] * b_input
    score_low = narrow(score_inputs)
    d_query_rows = matmul(score_low, key_weight)
    in_gain_part = jnp.sum(query_inputs * plain_scores + grad_inputs * plain_mixed, axis=0)
    in_bias_part = jnp.sum(
        query_inputs * score_sum[:, None] + grad_inputs * prob_sum[:, None], axis=0
    )
    query_scaled = query_inputs * g_input
    grad_scaled = grad_inputs * g_input
    query_away = query_scaled[:, :3] - jnp.mean(query_scaled, axis=1, keepdims=True)
    grad_away = grad_scaled[:, :3] - jnp.mean(grad_scaled, axis=1, keepdims=True)
    along = jnp.sum(d_scores * query_lines + cross_probs * grad_lines, axis=0) / input_width
    color_parts = jnp.einsum(
        "rj,rcy->jcy", query_away, d_scores, precision=lax.Precision.HIGHEST
    ) + jnp.einsum("rj,rcy->jcy", grad_away, cross_probs, precision=lax.Precision.HIGHEST)
    color_parts = deviation[None] * (
        color_parts - (colors - mean[None]) * deviation[None] * along[None]
    )
    color_parts = color_parts.reshape(3, grid_cols, tile_cols, grid_rows, tile_rows)
    color_parts = jnp.transpose(color_parts, (3, 1, 0, 4, 2)).reshape(
        grid_rows * grid_cols, 3, tile_rows, tile_cols
    )
    color_grad = lax.all_to_all(
        color_parts, ("rows", "cols"), split_axis=0, concat_axis=0, tiled=True
    ).reshape(image_count, grid_cols, 3, tile_rows, tile_cols)
    color_grad = jnp.transpose(jnp.sum(color_grad, axis=1), (1, 0, 2, 3))
    query_low = narrow(d_query_rows)
    d_latent, d_cross_gain, d_cross_bias = norm_back(
        latent_state, g_cross[0], b_cross[0], inner_right(query_low, cross_matrices[0])
    )
    latent_grad = gradient + d_latent
    in_gain_grad, in_bias_grad = lax.psum((in_gain_part, in_bias_part), ("rows", "cols"))
    vectors = jnp.stack(
        [
            d_cross_gain,
            cross_mlp_v[0],
            d_cross_bias,
            cross_mlp_v[1],
            jnp.sum(d_query_rows, axis=0),
            jnp.sum(to_float(d_attended), axis=0),
            d_cross_out_bias,
            cross_mlp_v[2],
            cross_mlp_v[3],
            d_self_gain,
            tower_mlp_v[0],
            d_self_bias,
            tower_mlp_v[1],
            jnp.sum(d_query_heads, axis=0),
            jnp.sum(d_tower_values, axis=0),
            d_self_out_bias,
            tower_mlp_v[2],
            tower_mlp_v[3],
        ]
    )
    vector_sums = lax.psum_scatter(vectors, ("rows", "cols"), scatter_dimension=1, tiled=True)
    lefts = jnp.stack(
        [
            normed_q,
            cross_stored[0],
            cross_stored[2],
            attended_low,
            normed_t,
            tower_stored[0],
            tower_stored[2],
            tower_mixed,
        ]
    )
    rights = jnp.stack(
        [
            query_low,
            cross_lows[0],
            cross_lows[1],
            cross_out_low,
            d_attended,
            query_rows,
            tq_low,
            tk_low,
            tv_low,
            tower_lows[0],
            tower_lows[1],
            tower_out_low,
        ]
    )
    small_lefts = jnp.stack([mixed_low, score_low])
    lefts = lax.all_gather(lefts, "cols", axis=1, tiled=True)
    small_lefts = lax.all_gather(small_lefts, "cols", axis=1, tiled=True)
    own = model_width // (grid_rows * grid_cols)
    rights = rights.reshape(rights.shape[0], rows_dev, grid_rows, grid_cols, own)
    rights = lax.all_to_all(
        jnp.transpose(rights, (3, 0, 1, 2, 4)), "cols", split_axis=0, concat_axis=0, tiled=False
    )
    rights = jnp.transpose(rights, (1, 0, 2, 3, 4)).reshape(
        rights.shape[1], grid_cols * rows_dev, grid_rows * own
    )
    pairs = ((0, 0), (1, 1), (2, 2), (3, 3), (4, 6), (4, 7), (4, 8), (5, 9), (6, 10), (7, 11))
    big = [inner_left(rights[k], lefts[i]).reshape(grid_rows, own, model_width) for i, k in pairs]
    small = [
        inner_left(rights[k], small_lefts[i]).reshape(grid_rows, own, input_width)
        for i, k in ((1, 5), (0, 4))
    ]
    big = lax.psum_scatter(jnp.stack(big, axis=1), "rows", scatter_dimension=0, tiled=False)
    small = lax.psum_scatter(jnp.stack(small, axis=1), "rows", scatter_dimension=0, tiled=False)
    big = jnp.transpose(big, (0, 2, 1))
    small = jnp.transpose(small, (0, 2, 1))
    all_sums = (
        big[:3],
        big[3],
        small,
        vector_sums[:2],
        vector_sums[2:9],
        big[4:9],
        big[9],
        vector_sums[9:11],
        vector_sums[11:],
    )
    cross_sums = all_sums[:5]
    self_sums = all_sums[5:]
    return (
        new_latents,
        latent_grad,
        color_grad,
        prior_cross_matrices + cross_sums[0],
        prior_cross_out + cross_sums[1],
        prior_input_matrices + cross_sums[2],
        in_gain_grad,
        in_bias_grad,
        cross_sums[3],
        cross_sums[4],
        self_sums[0],
        self_sums[1],
        self_sums[2],
        self_sums[3],
    )


STEPS_HELD = 8
GROUP = 12
XS = {0: 0, 3: 1, 4: 2, 5: 3, 6: 4}
LANES = 128
MESH = pl.DeviceIdType.MESH
WIDE = 3 * LANES


def own_dot(former, latter, former_dim, latter_dim):
    return lax.dot_general(
        former,
        latter,
        (((former_dim,), (latter_dim,)), ((), ())),
        preferred_element_type=jnp.float32,
    )


def selections(tile_cols, grid_cols, steps):
    held = STEPS_HELD
    blocks = -(-steps // held)
    place = np.zeros((grid_cols * 32, WIDE), np.float32)
    back = np.zeros((grid_cols * 32, blocks * LANES), np.float32)
    for tile in range(grid_cols):
        for channel in range(3):
            for offset in range(tile_cols):
                col = tile * tile_cols + offset
                line = tile * 32 + channel * tile_cols + offset
                place[line, channel * LANES + col] = 1
                half, step = divmod(col, steps)
                back[line, step * 16 + half * 8 + channel] = 1
    pick = np.zeros((7 * LANES, blocks * LANES), np.float32)
    for step in range(steps):
        for half in range(2):
            for slot, kind in enumerate((0, 1, 2, 3, 4, 3, 5, 6)):
                pick[kind * LANES + half * steps + step, step * 16 + half * 8 + slot] = 1
    spread = np.zeros((LANES, 2 * LANES), np.float32)
    for group in range(16):
        for channel in range(3):
            for slot in (3, 4):
                spread[group * 8 + slot, group * 8 + channel] = 1
            for slot in (6, 7):
                spread[group * 8 + slot, LANES + group * 8 + channel] = 1
    low = lambda values: np.asarray(values, ml_dtypes.bfloat16)
    return (low(place), low(pick), low(spread), low(back))


def norm_parts(values):
    middle = jnp.mean(values, axis=1, keepdims=True)
    centered = values - middle
    spread = jnp.mean(centered * centered, axis=1, keepdims=True)
    factor = lax.rsqrt(spread + EPS)
    return (centered * factor, factor)


def norm_forward(values, gain, offset):
    return narrow(norm_parts(values)[0] * gain + offset)


def norm_gradient(values, gain, gradient):
    plain, factor = norm_parts(values)
    inner = gradient * gain
    first = jnp.mean(inner, axis=1, keepdims=True)
    second = jnp.mean(inner * plain, axis=1, keepdims=True)
    return (
        factor * (inner - first - plain * second),
        jnp.sum(gradient * plain, axis=0, keepdims=True),
        jnp.sum(gradient, axis=0, keepdims=True),
    )


GELU_RATE = 0.7978845608028654
GELU_CUBE = 0.044715


def gelu_value(u):
    return 0.5 * u * (1.0 + jnp.tanh(GELU_RATE * (u + GELU_CUBE * u * u * u)))


def gelu_slope(u):
    bent = jnp.tanh(GELU_RATE * (u + GELU_CUBE * u * u * u))
    return 0.5 * (1.0 + bent) + 0.5 * u * (1.0 - bent * bent) * GELU_RATE * (
        1.0 + 3.0 * GELU_CUBE * u * u
    )


def waves(turns):
    near = turns - 2.0 * jnp.floor(turns * 0.5 + 0.5)
    return (jnp.sin(jnp.pi * near), jnp.cos(jnp.pi * near))


def axis_lines(place, slot):
    lane = lax.broadcasted_iota(jnp.int32, (place.shape[0], LANES), 1)
    band = lax.rem(lane, NBANDS)
    frequency = 1.0 + to_float(band) * ((FREQ_TOP - 1.0) / (NBANDS - 1))
    sine, cosine = waves(place * frequency)
    return jnp.concatenate(
        [jnp.where(lane < NBANDS, sine, cosine), jnp.where(lane == slot, place, 0.0)], axis=1
    )


def layer_kernel(
    sizes,
    boxes, latents, cotangent, colors, in_gain, in_bias, cross_gains, cross_biases, self_gains,
    self_biases, far_order, far_place, far_pick, far_spread, far_back,
    w_cross, w_out, w_self, w_self_out, w_input,
    new_latents, latent_grad, color_out, cross_total, out_total, self_total, self_out_total,
    input_parts, vector_out, input_vector_out,
    order, place, pick, spread, back, wts, win, win_raw, xbuf, xsmall, gsrc, gbuf, staged, paired, handed, crossed, staged_small, paired_small, handed_small, crossed_small, kept_small,
    line_rows, line_hid, line_right, line_staged, line_near, line_hand, line_sums,
    row_pair, row_hand, row_cross, row_kept, row_turned, row_done, biases,
    color_tiles, colstage, colbuf, img, img7, fa, ft, sl, ycoef, xcoef, yfeat, xfeat, mixrow,
    cgright, rowsum, colsum, cgacc, cgsend, cgbuf, cgsum, cgfin,
    act, lnvec, lnsend, lnbuf, vecsend, vecbuf,
    heads, probs, prob_grad, mix_s, mix_b, dmix_b, dqkv_s, dqkv_b,
    fixed_sem, weight_sem, x_send, x_recv, y_send, y_recv, g_send, g_recv, a_send, a_recv, r_send, r_recv, f_send, f_recv, l_send, l_recv,
    misc_send, misc_recv,
):
    grid_rows, grid_cols, rows, steps, tile_rows, tile_cols = sizes
    n_dev = grid_rows * grid_cols
    width = latents.shape[1]
    quads = grid_cols // 2
    chunk = width // grid_cols
    own = chunk // grid_rows
    tall = grid_rows * tile_rows
    z = lax.axis_index("rows")
    j = lax.axis_index("cols")
    core = lax.rem(j, 2)
    quad = j // 2
    me = z * grid_cols + j
    f32, bf16 = jnp.float32, jnp.bfloat16
    score_scale = width ** (-0.5)
    head_scale = HEAD_DIM ** (-0.5)

    def at_device(d):
        return {"rows": d // grid_cols, "cols": lax.rem(d, grid_cols)}

    def lanes_of(index):
        return pl.ds(pl.multiple_of(index * chunk, chunk), chunk)

    def push(src, dst, send, recv, where):
        pltpu.make_async_remote_copy(
            src_ref=src, dst_ref=dst, send_sem=send, recv_sem=recv, device_id=where,
            device_id_type=MESH,
        ).start()

    def wait_for(ref, sem):
        pltpu.make_async_copy(ref, ref, sem).wait()

    barrier = pltpu.get_barrier_semaphore()

    def greet_plane(step, carry):
        where = {"cols": lax.rem(j + step, grid_cols)}
        pl.semaphore_signal(barrier, inc=1, device_id=where, device_id_type=MESH)
        return carry

    def greet_line(step, carry):
        where = {"rows": lax.rem(z + step, grid_rows)}
        pl.semaphore_signal(barrier, inc=1, device_id=where, device_id_type=MESH)
        return carry

    lax.fori_loop(1, grid_rows, greet_line, 0)
    lax.fori_loop(1, grid_cols, greet_plane, 0)

    sources = (
        [w_cross.at[0], w_out, w_cross.at[1], w_cross.at[2]]
        + [w_self.at[0], w_self.at[1], w_self.at[2], w_self_out, w_self.at[3], w_self.at[4]]
    )
    CQ, CO, C1, C2, SQ, SK, SV, SO, S1, S2 = range(10)
    loads = [pltpu.make_async_copy(s, wts.at[k], weight_sem.at[k]) for k, s in enumerate(sources)]
    loads.append(pltpu.make_async_copy(w_input, win_raw, weight_sem.at[10]))
    loads[CQ].start()
    loads[10].start()
    fixed = ((far_order, order), (far_place, place), (far_pick, pick), (far_spread, spread), (far_back, back))
    fixed = [pltpu.make_async_copy(src, dst, fixed_sem.at[k]) for k, (src, dst) in enumerate(fixed)]
    for copy in fixed:
        copy.start()

    cgsum[...] = jnp.zeros(cgsum.shape, f32)
    for channel in range(3):
        for col in range(tile_cols):
            line = channel * tile_cols + col
            shown = to_float(colors[channel, col])
            for image in range(grid_rows):
                cgsum[image, line : line + 1, :tile_rows] = shown[image : image + 1]
    color_tiles[...] = narrow(cgsum[...])
    gc, bc = to_float(cross_gains[...]), to_float(cross_biases[...])
    gs, bs = to_float(self_gains[...]), to_float(self_biases[...])
    fixed[0].wait()
    gains_here = [to_float(ref[...]).reshape(1, -1) for ref in (in_gain, in_bias)]
    gains_here = jnp.concatenate(gains_here + [jnp.zeros((6, in_gain.shape[0]), f32)], axis=0)
    gains_here = own_dot(narrow(gains_here), order[...], 1, 1)
    gin, bin_ = gains_here[0:1], gains_here[1:2]
    lat = to_float(latents[...])
    nq = norm_forward(lat, gc[0:1], bc[0:1])
    xbuf[0, core, quad] = nq
    cot_low = cotangent[...]
    xbuf[XS[6], core, quad] = cot_low
    biases[...] = jnp.concatenate([bc, jnp.zeros((1, width), f32)], axis=0)
    pl.semaphore_wait(barrier, grid_cols + grid_rows - 2)

    def send_color(step, carry):
        image = lax.rem(z + step, grid_rows)
        push(color_tiles.at[image], colstage.at[z], misc_send.at[5], misc_recv.at[5], {"rows": image})
        return carry

    lax.fori_loop(1, grid_rows, send_color, 0)
    colstage[z] = color_tiles[z]

    def x_spread(block, sem):
        def one(step, carry):
            peer = 2 * lax.rem(quad + step, quads) + core
            push(block, block, x_send.at[sem], x_recv.at[sem], {"cols": peer})
            return carry

        lax.fori_loop(1, quads, one, 0)

    def x_relay(half, sem):
        wait_for(half.at[pl.ds(0, quads - 1)], x_recv.at[sem])
        push(half, half, y_send.at[sem], y_recv.at[sem], {"cols": j + 1 - 2 * core})

    def x_arrived(half, sem):
        wait_for(half, y_recv.at[sem])

    pieces = rows // 16
    sent = {}

    def spread_x(k):
        x_spread(xbuf.at[XS[k], core, quad], k)

    def background(point):
        for k, count in PLAN.get(point, ()):
            for piece in range(sent.get(k, 0), sent.get(k, 0) + count):
                x_spread(xbuf.at[XS[k], core, quad, pl.ds(piece * 16, 16)], k)
            sent[k] = sent.get(k, 0) + count

    def relay_x(k):
        x_relay(xbuf.at[XS[k], core], k)

    def have_x(k):
        x_arrived(xbuf.at[XS[k], 1 - core], k)

    def to_plane(step):
        peer = lax.rem(j + step, grid_cols)
        return peer, {"cols": peer}

    def regroup(values):
        tiles = [values[:, t * LANES : (t + 1) * LANES] for t in range(width // LANES)]
        piece = lax.broadcasted_iota(jnp.int32, tiles[0].shape, 1) // own
        result = []
        for peer in range(grid_cols):
            chunk_now = None
            for part in range(grid_rows):
                tile, offset = divmod((part * grid_cols + peer) * own, LANES)
                shift = (part * own - offset) % LANES
                moved = pltpu.roll(tiles[tile], shift, 1) if shift else tiles[tile]
                chunk_now = moved if part == 0 else jnp.where(piece == part, moved, chunk_now)
            result.append(chunk_now)
        return jnp.concatenate(result, axis=1)

    def spread_g(k, values):
        spread_plain(k, narrow(regroup(to_float(values))))

    def spread_plain(k, values):
        gsrc[k] = values

        def one(step, carry):
            peer, where = to_plane(step)
            push(gsrc.at[k, :, lanes_of(peer)], gbuf.at[k, core, quad], g_send.at[k], g_recv.at[k], where)
            return carry

        lax.fori_loop(1, grid_cols, one, 0)
        gbuf[k, core, quad] = gsrc[k, :, lanes_of(j)]

    def have_g(k):
        wait_for(gsrc.at[k, :, pl.ds(0, chunk * (grid_cols - 1))], g_recv.at[k])
        return gbuf[k].reshape(grid_cols * rows, chunk)

    partner = z + 1 - 2 * lax.rem(z, 2)
    across = lax.rem(z + 2, grid_rows)

    def block_at(part):
        return pl.ds(pl.multiple_of(part * own, own), own)

    def send_parts(src, pair, sem):
        for slot, part in enumerate((partner, lax.rem(partner + 2, grid_rows))):
            push(src.at[block_at(part)], pair.at[slot], r_send.at[sem], r_recv.at[sem], {"rows": partner})

    def join_parts(src, pair, hand, far, kept, sem):
        wait_for(pair, r_recv.at[sem])
        hand[...] = narrow(to_float(src[block_at(across)]) + to_float(pair[1]))
        push(hand, far, f_send.at[sem], f_recv.at[sem], {"rows": across})
        kept[...] = to_float(src[block_at(z)]) + to_float(pair[0])

    def kept_of(m):
        if m < 3:
            return cross_total.at[m]
        if m < 9:
            return self_total.at[m - 4]
        return self_out_total

    def slot_of(m):
        return 0 if m == 0 else m - 3

    def join(m):
        k = slot_of(m)
        join_parts(staged.at[k], paired.at[k], handed.at[k], crossed.at[k], kept_of(m), m)

    def columns_of(part):
        size = width // grid_rows
        return pl.ds(pl.multiple_of(part * size, size), size)

    def send_rows(src, sem):
        for slot, part in enumerate((partner, lax.rem(partner + 2, grid_rows))):
            push(src.at[:, columns_of(part)], row_pair.at[slot], r_send.at[sem], r_recv.at[sem], {"rows": partner})

    def join_rows(src, sem):
        wait_for(row_pair, r_recv.at[sem])
        row_hand[...] = narrow(to_float(src[:, columns_of(across)]) + to_float(row_pair[1]))
        push(row_hand, row_cross, f_send.at[sem], f_recv.at[sem], {"rows": across})
        row_kept[...] = to_float(src[:, columns_of(z)]) + to_float(row_pair[0])

    def finish_rows(sem):
        wait_for(row_cross, f_recv.at[sem])
        row_turned[...] = jnp.transpose(row_kept[...] + to_float(row_cross[...]))

        def one(step, carry):
            peer, where = to_plane(step)
            push(row_turned.at[block_at(peer)], row_done.at[:, lanes_of(j)], a_send.at[3], a_recv.at[3], where)
            return carry

        lax.fori_loop(1, grid_cols, one, 0)
        row_done[:, lanes_of(j)] = row_turned[block_at(j)]

    def to_line(step):
        part = lax.rem(z + step, grid_rows)
        return part, {"rows": part}

    def spread_line():
        def one(step, carry):
            part, where = to_line(step)
            push(line_rows.at[z], line_rows.at[z], x_send.at[1], x_recv.at[1], where)
            return carry

        lax.fori_loop(1, grid_rows, one, 0)

    def line_hidden(k, bias):
        wait_for(line_rows.at[pl.ds(0, grid_rows - 1)], x_recv.at[1])

        def one(n, carry):
            at = pl.ds(pl.multiple_of(n * 256, 256), 256)
            x = line_rows[...].reshape(grid_rows * rows, width)
            pre = own_dot(x, wts[k, :, at], 1, 0) + bias[:, at]
            line_hid[:, :, at] = narrow(gelu_value(pre)).reshape(grid_rows, rows, 256)
            return carry

        lax.fori_loop(0, width // 256, one, 0, unroll=2)

    def spread_columns(m, values):
        gsrc[m] = values

        def one(step, carry):
            part, where = to_line(step)
            push(
                gsrc.at[m, :, columns_of(part)], line_right.at[m - 1, z], g_send.at[m], g_recv.at[m], where
            )
            return carry

        lax.fori_loop(1, grid_rows, one, 0)
        line_right[m - 1, z] = gsrc[m, :, columns_of(z)]

    def line_part(m, left):
        wait_for(line_right.at[m - 1, pl.ds(0, grid_rows - 1)], g_recv.at[m])
        size = width // grid_rows
        turned = jnp.transpose(line_right[m - 1].reshape(grid_rows * rows, size))

        def one(n, carry):
            at = pl.ds(pl.multiple_of(n * 256, 256), 256)
            block = left[:, :, at].reshape(grid_rows * rows, 256)
            line_staged[m - 1, :, at] = narrow(own_dot(turned, block, 1, 0))
            return carry

        lax.fori_loop(0, width // 256, one, 0, unroll=4)

        for q in range(quads):
            push(
                line_staged.at[m - 1, block_at(2 * q + 1 - core)], line_near.at[m - 1, q],
                y_send.at[m], y_recv.at[m], {"cols": j + 1 - 2 * core},
            )

    def line_join(m):
        wait_for(line_near.at[m - 1], y_recv.at[m])
        for q in range(quads):
            both = to_float(line_staged[m - 1, block_at(2 * q + core)]) + to_float(line_near[m - 1, q])
            line_hand[m - 1, q] = narrow(both)

        def give(step, carry):
            q = lax.rem(quad + step, quads)
            push(
                line_hand.at[m - 1, q], line_sums.at[m - 1, quad], l_send.at[m - 1], l_recv.at[m - 1],
                {"cols": 2 * q + core},
            )
            return carry

        lax.fori_loop(1, quads, give, 0)
        line_sums[m - 1, quad] = line_hand[m - 1, quad]

    def line_total(m):
        wait_for(line_sums.at[m - 1, pl.ds(0, quads - 1)], l_recv.at[m - 1])
        result = to_float(line_sums[m - 1, 0])
        for q in range(1, quads):
            result = result + to_float(line_sums[m - 1, q])
        cross_total[m] = result

    def join_small(m):
        join_parts(
            staged_small.at[m], paired_small.at[m], handed_small.at[m], crossed_small.at[m],
            kept_small.at[m], 10 + m,
        )

    def weight_part(m, right, left):
        turned = jnp.transpose(right)

        def one(n, carry):
            at = pl.ds(pl.multiple_of(n * 256, 256), 256)
            block = left[:, :, :, at].reshape(grid_cols * rows, 256)
            staged[slot_of(m), :, at] = narrow(own_dot(turned, block, 1, 0))
            return carry

        lax.fori_loop(0, width // 256, one, 0, unroll=4)
        if m == 8:
            send_rows(staged.at[slot_of(m)], m)
        else:
            send_parts(staged.at[slot_of(m)], paired.at[slot_of(m)], m)

    def small_part(m, right, left):
        staged_small[m] = narrow(own_dot(right, left[...].reshape(grid_cols * rows, WIDE), 0, 0))
        send_parts(staged_small.at[m], paired_small.at[m], 10 + m)

    def times(x, k, out):
        def one(n, carry):
            at = pl.ds(pl.multiple_of(n * 256, 256), 256)
            out[:, at] = own_dot(x, wts[k, :, at], 1, 0)
            return carry

        lax.fori_loop(0, width // 256, one, 0, unroll=4)

    def times_t(x, k, out, add=False):
        def one(n, carry):
            at = pl.ds(pl.multiple_of(n * 256, 256), 256)
            result = own_dot(x, wts[k, at, :], 1, 1)
            out[:, at] = out[:, at] + result if add else result
            return carry

        lax.fori_loop(0, width // 256, one, 0, unroll=4)

    FIRST, SECOND, THIRD, PRE_C, PRE_S, TMP, ATT, GRAD = range(8)
    COT_BACK = GRAD
    tmp = act.at[TMP]

    wait_for(colstage.at[pl.ds(0, grid_rows - 1)], misc_recv.at[5])

    def send_strip(step, carry):
        peer, where = to_plane(step)
        push(colstage, colbuf.at[j], misc_send.at[0], misc_recv.at[0], where)
        return carry

    lax.fori_loop(1, grid_cols, send_strip, 0)
    colbuf[j] = colstage[...]
    loads[CQ].wait()
    for k in range(1, 10):
        loads[k].start()
    times(nq, CQ, tmp)
    query_low = narrow(tmp[...] + bc[2:3])
    spread_x(0)
    spread_g(7, query_low)
    spread_x(6)
    loads[10].wait()
    for k in range(2):
        win[k] = narrow(own_dot(order[...], win_raw[:, k, :], 1, 0))
    query_inputs = own_dot(query_low, win[0], 1, 1)
    spare = pl.ds(2 * LANES, 16)
    spare_row = lax.broadcasted_iota(jnp.int32, (16, width), 0)
    win[1, spare, :] = narrow(jnp.where(spare_row == 5, bc[3:4], to_float(win[1, spare, :])))

    box = [boxes[z, k] for k in range(4)]

    def filled(value, shape):
        return to_float(jnp.full(shape, value, jnp.int32))

    row_at = lax.broadcasted_iota(jnp.int32, (tall, 1), 0)
    y_place = -1.0 + 2.0 * to_float(row_at - box[0]) / filled(box[2] - 1, (tall, 1))
    y_lines = axis_lines(y_place, 3)
    y_sum = jnp.sum(y_lines, axis=1, keepdims=True)
    row_out = jnp.where((row_at >= box[0]) & (row_at < box[0] + box[2]), 0.0, NEG)
    yfeat[...] = narrow(y_lines)
    held_rows = xfeat.shape[1]
    col_lane = lax.broadcasted_iota(jnp.int32, (held_rows, LANES), 1)
    col_row = lax.broadcasted_iota(jnp.int32, (held_rows, LANES), 0)
    x_sum = jnp.zeros((1, LANES), f32)
    col_out = []
    for half in range(2):
        col_at = lax.broadcasted_iota(jnp.int32, (held_rows, 1), 0) + half * steps
        x_place = -1.0 + 2.0 * to_float(col_at - box[1]) / filled(box[3] - 1, (held_rows, 1))
        x_lines = axis_lines(x_place, 4)
        xfeat[half] = narrow(x_lines)
        here = (col_lane == col_row + half * steps) & (col_row < steps)
        x_sum = x_sum + jnp.sum(
            jnp.where(here, jnp.sum(x_lines, axis=1, keepdims=True), 0.0), axis=0, keepdims=True
        )
        col_out.append(jnp.where((col_at >= box[1]) & (col_at < box[1] + box[3]), 0.0, NEG))
    x_lane = lax.broadcasted_iota(jnp.int32, (1, LANES), 1)
    x_here = -1.0 + 2.0 * to_float(x_lane - box[1]) / filled(box[3] - 1, (1, LANES))
    count = 3 + 2 + 4 * NBANDS

    lane1 = lax.broadcasted_iota(jnp.int32, (rows, LANES), 1)
    lane_half = lax.broadcasted_iota(jnp.int32, (8, LANES), 1) // rows
    sub8 = lax.broadcasted_iota(jnp.int32, (8, LANES), 0)

    def twice(values):
        return jnp.concatenate([values, values], axis=0)

    def turn(values):
        return jnp.transpose(twice(values))[:8]

    def coefficients(scaled, extra):
        tail = scaled[:, 2 * LANES :]
        total = jnp.sum(scaled, axis=1, keepdims=True)
        turned = turn(jnp.where(lane1 == 5, total, jnp.where(lane1 == 6, extra, tail)))
        total_high = to_float(narrow(turned[5:6]))
        body = jnp.where(
            sub8 < 3, turned, jnp.where(sub8 < 5, -total_high, jnp.where(sub8 == 5, total_high - turned[5:6], 0.0))
        )
        body = narrow(jnp.concatenate(
            [jnp.where(lane_half == 0, body, 0.0), jnp.where(lane_half == 1, body, 0.0)], axis=0
        ))
        ones = jnp.where(sub8 >= 6, 1.0, 0.0)
        ones = narrow(jnp.concatenate(
            [jnp.where(lane_half == 0, ones, 0.0), jnp.where(lane_half == 1, ones, 0.0)], axis=0
        ))
        mixrow[...] = jnp.zeros(mixrow.shape, bf16)
        for held in range(STEPS_HELD):
            mixrow[held, held * 16 : held * 16 + 16, :] = jnp.concatenate([body, ones], axis=1)
        scaled_low = narrow(jnp.concatenate([scaled[:, :LANES], tail], axis=1))
        ycoef[...] = own_dot(yfeat[...], twice(scaled_low), 1, 1)
        scaled_low = narrow(jnp.concatenate([scaled[:, LANES : 2 * LANES], tail], axis=1))
        nothing = jnp.zeros_like(scaled_low)
        xcoef[...] = own_dot(xfeat[0], jnp.concatenate([scaled_low, nothing], axis=0), 1, 1) + own_dot(
            xfeat[1], jnp.concatenate([nothing, scaled_low], axis=0), 1, 1
        )
        return turned

    query_scaled = query_inputs * gin * score_scale
    coefficients(query_scaled, 0.0)
    ycoef[...] += row_out
    half_lane = lax.broadcasted_iota(jnp.int32, (held_rows, LANES), 1) // rows
    xcoef[...] += jnp.where(half_lane == 0, col_out[0], col_out[1])

    for copy in fixed[1:]:
        copy.wait()
    wait_for(colbuf.at[pl.ds(0, grid_cols - 1)], misc_recv.at[0])
    for part in range(grid_rows):
        at = pl.ds(part * tile_rows, tile_rows)
        tiles = colbuf[:, part].reshape(grid_cols * 32, LANES)
        img[at, :] = own_dot(tiles, place[...], 0, 0)[:tile_rows]
    c0, c1, c2 = img[:, :LANES], img[:, LANES : 2 * LANES], img[:, 2 * LANES :]
    mean = (c0 + c1 + c2 + y_sum + x_sum) * (1.0 / count)
    square = (c0 * c0 + c1 * c1 + c2 * c2 + y_place * y_place + x_here * x_here + 2.0 * NBANDS) * (
        1.0 / count
    )
    dev = lax.rsqrt(square - mean * mean + EPS)
    mean_low, dev_low = narrow(mean), narrow(dev)
    img7[...] = jnp.concatenate(
        [
            narrow(c0), narrow(c1), narrow(c2),
            mean_low, narrow(mean - to_float(mean_low)),
            dev_low, narrow(dev - to_float(dev_low)),
        ],
        axis=1,
    )
    blocks = fa.shape[0]
    for block in range(blocks):
        at = pl.ds(block * LANES, LANES)
        fa[block] = narrow(own_dot(img7[...], pick[:, at], 1, 0))
        turned = own_dot(pick[:, at], img7[...], 0, 1)
        line = lax.broadcasted_iota(jnp.int32, turned.shape, 0)
        ft[at, :] = narrow(jnp.where(lax.rem(line, 8) == 5, 1.0, turned))

    def step_lines(s):
        block, held = s // STEPS_HELD, lax.rem(s, STEPS_HELD)
        result = own_dot(fa[block], mixrow[held], 1, 0)
        deviation = result[:, LANES:]
        lines = (ycoef[...] + xcoef[pl.ds(s, 1), :] + result[:, :LANES]) * deviation
        return lines, deviation

    def pair_sums(s, weighted):
        at = pl.ds(pl.multiple_of(s * 16, 32), 32)
        both = own_dot(ft[at, :], jnp.concatenate([narrow(w) for w in weighted], axis=1), 1, 0)
        result = None
        for k in range(2):
            found = both[k * 16 : k * 16 + 16, k * LANES : (k + 1) * LANES]
            found = jnp.where(lane_half == 0, found[:8], found[8:])
            colsum[pl.ds(s + k, 1), :] = found[5:6]
            result = found if result is None else result + found
        return result

    def in_groups(one, first, last, start):
        def group(n, carry):
            rows_here = None
            for pair in range(GROUP // 2):
                weighted = []
                for k in range(2):
                    s = n * GROUP + pair * 2 + k
                    total, found, here = one(s, carry)
                    carry = (total, found)
                    weighted.append(here)
                    rows_here = here if rows_here is None else rows_here + here
                carry = (carry[0], carry[1] + pair_sums(n * GROUP + pair * 2, weighted))
            rowsum[...] += rows_here
            return carry

        return lax.fori_loop(first // GROUP, last // GROUP, group, start)

    def fold(values):
        return values[:rows] + values[rows:]

    def pixel_sums(found, factor):
        by_row = fold(own_dot(narrow(rowsum[...] * factor), yfeat[...], 0, 0))
        cols = narrow(colsum[...] * factor)
        by_col = own_dot(cols, xfeat[0], 0, 0)[:rows] + own_dot(cols, xfeat[1], 0, 0)[rows:]
        padded = jnp.concatenate([found * factor, jnp.zeros((LANES - 8, LANES), f32)], axis=0)
        sums = fold(jnp.transpose(padded))
        middle = sums[:, 3:4] + sums[:, 4:5]
        tail = jnp.where(lane1 < 3, sums, 0.0) + by_row[:, LANES:] + by_col[:, LANES:]
        return jnp.concatenate([by_row[:, :LANES], by_col[:, :LANES], tail], axis=1) - middle

    def other_half(line):
        return pltpu.roll(jnp.broadcast_to(line, (8, LANES)), rows, 1)[:1]

    def first_pass(s, best):
        lines, deviation = step_lines(s)
        sl[s] = lines
        return jnp.maximum(best, jnp.max(lines, axis=0, keepdims=True))

    best = lax.fori_loop(0, steps, first_pass, jnp.full((1, LANES), -3e38, f32), unroll=4)
    best = jnp.maximum(best, other_half(best))
    rowsum[...] = jnp.zeros(rowsum.shape, f32)
    colsum[...] = jnp.zeros(colsum.shape, f32)

    def second_pass(s, carry):
        total, found = carry
        block, held = s // STEPS_HELD, lax.rem(s, STEPS_HELD)
        deviation = own_dot(fa[block], mixrow[held][:, LANES:], 1, 0)
        weights = jnp.exp(sl[s] - best)
        total = total + jnp.sum(weights, axis=0, keepdims=True)
        return total, found, weights * deviation

    total, found = in_groups(
        second_pass, 0, steps, (jnp.zeros((1, LANES), f32), jnp.zeros((8, LANES), f32))
    )
    total = total + other_half(total)
    log_total = best + jnp.log(total)
    plain_mixed = pixel_sums(found, 1.0 / total)
    wide1 = lax.broadcasted_iota(jnp.int32, (rows, WIDE), 1)
    mixed_low = narrow(jnp.where(wide1 == 2 * LANES + 5, 1.0, plain_mixed * gin + bin_))
    xsmall[0, core, quad] = mixed_low
    x_spread(xsmall.at[0, core, quad], 8)
    relay_x(0)
    relay_x(6)
    attended = own_dot(mixed_low, win[1], 1, 0)
    act[ATT] = attended
    attended_low = narrow(attended)
    loads[CO].wait()
    times(attended_low, CO, tmp)
    first = lat + tmp[...] + bc[4:5]
    act[FIRST] = first
    normed_c = norm_forward(first, gc[1:2], bc[1:2])
    line_rows[z] = normed_c
    spread_line()
    loads[C1].wait()
    times(normed_c, C1, tmp)
    pre = tmp[...] + bc[5:6]
    act[PRE_C] = pre
    hidden_c = narrow(gelu_value(pre))
    loads[C2].wait()
    times(hidden_c, C2, tmp)
    second = act[FIRST] + tmp[...] + bc[6:7]
    act[SECOND] = second
    normed_t = norm_forward(second, gs[0:1], bs[0:1])
    xbuf[XS[4], core, quad] = normed_t
    mine = core * quads + quad

    def block_of(peer):
        return lax.rem(peer, 2) * quads + peer // 2

    def to_heads(kind, values):
        gsrc[9 + kind] = values

        def one(step, carry):
            peer, where = to_plane(step)
            push(
                gsrc.at[9 + kind, :, lanes_of(peer)], heads.at[kind, mine],
                a_send.at[4 + kind], a_recv.at[4 + kind], where,
            )
            return carry

        lax.fori_loop(1, grid_cols, one, 0)
        heads[kind, mine] = gsrc[9 + kind, :, lanes_of(j)]

    loads[SQ].wait()
    times(normed_t, SQ, tmp)
    to_heads(0, narrow(tmp[...] + bs[2:3]))
    loads[SK].wait()
    times(normed_t, SK, tmp)
    to_heads(1, narrow(tmp[...]))
    loads[SV].wait()
    times(normed_t, SV, tmp)
    to_heads(2, narrow(tmp[...] + bs[3:4]))
    background(0)
    loads[S2].wait()
    times_t(cot_low, S2, act.at[COT_BACK])
    x_relay(xsmall.at[0, core], 8)
    head_rows = grid_cols * rows
    per = 128
    each = per // rows

    for kind in range(3):
        wait_for(heads.at[kind, pl.ds(0, grid_cols - 1)], a_recv.at[4 + kind])

    def head_of(kind):
        return heads[kind].reshape(head_rows, chunk)

    def head_part(kind, n):
        return heads[kind, pl.ds(n * each, each)].reshape(per, chunk)

    def head_forward(n, carry):
        at = pl.ds(pl.multiple_of(n * per, per), per)
        scores = own_dot(head_part(0, n), head_of(1), 1, 1) * head_scale
        weights = jnp.exp(scores - jnp.max(scores, axis=1, keepdims=True))
        found_probs = weights / jnp.sum(weights, axis=1, keepdims=True)
        probs[at, :] = found_probs
        probs_low = narrow(found_probs)
        prob_grad[1, at, :] = probs_low
        mix_s[pl.ds(n * each, each)] = narrow(own_dot(probs_low, head_of(2), 1, 0)).reshape(each, rows, chunk)
        return carry

    lax.fori_loop(0, head_rows // per, head_forward, 0, unroll=2)

    def send_mixed(step, carry):
        peer, where = to_plane(step)
        push(mix_s.at[block_of(peer)], mix_b.at[:, lanes_of(j)], a_send.at[0], a_recv.at[0], where)
        return carry

    lax.fori_loop(1, grid_cols, send_mixed, 0)
    background(1)
    mix_b[:, lanes_of(j)] = mix_s[mine]
    loads[SO].wait()
    wait_for(mix_b.at[:, pl.ds(0, chunk * (grid_cols - 1))], a_recv.at[0])
    mixed_rows = mix_b[...]
    xbuf[XS[3], core, quad] = mixed_rows
    times(mixed_rows, SO, tmp)
    relay_x(4)
    third = act[SECOND] + tmp[...] + bs[4:5]
    act[THIRD] = third
    normed_s = norm_forward(third, gs[1:2], bs[1:2])
    xbuf[XS[5], core, quad] = normed_s
    background(2)
    loads[S1].wait()
    times(normed_s, S1, tmp)
    pre = tmp[...] + bs[5:6]
    act[PRE_S] = pre
    hidden_s = narrow(gelu_value(pre))
    spread_plain(5, hidden_s)
    background(3)
    times(hidden_s, S2, tmp)
    new_latents[...] = narrow(act[THIRD] + tmp[...] + bs[6:7])

    d_pre = act[COT_BACK] * gelu_slope(act[PRE_S])
    pre_low = narrow(d_pre)
    times_t(pre_low, S1, tmp)
    d_rows, lnvec[6:7, :], lnvec[7:8, :] = norm_gradient(act[THIRD], gs[1:2], tmp[...])
    gradient = to_float(cot_low) + d_rows
    act[GRAD] = gradient
    out_low = narrow(gradient)
    times_t(out_low, SO, tmp)
    mix_b2 = narrow(tmp[...])
    gsrc[12] = mix_b2

    def send_dmixed(step, carry):
        peer, where = to_plane(step)
        push(gsrc.at[12, :, lanes_of(peer)], dmix_b.at[mine], a_send.at[1], a_recv.at[1], where)
        return carry

    lax.fori_loop(1, grid_cols, send_dmixed, 0)
    dmix_b[mine] = gsrc[12, :, lanes_of(j)]
    background(4)
    spread_g(4, pre_low)
    line_hidden(C1, biases.at[5:6])
    have_x(6)
    weight_part(8, have_g(5), xbuf.at[XS[6]])
    spread_g(6, out_low)
    background(5)
    wait_for(dmix_b.at[pl.ds(0, grid_cols - 1)], a_recv.at[1])

    def from_heads(kind):
        def one(step, carry):
            peer, where = to_plane(step)
            push(
                dqkv_s.at[kind, block_of(peer)], dqkv_b.at[kind, :, lanes_of(j)],
                a_send.at[7 + kind], a_recv.at[7 + kind], where,
            )
            return carry

        lax.fori_loop(1, grid_cols, one, 0)
        dqkv_b[kind, :, lanes_of(j)] = dqkv_s[kind, mine]

    def rows_back(kind):
        wait_for(dqkv_b.at[kind, :, pl.ds(0, chunk * (grid_cols - 1))], a_recv.at[7 + kind])
        wait_for(heads.at[kind, pl.ds(0, grid_cols - 1)], a_send.at[4 + kind])
        spread_g(9 + kind, dqkv_b[kind])

    def put_head(kind, n, values):
        dqkv_s[kind, pl.ds(n * each, each)] = narrow(values).reshape(each, rows, chunk)

    d_mixed_all = dmix_b[...].reshape(head_rows, chunk)

    def head_values(n, carry):
        at = pl.ds(pl.multiple_of(n * per, per), per)
        put_head(2, n, own_dot(prob_grad[1, :, at], d_mixed_all, 0, 0))
        return carry

    def head_queries(n, carry):
        at = pl.ds(pl.multiple_of(n * per, per), per)
        d_mixed = dmix_b[pl.ds(n * each, each)].reshape(per, chunk)
        d_probs = own_dot(d_mixed, head_of(2), 1, 1)
        found_probs = probs[at, :]
        d_scores = found_probs * (d_probs - jnp.sum(found_probs * d_probs, axis=1, keepdims=True))
        d_low = narrow(d_scores * head_scale)
        prob_grad[0, at, :] = d_low
        put_head(0, n, own_dot(d_low, head_of(1), 1, 0))
        return carry

    def head_keys(n, carry):
        at = pl.ds(pl.multiple_of(n * per, per), per)
        put_head(1, n, own_dot(prob_grad[0, :, at], head_of(0), 0, 0))
        return carry

    lax.fori_loop(0, head_rows // per, head_values, 0, unroll=2)
    from_heads(2)
    background(6)
    lax.fori_loop(0, head_rows // per, head_queries, 0, unroll=2)
    from_heads(0)
    background(7)
    relay_x(3)
    lax.fori_loop(0, head_rows // per, head_keys, 0, unroll=2)
    from_heads(1)
    background(8)
    join_rows(staged.at[slot_of(8)], 8)

    def column_sum(values):
        return jnp.sum(to_float(values), axis=0, keepdims=True)

    have_x(3)
    right = have_g(6)
    bias_s4 = column_sum(right)
    weight_part(9, right, xbuf.at[XS[3]])
    rows_back(2)
    times_t(dqkv_b[2], SV, tmp)
    rows_back(0)
    times_t(dqkv_b[0], SQ, tmp, True)
    rows_back(1)
    times_t(dqkv_b[1], SK, tmp, True)
    background(9)
    d_rows, lnvec[4:5, :], lnvec[5:6, :] = norm_gradient(act[SECOND], gs[0:1], tmp[...])
    gradient = act[GRAD] + d_rows
    act[GRAD] = gradient
    second_low = narrow(gradient)
    spread_columns(2, second_low)
    lnvec[9:10, :] = jnp.sum(gradient, axis=0, keepdims=True)
    background(10)
    times_t(second_low, C2, tmp)
    d_pre = tmp[...] * gelu_slope(act[PRE_C])
    pre_low = narrow(d_pre)
    spread_columns(1, pre_low)
    lnvec[10:11, :] = jnp.sum(d_pre, axis=0, keepdims=True)
    background(11)
    join(9)
    have_x(4)
    for k in (2, 0, 1):
        right = have_g(9 + k)
        if k == 0:
            bias_s2 = column_sum(right)
        elif k == 2:
            bias_s3 = column_sum(right)
        weight_part(4 + k, right, xbuf.at[XS[4]])
    times_t(pre_low, C1, tmp)
    d_rows, lnvec[2:3, :], lnvec[3:4, :] = norm_gradient(act[FIRST], gc[1:2], tmp[...])
    gradient = act[GRAD] + d_rows
    act[GRAD] = gradient
    out_low = narrow(gradient)
    spread_g(3, out_low)
    relay_x(5)
    times_t(out_low, CO, tmp)
    d_attended = narrow(tmp[...])
    spread_g(8, d_attended)
    background(12)
    line_part(2, line_hid)
    line_part(1, line_rows)
    line_join(2)
    have_x(5)
    right = have_g(4)
    bias_s5 = column_sum(right)
    weight_part(7, right, xbuf.at[XS[5]])

    grad_inputs = own_dot(d_attended, win[1], 1, 1)
    d_attended = to_float(d_attended)
    shift = grad_inputs[:, 2 * LANES + 5 : 2 * LANES + 6]
    row_delta = jnp.sum(d_attended * act[ATT], axis=1, keepdims=True) - shift
    grad_shift = jnp.sum(grad_inputs * bin_, axis=1, keepdims=True)
    grad_scaled = grad_inputs * gin
    turned = coefficients(grad_scaled, grad_shift - row_delta)
    constant = turned[6:7]

    def away(scaled):
        values = scaled[:, 2 * LANES :] - jnp.sum(scaled, axis=1, keepdims=True) * (1.0 / count)
        values = jnp.where(lane1 < 3, values, 0.0)
        return jnp.concatenate([values, pltpu.roll(values, 8, 1)], axis=0)

    query_away, grad_away = away(query_scaled), away(grad_scaled)
    wide_lane = lax.broadcasted_iota(jnp.int32, (LANES, LANES), 1)
    wide_half = lax.broadcasted_iota(jnp.int32, (LANES, LANES), 0) // rows
    blank = jnp.zeros((LANES, LANES), bf16)
    for held in range(STEPS_HELD):
        group = wide_lane - held * 16 - wide_half * 8
        along = narrow(jnp.where((group >= 0) & (group < 3), 1.0, 0.0))
        colors_here = [query_away, grad_away]
        if held:
            colors_here = [pltpu.roll(v, held * 16, 1) for v in colors_here]
        cgright[held // 2, (held % 2) * WIDE : (held % 2 + 1) * WIDE, :] = jnp.concatenate(
            [
                jnp.concatenate([narrow(colors_here[0]), blank], axis=1),
                jnp.concatenate([narrow(colors_here[1]), blank], axis=1),
                jnp.concatenate([blank, along], axis=1),
            ],
            axis=0,
        )
    rowsum[...] = jnp.zeros(rowsum.shape, f32)
    colsum[...] = jnp.zeros(colsum.shape, f32)

    def kept_at(s):
        place_now = lax.rem(s, 6)
        line = pl.ds(pl.multiple_of((place_now // 2) * tall, 32), tall)
        lane = pl.ds(pl.multiple_of(lax.rem(place_now, 2) * WIDE, LANES), WIDE)
        return wts.at[4 + s // 6, line, lane]

    def back_pass(s, carry):
        total, found = carry
        lines, deviation = step_lines(s)
        scores = sl[s]
        found_probs = jnp.exp(scores - log_total)
        d_scores = found_probs * (lines + constant)
        kept_at(s)[...] = jnp.concatenate(
            [narrow(d_scores), narrow(found_probs), narrow(d_scores * scores + found_probs * lines)], axis=1
        )
        total = total + jnp.sum(d_scores, axis=0, keepdims=True)
        return total, found, d_scores * deviation

    def color_block(block):
        result = None
        for pair in range(block * STEPS_HELD // 2, min((block + 1) * STEPS_HELD, steps) // 2):
            line = pl.ds((pair % 3) * tall, tall)
            left = wts[4 + pair // 3, line, pl.ds(0, 2 * WIDE)]
            part = own_dot(left, cgright[pair % (STEPS_HELD // 2)], 1, 0)
            result = part if result is None else result + part
        cgacc[block] = result

    carry = (jnp.zeros((1, LANES), f32), jnp.zeros((8, LANES), f32))
    third_of = steps // 3
    line_join(1)
    carry = in_groups(back_pass, 0, third_of, carry)
    finish_rows(8)
    join(6)
    carry = in_groups(back_pass, third_of, 2 * third_of, carry)
    join(4)
    x_arrived(xsmall.at[0, 1 - core], 8)
    right = have_g(3)
    bias_c4 = column_sum(right)
    small_part(2, right, xsmall.at[0])
    right = have_g(8)
    bias_c3 = column_sum(right)
    small_part(1, right, xsmall.at[0])
    total, found = in_groups(back_pass, 2 * third_of, steps, carry)
    join(5)
    plain_scores = pixel_sums(found, 1.0) * score_scale
    total = total * score_scale
    score_total = fold(jnp.transpose(jnp.concatenate([total, jnp.zeros((LANES - 1, LANES), f32)], axis=0)))[:, 0:1]
    score_low = narrow(plain_scores * gin + score_total * bin_)
    xsmall[1, core, quad] = score_low
    x_spread(xsmall.at[1, core, quad], 9)

    def d_query_part(n, carry):
        at = pl.ds(pl.multiple_of(n * 256, 256), 256)
        tmp[:, at] = own_dot(score_low, win[0, :, at], 1, 0)
        return carry

    lax.fori_loop(0, width // 256, d_query_part, 0)
    query_grad_low = narrow(tmp[...])
    spread_g(0, query_grad_low)
    gain_part = jnp.sum(query_inputs * plain_scores + grad_inputs * plain_mixed, axis=0, keepdims=True)
    bias_part = jnp.sum(query_inputs * score_total + grad_inputs, axis=0, keepdims=True)
    cuts = [part[:, k * LANES : (k + 1) * LANES] for part in (gain_part, bias_part) for k in range(3)]
    shared = jnp.concatenate(cuts + [jnp.zeros((1, LANES), f32)], axis=0)
    times_t(query_grad_low, CQ, tmp)
    d_rows, lnvec[0:1, :], lnvec[1:2, :] = norm_gradient(to_float(latents[...]), gc[0:1], tmp[...])
    latent_grad[...] = act[GRAD] + d_rows
    lnvec[8:9, :] = jnp.sum(to_float(cotangent[...]), axis=0, keepdims=True)
    lines = regroup(lnvec[...])
    for peer in range(grid_cols):
        lnsend[peer] = jnp.concatenate(
            [lines[:11, peer * chunk : (peer + 1) * chunk], shared, jnp.zeros((6, LANES), f32)], axis=0
        )

    def send_ln(step, carry):
        peer, where = to_plane(step)
        push(lnsend.at[peer], lnbuf.at[j], misc_send.at[2], misc_recv.at[2], where)
        return carry

    lax.fori_loop(1, grid_cols, send_ln, 0)
    lnbuf[j] = lnsend[j]
    join(7)
    for block in range(0, blocks // 2):
        color_block(block)
    x_relay(xsmall.at[1, core], 9)
    have_x(0)
    right = have_g(0)
    bias_c2 = column_sum(right)
    weight_part(0, right, xbuf.at[0])
    for block in range(blocks // 2, blocks - 1):
        color_block(block)
    x_arrived(xsmall.at[1, 1 - core], 9)
    small_part(0, have_g(7), xsmall.at[1])
    color_block(blocks - 1)
    for m in (2, 1):
        join_small(m)

    for block in range(blocks):
        both = own_dot(fa[block], spread[...], 1, 0)
        center, factor = both[:, :LANES], both[:, LANES:]
        here = cgacc[block]
        cgacc[block, :, :LANES] = factor * (
            here[:, :LANES] - (to_float(fa[block]) - center) * factor * here[:, LANES:] * (1.0 / count)
        )
    for part in range(grid_rows):
        at = pl.ds(part * tile_rows, tile_rows)
        lines = jnp.concatenate([narrow(cgacc[block, at, :LANES]) for block in range(blocks)], axis=1)
        tiles = narrow(own_dot(back[...], lines, 1, 1))
        for tile in range(grid_cols):
            cgsend[tile, part, :, :tile_rows] = tiles[tile * 32 : tile * 32 + 32]
    cgbuf[j] = cgsend[j]

    def send_cg(step, carry):
        peer, where = to_plane(step)
        push(cgsend.at[peer], cgbuf.at[j], misc_send.at[3], misc_recv.at[3], where)
        return carry

    lax.fori_loop(1, grid_cols, send_cg, 0)

    wait_for(lnbuf.at[pl.ds(0, grid_cols - 1)], misc_recv.at[2])
    norms = lnbuf[0]
    for peer in range(1, grid_cols):
        norms = norms + lnbuf[peer]
    vecsend[...] = jnp.concatenate(
        [
            norms[:8], bias_c2, bias_c3, bias_c4, norms[10:11], norms[9:10], bias_s2, bias_s3,
            bias_s4, bias_s5, norms[8:9], jnp.zeros((6, chunk), f32), norms[11:18], jnp.zeros((1, chunk), f32),
        ],
        axis=0,
    )

    def send_vec(step, carry):
        where = {"rows": lax.rem(z + step, grid_rows)}
        push(vecsend, vecbuf.at[z], misc_send.at[4], misc_recv.at[4], where)
        return carry

    lax.fori_loop(1, grid_rows, send_vec, 0)
    vecbuf[z] = vecsend[...]
    join(0)
    join_small(0)
    wait_for(cgbuf.at[pl.ds(0, grid_cols - 1)], misc_recv.at[3])
    tiles = to_float(cgbuf[0])
    for peer in range(1, grid_cols):
        tiles = tiles + to_float(cgbuf[peer])
    cgsum[...] = tiles

    def send_tile(step, carry):
        part = lax.rem(z + step, grid_rows)
        push(cgsum.at[part], cgfin.at[z], misc_send.at[6], misc_recv.at[6], {"rows": part})
        return carry

    lax.fori_loop(1, grid_rows, send_tile, 0)
    cgfin[z] = cgsum[z]

    wait_for(vecbuf.at[pl.ds(0, grid_rows - 1)], misc_recv.at[4])
    vectors = vecbuf[0]
    for part in range(1, grid_rows):
        vectors = vectors + vecbuf[part]
    vector_out[...] = vectors[:24]
    input_vector_out[...] = vectors[24:]
    for m in (2, 1):
        line_total(m)
    for m in (7, 4, 5, 6, 9, 0):
        wait_for(crossed.at[slot_of(m)], f_recv.at[m])
        result = kept_of(m)[...] + to_float(crossed[slot_of(m)])
        kept_of(m)[...] = result
    wait_for(row_done.at[:, pl.ds(0, chunk * (grid_cols - 1))], a_recv.at[3])
    self_total[4] = row_done[...]
    sums = []
    for m in (2, 1, 0):
        wait_for(crossed_small.at[m], f_recv.at[10 + m])
        sums.append(kept_small[m] + to_float(crossed_small[m]))
    out_total[...] = own_dot(narrow(sums[0]), win[1], 1, 0)
    input_parts[1] = sums[1]
    input_parts[0] = sums[2]
    wait_for(cgfin.at[pl.ds(0, grid_rows - 1)], misc_recv.at[6])
    color_out[...] = cgfin[...]

    for k in (0, 3, 4, 5, 6):
        wait_for(xbuf.at[XS[k], 0, pl.ds(0, quads - 1)], x_send.at[k])
        wait_for(xbuf.at[XS[k], 0], y_send.at[k])
    wait_for(line_rows.at[pl.ds(0, grid_rows - 1)], x_send.at[1])
    for m in (1, 2):
        wait_for(line_right.at[m - 1, pl.ds(0, grid_rows - 1)], g_send.at[m])
        wait_for(line_near.at[m - 1], y_send.at[m])
        wait_for(line_sums.at[m - 1, pl.ds(0, quads - 1)], l_send.at[m - 1])
    for k in range(2):
        wait_for(xsmall.at[k, 0, pl.ds(0, quads - 1)], x_send.at[8 + k])
        wait_for(xsmall.at[k, 0], y_send.at[8 + k])
    for k in (0, 3, 4, 5, 6, 7, 8, 9, 10, 11):
        wait_for(gsrc.at[k, :, pl.ds(0, chunk * (grid_cols - 1))], g_send.at[k])
    wait_for(mix_s.at[pl.ds(0, grid_cols - 1)], a_send.at[0])
    wait_for(dmix_b.at[pl.ds(0, grid_cols - 1)], a_send.at[1])
    for kind in range(3):
        wait_for(dqkv_s.at[kind, pl.ds(0, grid_cols - 1)], a_send.at[7 + kind])
    wait_for(colbuf.at[pl.ds(0, grid_cols - 1)], misc_send.at[0])
    wait_for(row_turned.at[pl.ds(0, own * (grid_cols - 1))], a_send.at[3])
    wait_for(lnbuf.at[pl.ds(0, grid_cols - 1)], misc_send.at[2])
    wait_for(cgbuf.at[pl.ds(0, grid_cols - 1)], misc_send.at[3])
    wait_for(colstage.at[pl.ds(0, grid_rows - 1)], misc_send.at[5])
    wait_for(cgfin.at[pl.ds(0, grid_rows - 1)], misc_send.at[6])
    wait_for(row_pair, r_send.at[8])
    wait_for(row_hand, f_send.at[8])
    for m in (0, 4, 5, 6, 7, 9):
        wait_for(paired.at[slot_of(m)], r_send.at[m])
        wait_for(handed.at[slot_of(m)], f_send.at[m])
    for m in range(3):
        wait_for(paired_small.at[m], r_send.at[10 + m])
        wait_for(handed_small.at[m], f_send.at[10 + m])
    wait_for(vecbuf.at[pl.ds(0, grid_rows - 1)], misc_send.at[4])


def channel_order(count):
    n = NBANDS
    starts = ((5, n), (5 + 2 * n, n), (5 + n, n), (5 + 3 * n, n), (0, 5))
    order = np.concatenate([np.arange(start, start + size) for start, size in starts])
    result = np.zeros((WIDE, count), np.float32)
    result[np.arange(count), order] = 1
    return np.asarray(result, ml_dtypes.bfloat16)


def by_channel(lines):
    n = NBANDS
    parts = [lines[..., 4 * n : 4 * n + 5], lines[..., :n], lines[..., 2 * n : 3 * n]]
    parts += [lines[..., n : 2 * n], lines[..., 3 * n : 4 * n]]
    return jnp.concatenate(parts, axis=-1)


def finish_kernel(
    own, tile_rows, tile_cols,
    latents, latent_grad, colors, cross, out, self_parts, self_out, inputs, vectors, input_vectors,
    prior_cross, prior_out, prior_input,
    o_latents, o_latent_grad, o_colors, o_cross, o_out, o_input, o_gain, o_bias,
    o_cross_gains, o_cross_biases, o_self, o_self_out, o_self_gains, o_self_biases,
):
    o_latents[...] = latents[...]
    o_latent_grad[...] = latent_grad[...]
    for channel in range(3):
        for col in range(tile_cols):
            line = channel * tile_cols + col
            for image in range(colors.shape[0]):
                o_colors[channel, col, image : image + 1, :] = colors[image, line : line + 1, :tile_rows]
    o_cross[...] = prior_cross[...] + cross[...]
    o_out[...] = prior_out[...] + out[...]
    o_self[...] = self_parts[...]
    o_self_out[...] = self_out[...]
    for k in range(2):
        o_input[k] = prior_input[k] + by_channel(inputs[k])
    lines = input_vectors[...]
    for k, target in enumerate((o_gain, o_bias)):
        wide = jnp.concatenate([lines[3 * k + t : 3 * k + t + 1] for t in range(3)], axis=1)
        target[...] = by_channel(wide).reshape(-1)
    place = lax.axis_index("rows")
    width = vectors.shape[1]
    mine = pltpu.roll(vectors[...], lax.rem(width - place * own, width), 1)[:, :own]
    for target, rows in (
        (o_cross_gains, (0, 2)),
        (o_cross_biases, (1, 3, 8, 9, 10, 11, 12)),
        (o_self_gains, (4, 6)),
        (o_self_biases, (5, 7, 13, 14, 15, 16, 17)),
    ):
        for k, row in enumerate(rows):
            target[k : k + 1, :] = mine[row : row + 1]


def local_kernel(
    latents,
    pixel_colors,
    image_boxes,
    cotangent,
    cross_matrices,
    cross_out,
    input_matrices,
    in_gain,
    in_bias,
    cross_gains,
    cross_biases,
    self_matrices,
    self_out,
    self_gains,
    self_biases,
    prior_cross_matrices,
    prior_cross_out,
    prior_input_matrices,
):
    rows, width = latents.shape
    channels, image_count, tile_rows, tile_cols = pixel_colors.shape
    grid_rows = lax.axis_size("rows")
    grid_cols = lax.axis_size("cols")
    n_dev = grid_rows * grid_cols
    tall, wide = grid_rows * tile_rows, grid_cols * tile_cols
    steps = wide // 2
    chunk = width // grid_cols
    own = chunk // grid_rows
    quads = grid_cols // 2
    place, pick, spread, back = selections(tile_cols, grid_cols, steps)
    blocks = back.shape[1] // LANES
    held_rows = -(-steps // 8) * 8
    order = channel_order(input_matrices.shape[1])
    f32, bf16 = jnp.float32, jnp.bfloat16
    vmem = pl.BlockSpec(memory_space=pltpu.VMEM)
    away = pl.BlockSpec(memory_space=pl.ANY)
    shape = jax.ShapeDtypeStruct
    sizes = (grid_rows, grid_cols, rows, steps, tile_rows, tile_cols)
    dma = pltpu.SemaphoreType.DMA
    scratch = [
        ((10, width, width), bf16),
        ((2, WIDE, width), bf16),
        ((input_matrices.shape[1], 2, width), bf16),
        ((5, 2, quads, rows, width), bf16),
        ((2, 2, quads, rows, WIDE), bf16),
        ((13, rows, width), bf16),
        ((12, 2, quads, rows, chunk), bf16),
        ((7, chunk, width), bf16),
        ((7, 2, own, width), bf16),
        ((7, own, width), bf16),
        ((7, own, width), bf16),
        ((3, chunk, WIDE), bf16),
        ((3, 2, own, WIDE), bf16),
        ((3, own, WIDE), bf16),
        ((3, own, WIDE), bf16),
        ((3, own, WIDE), f32),
        ((grid_rows, rows, width), bf16),
        ((grid_rows, rows, width), bf16),
        ((2, grid_rows, rows, width // grid_rows), bf16),
        ((2, width // grid_rows, width), bf16),
        ((2, quads, own, width), bf16),
        ((2, quads, own, width), bf16),
        ((2, quads, own, width), bf16),
        ((2, chunk, width // grid_rows), bf16),
        ((chunk, width // grid_rows), bf16),
        ((chunk, width // grid_rows), bf16),
        ((chunk, width // grid_rows), f32),
        ((width // grid_rows, chunk), f32),
        ((own, width), f32),
        ((8, width), f32),
        ((grid_rows, 32, LANES), bf16),
        ((grid_rows, 32, LANES), bf16),
        ((grid_cols, grid_rows, 32, LANES), bf16),
        ((tall, WIDE), f32),
        ((tall, 7 * LANES), bf16),
        ((blocks, tall, LANES), bf16),
        ((blocks * LANES, tall), bf16),
        ((steps, tall, LANES), f32),
        ((tall, LANES), f32),
        ((held_rows, LANES), f32),
        ((tall, 2 * LANES), bf16),
        ((2, held_rows, 2 * LANES), bf16),
        ((STEPS_HELD, LANES, 2 * LANES), bf16),
        ((STEPS_HELD // 2, 2 * WIDE, 2 * LANES), bf16),
        ((tall, LANES), f32),
        ((held_rows, LANES), f32),
        ((blocks, tall, 2 * LANES), f32),
        ((grid_cols, grid_rows, 32, LANES), bf16),
        ((grid_cols, grid_rows, 32, LANES), bf16),
        ((grid_rows, 32, LANES), f32),
        ((grid_rows, 32, LANES), f32),
        ((8, rows, width), f32),
        ((16, width), f32),
        ((grid_cols, 24, chunk), f32),
        ((grid_cols, 24, chunk), f32),
        ((32, chunk), f32),
        ((grid_rows, 32, chunk), f32),
        ((3, grid_cols, rows, chunk), bf16),
        ((grid_cols * rows, grid_cols * rows), f32),
        ((2, grid_cols * rows, grid_cols * rows), bf16),
        ((grid_cols, rows, chunk), bf16),
        ((rows, width), bf16),
        ((grid_cols, rows, chunk), bf16),
        ((3, grid_cols, rows, chunk), bf16),
        ((3, rows, width), bf16),
    ]
    fixed = (order, place, pick, spread, back)
    scratch = [(values.shape, bf16) for values in fixed] + scratch
    scratch = [pltpu.VMEM(dims, kind) for dims, kind in scratch]
    scratch += [dma((count,)) for count in (5, 11, 10, 10, 10, 10, 12, 12, 10, 10, 13, 13, 13, 13, 2, 2, 7, 7)]
    outs = [
        ((rows, width), bf16),
        ((rows, width), f32),
        ((image_count, 32, LANES), f32),
        ((3, own, width), f32),
        ((own, width), f32),
        ((5, own, width), f32),
        ((own, width), f32),
        ((2, own, WIDE), f32),
        ((24, chunk), f32),
        ((8, LANES), f32),
    ]
    results = pl.pallas_call(
        functools.partial(layer_kernel, sizes),
        out_shape=[shape(dims, kind) for dims, kind in outs],
        in_specs=[pl.BlockSpec(memory_space=pltpu.SMEM)] + [vmem] * 9 + [away] * 10,
        out_specs=[vmem] * len(outs),
        scratch_shapes=scratch,
        compiler_params=pltpu.CompilerParams(
            collective_id=0, has_side_effects=True, vmem_limit_bytes=VMEM_BYTES
        ),
        cost_estimate=pl.CostEstimate(
            flops=20_000_000_000, bytes_accessed=40_000_000, transcendentals=4_000_000
        ),
    )(
        image_boxes,
        latents,
        cotangent,
        jnp.transpose(pixel_colors, (0, 3, 1, 2)),
        in_gain,
        in_bias,
        cross_gains,
        cross_biases,
        self_gains,
        self_biases,
        *fixed,
        cross_matrices,
        cross_out,
        self_matrices,
        self_out,
        jnp.transpose(input_matrices, (1, 0, 2)),
    )
    count = input_matrices.shape[1]
    last = [
        ((rows, width), bf16),
        ((rows, width), f32),
        ((channels, tile_cols, image_count, tile_rows), f32),
        ((3, own, width), f32),
        ((own, width), f32),
        ((2, own, count), f32),
        ((count,), f32),
        ((count,), f32),
        ((2, own), f32),
        ((7, own), f32),
        ((5, own, width), f32),
        ((own, width), f32),
        ((2, own), f32),
        ((7, own), f32),
    ]
    done = pl.pallas_call(
        functools.partial(finish_kernel, own, tile_rows, tile_cols),
        out_shape=[shape(dims, kind) for dims, kind in last],
        in_specs=[vmem] * (len(outs) + 3),
        out_specs=[vmem] * len(last),
        compiler_params=pltpu.CompilerParams(vmem_limit_bytes=VMEM_BYTES),
    )(
        *results,
        jnp.transpose(prior_cross_matrices, (0, 2, 1)),
        jnp.transpose(prior_cross_out),
        jnp.transpose(prior_input_matrices, (0, 2, 1)),
    )
    (new_latents, latent_grad, colors, cross_total, out_total, input_total, gain, bias) = done[:8]
    cross_gain, cross_bias, self_total, self_out_total, self_gain, self_bias = done[8:]
    return (
        new_latents,
        latent_grad,
        jnp.transpose(colors, (0, 2, 3, 1)),
        jnp.transpose(cross_total, (0, 2, 1)),
        jnp.transpose(out_total),
        jnp.transpose(input_total, (0, 2, 1)),
        gain,
        bias,
        cross_gain,
        cross_bias,
        jnp.transpose(self_total, (0, 2, 1)),
        jnp.transpose(self_out_total),
        self_gain,
        self_bias,
    )


def solution(mesh):
    placed = (
        P(("rows", "cols"), None),
        P(None, None, "rows", "cols"),
        P(),
        P(("rows", "cols"), None),
        P(),
        P(),
        P(),
        P(),
        P(),
        P(),
        P(),
        P(),
        P(),
        P(),
        P(),
        P(None, None, ("rows", "cols")),
        P(None, ("rows", "cols")),
        P(None, None, ("rows", "cols")),
    )
    one_head_each = mesh.shape["cols"] == HEADS
    return jax.shard_map(
        local_kernel if one_head_each else local,
        mesh=mesh,
        in_specs=placed,
        out_specs=(
            P(("rows", "cols"), None),
            P(("rows", "cols"), None),
            P(None, None, "rows", "cols"),
            P(None, None, ("rows", "cols")),
            P(None, ("rows", "cols")),
            P(None, None, ("rows", "cols")),
            P(),
            P(),
            P(None, ("rows", "cols")),
            P(None, ("rows", "cols")),
            P(None, None, ("rows", "cols")),
            P(None, ("rows", "cols")),
            P(None, ("rows", "cols")),
            P(None, ("rows", "cols")),
        ),
        check_vma=False,
    )
```

```python
import functools

import jax
import jax.numpy as jnp
import ml_dtypes
import numpy as np
from jax import lax
from jax.experimental import pallas as pl
from jax.experimental.pallas import tpu as pltpu
from jax.sharding import PartitionSpec as P

HEADS = 8
LATENTS = 512
NBANDS = 64
HEAD_DIM = 128


EPS = 1e-05
NEG = -1e30
FREQ_TOP = 112.0
VMEM_BYTES = 63 * 1024 * 1024
PLAN = {0: ((4, 4),), 2: ((3, 2),), 4: ((3, 2),), 9: ((5, 4),)}


def narrow(values):
    return values.astype(jnp.bfloat16)


def to_float(values):
    return values.astype(jnp.float32)


def matmul(former, latter):
    return jnp.dot(former, latter, preferred_element_type=jnp.float32)


def inner_left(former, latter):
    return lax.dot_general(
        former, latter, (((0,), (0,)), ((), ())), preferred_element_type=jnp.float32
    )


def inner_right(former, latter):
    return lax.dot_general(
        former, latter, (((1,), (1,)), ((), ())), preferred_element_type=jnp.float32
    )


def layer_norm(values, gain, offset):
    middle = jnp.mean(values, axis=-1, keepdims=True)
    centered = values - middle
    spread = jnp.mean(centered * centered, axis=-1, keepdims=True)
    return centered * lax.rsqrt(spread + EPS) * gain + offset


def norm_back(values, gain, offset, gradient):
    result, pullback = jax.vjp(layer_norm, values, gain, offset)
    return pullback(gradient)


def gelu_tanh(values):
    return jax.nn.gelu(values, approximate=True)


def gelu_back(pre_gelu, gradient):
    result, pullback = jax.vjp(gelu_tanh, pre_gelu)
    return pullback(gradient)[0]


def axis_features(places, extent):
    frequency = 1.0 + jnp.arange(NBANDS, dtype=jnp.float32) * ((FREQ_TOP - 1.0) / (NBANDS - 1))
    angle = jnp.pi * places[:, None] * frequency[None, :]
    return (places, jnp.sin(angle), jnp.cos(angle))


def canvas_of(colors, image_box):
    channels, wide, tall = colors.shape
    top, left, height, width = image_box[0], image_box[1], image_box[2], image_box[3]
    row_at = jnp.arange(tall, dtype=jnp.int32)
    col_at = jnp.arange(wide, dtype=jnp.int32)
    y_place = -1.0 + 2.0 * to_float(row_at - top) / to_float(height - 1)
    x_place = -1.0 + 2.0 * to_float(col_at - left) / to_float(width - 1)
    y_parts = axis_features(y_place, height)
    x_parts = axis_features(x_place, width)
    y_all = jnp.concatenate([y_parts[0][:, None], y_parts[1], y_parts[2]], axis=1)
    x_all = jnp.concatenate([x_parts[0][:, None], x_parts[1], x_parts[2]], axis=1)
    count = channels + 2 + 4 * NBANDS
    color_sum = jnp.sum(colors, axis=0)
    color_square = jnp.sum(colors * colors, axis=0)
    mean = (color_sum + jnp.sum(y_all, axis=1)[None, :] + jnp.sum(x_all, axis=1)[:, None]) / count
    square = (
        color_square
        + jnp.sum(y_all * y_all, axis=1)[None, :]
        + jnp.sum(x_all * x_all, axis=1)[:, None]
    ) / count
    deviation = lax.rsqrt(square - mean * mean + EPS)
    row_in = (row_at >= top) & (row_at < top + height)
    col_in = (col_at >= left) & (col_at < left + width)
    return (y_all, x_all, mean, deviation, row_in, col_in)


def split_channels(rows, channels):
    n = NBANDS
    c = channels
    y_part = jnp.concatenate(
        [rows[:, c : c + 1], rows[:, c + 2 : c + 2 + n], rows[:, c + 2 + 2 * n : c + 2 + 3 * n]],
        axis=1,
    )
    x_part = jnp.concatenate(
        [
            rows[:, c + 1 : c + 2],
            rows[:, c + 2 + n : c + 2 + 2 * n],
            rows[:, c + 2 + 3 * n : c + 2 + 4 * n],
        ],
        axis=1,
    )
    return (rows[:, :c], y_part, x_part)


def join_channels(color_part, y_part, x_part):
    n = NBANDS
    return jnp.concatenate(
        [
            color_part,
            y_part[:, :1],
            x_part[:, :1],
            y_part[:, 1 : n + 1],
            x_part[:, 1 : n + 1],
            y_part[:, n + 1 :],
            x_part[:, n + 1 :],
        ],
        axis=1,
    )


def against_pixels(rows, colors, canvas):
    y_all, x_all, mean, deviation = canvas[:4]
    color_part, y_part, x_part = split_channels(rows, colors.shape[0])
    by_row = inner_right(narrow(y_part), narrow(y_all))
    by_col = inner_right(narrow(x_part), narrow(x_all))
    total = by_row[:, None, :] + by_col[:, :, None]
    for j in range(colors.shape[0]):
        total = total + color_part[:, j][:, None, None] * colors[j][None]
    total = total - jnp.sum(rows, axis=1)[:, None, None] * mean[None]
    return total * deviation[None]


def over_pixels(weights, colors, canvas):
    y_all, x_all, mean, deviation = canvas[:4]
    scaled = weights * deviation[None]
    y_part = matmul(narrow(jnp.sum(scaled, axis=1)), narrow(y_all))
    x_part = matmul(narrow(jnp.sum(scaled, axis=2)), narrow(x_all))
    color_part = jnp.stack(
        [jnp.sum(scaled * colors[j][None], axis=(1, 2)) for j in range(colors.shape[0])], axis=1
    )
    middle = jnp.sum(scaled * mean[None], axis=(1, 2))
    return join_channels(color_part, y_part, x_part) - middle[:, None]


def mlp_forward(row_values, gain, offset, w_in, b_in, w_out, b_out):
    normed = narrow(layer_norm(row_values, gain, offset))
    pre_gelu = matmul(normed, w_in) + b_in
    hidden = narrow(gelu_tanh(pre_gelu))
    return (matmul(hidden, w_out) + b_out, (normed, pre_gelu, hidden))


def mlp_backward(row_values, gain, offset, w_in, w_out, stored, gradient):
    normed, pre_gelu, hidden = stored
    grad_low = narrow(gradient)
    d_w_out = inner_left(hidden, grad_low)
    d_b_out = jnp.sum(gradient, axis=0)
    d_pre = gelu_back(pre_gelu, inner_right(grad_low, w_out))
    pre_low = narrow(d_pre)
    d_w_in = inner_left(normed, pre_low)
    d_b_in = jnp.sum(d_pre, axis=0)
    d_rows, d_gain, d_offset = norm_back(row_values, gain, offset, inner_right(pre_low, w_in))
    return (
        gradient + d_rows,
        (d_w_in, d_w_out),
        (d_gain, d_offset, d_b_in, d_b_out),
        (pre_low, grad_low),
    )


def local(
    latents,
    pixel_colors,
    image_boxes,
    cotangent,
    cross_matrices,
    cross_out,
    input_matrices,
    in_gain,
    in_bias,
    cross_gains,
    cross_biases,
    self_matrices,
    self_out,
    self_gains,
    self_biases,
    prior_cross_matrices,
    prior_cross_out,
    prior_input_matrices,
):
    rows_dev = latents.shape[0]
    model_width = latents.shape[1]
    image_count = image_boxes.shape[0]
    tile_rows = pixel_colors.shape[2]
    tile_cols = pixel_colors.shape[3]
    input_width = input_matrices.shape[1]
    grid_rows = lax.axis_size("rows")
    grid_cols = lax.axis_size("cols")
    all_rows = rows_dev * grid_rows * grid_cols
    row_place = lax.axis_index("rows")
    col_place = lax.axis_index("cols")
    row_start = row_place * tile_rows
    col_start = col_place * tile_cols
    score_scale = model_width ** (-0.5)
    head_scale = HEAD_DIM ** (-0.5)
    g_cross = to_float(cross_gains)
    b_cross = to_float(cross_biases)
    g_self = to_float(self_gains)
    b_self = to_float(self_biases)
    g_input = to_float(in_gain)
    b_input = to_float(in_bias)
    latent_state = to_float(latents)
    normed_q = narrow(layer_norm(latent_state, g_cross[0], b_cross[0]))
    query_rows = narrow(matmul(normed_q, cross_matrices[0]) + b_cross[2])
    colors_low = lax.all_gather(pixel_colors, ("rows", "cols"), axis=0, tiled=False)
    colors_low = lax.dynamic_index_in_dim(colors_low, row_place, axis=2, keepdims=False)
    colors_low = colors_low.reshape(grid_rows, grid_cols, 3, tile_rows, tile_cols)
    colors = to_float(
        jnp.transpose(colors_low, (2, 1, 4, 0, 3)).reshape(
            3, grid_cols * tile_cols, grid_rows * tile_rows
        )
    )
    image_box = lax.dynamic_index_in_dim(image_boxes, row_place, axis=0, keepdims=False)
    canvas = canvas_of(colors, image_box)
    mean, deviation, row_in, col_in = canvas[2:]
    inside = (col_in[:, None] & row_in[None, :])[None]
    key_weight = input_matrices[0]
    value_weight = input_matrices[1]
    query_inputs = inner_right(query_rows, key_weight)
    query_lines = against_pixels(query_inputs * g_input, colors, canvas)
    query_shift = jnp.sum(query_inputs * b_input, axis=1)
    scores = jnp.where(
        inside, (query_lines + query_shift[:, None, None]) * score_scale, NEG
    )
    peak_score = jnp.max(scores, axis=(1, 2), keepdims=True)
    weights = jnp.where(inside, jnp.exp(scores - peak_score), 0.0)
    cross_probs = weights / jnp.sum(weights, axis=(1, 2), keepdims=True)
    plain_mixed = over_pixels(cross_probs, colors, canvas)
    mixed_inputs = (
        plain_mixed * g_input + jnp.sum(cross_probs, axis=(1, 2))[:, None] * b_input
    )
    mixed_low = narrow(mixed_inputs)
    attended = matmul(mixed_low, value_weight) + b_cross[3]
    attended_low = narrow(attended)
    first = latent_state + matmul(attended_low, cross_out) + b_cross[4]
    branch, cross_stored = mlp_forward(
        first, g_cross[1], b_cross[1], cross_matrices[1], b_cross[5], cross_matrices[2], b_cross[6]
    )
    second = first + branch
    normed_t = narrow(layer_norm(second, g_self[0], b_self[0]))
    tower_queries = narrow(matmul(normed_t, self_matrices[0]) + b_self[2])
    tower_keys = narrow(matmul(normed_t, self_matrices[1]))
    tower_values = narrow(matmul(normed_t, self_matrices[2]) + b_self[3])
    keys_group, values_group = (
        lax.all_gather(tower_keys, "cols", axis=0, tiled=True),
        lax.all_gather(tower_values, "cols", axis=0, tiled=True),
    )
    group_rows = keys_group.shape[0]
    query_image = (
        (row_place * grid_cols + col_place) * rows_dev + jnp.arange(rows_dev, dtype=jnp.int32)
    ) // LATENTS
    key_image = (row_place * group_rows + jnp.arange(group_rows, dtype=jnp.int32)) // LATENTS
    same_image = (query_image[:, None] == key_image[None, :])[None]
    query_heads = tower_queries.reshape(rows_dev, HEADS, HEAD_DIM)
    key_heads = keys_group.reshape(group_rows, HEADS, HEAD_DIM)
    value_heads = values_group.reshape(group_rows, HEADS, HEAD_DIM)
    head_scores = jnp.where(
        same_image,
        jnp.einsum("qhd,khd->hqk", query_heads, key_heads, preferred_element_type=jnp.float32)
        * head_scale,
        NEG,
    )
    head_weights = jnp.where(
        same_image, jnp.exp(head_scores - jnp.max(head_scores, axis=2, keepdims=True)), 0.0
    )
    head_probs = head_weights / jnp.sum(head_weights, axis=2, keepdims=True)
    probs_low = narrow(head_probs)
    tower_mixed = narrow(
        jnp.einsum(
            "hqk,khd->qhd", probs_low, value_heads, preferred_element_type=jnp.float32
        ).reshape(rows_dev, model_width)
    )
    third = second + matmul(tower_mixed, self_out) + b_self[4]
    branch, tower_stored = mlp_forward(
        third, g_self[1], b_self[1], self_matrices[3], b_self[5], self_matrices[4], b_self[6]
    )
    new_latents = narrow(third + branch)
    gradient = to_float(cotangent)
    gradient, tower_mlp_w, tower_mlp_v, tower_lows = mlp_backward(
        third, g_self[1], b_self[1], self_matrices[3], self_matrices[4], tower_stored, gradient
    )
    tower_out_low = narrow(gradient)
    d_self_out = inner_left(tower_mixed, tower_out_low)
    d_self_out_bias = jnp.sum(gradient, axis=0)
    d_mixed = narrow(inner_right(tower_out_low, self_out)).reshape(rows_dev, HEADS, HEAD_DIM)
    d_probs = jnp.einsum("qhd,khd->hqk", d_mixed, value_heads, preferred_element_type=jnp.float32)
    d_value_heads = jnp.einsum(
        "hqk,qhd->khd", probs_low, d_mixed, preferred_element_type=jnp.float32
    )
    d_scores = head_probs * (d_probs - jnp.sum(head_probs * d_probs, axis=2, keepdims=True))
    d_scores_low = narrow(d_scores * head_scale)
    d_query_heads = jnp.einsum(
        "hqk,khd->qhd", d_scores_low, key_heads, preferred_element_type=jnp.float32
    ).reshape(rows_dev, model_width)
    d_key_heads = jnp.einsum(
        "hqk,qhd->khd", d_scores_low, query_heads, preferred_element_type=jnp.float32
    )
    d_tower_keys, d_tower_values = (
        lax.psum_scatter(
            d_key_heads.reshape(group_rows, model_width).astype(jnp.bfloat16),
            "cols",
            scatter_dimension=0,
            tiled=True,
        ).astype(jnp.float32),
        lax.psum_scatter(
            d_value_heads.reshape(group_rows, model_width).astype(jnp.bfloat16),
            "cols",
            scatter_dimension=0,
            tiled=True,
        ).astype(jnp.float32),
    )
    tq_low = narrow(d_query_heads)
    tk_low = narrow(d_tower_keys)
    tv_low = narrow(d_tower_values)
    d_normed_t = (
        inner_right(tq_low, self_matrices[0])
        + inner_right(tk_low, self_matrices[1])
        + inner_right(tv_low, self_matrices[2])
    )
    d_second, d_self_gain, d_self_bias = norm_back(second, g_self[0], b_self[0], d_normed_t)
    gradient = gradient + d_second
    self_gain_grad = jnp.stack([d_self_gain, tower_mlp_v[0]])
    self_bias_grad = jnp.stack(
        [
            d_self_bias,
            tower_mlp_v[1],
            jnp.sum(d_query_heads, axis=0),
            jnp.sum(d_tower_values, axis=0),
            d_self_out_bias,
            tower_mlp_v[2],
            tower_mlp_v[3],
        ]
    )
    gradient, cross_mlp_w, cross_mlp_v, cross_lows = mlp_backward(
        first, g_cross[1], b_cross[1], cross_matrices[1], cross_matrices[2], cross_stored, gradient
    )
    cross_out_low = narrow(gradient)
    d_cross_out = inner_left(attended_low, cross_out_low)
    d_cross_out_bias = jnp.sum(gradient, axis=0)
    d_attended = narrow(inner_right(cross_out_low, cross_out))
    value_shift = jnp.sum(to_float(d_attended) * b_cross[3], axis=1)
    row_delta = jnp.sum(to_float(d_attended) * attended, axis=1) - value_shift
    grad_inputs = inner_right(d_attended, value_weight)
    grad_shift = jnp.sum(grad_inputs * b_input, axis=1)
    grad_lines = against_pixels(grad_inputs * g_input, colors, canvas)
    d_scores = (
        cross_probs * (grad_lines + (grad_shift - row_delta)[:, None, None]) * score_scale
    )
    plain_scores = over_pixels(d_scores, colors, canvas)
    score_sum = jnp.sum(d_scores, axis=(1, 2))
    prob_sum = jnp.sum(cross_probs, axis=(1, 2))
    score_inputs = plain_scores * g_input + score_sum[:, None] * b_input
    score_low = narrow(score_inputs)
    d_query_rows = matmul(score_low, key_weight)
    in_gain_part = jnp.sum(query_inputs * plain_scores + grad_inputs * plain_mixed, axis=0)
    in_bias_part = jnp.sum(
        query_inputs * score_sum[:, None] + grad_inputs * prob_sum[:, None], axis=0
    )
    query_scaled = query_inputs * g_input
    grad_scaled = grad_inputs * g_input
    query_away = query_scaled[:, :3] - jnp.mean(query_scaled, axis=1, keepdims=True)
    grad_away = grad_scaled[:, :3] - jnp.mean(grad_scaled, axis=1, keepdims=True)
    along = jnp.sum(d_scores * query_lines + cross_probs * grad_lines, axis=0) / input_width
    color_parts = jnp.einsum(
        "rj,rcy->jcy", query_away, d_scores, precision=lax.Precision.HIGHEST
    ) + jnp.einsum("rj,rcy->jcy", grad_away, cross_probs, precision=lax.Precision.HIGHEST)
    color_parts = deviation[None] * (
        color_parts - (colors - mean[None]) * deviation[None] * along[None]
    )
    color_parts = color_parts.reshape(3, grid_cols, tile_cols, grid_rows, tile_rows)
    color_parts = jnp.transpose(color_parts, (3, 1, 0, 4, 2)).reshape(
        grid_rows * grid_cols, 3, tile_rows, tile_cols
    )
    color_grad = lax.all_to_all(
        color_parts, ("rows", "cols"), split_axis=0, concat_axis=0, tiled=True
    ).reshape(image_count, grid_cols, 3, tile_rows, tile_cols)
    color_grad = jnp.transpose(jnp.sum(color_grad, axis=1), (1, 0, 2, 3))
    query_low = narrow(d_query_rows)
    d_latent, d_cross_gain, d_cross_bias = norm_back(
        latent_state, g_cross[0], b_cross[0], inner_right(query_low, cross_matrices[0])
    )
    latent_grad = gradient + d_latent
    in_gain_grad, in_bias_grad = lax.psum((in_gain_part, in_bias_part), ("rows", "cols"))
    vectors = jnp.stack(
        [
            d_cross_gain,
            cross_mlp_v[0],
            d_cross_bias,
            cross_mlp_v[1],
            jnp.sum(d_query_rows, axis=0),
            jnp.sum(to_float(d_attended), axis=0),
            d_cross_out_bias,
            cross_mlp_v[2],
            cross_mlp_v[3],
            d_self_gain,
            tower_mlp_v[0],
            d_self_bias,
            tower_mlp_v[1],
            jnp.sum(d_query_heads, axis=0),
            jnp.sum(d_tower_values, axis=0),
            d_self_out_bias,
            tower_mlp_v[2],
            tower_mlp_v[3],
        ]
    )
    vector_sums = lax.psum_scatter(vectors, ("rows", "cols"), scatter_dimension=1, tiled=True)
    lefts = jnp.stack(
        [
            normed_q,
            cross_stored[0],
            cross_stored[2],
            attended_low,
            normed_t,
            tower_stored[0],
            tower_stored[2],
            tower_mixed,
        ]
    )
    rights = jnp.stack(
        [
            query_low,
            cross_lows[0],
            cross_lows[1],
            cross_out_low,
            d_attended,
            query_rows,
            tq_low,
            tk_low,
            tv_low,
            tower_lows[0],
            tower_lows[1],
            tower_out_low,
        ]
    )
    small_lefts = jnp.stack([mixed_low, score_low])
    lefts = lax.all_gather(lefts, "cols", axis=1, tiled=True)
    small_lefts = lax.all_gather(small_lefts, "cols", axis=1, tiled=True)
    own = model_width // (grid_rows * grid_cols)
    rights = rights.reshape(rights.shape[0], rows_dev, grid_rows, grid_cols, own)
    rights = lax.all_to_all(
        jnp.transpose(rights, (3, 0, 1, 2, 4)), "cols", split_axis=0, concat_axis=0, tiled=False
    )
    rights = jnp.transpose(rights, (1, 0, 2, 3, 4)).reshape(
        rights.shape[1], grid_cols * rows_dev, grid_rows * own
    )
    pairs = ((0, 0), (1, 1), (2, 2), (3, 3), (4, 6), (4, 7), (4, 8), (5, 9), (6, 10), (7, 11))
    big = [inner_left(rights[k], lefts[i]).reshape(grid_rows, own, model_width) for i, k in pairs]
    small = [
        inner_left(rights[k], small_lefts[i]).reshape(grid_rows, own, input_width)
        for i, k in ((1, 5), (0, 4))
    ]
    big = lax.psum_scatter(jnp.stack(big, axis=1), "rows", scatter_dimension=0, tiled=False)
    small = lax.psum_scatter(jnp.stack(small, axis=1), "rows", scatter_dimension=0, tiled=False)
    big = jnp.transpose(big, (0, 2, 1))
    small = jnp.transpose(small, (0, 2, 1))
    all_sums = (
        big[:3],
        big[3],
        small,
        vector_sums[:2],
        vector_sums[2:9],
        big[4:9],
        big[9],
        vector_sums[9:11],
        vector_sums[11:],
    )
    cross_sums = all_sums[:5]
    self_sums = all_sums[5:]
    return (
        new_latents,
        latent_grad,
        color_grad,
        prior_cross_matrices + cross_sums[0],
        prior_cross_out + cross_sums[1],
        prior_input_matrices + cross_sums[2],
        in_gain_grad,
        in_bias_grad,
        cross_sums[3],
        cross_sums[4],
        self_sums[0],
        self_sums[1],
        self_sums[2],
        self_sums[3],
    )


STEPS_HELD = 8
GROUP = 12
XS = {0: 0, 3: 1, 4: 2, 5: 3, 6: 4}
LANES = 128
MESH = pl.DeviceIdType.MESH
WIDE = 3 * LANES


def own_dot(former, latter, former_dim, latter_dim):
    return lax.dot_general(
        former,
        latter,
        (((former_dim,), (latter_dim,)), ((), ())),
        preferred_element_type=jnp.float32,
    )


def selections(tile_cols, grid_cols, steps):
    held = STEPS_HELD
    blocks = -(-steps // held)
    place = np.zeros((grid_cols * 32, WIDE), np.float32)
    back = np.zeros((grid_cols * 32, blocks * LANES), np.float32)
    for tile in range(grid_cols):
        for channel in range(3):
            for offset in range(tile_cols):
                col = tile * tile_cols + offset
                line = tile * 32 + channel * tile_cols + offset
                place[line, channel * LANES + col] = 1
                half, step = divmod(col, steps)
                back[line, step * 16 + half * 8 + channel] = 1
    pick = np.zeros((7 * LANES, blocks * LANES), np.float32)
    for step in range(steps):
        for half in range(2):
            for slot, kind in enumerate((0, 1, 2, 3, 4, 3, 5, 6)):
                pick[kind * LANES + half * steps + step, step * 16 + half * 8 + slot] = 1
    spread = np.zeros((LANES, 2 * LANES), np.float32)
    for group in range(16):
        for channel in range(3):
            for slot in (3, 4):
                spread[group * 8 + slot, group * 8 + channel] = 1
            for slot in (6, 7):
                spread[group * 8 + slot, LANES + group * 8 + channel] = 1
    low = lambda values: np.asarray(values, ml_dtypes.bfloat16)
    return (low(place), low(pick), low(spread), low(back))


def norm_parts(values):
    middle = jnp.mean(values, axis=1, keepdims=True)
    centered = values - middle
    spread = jnp.mean(centered * centered, axis=1, keepdims=True)
    factor = lax.rsqrt(spread + EPS)
    return (centered * factor, factor)


def norm_forward(values, gain, offset):
    return narrow(norm_parts(values)[0] * gain + offset)


def norm_gradient(values, gain, gradient):
    plain, factor = norm_parts(values)
    inner = gradient * gain
    first = jnp.mean(inner, axis=1, keepdims=True)
    second = jnp.mean(inner * plain, axis=1, keepdims=True)
    return (
        factor * (inner - first - plain * second),
        jnp.sum(gradient * plain, axis=0, keepdims=True),
        jnp.sum(gradient, axis=0, keepdims=True),
    )


GELU_RATE = 0.7978845608028654
GELU_CUBE = 0.044715


def gelu_value(u):
    return 0.5 * u * (1.0 + jnp.tanh(GELU_RATE * (u + GELU_CUBE * u * u * u)))


def gelu_slope(u):
    bent = jnp.tanh(GELU_RATE * (u + GELU_CUBE * u * u * u))
    return 0.5 * (1.0 + bent) + 0.5 * u * (1.0 - bent * bent) * GELU_RATE * (
        1.0 + 3.0 * GELU_CUBE * u * u
    )


def waves(turns):
    near = turns - 2.0 * jnp.floor(turns * 0.5 + 0.5)
    return (jnp.sin(jnp.pi * near), jnp.cos(jnp.pi * near))


def axis_lines(place, slot):
    lane = lax.broadcasted_iota(jnp.int32, (place.shape[0], LANES), 1)
    band = lax.rem(lane, NBANDS)
    frequency = 1.0 + to_float(band) * ((FREQ_TOP - 1.0) / (NBANDS - 1))
    sine, cosine = waves(place * frequency)
    return jnp.concatenate(
        [jnp.where(lane < NBANDS, sine, cosine), jnp.where(lane == slot, place, 0.0)], axis=1
    )


def layer_kernel(
    sizes,
    boxes, latents, cotangent, colors, in_gain, in_bias, cross_gains, cross_biases, self_gains,
    self_biases, far_order, far_place, far_pick, far_spread, far_back,
    w_cross, w_out, w_self, w_self_out, w_input,
    new_latents, latent_grad, color_out, cross_total, out_total, self_total, self_out_total,
    input_parts, vector_out, input_vector_out,
    order, place, pick, spread, back, wts, win, win_raw, xbuf, xsmall, gsrc, gbuf, staged, paired, handed, crossed, staged_small, paired_small, handed_small, crossed_small, kept_small,
    line_rows, line_hid, line_right, line_staged, line_near, line_hand, line_sums,
    row_pair, row_hand, row_cross, row_kept, row_turned, row_done, biases,
    color_tiles, colstage, colbuf, img, img7, fa, ft, sl, ycoef, xcoef, yfeat, xfeat, mixrow,
    cgright, rowsum, colsum, cgacc, cgsend, cgbuf, cgsum, cgfin,
    act, lnvec, lnsend, lnbuf, vecsend, vecbuf,
    heads, probs, prob_grad, mix_s, mix_b, dmix_b, dqkv_s, dqkv_b,
    fixed_sem, weight_sem, x_send, x_recv, y_send, y_recv, g_send, g_recv, a_send, a_recv, r_send, r_recv, f_send, f_recv, l_send, l_recv,
    misc_send, misc_recv,
):
    grid_rows, grid_cols, rows, steps, tile_rows, tile_cols = sizes
    n_dev = grid_rows * grid_cols
    width = latents.shape[1]
    quads = grid_cols // 2
    chunk = width // grid_cols
    own = chunk // grid_rows
    tall = grid_rows * tile_rows
    z = lax.axis_index("rows")
    j = lax.axis_index("cols")
    core = lax.rem(j, 2)
    quad = j // 2
    me = z * grid_cols + j
    f32, bf16 = jnp.float32, jnp.bfloat16
    score_scale = width ** (-0.5)
    head_scale = HEAD_DIM ** (-0.5)

    def at_device(d):
        return {"rows": d // grid_cols, "cols": lax.rem(d, grid_cols)}

    def lanes_of(index):
        return pl.ds(pl.multiple_of(index * chunk, chunk), chunk)

    def push(src, dst, send, recv, where):
        pltpu.make_async_remote_copy(
            src_ref=src, dst_ref=dst, send_sem=send, recv_sem=recv, device_id=where,
            device_id_type=MESH,
        ).start()

    def wait_for(ref, sem):
        pltpu.make_async_copy(ref, ref, sem).wait()

    barrier = pltpu.get_barrier_semaphore()

    def greet_plane(step, carry):
        where = {"cols": lax.rem(j + step, grid_cols)}
        pl.semaphore_signal(barrier, inc=1, device_id=where, device_id_type=MESH)
        return carry

    def greet_line(step, carry):
        where = {"rows": lax.rem(z + step, grid_rows)}
        pl.semaphore_signal(barrier, inc=1, device_id=where, device_id_type=MESH)
        return carry

    lax.fori_loop(1, grid_rows, greet_line, 0)
    lax.fori_loop(1, grid_cols, greet_plane, 0)

    sources = (
        [w_cross.at[0], w_out, w_cross.at[1], w_cross.at[2]]
        + [w_self.at[0], w_self.at[1], w_self.at[2], w_self_out, w_self.at[3], w_self.at[4]]
    )
    CQ, CO, C1, C2, SQ, SK, SV, SO, S1, S2 = range(10)
    loads = [pltpu.make_async_copy(s, wts.at[k], weight_sem.at[k]) for k, s in enumerate(sources)]
    loads.append(pltpu.make_async_copy(w_input, win_raw, weight_sem.at[10]))
    loads[CQ].start()
    loads[10].start()
    fixed = ((far_order, order), (far_place, place), (far_pick, pick), (far_spread, spread), (far_back, back))
    fixed = [pltpu.make_async_copy(src, dst, fixed_sem.at[k]) for k, (src, dst) in enumerate(fixed)]
    for copy in fixed:
        copy.start()

    cgsum[...] = jnp.zeros(cgsum.shape, f32)
    for channel in range(3):
        for col in range(tile_cols):
            line = channel * tile_cols + col
            shown = to_float(colors[channel, col])
            for image in range(grid_rows):
                cgsum[image, line : line + 1, :tile_rows] = shown[image : image + 1]
    color_tiles[...] = narrow(cgsum[...])
    gc, bc = to_float(cross_gains[...]), to_float(cross_biases[...])
    gs, bs = to_float(self_gains[...]), to_float(self_biases[...])
    fixed[0].wait()
    gains_here = [to_float(ref[...]).reshape(1, -1) for ref in (in_gain, in_bias)]
    gains_here = jnp.concatenate(gains_here + [jnp.zeros((6, in_gain.shape[0]), f32)], axis=0)
    gains_here = own_dot(narrow(gains_here), order[...], 1, 1)
    gin, bin_ = gains_here[0:1], gains_here[1:2]
    lat = to_float(latents[...])
    nq = norm_forward(lat, gc[0:1], bc[0:1])
    xbuf[0, core, quad] = nq
    cot_low = cotangent[...]
    xbuf[XS[6], core, quad] = cot_low
    biases[...] = jnp.concatenate([bc, jnp.zeros((1, width), f32)], axis=0)
    pl.semaphore_wait(barrier, grid_cols + grid_rows - 2)

    def send_color(step, carry):
        image = lax.rem(z + step, grid_rows)
        push(color_tiles.at[image], colstage.at[z], misc_send.at[5], misc_recv.at[5], {"rows": image})
        return carry

    lax.fori_loop(1, grid_rows, send_color, 0)
    colstage[z] = color_tiles[z]

    def x_spread(block, sem):
        def one(step, carry):
            peer = 2 * lax.rem(quad + step, quads) + core
            push(block, block, x_send.at[sem], x_recv.at[sem], {"cols": peer})
            return carry

        lax.fori_loop(1, quads, one, 0)

    def x_relay(half, sem):
        wait_for(half.at[pl.ds(0, quads - 1)], x_recv.at[sem])
        push(half, half, y_send.at[sem], y_recv.at[sem], {"cols": j + 1 - 2 * core})

    def x_arrived(half, sem):
        wait_for(half, y_recv.at[sem])

    pieces = rows // 16
    sent = {}

    def spread_x(k):
        x_spread(xbuf.at[XS[k], core, quad], k)

    def background(point):
        for k, count in PLAN.get(point, ()):
            for piece in range(sent.get(k, 0), sent.get(k, 0) + count):
                x_spread(xbuf.at[XS[k], core, quad, pl.ds(piece * 16, 16)], k)
            sent[k] = sent.get(k, 0) + count

    def relay_x(k):
        x_relay(xbuf.at[XS[k], core], k)

    def have_x(k):
        x_arrived(xbuf.at[XS[k], 1 - core], k)

    def to_plane(step):
        peer = lax.rem(j + step, grid_cols)
        return peer, {"cols": peer}

    def regroup(values):
        tiles = [values[:, t * LANES : (t + 1) * LANES] for t in range(width // LANES)]
        piece = lax.broadcasted_iota(jnp.int32, tiles[0].shape, 1) // own
        result = []
        for peer in range(grid_cols):
            chunk_now = None
            for part in range(grid_rows):
                tile, offset = divmod((part * grid_cols + peer) * own, LANES)
                shift = (part * own - offset) % LANES
                moved = pltpu.roll(tiles[tile], shift, 1) if shift else tiles[tile]
                chunk_now = moved if part == 0 else jnp.where(piece == part, moved, chunk_now)
            result.append(chunk_now)
        return jnp.concatenate(result, axis=1)

    def spread_g(k, values):
        spread_plain(k, narrow(regroup(to_float(values))))

    def spread_plain(k, values):
        gsrc[k] = values

        def one(step, carry):
            peer, where = to_plane(step)
            push(gsrc.at[k, :, lanes_of(peer)], gbuf.at[k, core, quad], g_send.at[k], g_recv.at[k], where)
            return carry

        lax.fori_loop(1, grid_cols, one, 0)
        gbuf[k, core, quad] = gsrc[k, :, lanes_of(j)]

    def have_g(k):
        wait_for(gsrc.at[k, :, pl.ds(0, chunk * (grid_cols - 1))], g_recv.at[k])
        return gbuf[k].reshape(grid_cols * rows, chunk)

    partner = z + 1 - 2 * lax.rem(z, 2)
    across = lax.rem(z + 2, grid_rows)

    def block_at(part):
        return pl.ds(pl.multiple_of(part * own, own), own)

    def send_parts(src, pair, sem):
        for slot, part in enumerate((partner, lax.rem(partner + 2, grid_rows))):
            push(src.at[block_at(part)], pair.at[slot], r_send.at[sem], r_recv.at[sem], {"rows": partner})

    def join_parts(src, pair, hand, far, kept, sem):
        wait_for(pair, r_recv.at[sem])
        hand[...] = narrow(to_float(src[block_at(across)]) + to_float(pair[1]))
        push(hand, far, f_send.at[sem], f_recv.at[sem], {"rows": across})
        kept[...] = to_float(src[block_at(z)]) + to_float(pair[0])

    def kept_of(m):
        if m < 3:
            return cross_total.at[m]
        if m < 9:
            return self_total.at[m - 4]
        return self_out_total

    def slot_of(m):
        return 0 if m == 0 else m - 3

    def join(m):
        k = slot_of(m)
        join_parts(staged.at[k], paired.at[k], handed.at[k], crossed.at[k], kept_of(m), m)

    def columns_of(part):
        size = width // grid_rows
        return pl.ds(pl.multiple_of(part * size, size), size)

    def send_rows(src, sem):
        for slot, part in enumerate((partner, lax.rem(partner + 2, grid_rows))):
            push(src.at[:, columns_of(part)], row_pair.at[slot], r_send.at[sem], r_recv.at[sem], {"rows": partner})

    def join_rows(src, sem):
        wait_for(row_pair, r_recv.at[sem])
        row_hand[...] = narrow(to_float(src[:, columns_of(across)]) + to_float(row_pair[1]))
        push(row_hand, row_cross, f_send.at[sem], f_recv.at[sem], {"rows": across})
        row_kept[...] = to_float(src[:, columns_of(z)]) + to_float(row_pair[0])

    def finish_rows(sem):
        wait_for(row_cross, f_recv.at[sem])
        row_turned[...] = jnp.transpose(row_kept[...] + to_float(row_cross[...]))

        def one(step, carry):
            peer, where = to_plane(step)
            push(row_turned.at[block_at(peer)], row_done.at[:, lanes_of(j)], a_send.at[3], a_recv.at[3], where)
            return carry

        lax.fori_loop(1, grid_cols, one, 0)
        row_done[:, lanes_of(j)] = row_turned[block_at(j)]

    def to_line(step):
        part = lax.rem(z + step, grid_rows)
        return part, {"rows": part}

    def spread_line():
        def one(step, carry):
            part, where = to_line(step)
            push(line_rows.at[z], line_rows.at[z], x_send.at[1], x_recv.at[1], where)
            return carry

        lax.fori_loop(1, grid_rows, one, 0)

    def line_hidden(k, bias):
        wait_for(line_rows.at[pl.ds(0, grid_rows - 1)], x_recv.at[1])

        def one(n, carry):
            at = pl.ds(pl.multiple_of(n * 256, 256), 256)
            x = line_rows[...].reshape(grid_rows * rows, width)
            pre = own_dot(x, wts[k, :, at], 1, 0) + bias[:, at]
            line_hid[:, :, at] = narrow(gelu_value(pre)).reshape(grid_rows, rows, 256)
            return carry

        lax.fori_loop(0, width // 256, one, 0, unroll=2)

    def spread_columns(m, values):
        gsrc[m] = values

        def one(step, carry):
            part, where = to_line(step)
            push(
                gsrc.at[m, :, columns_of(part)], line_right.at[m - 1, z], g_send.at[m], g_recv.at[m], where
            )
            return carry

        lax.fori_loop(1, grid_rows, one, 0)
        line_right[m - 1, z] = gsrc[m, :, columns_of(z)]

    def line_part(m, left):
        wait_for(line_right.at[m - 1, pl.ds(0, grid_rows - 1)], g_recv.at[m])
        size = width // grid_rows
        turned = jnp.transpose(line_right[m - 1].reshape(grid_rows * rows, size))

        def one(n, carry):
            at = pl.ds(pl.multiple_of(n * 256, 256), 256)
            block = left[:, :, at].reshape(grid_rows * rows, 256)
            line_staged[m - 1, :, at] = narrow(own_dot(turned, block, 1, 0))
            return carry

        lax.fori_loop(0, width // 256, one, 0, unroll=4)

        for q in range(quads):
            push(
                line_staged.at[m - 1, block_at(2 * q + 1 - core)], line_near.at[m - 1, q],
                y_send.at[m], y_recv.at[m], {"cols": j + 1 - 2 * core},
            )

    def line_join(m):
        wait_for(line_near.at[m - 1], y_recv.at[m])
        for q in range(quads):
            both = to_float(line_staged[m - 1, block_at(2 * q + core)]) + to_float(line_near[m - 1, q])
            line_hand[m - 1, q] = narrow(both)

        def give(step, carry):
            q = lax.rem(quad + step, quads)
            push(
                line_hand.at[m - 1, q], line_sums.at[m - 1, quad], l_send.at[m - 1], l_recv.at[m - 1],
                {"cols": 2 * q + core},
            )
            return carry

        lax.fori_loop(1, quads, give, 0)
        line_sums[m - 1, quad] = line_hand[m - 1, quad]

    def line_total(m):
        wait_for(line_sums.at[m - 1, pl.ds(0, quads - 1)], l_recv.at[m - 1])
        result = to_float(line_sums[m - 1, 0])
        for q in range(1, quads):
            result = result + to_float(line_sums[m - 1, q])
        cross_total[m] = result

    def join_small(m):
        join_parts(
            staged_small.at[m], paired_small.at[m], handed_small.at[m], crossed_small.at[m],
            kept_small.at[m], 10 + m,
        )

    def weight_part(m, right, left):
        turned = jnp.transpose(right)

        def one(n, carry):
            at = pl.ds(pl.multiple_of(n * 256, 256), 256)
            block = left[:, :, :, at].reshape(grid_cols * rows, 256)
            staged[slot_of(m), :, at] = narrow(own_dot(turned, block, 1, 0))
            return carry

        lax.fori_loop(0, width // 256, one, 0, unroll=4)
        if m == 8:
            send_rows(staged.at[slot_of(m)], m)
        else:
            send_parts(staged.at[slot_of(m)], paired.at[slot_of(m)], m)

    def small_part(m, right, left):
        staged_small[m] = narrow(own_dot(right, left[...].reshape(grid_cols * rows, WIDE), 0, 0))
        send_parts(staged_small.at[m], paired_small.at[m], 10 + m)

    def times(x, k, out):
        def one(n, carry):
            at = pl.ds(pl.multiple_of(n * 256, 256), 256)
            out[:, at] = own_dot(x, wts[k, :, at], 1, 0)
            return carry

        lax.fori_loop(0, width // 256, one, 0, unroll=4)

    def times_t(x, k, out, add=False):
        def one(n, carry):
            at = pl.ds(pl.multiple_of(n * 256, 256), 256)
            result = own_dot(x, wts[k, at, :], 1, 1)
            out[:, at] = out[:, at] + result if add else result
            return carry

        lax.fori_loop(0, width // 256, one, 0, unroll=4)

    FIRST, SECOND, THIRD, PRE_C, PRE_S, TMP, ATT, GRAD = range(8)
    COT_BACK = GRAD
    tmp = act.at[TMP]

    wait_for(colstage.at[pl.ds(0, grid_rows - 1)], misc_recv.at[5])

    def send_strip(step, carry):
        peer, where = to_plane(step)
        push(colstage, colbuf.at[j], misc_send.at[0], misc_recv.at[0], where)
        return carry

    lax.fori_loop(1, grid_cols, send_strip, 0)
    colbuf[j] = colstage[...]
    loads[CQ].wait()
    for k in range(1, 10):
        loads[k].start()
    times(nq, CQ, tmp)
    query_low = narrow(tmp[...] + bc[2:3])
    spread_x(0)
    spread_g(7, query_low)
    spread_x(6)
    loads[10].wait()
    for k in range(2):
        win[k] = narrow(own_dot(order[...], win_raw[:, k, :], 1, 0))
    query_inputs = own_dot(query_low, win[0], 1, 1)
    spare = pl.ds(2 * LANES, 16)
    spare_row = lax.broadcasted_iota(jnp.int32, (16, width), 0)
    win[1, spare, :] = narrow(jnp.where(spare_row == 5, bc[3:4], to_float(win[1, spare, :])))

    box = [boxes[z, k] for k in range(4)]

    def filled(value, shape):
        return to_float(jnp.full(shape, value, jnp.int32))

    row_at = lax.broadcasted_iota(jnp.int32, (tall, 1), 0)
    y_place = -1.0 + 2.0 * to_float(row_at - box[0]) / filled(box[2] - 1, (tall, 1))
    y_lines = axis_lines(y_place, 3)
    y_sum = jnp.sum(y_lines, axis=1, keepdims=True)
    row_out = jnp.where((row_at >= box[0]) & (row_at < box[0] + box[2]), 0.0, NEG)
    yfeat[...] = narrow(y_lines)
    held_rows = xfeat.shape[1]
    col_lane = lax.broadcasted_iota(jnp.int32, (held_rows, LANES), 1)
    col_row = lax.broadcasted_iota(jnp.int32, (held_rows, LANES), 0)
    x_sum = jnp.zeros((1, LANES), f32)
    col_out = []
    for half in range(2):
        col_at = lax.broadcasted_iota(jnp.int32, (held_rows, 1), 0) + half * steps
        x_place = -1.0 + 2.0 * to_float(col_at - box[1]) / filled(box[3] - 1, (held_rows, 1))
        x_lines = axis_lines(x_place, 4)
        xfeat[half] = narrow(x_lines)
        here = (col_lane == col_row + half * steps) & (col_row < steps)
        x_sum = x_sum + jnp.sum(
            jnp.where(here, jnp.sum(x_lines, axis=1, keepdims=True), 0.0), axis=0, keepdims=True
        )
        col_out.append(jnp.where((col_at >= box[1]) & (col_at < box[1] + box[3]), 0.0, NEG))
    x_lane = lax.broadcasted_iota(jnp.int32, (1, LANES), 1)
    x_here = -1.0 + 2.0 * to_float(x_lane - box[1]) / filled(box[3] - 1, (1, LANES))
    count = 3 + 2 + 4 * NBANDS

    lane1 = lax.broadcasted_iota(jnp.int32, (rows, LANES), 1)
    lane_half = lax.broadcasted_iota(jnp.int32, (8, LANES), 1) // rows
    sub8 = lax.broadcasted_iota(jnp.int32, (8, LANES), 0)

    def twice(values):
        return jnp.concatenate([values, values], axis=0)

    def turn(values):
        return jnp.transpose(twice(values))[:8]

    def coefficients(scaled, extra):
        tail = scaled[:, 2 * LANES :]
        total = jnp.sum(scaled, axis=1, keepdims=True)
        turned = turn(jnp.where(lane1 == 5, total, jnp.where(lane1 == 6, extra, tail)))
        total_high = to_float(narrow(turned[5:6]))
        body = jnp.where(
            sub8 < 3, turned, jnp.where(sub8 < 5, -total_high, jnp.where(sub8 == 5, total_high - turned[5:6], 0.0))
        )
        body = narrow(jnp.concatenate(
            [jnp.where(lane_half == 0, body, 0.0), jnp.where(lane_half == 1, body, 0.0)], axis=0
        ))
        ones = jnp.where(sub8 >= 6, 1.0, 0.0)
        ones = narrow(jnp.concatenate(
            [jnp.where(lane_half == 0, ones, 0.0), jnp.where(lane_half == 1, ones, 0.0)], axis=0
        ))
        mixrow[...] = jnp.zeros(mixrow.shape, bf16)
        for held in range(STEPS_HELD):
            mixrow[held, held * 16 : held * 16 + 16, :] = jnp.concatenate([body, ones], axis=1)
        scaled_low = narrow(jnp.concatenate([scaled[:, :LANES], tail], axis=1))
        ycoef[...] = own_dot(yfeat[...], twice(scaled_low), 1, 1)
        scaled_low = narrow(jnp.concatenate([scaled[:, LANES : 2 * LANES], tail], axis=1))
        nothing = jnp.zeros_like(scaled_low)
        xcoef[...] = own_dot(xfeat[0], jnp.concatenate([scaled_low, nothing], axis=0), 1, 1) + own_dot(
            xfeat[1], jnp.concatenate([nothing, scaled_low], axis=0), 1, 1
        )
        return turned

    query_scaled = query_inputs * gin * score_scale
    coefficients(query_scaled, 0.0)
    ycoef[...] += row_out
    half_lane = lax.broadcasted_iota(jnp.int32, (held_rows, LANES), 1) // rows
    xcoef[...] += jnp.where(half_lane == 0, col_out[0], col_out[1])

    for copy in fixed[1:]:
        copy.wait()
    wait_for(colbuf.at[pl.ds(0, grid_cols - 1)], misc_recv.at[0])
    for part in range(grid_rows):
        at = pl.ds(part * tile_rows, tile_rows)
        tiles = colbuf[:, part].reshape(grid_cols * 32, LANES)
        img[at, :] = own_dot(tiles, place[...], 0, 0)[:tile_rows]
    c0, c1, c2 = img[:, :LANES], img[:, LANES : 2 * LANES], img[:, 2 * LANES :]
    mean = (c0 + c1 + c2 + y_sum + x_sum) * (1.0 / count)
    square = (c0 * c0 + c1 * c1 + c2 * c2 + y_place * y_place + x_here * x_here + 2.0 * NBANDS) * (
        1.0 / count
    )
    dev = lax.rsqrt(square - mean * mean + EPS)
    mean_low, dev_low = narrow(mean), narrow(dev)
    img7[...] = jnp.concatenate(
        [
            narrow(c0), narrow(c1), narrow(c2),
            mean_low, narrow(mean - to_float(mean_low)),
            dev_low, narrow(dev - to_float(dev_low)),
        ],
        axis=1,
    )
    blocks = fa.shape[0]
    for block in range(blocks):
        at = pl.ds(block * LANES, LANES)
        fa[block] = narrow(own_dot(img7[...], pick[:, at], 1, 0))
        turned = own_dot(pick[:, at], img7[...], 0, 1)
        line = lax.broadcasted_iota(jnp.int32, turned.shape, 0)
        ft[at, :] = narrow(jnp.where(lax.rem(line, 8) == 5, 1.0, turned))

    def step_lines(s):
        block, held = s // STEPS_HELD, lax.rem(s, STEPS_HELD)
        result = own_dot(fa[block], mixrow[held], 1, 0)
        deviation = result[:, LANES:]
        lines = (ycoef[...] + xcoef[pl.ds(s, 1), :] + result[:, :LANES]) * deviation
        return lines, deviation

    def pair_sums(s, weighted):
        at = pl.ds(pl.multiple_of(s * 16, 32), 32)
        both = own_dot(ft[at, :], jnp.concatenate([narrow(w) for w in weighted], axis=1), 1, 0)
        result = None
        for k in range(2):
            found = both[k * 16 : k * 16 + 16, k * LANES : (k + 1) * LANES]
            found = jnp.where(lane_half == 0, found[:8], found[8:])
            colsum[pl.ds(s + k, 1), :] = found[5:6]
            result = found if result is None else result + found
        return result

    def in_groups(one, first, last, start):
        def group(n, carry):
            rows_here = None
            for pair in range(GROUP // 2):
                weighted = []
                for k in range(2):
                    s = n * GROUP + pair * 2 + k
                    total, found, here = one(s, carry)
                    carry = (total, found)
                    weighted.append(here)
                    rows_here = here if rows_here is None else rows_here + here
                carry = (carry[0], carry[1] + pair_sums(n * GROUP + pair * 2, weighted))
            rowsum[...] += rows_here
            return carry

        return lax.fori_loop(first // GROUP, last // GROUP, group, start)

    def fold(values):
        return values[:rows] + values[rows:]

    def pixel_sums(found, factor):
        by_row = fold(own_dot(narrow(rowsum[...] * factor), yfeat[...], 0, 0))
        cols = narrow(colsum[...] * factor)
        by_col = own_dot(cols, xfeat[0], 0, 0)[:rows] + own_dot(cols, xfeat[1], 0, 0)[rows:]
        padded = jnp.concatenate([found * factor, jnp.zeros((LANES - 8, LANES), f32)], axis=0)
        sums = fold(jnp.transpose(padded))
        middle = sums[:, 3:4] + sums[:, 4:5]
        tail = jnp.where(lane1 < 3, sums, 0.0) + by_row[:, LANES:] + by_col[:, LANES:]
        return jnp.concatenate([by_row[:, :LANES], by_col[:, :LANES], tail], axis=1) - middle

    def other_half(line):
        return pltpu.roll(jnp.broadcast_to(line, (8, LANES)), rows, 1)[:1]

    def first_pass(s, best):
        lines, deviation = step_lines(s)
        sl[s] = lines
        return jnp.maximum(best, jnp.max(lines, axis=0, keepdims=True))

    best = lax.fori_loop(0, steps, first_pass, jnp.full((1, LANES), -3e38, f32), unroll=4)
    best = jnp.maximum(best, other_half(best))
    rowsum[...] = jnp.zeros(rowsum.shape, f32)
    colsum[...] = jnp.zeros(colsum.shape, f32)

    def second_pass(s, carry):
        total, found = carry
        block, held = s // STEPS_HELD, lax.rem(s, STEPS_HELD)
        deviation = own_dot(fa[block], mixrow[held][:, LANES:], 1, 0)
        weights = jnp.exp(sl[s] - best)
        total = total + jnp.sum(weights, axis=0, keepdims=True)
        return total, found, weights * deviation

    total, found = in_groups(
        second_pass, 0, steps, (jnp.zeros((1, LANES), f32), jnp.zeros((8, LANES), f32))
    )
    total = total + other_half(total)
    log_total = best + jnp.log(total)
    plain_mixed = pixel_sums(found, 1.0 / total)
    wide1 = lax.broadcasted_iota(jnp.int32, (rows, WIDE), 1)
    mixed_low = narrow(jnp.where(wide1 == 2 * LANES + 5, 1.0, plain_mixed * gin + bin_))
    xsmall[0, core, quad] = mixed_low
    relay_x(0)
    relay_x(6)
    attended = own_dot(mixed_low, win[1], 1, 0)
    act[ATT] = attended
    attended_low = narrow(attended)
    loads[CO].wait()
    times(attended_low, CO, tmp)
    first = lat + tmp[...] + bc[4:5]
    act[FIRST] = first
    normed_c = norm_forward(first, gc[1:2], bc[1:2])
    line_rows[z] = normed_c
    spread_line()
    loads[C1].wait()
    times(normed_c, C1, tmp)
    pre = tmp[...] + bc[5:6]
    act[PRE_C] = pre
    hidden_c = narrow(gelu_value(pre))
    loads[C2].wait()
    times(hidden_c, C2, tmp)
    second = act[FIRST] + tmp[...] + bc[6:7]
    act[SECOND] = second
    normed_t = norm_forward(second, gs[0:1], bs[0:1])
    xbuf[XS[4], core, quad] = normed_t
    mine = core * quads + quad

    def block_of(peer):
        return lax.rem(peer, 2) * quads + peer // 2

    def to_heads(kind, values):
        gsrc[9 + kind] = values

        def one(step, carry):
            peer, where = to_plane(step)
            push(
                gsrc.at[9 + kind, :, lanes_of(peer)], heads.at[kind, mine],
                a_send.at[4 + kind], a_recv.at[4 + kind], where,
            )
            return carry

        lax.fori_loop(1, grid_cols, one, 0)
        heads[kind, mine] = gsrc[9 + kind, :, lanes_of(j)]

    loads[SQ].wait()
    times(normed_t, SQ, tmp)
    to_heads(0, narrow(tmp[...] + bs[2:3]))
    loads[SK].wait()
    times(normed_t, SK, tmp)
    to_heads(1, narrow(tmp[...]))
    loads[SV].wait()
    times(normed_t, SV, tmp)
    to_heads(2, narrow(tmp[...] + bs[3:4]))
    background(0)
    loads[S2].wait()
    times_t(cot_low, S2, act.at[COT_BACK])
    head_rows = grid_cols * rows
    per = 128
    each = per // rows

    for kind in range(3):
        wait_for(heads.at[kind, pl.ds(0, grid_cols - 1)], a_recv.at[4 + kind])

    def head_of(kind):
        return heads[kind].reshape(head_rows, chunk)

    def head_part(kind, n):
        return heads[kind, pl.ds(n * each, each)].reshape(per, chunk)

    def head_forward(n, carry):
        at = pl.ds(pl.multiple_of(n * per, per), per)
        scores = own_dot(head_part(0, n), head_of(1), 1, 1) * head_scale
        weights = jnp.exp(scores - jnp.max(scores, axis=1, keepdims=True))
        found_probs = weights / jnp.sum(weights, axis=1, keepdims=True)
        probs[at, :] = found_probs
        probs_low = narrow(found_probs)
        prob_grad[1, at, :] = probs_low
        mix_s[pl.ds(n * each, each)] = narrow(own_dot(probs_low, head_of(2), 1, 0)).reshape(each, rows, chunk)
        return carry

    lax.fori_loop(0, head_rows // per, head_forward, 0, unroll=2)

    def send_mixed(step, carry):
        peer, where = to_plane(step)
        push(mix_s.at[block_of(peer)], mix_b.at[:, lanes_of(j)], a_send.at[0], a_recv.at[0], where)
        return carry

    lax.fori_loop(1, grid_cols, send_mixed, 0)
    background(1)
    mix_b[:, lanes_of(j)] = mix_s[mine]
    loads[SO].wait()
    wait_for(mix_b.at[:, pl.ds(0, chunk * (grid_cols - 1))], a_recv.at[0])
    mixed_rows = mix_b[...]
    xbuf[XS[3], core, quad] = mixed_rows
    times(mixed_rows, SO, tmp)
    relay_x(4)
    third = act[SECOND] + tmp[...] + bs[4:5]
    act[THIRD] = third
    normed_s = norm_forward(third, gs[1:2], bs[1:2])
    xbuf[XS[5], core, quad] = normed_s
    background(2)
    loads[S1].wait()
    times(normed_s, S1, tmp)
    pre = tmp[...] + bs[5:6]
    act[PRE_S] = pre
    hidden_s = narrow(gelu_value(pre))
    spread_plain(5, hidden_s)
    background(3)
    times(hidden_s, S2, tmp)
    new_latents[...] = narrow(act[THIRD] + tmp[...] + bs[6:7])

    d_pre = act[COT_BACK] * gelu_slope(act[PRE_S])
    pre_low = narrow(d_pre)
    times_t(pre_low, S1, tmp)
    d_rows, lnvec[6:7, :], lnvec[7:8, :] = norm_gradient(act[THIRD], gs[1:2], tmp[...])
    gradient = to_float(cot_low) + d_rows
    act[GRAD] = gradient
    out_low = narrow(gradient)
    times_t(out_low, SO, tmp)
    mix_b2 = narrow(tmp[...])
    gsrc[12] = mix_b2

    def send_dmixed(step, carry):
        peer, where = to_plane(step)
        push(gsrc.at[12, :, lanes_of(peer)], dmix_b.at[mine], a_send.at[1], a_recv.at[1], where)
        return carry

    lax.fori_loop(1, grid_cols, send_dmixed, 0)
    dmix_b[mine] = gsrc[12, :, lanes_of(j)]
    background(4)
    spread_g(4, pre_low)
    line_hidden(C1, biases.at[5:6])
    have_x(6)
    weight_part(8, have_g(5), xbuf.at[XS[6]])
    spread_g(6, out_low)
    background(5)
    wait_for(dmix_b.at[pl.ds(0, grid_cols - 1)], a_recv.at[1])

    def from_heads(kind):
        def one(step, carry):
            peer, where = to_plane(step)
            push(
                dqkv_s.at[kind, block_of(peer)], dqkv_b.at[kind, :, lanes_of(j)],
                a_send.at[7 + kind], a_recv.at[7 + kind], where,
            )
            return carry

        lax.fori_loop(1, grid_cols, one, 0)
        dqkv_b[kind, :, lanes_of(j)] = dqkv_s[kind, mine]

    def rows_back(kind):
        wait_for(dqkv_b.at[kind, :, pl.ds(0, chunk * (grid_cols - 1))], a_recv.at[7 + kind])
        wait_for(heads.at[kind, pl.ds(0, grid_cols - 1)], a_send.at[4 + kind])
        spread_g(9 + kind, dqkv_b[kind])

    def put_head(kind, n, values):
        dqkv_s[kind, pl.ds(n * each, each)] = narrow(values).reshape(each, rows, chunk)

    d_mixed_all = dmix_b[...].reshape(head_rows, chunk)

    def head_values(n, carry):
        at = pl.ds(pl.multiple_of(n * per, per), per)
        put_head(2, n, own_dot(prob_grad[1, :, at], d_mixed_all, 0, 0))
        return carry

    def head_queries(n, carry):
        at = pl.ds(pl.multiple_of(n * per, per), per)
        d_mixed = dmix_b[pl.ds(n * each, each)].reshape(per, chunk)
        d_probs = own_dot(d_mixed, head_of(2), 1, 1)
        found_probs = probs[at, :]
        d_scores = found_probs * (d_probs - jnp.sum(found_probs * d_probs, axis=1, keepdims=True))
        d_low = narrow(d_scores * head_scale)
        prob_grad[0, at, :] = d_low
        put_head(0, n, own_dot(d_low, head_of(1), 1, 0))
        return carry

    def head_keys(n, carry):
        at = pl.ds(pl.multiple_of(n * per, per), per)
        put_head(1, n, own_dot(prob_grad[0, :, at], head_of(0), 0, 0))
        return carry

    lax.fori_loop(0, head_rows // per, head_values, 0, unroll=2)
    from_heads(2)
    background(6)
    lax.fori_loop(0, head_rows // per, head_queries, 0, unroll=2)
    from_heads(0)
    background(7)
    relay_x(3)
    lax.fori_loop(0, head_rows // per, head_keys, 0, unroll=2)
    from_heads(1)
    background(8)
    join_rows(staged.at[slot_of(8)], 8)

    def column_sum(values):
        return jnp.sum(to_float(values), axis=0, keepdims=True)

    have_x(3)
    right = have_g(6)
    bias_s4 = column_sum(right)
    weight_part(9, right, xbuf.at[XS[3]])
    rows_back(2)
    times_t(dqkv_b[2], SV, tmp)
    rows_back(0)
    times_t(dqkv_b[0], SQ, tmp, True)
    rows_back(1)
    times_t(dqkv_b[1], SK, tmp, True)
    background(9)
    x_spread(xsmall.at[0, core, quad], 8)
    d_rows, lnvec[4:5, :], lnvec[5:6, :] = norm_gradient(act[SECOND], gs[0:1], tmp[...])
    gradient = act[GRAD] + d_rows
    act[GRAD] = gradient
    second_low = narrow(gradient)
    spread_columns(2, second_low)
    lnvec[9:10, :] = jnp.sum(gradient, axis=0, keepdims=True)
    background(10)
    times_t(second_low, C2, tmp)
    d_pre = tmp[...] * gelu_slope(act[PRE_C])
    pre_low = narrow(d_pre)
    spread_columns(1, pre_low)
    lnvec[10:11, :] = jnp.sum(d_pre, axis=0, keepdims=True)
    background(11)
    join(9)
    have_x(4)
    for k in (2, 0, 1):
        right = have_g(9 + k)
        if k == 0:
            bias_s2 = column_sum(right)
        elif k == 2:
            bias_s3 = column_sum(right)
        weight_part(4 + k, right, xbuf.at[XS[4]])
    times_t(pre_low, C1, tmp)
    d_rows, lnvec[2:3, :], lnvec[3:4, :] = norm_gradient(act[FIRST], gc[1:2], tmp[...])
    gradient = act[GRAD] + d_rows
    act[GRAD] = gradient
    out_low = narrow(gradient)
    spread_g(3, out_low)
    relay_x(5)
    times_t(out_low, CO, tmp)
    d_attended = narrow(tmp[...])
    spread_g(8, d_attended)
    background(12)
    line_part(2, line_hid)
    line_part(1, line_rows)
    line_join(2)
    have_x(5)
    right = have_g(4)
    bias_s5 = column_sum(right)
    weight_part(7, right, xbuf.at[XS[5]])

    grad_inputs = own_dot(d_attended, win[1], 1, 1)
    d_attended = to_float(d_attended)
    shift = grad_inputs[:, 2 * LANES + 5 : 2 * LANES + 6]
    row_delta = jnp.sum(d_attended * act[ATT], axis=1, keepdims=True) - shift
    grad_shift = jnp.sum(grad_inputs * bin_, axis=1, keepdims=True)
    grad_scaled = grad_inputs * gin
    turned = coefficients(grad_scaled, grad_shift - row_delta)
    constant = turned[6:7]

    def away(scaled):
        values = scaled[:, 2 * LANES :] - jnp.sum(scaled, axis=1, keepdims=True) * (1.0 / count)
        values = jnp.where(lane1 < 3, values, 0.0)
        return jnp.concatenate([values, pltpu.roll(values, 8, 1)], axis=0)

    query_away, grad_away = away(query_scaled), away(grad_scaled)
    wide_lane = lax.broadcasted_iota(jnp.int32, (LANES, LANES), 1)
    wide_half = lax.broadcasted_iota(jnp.int32, (LANES, LANES), 0) // rows
    blank = jnp.zeros((LANES, LANES), bf16)
    for held in range(STEPS_HELD):
        group = wide_lane - held * 16 - wide_half * 8
        along = narrow(jnp.where((group >= 0) & (group < 3), 1.0, 0.0))
        colors_here = [query_away, grad_away]
        if held:
            colors_here = [pltpu.roll(v, held * 16, 1) for v in colors_here]
        cgright[held // 2, (held % 2) * WIDE : (held % 2 + 1) * WIDE, :] = jnp.concatenate(
            [
                jnp.concatenate([narrow(colors_here[0]), blank], axis=1),
                jnp.concatenate([narrow(colors_here[1]), blank], axis=1),
                jnp.concatenate([blank, along], axis=1),
            ],
            axis=0,
        )
    rowsum[...] = jnp.zeros(rowsum.shape, f32)
    colsum[...] = jnp.zeros(colsum.shape, f32)

    def kept_at(s):
        place_now = lax.rem(s, 6)
        line = pl.ds(pl.multiple_of((place_now // 2) * tall, 32), tall)
        lane = pl.ds(pl.multiple_of(lax.rem(place_now, 2) * WIDE, LANES), WIDE)
        return wts.at[4 + s // 6, line, lane]

    def back_pass(s, carry):
        total, found = carry
        lines, deviation = step_lines(s)
        scores = sl[s]
        found_probs = jnp.exp(scores - log_total)
        d_scores = found_probs * (lines + constant)
        kept_at(s)[...] = jnp.concatenate(
            [narrow(d_scores), narrow(found_probs), narrow(d_scores * scores + found_probs * lines)], axis=1
        )
        total = total + jnp.sum(d_scores, axis=0, keepdims=True)
        return total, found, d_scores * deviation

    def color_block(block):
        result = None
        for pair in range(block * STEPS_HELD // 2, min((block + 1) * STEPS_HELD, steps) // 2):
            line = pl.ds((pair % 3) * tall, tall)
            left = wts[4 + pair // 3, line, pl.ds(0, 2 * WIDE)]
            part = own_dot(left, cgright[pair % (STEPS_HELD // 2)], 1, 0)
            result = part if result is None else result + part
        cgacc[block] = result

    carry = (jnp.zeros((1, LANES), f32), jnp.zeros((8, LANES), f32))
    third_of = steps // 3
    line_join(1)
    x_relay(xsmall.at[0, core], 8)
    carry = in_groups(back_pass, 0, third_of, carry)
    finish_rows(8)
    join(6)
    carry = in_groups(back_pass, third_of, 2 * third_of, carry)
    join(4)
    x_arrived(xsmall.at[0, 1 - core], 8)
    right = have_g(3)
    bias_c4 = column_sum(right)
    small_part(2, right, xsmall.at[0])
    right = have_g(8)
    bias_c3 = column_sum(right)
    small_part(1, right, xsmall.at[0])
    total, found = in_groups(back_pass, 2 * third_of, steps, carry)
    join(5)
    plain_scores = pixel_sums(found, 1.0) * score_scale
    total = total * score_scale
    score_total = fold(jnp.transpose(jnp.concatenate([total, jnp.zeros((LANES - 1, LANES), f32)], axis=0)))[:, 0:1]
    score_low = narrow(plain_scores * gin + score_total * bin_)
    xsmall[1, core, quad] = score_low

    def d_query_part(n, carry):
        at = pl.ds(pl.multiple_of(n * 256, 256), 256)
        tmp[:, at] = own_dot(score_low, win[0, :, at], 1, 0)
        return carry

    lax.fori_loop(0, width // 256, d_query_part, 0, unroll=4)
    query_grad_low = narrow(tmp[...])
    spread_g(0, query_grad_low)
    x_spread(xsmall.at[1, core, quad], 9)
    gain_part = jnp.sum(query_inputs * plain_scores + grad_inputs * plain_mixed, axis=0, keepdims=True)
    bias_part = jnp.sum(query_inputs * score_total + grad_inputs, axis=0, keepdims=True)
    cuts = [part[:, k * LANES : (k + 1) * LANES] for part in (gain_part, bias_part) for k in range(3)]
    shared = jnp.concatenate(cuts + [jnp.zeros((1, LANES), f32)], axis=0)
    times_t(query_grad_low, CQ, tmp)
    d_rows, lnvec[0:1, :], lnvec[1:2, :] = norm_gradient(to_float(latents[...]), gc[0:1], tmp[...])
    latent_grad[...] = act[GRAD] + d_rows
    lnvec[8:9, :] = jnp.sum(to_float(cotangent[...]), axis=0, keepdims=True)
    lines = regroup(lnvec[...])
    for peer in range(grid_cols):
        lnsend[peer] = jnp.concatenate(
            [lines[:11, peer * chunk : (peer + 1) * chunk], shared, jnp.zeros((6, LANES), f32)], axis=0
        )

    def send_ln(step, carry):
        peer, where = to_plane(step)
        push(lnsend.at[peer], lnbuf.at[j], misc_send.at[2], misc_recv.at[2], where)
        return carry

    lax.fori_loop(1, grid_cols, send_ln, 0)
    lnbuf[j] = lnsend[j]
    join(7)
    for block in range(0, blocks // 2):
        color_block(block)
    have_x(0)
    right = have_g(0)
    bias_c2 = column_sum(right)
    weight_part(0, right, xbuf.at[0])
    x_relay(xsmall.at[1, core], 9)
    for block in range(blocks // 2, blocks - 1):
        color_block(block)
    color_block(blocks - 1)
    x_arrived(xsmall.at[1, 1 - core], 9)
    small_part(0, have_g(7), xsmall.at[1])
    for m in (2, 1):
        join_small(m)

    for block in range(blocks):
        both = own_dot(fa[block], spread[...], 1, 0)
        center, factor = both[:, :LANES], both[:, LANES:]
        here = cgacc[block]
        cgacc[block, :, :LANES] = factor * (
            here[:, :LANES] - (to_float(fa[block]) - center) * factor * here[:, LANES:] * (1.0 / count)
        )
    for part in range(grid_rows):
        at = pl.ds(part * tile_rows, tile_rows)
        lines = jnp.concatenate([narrow(cgacc[block, at, :LANES]) for block in range(blocks)], axis=1)
        tiles = narrow(own_dot(back[...], lines, 1, 1))
        for tile in range(grid_cols):
            cgsend[tile, part, :, :tile_rows] = tiles[tile * 32 : tile * 32 + 32]
    cgbuf[j] = cgsend[j]

    def send_cg(step, carry):
        peer, where = to_plane(step)
        push(cgsend.at[peer], cgbuf.at[j], misc_send.at[3], misc_recv.at[3], where)
        return carry

    lax.fori_loop(1, grid_cols, send_cg, 0)

    wait_for(lnbuf.at[pl.ds(0, grid_cols - 1)], misc_recv.at[2])
    norms = lnbuf[0]
    for peer in range(1, grid_cols):
        norms = norms + lnbuf[peer]
    vecsend[...] = jnp.concatenate(
        [
            norms[:8], bias_c2, bias_c3, bias_c4, norms[10:11], norms[9:10], bias_s2, bias_s3,
            bias_s4, bias_s5, norms[8:9], jnp.zeros((6, chunk), f32), norms[11:18], jnp.zeros((1, chunk), f32),
        ],
        axis=0,
    )

    def send_vec(step, carry):
        where = {"rows": lax.rem(z + step, grid_rows)}
        push(vecsend, vecbuf.at[z], misc_send.at[4], misc_recv.at[4], where)
        return carry

    lax.fori_loop(1, grid_rows, send_vec, 0)
    vecbuf[z] = vecsend[...]
    join(0)
    join_small(0)
    wait_for(cgbuf.at[pl.ds(0, grid_cols - 1)], misc_recv.at[3])
    tiles = to_float(cgbuf[0])
    for peer in range(1, grid_cols):
        tiles = tiles + to_float(cgbuf[peer])
    cgsum[...] = tiles

    def send_tile(step, carry):
        part = lax.rem(z + step, grid_rows)
        push(cgsum.at[part], cgfin.at[z], misc_send.at[6], misc_recv.at[6], {"rows": part})
        return carry

    lax.fori_loop(1, grid_rows, send_tile, 0)
    cgfin[z] = cgsum[z]

    wait_for(vecbuf.at[pl.ds(0, grid_rows - 1)], misc_recv.at[4])
    vectors = vecbuf[0]
    for part in range(1, grid_rows):
        vectors = vectors + vecbuf[part]
    vector_out[...] = vectors[:24]
    input_vector_out[...] = vectors[24:]
    for m in (2, 1):
        line_total(m)
    for m in (7, 4, 5, 6, 9, 0):
        wait_for(crossed.at[slot_of(m)], f_recv.at[m])
        result = kept_of(m)[...] + to_float(crossed[slot_of(m)])
        kept_of(m)[...] = result
    wait_for(row_done.at[:, pl.ds(0, chunk * (grid_cols - 1))], a_recv.at[3])
    self_total[4] = row_done[...]
    sums = []
    for m in (2, 1, 0):
        wait_for(crossed_small.at[m], f_recv.at[10 + m])
        sums.append(kept_small[m] + to_float(crossed_small[m]))
    out_total[...] = own_dot(narrow(sums[0]), win[1], 1, 0)
    input_parts[1] = sums[1]
    input_parts[0] = sums[2]
    wait_for(cgfin.at[pl.ds(0, grid_rows - 1)], misc_recv.at[6])
    color_out[...] = cgfin[...]

    for k in (0, 3, 4, 5, 6):
        wait_for(xbuf.at[XS[k], 0, pl.ds(0, quads - 1)], x_send.at[k])
        wait_for(xbuf.at[XS[k], 0], y_send.at[k])
    wait_for(line_rows.at[pl.ds(0, grid_rows - 1)], x_send.at[1])
    for m in (1, 2):
        wait_for(line_right.at[m - 1, pl.ds(0, grid_rows - 1)], g_send.at[m])
        wait_for(line_near.at[m - 1], y_send.at[m])
        wait_for(line_sums.at[m - 1, pl.ds(0, quads - 1)], l_send.at[m - 1])
    for k in range(2):
        wait_for(xsmall.at[k, 0, pl.ds(0, quads - 1)], x_send.at[8 + k])
        wait_for(xsmall.at[k, 0], y_send.at[8 + k])
    for k in (0, 3, 4, 5, 6, 7, 8, 9, 10, 11):
        wait_for(gsrc.at[k, :, pl.ds(0, chunk * (grid_cols - 1))], g_send.at[k])
    wait_for(mix_s.at[pl.ds(0, grid_cols - 1)], a_send.at[0])
    wait_for(dmix_b.at[pl.ds(0, grid_cols - 1)], a_send.at[1])
    for kind in range(3):
        wait_for(dqkv_s.at[kind, pl.ds(0, grid_cols - 1)], a_send.at[7 + kind])
    wait_for(colbuf.at[pl.ds(0, grid_cols - 1)], misc_send.at[0])
    wait_for(row_turned.at[pl.ds(0, own * (grid_cols - 1))], a_send.at[3])
    wait_for(lnbuf.at[pl.ds(0, grid_cols - 1)], misc_send.at[2])
    wait_for(cgbuf.at[pl.ds(0, grid_cols - 1)], misc_send.at[3])
    wait_for(colstage.at[pl.ds(0, grid_rows - 1)], misc_send.at[5])
    wait_for(cgfin.at[pl.ds(0, grid_rows - 1)], misc_send.at[6])
    wait_for(row_pair, r_send.at[8])
    wait_for(row_hand, f_send.at[8])
    for m in (0, 4, 5, 6, 7, 9):
        wait_for(paired.at[slot_of(m)], r_send.at[m])
        wait_for(handed.at[slot_of(m)], f_send.at[m])
    for m in range(3):
        wait_for(paired_small.at[m], r_send.at[10 + m])
        wait_for(handed_small.at[m], f_send.at[10 + m])
    wait_for(vecbuf.at[pl.ds(0, grid_rows - 1)], misc_send.at[4])


def channel_order(count):
    n = NBANDS
    starts = ((5, n), (5 + 2 * n, n), (5 + n, n), (5 + 3 * n, n), (0, 5))
    order = np.concatenate([np.arange(start, start + size) for start, size in starts])
    result = np.zeros((WIDE, count), np.float32)
    result[np.arange(count), order] = 1
    return np.asarray(result, ml_dtypes.bfloat16)


def by_channel(lines):
    n = NBANDS
    parts = [lines[..., 4 * n : 4 * n + 5], lines[..., :n], lines[..., 2 * n : 3 * n]]
    parts += [lines[..., n : 2 * n], lines[..., 3 * n : 4 * n]]
    return jnp.concatenate(parts, axis=-1)


def finish_kernel(
    own, tile_rows, tile_cols,
    latents, latent_grad, colors, cross, out, self_parts, self_out, inputs, vectors, input_vectors,
    prior_cross, prior_out, prior_input,
    o_latents, o_latent_grad, o_colors, o_cross, o_out, o_input, o_gain, o_bias,
    o_cross_gains, o_cross_biases, o_self, o_self_out, o_self_gains, o_self_biases,
):
    o_latents[...] = latents[...]
    o_latent_grad[...] = latent_grad[...]
    for channel in range(3):
        for col in range(tile_cols):
            line = channel * tile_cols + col
            for image in range(colors.shape[0]):
                o_colors[channel, col, image : image + 1, :] = colors[image, line : line + 1, :tile_rows]
    o_cross[...] = prior_cross[...] + cross[...]
    o_out[...] = prior_out[...] + out[...]
    o_self[...] = self_parts[...]
    o_self_out[...] = self_out[...]
    for k in range(2):
        o_input[k] = prior_input[k] + by_channel(inputs[k])
    lines = input_vectors[...]
    for k, target in enumerate((o_gain, o_bias)):
        wide = jnp.concatenate([lines[3 * k + t : 3 * k + t + 1] for t in range(3)], axis=1)
        target[...] = by_channel(wide).reshape(-1)
    place = lax.axis_index("rows")
    width = vectors.shape[1]
    mine = pltpu.roll(vectors[...], lax.rem(width - place * own, width), 1)[:, :own]
    for target, rows in (
        (o_cross_gains, (0, 2)),
        (o_cross_biases, (1, 3, 8, 9, 10, 11, 12)),
        (o_self_gains, (4, 6)),
        (o_self_biases, (5, 7, 13, 14, 15, 16, 17)),
    ):
        for k, row in enumerate(rows):
            target[k : k + 1, :] = mine[row : row + 1]


def local_kernel(
    latents,
    pixel_colors,
    image_boxes,
    cotangent,
    cross_matrices,
    cross_out,
    input_matrices,
    in_gain,
    in_bias,
    cross_gains,
    cross_biases,
    self_matrices,
    self_out,
    self_gains,
    self_biases,
    prior_cross_matrices,
    prior_cross_out,
    prior_input_matrices,
):
    rows, width = latents.shape
    channels, image_count, tile_rows, tile_cols = pixel_colors.shape
    grid_rows = lax.axis_size("rows")
    grid_cols = lax.axis_size("cols")
    n_dev = grid_rows * grid_cols
    tall, wide = grid_rows * tile_rows, grid_cols * tile_cols
    steps = wide // 2
    chunk = width // grid_cols
    own = chunk // grid_rows
    quads = grid_cols // 2
    place, pick, spread, back = selections(tile_cols, grid_cols, steps)
    blocks = back.shape[1] // LANES
    held_rows = -(-steps // 8) * 8
    order = channel_order(input_matrices.shape[1])
    f32, bf16 = jnp.float32, jnp.bfloat16
    vmem = pl.BlockSpec(memory_space=pltpu.VMEM)
    away = pl.BlockSpec(memory_space=pl.ANY)
    shape = jax.ShapeDtypeStruct
    sizes = (grid_rows, grid_cols, rows, steps, tile_rows, tile_cols)
    dma = pltpu.SemaphoreType.DMA
    scratch = [
        ((10, width, width), bf16),
        ((2, WIDE, width), bf16),
        ((input_matrices.shape[1], 2, width), bf16),
        ((5, 2, quads, rows, width), bf16),
        ((2, 2, quads, rows, WIDE), bf16),
        ((13, rows, width), bf16),
        ((12, 2, quads, rows, chunk), bf16),
        ((7, chunk, width), bf16),
        ((7, 2, own, width), bf16),
        ((7, own, width), bf16),
        ((7, own, width), bf16),
        ((3, chunk, WIDE), bf16),
        ((3, 2, own, WIDE), bf16),
        ((3, own, WIDE), bf16),
        ((3, own, WIDE), bf16),
        ((3, own, WIDE), f32),
        ((grid_rows, rows, width), bf16),
        ((grid_rows, rows, width), bf16),
        ((2, grid_rows, rows, width // grid_rows), bf16),
        ((2, width // grid_rows, width), bf16),
        ((2, quads, own, width), bf16),
        ((2, quads, own, width), bf16),
        ((2, quads, own, width), bf16),
        ((2, chunk, width // grid_rows), bf16),
        ((chunk, width // grid_rows), bf16),
        ((chunk, width // grid_rows), bf16),
        ((chunk, width // grid_rows), f32),
        ((width // grid_rows, chunk), f32),
        ((own, width), f32),
        ((8, width), f32),
        ((grid_rows, 32, LANES), bf16),
        ((grid_rows, 32, LANES), bf16),
        ((grid_cols, grid_rows, 32, LANES), bf16),
        ((tall, WIDE), f32),
        ((tall, 7 * LANES), bf16),
        ((blocks, tall, LANES), bf16),
        ((blocks * LANES, tall), bf16),
        ((steps, tall, LANES), f32),
        ((tall, LANES), f32),
        ((held_rows, LANES), f32),
        ((tall, 2 * LANES), bf16),
        ((2, held_rows, 2 * LANES), bf16),
        ((STEPS_HELD, LANES, 2 * LANES), bf16),
        ((STEPS_HELD // 2, 2 * WIDE, 2 * LANES), bf16),
        ((tall, LANES), f32),
        ((held_rows, LANES), f32),
        ((blocks, tall, 2 * LANES), f32),
        ((grid_cols, grid_rows, 32, LANES), bf16),
        ((grid_cols, grid_rows, 32, LANES), bf16),
        ((grid_rows, 32, LANES), f32),
        ((grid_rows, 32, LANES), f32),
        ((8, rows, width), f32),
        ((16, width), f32),
        ((grid_cols, 24, chunk), f32),
        ((grid_cols, 24, chunk), f32),
        ((32, chunk), f32),
        ((grid_rows, 32, chunk), f32),
        ((3, grid_cols, rows, chunk), bf16),
        ((grid_cols * rows, grid_cols * rows), f32),
        ((2, grid_cols * rows, grid_cols * rows), bf16),
        ((grid_cols, rows, chunk), bf16),
        ((rows, width), bf16),
        ((grid_cols, rows, chunk), bf16),
        ((3, grid_cols, rows, chunk), bf16),
        ((3, rows, width), bf16),
    ]
    fixed = (order, place, pick, spread, back)
    scratch = [(values.shape, bf16) for values in fixed] + scratch
    scratch = [pltpu.VMEM(dims, kind) for dims, kind in scratch]
    scratch += [dma((count,)) for count in (5, 11, 10, 10, 10, 10, 12, 12, 10, 10, 13, 13, 13, 13, 2, 2, 7, 7)]
    outs = [
        ((rows, width), bf16),
        ((rows, width), f32),
        ((image_count, 32, LANES), f32),
        ((3, own, width), f32),
        ((own, width), f32),
        ((5, own, width), f32),
        ((own, width), f32),
        ((2, own, WIDE), f32),
        ((24, chunk), f32),
        ((8, LANES), f32),
    ]
    results = pl.pallas_call(
        functools.partial(layer_kernel, sizes),
        out_shape=[shape(dims, kind) for dims, kind in outs],
        in_specs=[pl.BlockSpec(memory_space=pltpu.SMEM)] + [vmem] * 9 + [away] * 10,
        out_specs=[vmem] * len(outs),
        scratch_shapes=scratch,
        compiler_params=pltpu.CompilerParams(
            collective_id=0, has_side_effects=True, vmem_limit_bytes=VMEM_BYTES
        ),
        cost_estimate=pl.CostEstimate(
            flops=20_000_000_000, bytes_accessed=40_000_000, transcendentals=4_000_000
        ),
    )(
        image_boxes,
        latents,
        cotangent,
        jnp.transpose(pixel_colors, (0, 3, 1, 2)),
        in_gain,
        in_bias,
        cross_gains,
        cross_biases,
        self_gains,
        self_biases,
        *fixed,
        cross_matrices,
        cross_out,
        self_matrices,
        self_out,
        jnp.transpose(input_matrices, (1, 0, 2)),
    )
    count = input_matrices.shape[1]
    last = [
        ((rows, width), bf16),
        ((rows, width), f32),
        ((channels, tile_cols, image_count, tile_rows), f32),
        ((3, own, width), f32),
        ((own, width), f32),
        ((2, own, count), f32),
        ((count,), f32),
        ((count,), f32),
        ((2, own), f32),
        ((7, own), f32),
        ((5, own, width), f32),
        ((own, width), f32),
        ((2, own), f32),
        ((7, own), f32),
    ]
    done = pl.pallas_call(
        functools.partial(finish_kernel, own, tile_rows, tile_cols),
        out_shape=[shape(dims, kind) for dims, kind in last],
        in_specs=[vmem] * (len(outs) + 3),
        out_specs=[vmem] * len(last),
        compiler_params=pltpu.CompilerParams(vmem_limit_bytes=VMEM_BYTES),
    )(
        *results,
        jnp.transpose(prior_cross_matrices, (0, 2, 1)),
        jnp.transpose(prior_cross_out),
        jnp.transpose(prior_input_matrices, (0, 2, 1)),
    )
    (new_latents, latent_grad, colors, cross_total, out_total, input_total, gain, bias) = done[:8]
    cross_gain, cross_bias, self_total, self_out_total, self_gain, self_bias = done[8:]
    return (
        new_latents,
        latent_grad,
        jnp.transpose(colors, (0, 2, 3, 1)),
        jnp.transpose(cross_total, (0, 2, 1)),
        jnp.transpose(out_total),
        jnp.transpose(input_total, (0, 2, 1)),
        gain,
        bias,
        cross_gain,
        cross_bias,
        jnp.transpose(self_total, (0, 2, 1)),
        jnp.transpose(self_out_total),
        self_gain,
        self_bias,
    )


def solution(mesh):
    placed = (
        P(("rows", "cols"), None),
        P(None, None, "rows", "cols"),
        P(),
        P(("rows", "cols"), None),
        P(),
        P(),
        P(),
        P(),
        P(),
        P(),
        P(),
        P(),
        P(),
        P(),
        P(),
        P(None, None, ("rows", "cols")),
        P(None, ("rows", "cols")),
        P(None, None, ("rows", "cols")),
    )
    one_head_each = mesh.shape["cols"] == HEADS
    return jax.shard_map(
        local_kernel if one_head_each else local,
        mesh=mesh,
        in_specs=placed,
        out_specs=(
            P(("rows", "cols"), None),
            P(("rows", "cols"), None),
            P(None, None, "rows", "cols"),
            P(None, None, ("rows", "cols")),
            P(None, ("rows", "cols")),
            P(None, None, ("rows", "cols")),
            P(),
            P(),
            P(None, ("rows", "cols")),
            P(None, ("rows", "cols")),
            P(None, None, ("rows", "cols")),
            P(None, ("rows", "cols")),
            P(None, ("rows", "cols")),
            P(None, ("rows", "cols")),
        ),
        check_vma=False,
    )
```
